32 devices in a mesh: dp: 4 (over y, x), wide: 8 (over z, core).
Axes of the slice: x: 2, y: 2, z: 4, core: 2. Of those that a mesh axis runs over, the one named last changes fastest.
Arguments:
- images: bfloat16 [2048, 49, 192], P(('dp', 'wide')), may hold values from -18 to 18
- dom_label: int32 [2048], P(('dp', 'wide')), may hold values from 0 to 7, as said below
- class_label: int32 [2048], P(('dp', 'wide')), may hold values from 0 to 999
- expand_weight: float32 [1152, 1536], P('wide'), may hold values from -0.3125 to 0.3125
- expand_first: float32 [1152, 1536], P('wide'), may hold values from -0.0006629126 to 0.0006629126
- expand_second: float32 [1152, 1536], P('wide'), may hold values from 6.1035155e-09 to 2.4414062e-08
- expand_state: float32 [2, 8, 1152, 4], P(None, None, 'wide'), may hold values from -1 to 1, as said below
- project_weight: float32 [320, 9216], P('wide'), may hold values from -0.125 to 0.125
- project_first: float32 [320, 9216], P('wide'), may hold values from -0.0006629126 to 0.0006629126
- project_second: float32 [320, 9216], P('wide'), may hold values from 6.103516e-08 to 2.4414064e-07
- project_state: float32 [2, 8, 320, 4], P(None, None, 'wide'), may hold values from -1 to 1, as said below
- head_weight: float32 [1280, 2560], P('wide'), may hold values from -0.25 to 0.25
- head_first: float32 [1280, 2560], P('wide'), may hold values from -0.0006629126 to 0.0006629126
- head_second: float32 [1280, 2560], P('wide'), may hold values from 6.103516e-08 to 2.4414064e-07
- head_state: float32 [2, 8, 1280, 4], P(None, None, 'wide'), may hold values from -1 to 1, as said below
- depth_weight: float32 [8, 9, 1152], P(None, None, 'wide'), may hold values from -1.5 to 1.5
- depth_first: float32 [8, 9, 1152], P(None, None, 'wide'), may hold values from -0.0006629126 to 0.0006629126
- depth_second: float32 [8, 9, 1152], P(None, None, 'wide'), may hold values from 6.103516e-08 to 2.4414064e-07
- classifier_weight: float32 [1280, 1000], P('wide'), may hold values from -0.3125 to 0.3125
- classifier_first: float32 [1280, 1000], P('wide'), may hold values from -0.00041926274 to 0.00041926274
- classifier_second: float32 [1280, 1000], P('wide'), may hold values from 2.4414062e-08 to 9.765625e-08
- excite_weight: float32 [2, 1152, 48], replicated, may hold values from -0.4 to 0.4
- excite_first: float32 [2, 1152, 48], replicated, may hold values from -0.0006629126 to 0.0006629126
- excite_second: float32 [2, 1152, 48], replicated, may hold values from 6.103516e-08 to 2.4414064e-07
- router_weight: float32 [512, 8], replicated, may hold values from -1.25 to 1.25
- router_first: float32 [512, 8], replicated, may hold values from -0.0006629126 to 0.0006629126
- router_second: float32 [512, 8], replicated, may hold values from 6.103516e-08 to 2.4414064e-07
- gains_weight: float32 [5400], replicated, may hold values from 0.5 to 1.5
- gains_first: float32 [5400], replicated, may hold values from -0.0013258252 to 0.0013258252
- gains_second: float32 [5400], replicated, may hold values from 2.4414064e-07 to 9.765625e-07
Outputs:
- loss: float32 [], replicated
- expand_moment: float32 [1152, 1536], P('wide')
- expand_rotated: float32 [1152, 1536], P('wide')
- expand_basis: float32 [2, 8, 1152, 4], P(None, None, 'wide')
- expand_master: float32 [1152, 1536], P('wide')
- project_moment: float32 [320, 9216], P('wide')
- project_rotated: float32 [320, 9216], P('wide')
- project_basis: float32 [2, 8, 320, 4], P(None, None, 'wide')
- project_master: float32 [320, 9216], P('wide')
- head_moment: float32 [1280, 2560], P('wide')
- head_rotated: float32 [1280, 2560], P('wide')
- head_basis: float32 [2, 8, 1280, 4], P(None, None, 'wide')
- head_master: float32 [1280, 2560], P('wide')
- depth_moment: float32 [8, 9, 1152], P(None, None, 'wide')
- depth_squares: float32 [8, 9, 1152], P(None, None, 'wide')
- depth_master: float32 [8, 9, 1152], P(None, None, 'wide')
- classifier_moment: float32 [1280, 1000], P('wide')
- classifier_squares: float32 [1280, 1000], P('wide')
- classifier_master: float32 [1280, 1000], P('wide')
- excite_moment: float32 [2, 1152, 48], replicated
- excite_squares: float32 [2, 1152, 48], replicated
- excite_master: float32 [2, 1152, 48], replicated
- router_moment: float32 [512, 8], replicated
- router_squares: float32 [512, 8], replicated
- router_master: float32 [512, 8], replicated
- gains_moment: float32 [5400], replicated
- gains_squares: float32 [5400], replicated
- gains_master: float32 [5400], replicated
The draws below stay inside these ranges and needn't reach their ends.
Inputs may be any that keep to these rules, and one draw needn't show every extreme that they name: `dom_label`: nondecreasing along the images, so that the images come grouped by dominant expert; every expert is some image's, some far more often than others. `expand_state`: first half: per expert and block of 4 output channels a positive diagonal matrix of trace one; second half: an orthogonal matrix per block. `project_state`: as expand_state. `head_state`: as expand_state.
All inputs are finite; a program needn't handle non-finite values.
Results may differ from the reference program's by a relative error of at most 0.02.
Values may be sent and summed in bfloat16 or wider, within the bound.
A program may use at most 576 MiB of HBM per device.

```python
import math
import jax
import jax.numpy as jnp
from jax import lax

IMG_DEV = 64
IMAGES = 2048
SIDE = 7
PIX = 49
KSIZE = 3
EXPERTS = 8
BLK = 4
STEP = 10
C_IN = 192
C_MID = 1152
C_SE = 48
C_OUT = 320
C_HEAD = 1280
CLASSES = 1000
VEC = 5400


def draw_images(key, part):
    key = jax.random.fold_in(key, 11)
    rise = jnp.arange(IMAGES, dtype=jnp.float32) / (IMAGES - 1)
    base = jnp.clip(jax.random.normal(key, (IMAGES, PIX, C_IN), jnp.float32), -6.0, 6.0)
    scale = 1.0 + 2.0 * rise
    return (base * scale[:, None, None]).astype(jnp.bfloat16)


def draw_dom_label(key, part):
    key = jax.random.fold_in(key, 12)
    first, second = jax.random.split(key)
    raw = jax.random.randint(first, (IMAGES,), 0, 36)
    raw = raw.at[:EXPERTS].set(jnp.array([0, 16, 24, 28, 31, 33, 34, 35], dtype=jnp.int32))
    edges = jnp.array([16, 24, 28, 31, 33, 34, 35], dtype=jnp.int32)
    level = jnp.sum((raw[:, None] >= edges[None, :]).astype(jnp.int32), axis=1)
    order = jax.random.permutation(second, EXPERTS).astype(jnp.int32)
    return jnp.sort(order[level])


def block_state(key, width):
    first, second, third = jax.random.split(key, 3)
    diag = jnp.exp(jax.random.uniform(first, (EXPERTS, width // BLK, BLK), jnp.float32, 0.0, 1.3862944))
    diag = diag / jnp.sum(diag, axis=-1, keepdims=True)
    eye = jnp.eye(BLK, dtype=jnp.float32)
    stats = diag[..., None] * eye
    sizes_abs = jax.random.uniform(second, (EXPERTS, width // BLK, BLK), jnp.float32, 0.5, 1.5)
    signs = jnp.where(jax.random.bernoulli(third, 0.5, (EXPERTS, width // BLK, BLK)), 1.0, -1.0)
    axis_vec = sizes_abs * signs
    norm = jnp.sum(axis_vec * axis_vec, axis=-1, keepdims=True)
    basis = eye - 2.0 * axis_vec[..., :, None] * axis_vec[..., None, :] / norm[..., None]
    return jnp.stack([stats.reshape(EXPERTS, width, BLK), basis.reshape(EXPERTS, width, BLK)])


def draw_expand_state(key, part):
    key = jax.random.fold_in(key, 13)
    return block_state(key, C_MID)


def draw_project_state(key, part):
    key = jax.random.fold_in(key, 14)
    return block_state(key, C_OUT)


def draw_head_state(key, part):
    key = jax.random.fold_in(key, 15)
    return block_state(key, C_HEAD)


def plant(result, rng, low, largest):
    longest = result.shape.index(max(result.shape))
    spots = []
    for shift in (0, 1):
        where = [jax.random.randint(jax.random.fold_in(rng, axis), (), 0, length) for axis, length in enumerate(result.shape)]
        where[longest] = (where[longest] + shift) % result.shape[longest]
        spots.append(tuple(where))
    return result.at[spots[0]].set(low).at[spots[1]].set(largest)


def steps_of(key, shape, cuts, low, top_value):
    level, own = 1.0, jax.random.fold_in(key, 6)
    for axis_at, blocks in cuts:
        heights = jnp.exp(jax.random.uniform(jax.random.fold_in(own, axis_at), (blocks,), jnp.float32, low / len(cuts), top_value / len(cuts)))
        level = level * jnp.repeat(heights, shape[axis_at] // blocks).reshape([-1 if axis == axis_at else 1 for axis in range(len(shape))])
    return level


def bell_draw(key, dims, scale, limit, shards=(), kind=jnp.bfloat16):
    result = jax.random.normal(key, dims, jnp.float32) * scale
    if len(shards) > 0:
        result = steps_of(key, dims, shards, -0.22, 0.18) * result
    return jnp.clip(result, min=-limit, max=limit).astype(kind)


def setup_inputs(seed: int = 0) -> dict:
    seeds = jax.random.split(jax.random.key(seed), 31)
    return {
        "images": draw_images(jax.random.fold_in(seeds[30], 71), 0),
        "dom_label": draw_dom_label(jax.random.fold_in(seeds[30], 71), 0),
        "class_label": plant(jax.random.randint(seeds[2], (IMAGES,), 0, CLASSES), jax.random.fold_in(seeds[2], 1), 0, CLASSES - 1).astype(jnp.int32),
        "expand_weight": bell_draw(seeds[3], (C_MID, EXPERTS * C_IN), (2 * C_IN) ** -0.5, 0.3125, ((0, 8),), jnp.float32),
        "expand_first": bell_draw(seeds[4], (C_MID, EXPERTS * C_IN), (0.0055 / IMAGES ** 0.5), 0.0006629126, ((0, 8),), jnp.float32),
        "expand_second": jnp.clip(jnp.exp(math.log(2.4414061883248905e-08) - 1.3862944 * jax.random.uniform(seeds[5], (C_MID, EXPERTS * C_IN), jnp.float32) ** steps_of(seeds[5], (C_MID, EXPERTS * C_IN), ((0, 8),), -0.2, 0.2)), 6.103515470812226e-09, 2.4414061883248905e-08),
        "expand_state": draw_expand_state(jax.random.fold_in(seeds[30], 71), 0),
        "project_weight": bell_draw(seeds[7], (C_OUT, EXPERTS * C_MID), (2 * C_MID) ** -0.5, 0.125, ((0, 8),), jnp.float32),
        "project_first": bell_draw(seeds[8], (C_OUT, EXPERTS * C_MID), (0.0055 / IMAGES ** 0.5), 0.0006629126, ((0, 8),), jnp.float32),
        "project_second": jnp.clip(jnp.exp(math.log(2.4414063659605745e-07) - 1.3862944 * jax.random.uniform(seeds[9], (C_OUT, EXPERTS * C_MID), jnp.float32) ** steps_of(seeds[9], (C_OUT, EXPERTS * C_MID), ((0, 8),), -0.2, 0.2)), 6.103515914901436e-08, 2.4414063659605745e-07),
        "project_state": draw_project_state(jax.random.fold_in(seeds[30], 71), 0),
        "head_weight": bell_draw(seeds[11], (C_HEAD, EXPERTS * C_OUT), (2 * C_OUT) ** -0.5, 0.25, ((0, 8),), jnp.float32),
        "head_first": bell_draw(seeds[12], (C_HEAD, EXPERTS * C_OUT), (0.0055 / IMAGES ** 0.5), 0.0006629126, ((0, 8),), jnp.float32),
        "head_second": jnp.clip(jnp.exp(math.log(2.4414063659605745e-07) - 1.3862944 * jax.random.uniform(seeds[13], (C_HEAD, EXPERTS * C_OUT), jnp.float32) ** steps_of(seeds[13], (C_HEAD, EXPERTS * C_OUT), ((0, 8),), -0.2, 0.2)), 6.103515914901436e-08, 2.4414063659605745e-07),
        "head_state": draw_head_state(jax.random.fold_in(seeds[30], 71), 0),
        "depth_weight": bell_draw(seeds[15], (EXPERTS, KSIZE * KSIZE, C_MID), (2 * KSIZE * KSIZE) ** -0.5, 1.5, ((2, 8),), jnp.float32),
        "depth_first": bell_draw(seeds[16], (EXPERTS, KSIZE * KSIZE, C_MID), (0.0055 / IMAGES ** 0.5), 0.0006629126, ((2, 8),), jnp.float32),
        "depth_second": jnp.clip(jnp.exp(math.log(2.4414063659605745e-07) - 1.3862944 * jax.random.uniform(seeds[17], (EXPERTS, KSIZE * KSIZE, C_MID), jnp.float32) ** steps_of(seeds[17], (EXPERTS, KSIZE * KSIZE, C_MID), ((2, 8),), -0.2, 0.2)), 6.103515914901436e-08, 2.4414063659605745e-07),
        "classifier_weight": bell_draw(seeds[18], (C_HEAD, CLASSES), (C_HEAD // 4) ** -0.5, 0.3125, ((0, 8),), jnp.float32),
        "classifier_first": bell_draw(seeds[19], (C_HEAD, CLASSES), (0.11 / (IMAGES * CLASSES) ** 0.5), 0.00041926274, ((0, 8),), jnp.float32),
        "classifier_second": jnp.clip(jnp.exp(math.log(9.765624753299562e-08) - 1.3862944 * jax.random.uniform(seeds[20], (C_HEAD, CLASSES), jnp.float32) ** steps_of(seeds[20], (C_HEAD, CLASSES), ((0, 8),), -0.2, 0.2)), 2.4414061883248905e-08, 9.765624753299562e-08),
        "excite_weight": bell_draw(seeds[21], (2, C_MID, C_SE), 0.08, 0.4, (), jnp.float32),
        "excite_first": bell_draw(seeds[22], (2, C_MID, C_SE), (0.0055 / IMAGES ** 0.5), 0.0006629126, (), jnp.float32),
        "excite_second": jnp.clip(jnp.exp(jax.random.uniform(seeds[23], (2, C_MID, C_SE), jnp.float32, math.log(6.103515914901436e-08), math.log(2.4414063659605745e-07))), 6.103515914901436e-08, 2.4414063659605745e-07),
        "router_weight": bell_draw(seeds[24], (C_IN + C_OUT, EXPERTS), (C_IN // 9) ** -0.5, 1.25, (), jnp.float32),
        "router_first": bell_draw(seeds[25], (C_IN + C_OUT, EXPERTS), (0.0055 / IMAGES ** 0.5), 0.0006629126, (), jnp.float32),
        "router_second": jnp.clip(jnp.exp(jax.random.uniform(seeds[26], (C_IN + C_OUT, EXPERTS), jnp.float32, math.log(6.103515914901436e-08), math.log(2.4414063659605745e-07))), 6.103515914901436e-08, 2.4414063659605745e-07),
        "gains_weight": jnp.clip(jax.random.uniform(seeds[27], (VEC,), jnp.float32, 0.5, 1.5), 0.5, 1.5),
        "gains_first": bell_draw(seeds[28], (VEC,), (0.011 / IMAGES ** 0.5), 0.0013258252, (), jnp.float32),
        "gains_second": jnp.clip(jnp.exp(jax.random.uniform(seeds[29], (VEC,), jnp.float32, math.log(2.4414063659605745e-07), math.log(9.765625463842298e-07))), 2.4414063659605745e-07, 9.765625463842298e-07),
    }


HIGH = lax.Precision.HIGHEST
beta_one = 0.9
beta_two = 0.95
eps_adam = 1e-08
eps_norm = 1e-05
decay = 0.01
rate_matrix = 0.08
rate_gains = 0.5
boost = 1.0
balance_weight = 4.0
stat_gain = 15000.0

@jax.custom_vjp
def low(v):
    return lax.optimization_barrier(v.astype(jnp.bfloat16)).astype(jnp.float32)

@jax.custom_vjp
def low_back(v):
    return v

def low_keep(v):
    return (low(v), None)

def low_pass(kept, grad):
    return (grad,)

def back_keep(v):
    return (v, None)

def back_low(kept, grad):
    return (low(grad),)
low.defvjp(low_keep, low_pass)
low_back.defvjp(back_keep, back_low)

def silu(value):
    return value * jax.nn.sigmoid(value)

def depthwise(act, kern):
    grid = act.reshape(act.shape[0], SIDE, SIDE, act.shape[-1])
    margin = KSIZE // 2
    padded = jnp.pad(grid, ((0, 0), (margin, margin), (margin, margin), (0, 0)))
    total = jnp.zeros_like(grid)
    for tap in range(KSIZE * KSIZE):
        row_at = tap // KSIZE
        col_at = tap % KSIZE
        total = total + padded[:, row_at:row_at + SIDE, col_at:col_at + SIDE, :] * kern[:, tap][:, None, None, :]
    return total.reshape(act.shape)

def excite_branch(hidden, kern_depth, excite_w, bias_se, bias_ex):
    act = silu(depthwise(silu(hidden), kern_depth))
    pooled = lax.optimization_barrier(jnp.mean(act, axis=1))
    squeeze = silu(jnp.dot(pooled, excite_w[0], precision=HIGH) + bias_se)
    gate = jax.nn.sigmoid(jnp.dot(squeeze, excite_w[1].T, precision=HIGH) + bias_ex)
    return act * gate[:, None, :]

def split_gains(gains):
    widths = [C_SE, C_MID, C_OUT, C_OUT, C_HEAD, C_HEAD, CLASSES]
    pieces = []
    start = 0
    for width in widths:
        pieces.append(gains[start:start + width])
        start = start + width
    return pieces

def mixed(route, flat):
    cube = flat.reshape(flat.shape[0], EXPERTS, -1)
    return jnp.einsum('ne,dec->ncd', route, cube, precision=HIGH)

def routed_kernel(route, flat):
    return low(low_back(mixed(route, flat)))

def convolve(act, kern):
    return jnp.einsum('npc,ncd->npd', act, kern, precision=HIGH)

def normalize(value, gain, shift):
    count = value.shape[0] * value.shape[1] * value.shape[2]
    center = lax.optimization_barrier(jnp.sum(value, axis=(0, 1, 2))) / count
    square = lax.optimization_barrier(jnp.sum(value * value, axis=(0, 1, 2))) / count
    return (value - center) * lax.rsqrt(square - center * center + eps_norm) * gain + shift

def spread(route):
    means = lax.optimization_barrier(jnp.mean(route, axis=0))
    return jnp.mean((means - jnp.mean(means)) ** 2)

def forward(weights, images, dom_label, class_label):
    expand_w, depth_w, project_w, head_w, class_w, excite_w, router_w, gains_w = weights
    bias_se, bias_ex, gain_one, shift_one, gain_two, shift_two, bias_cls = split_gains(gains_w)
    hot = (dom_label[:, None] == jnp.arange(EXPERTS)[None, :]).astype(jnp.float32)
    route_one = jax.nn.sigmoid(jnp.dot(lax.optimization_barrier(jnp.mean(images, axis=1)), router_w[:C_IN], precision=HIGH) + boost * hot)
    route_one_low = low(route_one)
    blocks = images.shape[0] // IMG_DEV
    image_blocks = images.reshape(blocks, IMG_DEV, PIX, C_IN)
    expand_low = low(expand_w)
    depth_low = low(depth_w)
    project_low = low(project_w)
    head_low = low(head_w)
    class_low = low(class_w)

    def block_one(pair):
        inputs, route = pair
        hidden = low_back(convolve(inputs, routed_kernel(route, expand_low)))
        kern_depth = jnp.einsum('ne,ekc->nkc', route, depth_low, precision=HIGH)
        scaled = low(excite_branch(hidden, kern_depth, excite_w, bias_se, bias_ex))
        return low_back(convolve(scaled, routed_kernel(route, project_low)))
    before = lax.map(jax.checkpoint(block_one), (image_blocks, route_one_low.reshape(blocks, IMG_DEV, EXPERTS)))
    normed = low(normalize(before, gain_one, shift_one))
    pooled = lax.optimization_barrier(jnp.mean(normed, axis=2)).reshape(-1, C_OUT)
    route_two = jax.nn.sigmoid(jnp.dot(pooled, router_w[C_IN:], precision=HIGH) + boost * hot)
    route_two_low = low(route_two)

    def block_two(pair):
        inputs, route = pair
        return low_back(convolve(inputs, routed_kernel(route, head_low)))
    widened = lax.map(jax.checkpoint(block_two), (normed, route_two_low.reshape(blocks, IMG_DEV, EXPERTS)))
    lifted = normalize(widened, gain_two, shift_two)
    feats = low(lax.optimization_barrier(jnp.mean(silu(lifted), axis=2)).reshape(-1, C_HEAD))
    logits = low_back(jnp.dot(feats, class_low, precision=HIGH) + bias_cls)
    top = lax.optimization_barrier(jnp.max(logits, axis=1, keepdims=True))
    total = top[:, 0] + jnp.log(lax.optimization_barrier(jnp.sum(jnp.exp(logits - top), axis=1)))
    picked = lax.optimization_barrier(jnp.sum(logits * (class_label[:, None] == jnp.arange(CLASSES)[None, :]).astype(jnp.float32), axis=1))
    return jnp.mean(total - picked) + balance_weight * (spread(route_one) + spread(route_two))

def orthonormal(matrix):
    columns = []
    for index in range(BLK):
        column = matrix[..., index]
        for previous in columns:
            column = column - lax.optimization_barrier(jnp.sum(previous * column, axis=-1, keepdims=True)) * previous
        column = column * lax.rsqrt(lax.optimization_barrier(jnp.sum(column * column, axis=-1, keepdims=True)))
        columns.append(column)
    return jnp.stack(columns, axis=-1)

def to_cube(flat):
    return flat.reshape(flat.shape[0], EXPERTS, -1).transpose(1, 2, 0)

def to_flat(cube):
    return cube.transpose(2, 0, 1).reshape(cube.shape[2], -1)

def soap_cube(weight, grad, first, second, state, every):
    blocks = weight.shape[2] // BLK
    gained = stat_gain * every / grad.shape[1]
    corr_one = 1.0 - beta_one ** STEP
    corr_two = 1.0 - beta_two ** STEP
    stats = state[0].reshape(EXPERTS, blocks, BLK, BLK)
    basis = state[1].reshape(EXPERTS, blocks, BLK, BLK)
    cut = grad.reshape(EXPERTS, grad.shape[1], blocks, BLK)
    turned = jnp.einsum('eibj,ebjl->eibl', cut, basis, precision=HIGH)
    first_new = beta_one * first + (1.0 - beta_one) * grad
    second_new = beta_two * second + (1.0 - beta_two) * (turned * turned).reshape(grad.shape)
    moment = jnp.einsum('eibj,ebjl->eibl', first_new.reshape(cut.shape), basis, precision=HIGH)
    ratio = moment / corr_one / (jnp.sqrt(second_new.reshape(cut.shape) / corr_two) + eps_adam)
    back = jnp.einsum('eibl,ebjl->eibj', ratio, basis, precision=HIGH).reshape(grad.shape)
    weight_new = weight - rate_matrix * (back + decay * weight)
    summed = beta_two * stats + (1.0 - beta_two) * gained * jnp.einsum('eibj,eibl->ebjl', cut, cut, precision=HIGH)
    trace = lax.optimization_barrier(jnp.sum(jnp.diagonal(summed, axis1=-2, axis2=-1), axis=-1))
    stats_new = summed / trace[..., None, None]
    basis_new = orthonormal(jnp.einsum('ebjl,eblm->ebjm', stats_new, basis, precision=HIGH))
    state_new = jnp.stack([stats_new.reshape(state[0].shape), basis_new.reshape(state[1].shape)])
    return (first_new, second_new, state_new, weight_new)

def soap(weight, grad, first, second, state, every):
    first_new, second_new, state_new, weight_new = soap_cube(to_cube(weight), to_cube(grad), to_cube(first), to_cube(second), state, every)
    return (to_flat(first_new), to_flat(second_new), state_new, to_flat(weight_new))

def adam(weight, grad, first, second, rate):
    corr_one = 1.0 - beta_one ** STEP
    corr_two = 1.0 - beta_two ** STEP
    first_new = beta_one * first + (1.0 - beta_one) * grad
    second_new = beta_two * second + (1.0 - beta_two) * grad * grad
    weight_new = weight - rate * (first_new / corr_one / (jnp.sqrt(second_new / corr_two) + eps_adam) + decay * weight)
    return (first_new, second_new, weight_new)

def reference(images, dom_label, class_label, expand_weight, expand_first, expand_second, expand_state, project_weight, project_first, project_second, project_state, head_weight, head_first, head_second, head_state, depth_weight, depth_first, depth_second, classifier_weight, classifier_first, classifier_second, excite_weight, excite_first, excite_second, router_weight, router_first, router_second, gains_weight, gains_first, gains_second):
    weights = (expand_weight, depth_weight, project_weight, head_weight, classifier_weight, excite_weight, router_weight, gains_weight)
    inputs = images.astype(jnp.float32)
    loss, pull = jax.vjp(lambda params: forward(params, inputs, dom_label, class_label), weights)
    grads = pull(jnp.ones_like(loss))[0]
    expand_out = soap(expand_weight, grads[0], expand_first, expand_second, expand_state, IMAGES)
    project_out = soap(project_weight, grads[2], project_first, project_second, project_state, IMAGES)
    head_out = soap(head_weight, grads[3], head_first, head_second, head_state, IMAGES)
    depth_out = adam(depth_weight, grads[1], depth_first, depth_second, rate_matrix)
    class_out = adam(classifier_weight, grads[4], classifier_first, classifier_second, rate_matrix)
    excite_out = adam(excite_weight, grads[5], excite_first, excite_second, rate_matrix)
    router_out = adam(router_weight, grads[6], router_first, router_second, rate_matrix)
    gains_out = adam(gains_weight, grads[7], gains_first, gains_second, rate_gains)
    return (loss, expand_out[0], expand_out[1], expand_out[2], expand_out[3], project_out[0], project_out[1], project_out[2], project_out[3], head_out[0], head_out[1], head_out[2], head_out[3], depth_out[0], depth_out[1], depth_out[2], class_out[0], class_out[1], class_out[2], excite_out[0], excite_out[1], excite_out[2], router_out[0], router_out[1], router_out[2], gains_out[0], gains_out[1], gains_out[2])
```

```python
import functools

import jax
import jax.numpy as jnp
from jax import lax
from jax.experimental import pallas as pl
from jax.experimental.pallas import tpu as pltpu
from jax.sharding import PartitionSpec as P

SIDE = 7
PIX = 49
KSIZE = 3
EXPERTS = 8
BLK = 4
STEP = 10
C_IN = 192
C_MID = 1152
C_SE = 48
C_OUT = 320
C_HEAD = 1280
CLASSES = 1000


HIGH = lax.Precision.HIGHEST
beta_one = 0.9
beta_two = 0.95
eps_adam = 1e-08
eps_norm = 1e-05
decay = 0.01
rate_matrix = 0.08
rate_gains = 0.5
boost = 1.0
balance_weight = 4.0
stat_gain = 15000.0


def silu(value):
    return value * jax.nn.sigmoid(value)


def silu_slope(value):
    sig = jax.nn.sigmoid(value)
    return sig * (1.0 + value * (1.0 - sig))


def depthwise(act, kern):
    grid = act.reshape((SIDE, SIDE) + act.shape[1:])
    padded = jnp.pad(grid, ((1, 1), (1, 1), (0, 0), (0, 0)))
    total = jnp.zeros_like(grid)
    for tap in range(KSIZE * KSIZE):
        row_at = tap // KSIZE
        col_at = tap % KSIZE
        total = total + padded[row_at : row_at + SIDE, col_at : col_at + SIDE] * kern[tap]
    return total.reshape(act.shape)


def depthwise_kern_grad(act, grad_out):
    grid = act.reshape((SIDE, SIDE) + act.shape[1:])
    padded = jnp.pad(grid, ((1, 1), (1, 1), (0, 0), (0, 0)))
    grad = grad_out.reshape((SIDE, SIDE) + act.shape[1:])
    taps = []
    for tap in range(KSIZE * KSIZE):
        row_at = tap // KSIZE
        col_at = tap % KSIZE
        window = padded[row_at : row_at + SIDE, col_at : col_at + SIDE]
        taps.append(jnp.sum(window * grad, axis=(0, 1)))
    return jnp.stack(taps)


MESH = pl.DeviceIdType.MESH


def sum_kernel(n_wide, n_dp, x_ref, o_ref, wide_slots, dp_slots, part, s_wide, r_wide, s_dp, r_dp):
    me_wide = lax.axis_index("wide")
    me_dp = lax.axis_index("dp")
    barrier = pltpu.get_barrier_semaphore()
    for k in range(1, n_wide):
        pl.semaphore_signal(
            barrier, inc=1, device_id={"wide": lax.rem(me_wide + k, n_wide)}, device_id_type=MESH
        )
    for k in range(1, n_dp):
        pl.semaphore_signal(
            barrier, inc=1, device_id={"dp": lax.rem(me_dp + k, n_dp)}, device_id_type=MESH
        )
    pl.semaphore_wait(barrier, n_wide + n_dp - 2)

    def exchange(src, slots, me, axis, size, send, recv):
        copies = []
        for k in range(1, size):
            copy = pltpu.make_async_remote_copy(
                src_ref=src,
                dst_ref=slots.at[me],
                send_sem=send.at[k],
                recv_sem=recv.at[k],
                device_id={axis: lax.rem(me + k, size)},
                device_id_type=MESH,
            )
            copy.start()
            copies.append(copy)
        slots[me] = src[...]
        for copy in copies:
            copy.wait()
        total = slots[0]
        for k in range(1, size):
            total = total + slots[k]
        return total

    part[...] = exchange(x_ref, wide_slots, me_wide, "wide", n_wide, s_wide, r_wide)
    o_ref[...] = exchange(part, dp_slots, me_dp, "dp", n_dp, s_dp, r_dp)


def sum_all(parts, ident):
    shapes = [part.shape for part in parts]
    sizes = [part.size for part in parts]
    flat = jnp.concatenate([part.reshape(-1) for part in parts])
    rows = -(-flat.size // 1024) * 8
    flat = jnp.pad(flat, (0, rows * 128 - flat.size)).reshape(rows, 128)
    n_wide = lax.axis_size("wide")
    n_dp = lax.axis_size("dp")
    out = pl.pallas_call(
        functools.partial(sum_kernel, n_wide, n_dp),
        out_shape=jax.ShapeDtypeStruct((rows, 128), jnp.float32),
        in_specs=[pl.BlockSpec(memory_space=pltpu.VMEM)],
        out_specs=pl.BlockSpec(memory_space=pltpu.VMEM),
        scratch_shapes=[
            pltpu.VMEM((n_wide, rows, 128), jnp.float32),
            pltpu.VMEM((n_dp, rows, 128), jnp.float32),
            pltpu.VMEM((rows, 128), jnp.float32),
            pltpu.SemaphoreType.DMA((n_wide,)),
            pltpu.SemaphoreType.DMA((n_wide,)),
            pltpu.SemaphoreType.DMA((n_dp,)),
            pltpu.SemaphoreType.DMA((n_dp,)),
        ],
        compiler_params=pltpu.CompilerParams(collective_id=ident, has_side_effects=True),
    )(flat)
    out = out.reshape(-1)
    found = []
    start = 0
    for shape, size in zip(shapes, sizes):
        found.append(out[start : start + size].reshape(shape))
        start = start + size
    return found


def rows_nt(left, right):
    return lax.dot_general(
        left, right, (((1,), (1,)), ((), ())), preferred_element_type=jnp.float32
    )


def rows_tn(left, right):
    return lax.dot_general(
        left, right, (((0,), (0,)), ((), ())), preferred_element_type=jnp.float32
    )


def scaled_by(route, act):
    cube = act[:, :, None, :] * route[None, :, :, None]
    return cube.reshape(act.shape[0] * act.shape[1], -1)


def split_gains(gains):
    widths = [C_SE, C_MID, C_OUT, C_OUT, C_HEAD, C_HEAD, CLASSES]
    pieces = []
    start = 0
    for width in widths:
        pieces.append(gains[start : start + width])
        start = start + width
    return pieces


def balance_grad(means, every):
    return balance_weight * 2.0 * (means - jnp.mean(means)) / (EXPERTS * every)


def orthonormal(matrix):
    columns = []
    for index in range(BLK):
        column = matrix[..., index]
        for previous in columns:
            column = column - jnp.sum(previous * column, axis=-1, keepdims=True) * previous
        column = column * lax.rsqrt(jnp.sum(column * column, axis=-1, keepdims=True))
        columns.append(column)
    return jnp.stack(columns, axis=-1)


def to_cube(flat):
    return flat.reshape(flat.shape[0], EXPERTS, -1).transpose(1, 2, 0)


def to_flat(cube):
    return cube.transpose(2, 0, 1).reshape(cube.shape[2], -1)


def soap_cube(weight, grad, first, second, state, every):
    blocks = weight.shape[2] // BLK
    gained = stat_gain * every / grad.shape[1]
    corr_one = 1.0 - beta_one**STEP
    corr_two = 1.0 - beta_two**STEP
    stats = state[0].reshape(EXPERTS, blocks, BLK, BLK)
    basis = state[1].reshape(EXPERTS, blocks, BLK, BLK)
    cut = grad.reshape(EXPERTS, grad.shape[1], blocks, BLK)
    turned = jnp.einsum("eibj,ebjl->eibl", cut, basis, precision=HIGH)
    first_new = beta_one * first + (1.0 - beta_one) * grad
    second_new = beta_two * second + (1.0 - beta_two) * (turned * turned).reshape(grad.shape)
    moment = jnp.einsum("eibj,ebjl->eibl", first_new.reshape(cut.shape), basis, precision=HIGH)
    ratio = moment / corr_one / (jnp.sqrt(second_new.reshape(cut.shape) / corr_two) + eps_adam)
    back = jnp.einsum("eibl,ebjl->eibj", ratio, basis, precision=HIGH).reshape(grad.shape)
    weight_new = weight - rate_matrix * (back + decay * weight)
    summed = beta_two * stats + (1.0 - beta_two) * gained * jnp.einsum(
        "eibj,eibl->ebjl", cut, cut, precision=HIGH
    )
    trace = jnp.sum(jnp.diagonal(summed, axis1=-2, axis2=-1), axis=-1)
    stats_new = summed / trace[..., None, None]
    basis_new = orthonormal(jnp.einsum("ebjl,eblm->ebjm", stats_new, basis, precision=HIGH))
    state_new = jnp.stack([stats_new.reshape(state[0].shape), basis_new.reshape(state[1].shape)])
    return (first_new, second_new, state_new, weight_new)


def soap(weight, grad, first, second, state, every):
    first_new, second_new, state_new, weight_new = soap_cube(
        to_cube(weight), to_cube(grad), to_cube(first), to_cube(second), state, every
    )
    return (to_flat(first_new), to_flat(second_new), state_new, to_flat(weight_new))


def adam(weight, grad, first, second, rate):
    corr_one = 1.0 - beta_one**STEP
    corr_two = 1.0 - beta_two**STEP
    first_new = beta_one * first + (1.0 - beta_one) * grad
    second_new = beta_two * second + (1.0 - beta_two) * grad * grad
    weight_new = weight - rate * (
        first_new / corr_one / (jnp.sqrt(second_new / corr_two) + eps_adam) + decay * weight
    )
    return (first_new, second_new, weight_new)


def local(
    images,
    dom_label,
    class_label,
    expand_weight,
    expand_first,
    expand_second,
    expand_state,
    project_weight,
    project_first,
    project_second,
    project_state,
    head_weight,
    head_first,
    head_second,
    head_state,
    depth_weight,
    depth_first,
    depth_second,
    classifier_weight,
    classifier_first,
    classifier_second,
    excite_weight,
    excite_first,
    excite_second,
    router_weight,
    router_first,
    router_second,
    gains_weight,
    gains_first,
    gains_second,
):
    low_type = jnp.bfloat16
    count_images = images.shape[0]
    every = images.shape[0] * lax.axis_size("dp") * lax.axis_size("wide")
    count = every * PIX
    rows = PIX * count_images
    bias_se, bias_ex, gain_one, shift_one, gain_two, shift_two, bias_cls = split_gains(gains_weight)
    hot = (dom_label[:, None] == jnp.arange(EXPERTS)[None, :]).astype(jnp.float32)
    class_hot = (class_label[:, None] == jnp.arange(CLASSES)[None, :]).astype(jnp.float32)
    img = images.transpose(1, 0, 2)
    expand_low = lax.all_gather(expand_weight.astype(low_type), "wide", axis=0, tiled=True)
    project_low = lax.all_gather(project_weight.astype(low_type), "wide", axis=0, tiled=True)
    head_low = lax.all_gather(head_weight.astype(low_type), "wide", axis=0, tiled=True)
    class_low = lax.all_gather(classifier_weight.astype(low_type), "wide", axis=0, tiled=True)
    depth_own = depth_weight.astype(low_type).transpose(2, 0, 1).reshape(depth_weight.shape[2], -1)
    depth_low = lax.all_gather(depth_own, "wide", axis=0, tiled=True)
    depth_low = depth_low.reshape(C_MID, EXPERTS, KSIZE * KSIZE).transpose(1, 2, 0)
    project_cube = project_low.reshape(C_OUT, EXPERTS, C_MID).transpose(1, 0, 2)
    project_cube = project_cube.reshape(EXPERTS * C_OUT, C_MID)

    pooled_one = jnp.mean(img.astype(jnp.float32), axis=0)
    route_one = jax.nn.sigmoid(
        jnp.dot(pooled_one, router_weight[:C_IN], precision=HIGH) + boost * hot
    )
    r_one = route_one.astype(low_type)
    img_routed = scaled_by(r_one, img)
    hidden = rows_nt(img_routed, expand_low).reshape(PIX, count_images, C_MID)
    kern_depth = jnp.einsum(
        "ne,ekc->knc", r_one, depth_low, preferred_element_type=jnp.float32
    )
    start = silu(hidden)
    turned = depthwise(start, kern_depth)
    act = silu(turned)
    pooled_act = jnp.mean(act, axis=0)
    squeeze_in = jnp.dot(pooled_act, excite_weight[0], precision=HIGH) + bias_se
    squeeze = silu(squeeze_in)
    gate = jax.nn.sigmoid(jnp.dot(squeeze, excite_weight[1].T, precision=HIGH) + bias_ex)
    scaled = (act * gate).astype(low_type)
    scaled_rows = scaled.reshape(rows, C_MID)
    each = rows_nt(scaled_rows, project_cube).astype(low_type)
    each = each.reshape(PIX, count_images, EXPERTS, C_OUT)
    r_one_wide = r_one.astype(jnp.float32)[None, :, :, None]
    before = jnp.sum(each.astype(jnp.float32) * r_one_wide, axis=2)
    sums_one = sum_all(
        (
            jnp.sum(before, axis=(0, 1)),
            jnp.sum(before * before, axis=(0, 1)),
            jnp.sum(route_one, axis=0),
        ),
        1,
    )
    center_one = sums_one[0] / count
    inv_one = lax.rsqrt(sums_one[1] / count - center_one * center_one + eps_norm)
    hat_one = (before - center_one) * inv_one
    normed = (hat_one * gain_one + shift_one).astype(low_type)
    pooled_two = jnp.mean(normed.astype(jnp.float32), axis=0)
    route_two = jax.nn.sigmoid(
        jnp.dot(pooled_two, router_weight[C_IN:], precision=HIGH) + boost * hot
    )
    r_two = route_two.astype(low_type)
    normed_routed = scaled_by(r_two, normed)
    widened = rows_nt(normed_routed, head_low).reshape(PIX, count_images, C_HEAD)
    sums_two = sum_all(
        (
            jnp.sum(widened, axis=(0, 1)),
            jnp.sum(widened * widened, axis=(0, 1)),
            jnp.sum(route_two, axis=0),
        ),
        2,
    )
    center_two = sums_two[0] / count
    inv_two = lax.rsqrt(sums_two[1] / count - center_two * center_two + eps_norm)
    hat_two = (widened - center_two) * inv_two
    lifted = hat_two * gain_two + shift_two
    feats = jnp.mean(silu(lifted), axis=0).astype(low_type)
    logits = jnp.dot(feats, class_low, preferred_element_type=jnp.float32) + bias_cls
    top = jnp.max(logits, axis=1, keepdims=True)
    powers = jnp.exp(logits - top)
    totals = jnp.sum(powers, axis=1, keepdims=True)
    cross_part = jnp.sum(top[:, 0] + jnp.log(totals[:, 0]) - jnp.sum(logits * class_hot, axis=1))
    means_one = sums_one[2] / every
    means_two = sums_two[2] / every

    grad_logits = ((powers / totals - class_hot) / every).astype(low_type)
    grad_class = rows_tn(feats, grad_logits)
    grad_bias_cls = jnp.sum(grad_logits.astype(jnp.float32), axis=0)
    grad_feats = rows_nt(grad_logits, class_low)
    grad_lifted = grad_feats / PIX * silu_slope(lifted)
    back_two = sum_all(
        (jnp.sum(grad_lifted, axis=(0, 1)), jnp.sum(grad_lifted * hat_two, axis=(0, 1))), 3
    )
    grad_widened = (
        inv_two * gain_two * (grad_lifted - back_two[0] / count - hat_two * back_two[1] / count)
    ).astype(low_type)
    grad_widened_rows = grad_widened.reshape(rows, C_HEAD)
    grad_head = rows_tn(grad_widened_rows, normed_routed)
    turned_two = jnp.dot(grad_widened_rows, head_low, preferred_element_type=jnp.float32)
    turned_two = turned_two.reshape(PIX, count_images, EXPERTS, C_OUT)
    grad_route_two = jnp.sum(
        turned_two * normed.astype(jnp.float32)[:, :, None, :], axis=(0, 3)
    ) + balance_grad(means_two, every)
    grad_logit_two = grad_route_two * route_two * (1.0 - route_two)
    grad_router_two = jnp.dot(pooled_two.T, grad_logit_two, precision=HIGH)
    grad_normed = (
        jnp.sum(turned_two * r_two.astype(jnp.float32)[None, :, :, None], axis=2)
        + jnp.dot(grad_logit_two, router_weight[C_IN:].T, precision=HIGH) / PIX
    )
    back_one = sum_all(
        (jnp.sum(grad_normed, axis=(0, 1)), jnp.sum(grad_normed * hat_one, axis=(0, 1))), 4
    )
    grad_before = (
        inv_one * gain_one * (grad_normed - back_one[0] / count - hat_one * back_one[1] / count)
    ).astype(low_type)

    before_routed = scaled_by(r_one, grad_before)
    grad_project = rows_tn(before_routed, scaled_rows).reshape(EXPERTS, C_OUT, C_MID)
    grad_project = grad_project.transpose(1, 0, 2).reshape(C_OUT, EXPERTS * C_MID)
    route_project = jnp.sum(
        each.astype(jnp.float32) * grad_before.astype(jnp.float32)[:, :, None, :], axis=(0, 3)
    )
    grad_scaled = jnp.dot(before_routed, project_cube, preferred_element_type=jnp.float32)
    grad_scaled = grad_scaled.reshape(PIX, count_images, C_MID)
    grad_gate = jnp.sum(grad_scaled * act, axis=0)
    grad_gate = grad_gate * gate * (1.0 - gate)
    grad_squeeze = jnp.dot(grad_gate, excite_weight[1], precision=HIGH) * silu_slope(squeeze_in)
    grad_excite = jnp.stack(
        [
            jnp.dot(pooled_act.T, grad_squeeze, precision=HIGH),
            jnp.dot(grad_gate.T, squeeze, precision=HIGH),
        ]
    )
    grad_pooled = jnp.dot(grad_squeeze, excite_weight[0].T, precision=HIGH)
    grad_turned = (grad_scaled * gate + grad_pooled / PIX) * silu_slope(turned)
    kern_depth_grad = depthwise_kern_grad(start, grad_turned)
    grad_start = depthwise(grad_turned, kern_depth[::-1])
    grad_hidden = (grad_start * silu_slope(hidden)).astype(low_type).reshape(rows, C_MID)
    grad_expand = rows_tn(grad_hidden, img_routed)
    turned_one = jnp.dot(grad_hidden, expand_low, preferred_element_type=jnp.float32)
    turned_one = turned_one.reshape(PIX, count_images, EXPERTS, C_IN)
    route_expand = jnp.sum(turned_one * img.astype(jnp.float32)[:, :, None, :], axis=(0, 3))
    grad_depth = jnp.einsum(
        "ne,knc->ekc", r_one.astype(jnp.float32), kern_depth_grad, precision=HIGH
    )
    depth_term = jnp.einsum(
        "knc,ekc->ne", kern_depth_grad, depth_low.astype(jnp.float32), precision=HIGH
    )
    grad_route_one = route_expand + route_project + depth_term + balance_grad(means_one, every)
    grad_logit_one = grad_route_one * route_one * (1.0 - route_one)
    grad_router_one = jnp.dot(pooled_one.T, grad_logit_one, precision=HIGH)
    grad_bias_se = jnp.sum(grad_squeeze, axis=0)
    grad_bias_ex = jnp.sum(grad_gate, axis=0)
    small = lax.psum(
        (
            grad_excite,
            jnp.concatenate([grad_router_one, grad_router_two], axis=0),
            jnp.concatenate([grad_bias_se, grad_bias_ex, grad_bias_cls]),
            cross_part,
        ),
        ("dp", "wide"),
    )
    full = (grad_expand, grad_depth, grad_project, grad_head, grad_class)
    shares = (
        lax.psum_scatter(
            full[0].astype(jnp.bfloat16), "wide", scatter_dimension=0, tiled=True
        ).astype(jnp.float32),
        lax.psum_scatter(
            full[1].transpose(2, 0, 1).astype(jnp.bfloat16).reshape(C_MID, -1), "wide", scatter_dimension=0, tiled=True
        ).astype(jnp.float32),
        lax.psum_scatter(
            full[2].astype(jnp.bfloat16), "wide", scatter_dimension=0, tiled=True
        ).astype(jnp.float32),
        lax.psum_scatter(
            full[3].astype(jnp.bfloat16), "wide", scatter_dimension=0, tiled=True
        ).astype(jnp.float32),
        lax.psum_scatter(
            full[4].astype(jnp.bfloat16), "wide", scatter_dimension=0, tiled=True
        ).astype(jnp.float32),
    )
    reduced = (
        lax.psum(shares[0].astype(jnp.bfloat16), "dp").astype(jnp.float32),
        lax.psum(shares[1].astype(jnp.bfloat16), "dp").astype(jnp.float32),
        lax.psum(shares[2].astype(jnp.bfloat16), "dp").astype(jnp.float32),
        lax.psum(shares[3].astype(jnp.bfloat16), "dp").astype(jnp.float32),
        lax.psum(shares[4].astype(jnp.bfloat16), "dp").astype(jnp.float32),
    )
    depth_reduced = reduced[1].reshape(-1, EXPERTS, KSIZE * KSIZE).transpose(1, 2, 0)
    loss = small[3] / every + balance_weight * (
        jnp.mean((means_one - jnp.mean(means_one)) ** 2)
        + jnp.mean((means_two - jnp.mean(means_two)) ** 2)
    )
    bias_grads = small[2]
    grad_gains = jnp.concatenate(
        [
            bias_grads[: C_SE + C_MID],
            back_one[1],
            back_one[0],
            back_two[1],
            back_two[0],
            bias_grads[C_SE + C_MID :],
        ]
    )
    expand_out = soap(expand_weight, reduced[0], expand_first, expand_second, expand_state, every)
    project_out = soap(
        project_weight, reduced[2], project_first, project_second, project_state, every
    )
    head_out = soap(head_weight, reduced[3], head_first, head_second, head_state, every)
    depth_out = adam(depth_weight, depth_reduced, depth_first, depth_second, rate_matrix)
    class_out = adam(
        classifier_weight, reduced[4], classifier_first, classifier_second, rate_matrix
    )
    excite_out = adam(excite_weight, small[0], excite_first, excite_second, rate_matrix)
    router_out = adam(router_weight, small[1], router_first, router_second, rate_matrix)
    gains_out = adam(gains_weight, grad_gains, gains_first, gains_second, rate_gains)
    return (
        loss,
        expand_out[0],
        expand_out[1],
        expand_out[2],
        expand_out[3],
        project_out[0],
        project_out[1],
        project_out[2],
        project_out[3],
        head_out[0],
        head_out[1],
        head_out[2],
        head_out[3],
        depth_out[0],
        depth_out[1],
        depth_out[2],
        class_out[0],
        class_out[1],
        class_out[2],
        excite_out[0],
        excite_out[1],
        excite_out[2],
        router_out[0],
        router_out[1],
        router_out[2],
        gains_out[0],
        gains_out[1],
        gains_out[2],
    )


def solution(mesh):
    return jax.shard_map(
        local,
        mesh=mesh,
        in_specs=(
            P(("dp", "wide"), None, None),
            P(("dp", "wide")),
            P(("dp", "wide")),
            P("wide", None),
            P("wide", None),
            P("wide", None),
            P(None, None, "wide", None),
            P("wide", None),
            P("wide", None),
            P("wide", None),
            P(None, None, "wide", None),
            P("wide", None),
            P("wide", None),
            P("wide", None),
            P(None, None, "wide", None),
            P(None, None, "wide"),
            P(None, None, "wide"),
            P(None, None, "wide"),
            P("wide", None),
            P("wide", None),
            P("wide", None),
            P(),
            P(),
            P(),
            P(),
            P(),
            P(),
            P(),
            P(),
            P(),
        ),
        out_specs=(
            P(),
            P("wide", None),
            P("wide", None),
            P(None, None, "wide", None),
            P("wide", None),
            P("wide", None),
            P("wide", None),
            P(None, None, "wide", None),
            P("wide", None),
            P("wide", None),
            P("wide", None),
            P(None, None, "wide", None),
            P("wide", None),
            P(None, None, "wide"),
            P(None, None, "wide"),
            P(None, None, "wide"),
            P("wide", None),
            P("wide", None),
            P("wide", None),
            P(),
            P(),
            P(),
            P(),
            P(),
            P(),
            P(),
            P(),
            P(),
        ),
        check_vma=False,
    )
```

```python
import functools

import jax
import jax.numpy as jnp
from jax import lax
from jax.experimental import pallas as pl
from jax.experimental.pallas import tpu as pltpu
from jax.sharding import PartitionSpec as P

SIDE = 7
PIX = 49
KSIZE = 3
EXPERTS = 8
BLK = 4
STEP = 10
C_IN = 192
C_MID = 1152
C_SE = 48
C_OUT = 320
C_HEAD = 1280
CLASSES = 1000


HIGH = lax.Precision.HIGHEST
beta_one = 0.9
beta_two = 0.95
eps_adam = 1e-08
eps_norm = 1e-05
decay = 0.01
rate_matrix = 0.08
rate_gains = 0.5
boost = 1.0
balance_weight = 4.0
stat_gain = 15000.0


def split_gains(gains):
    widths = [C_SE, C_MID, C_OUT, C_OUT, C_HEAD, C_HEAD, CLASSES]
    pieces = []
    start = 0
    for width in widths:
        pieces.append(gains[start : start + width])
        start = start + width
    return pieces


MESH = pl.DeviceIdType.MESH


def sum_kernel(n_wide, n_dp, x_ref, o_ref, wide_slots, dp_slots, part, s_wide, r_wide, s_dp, r_dp):
    me_wide = lax.axis_index("wide")
    me_dp = lax.axis_index("dp")
    barrier = pltpu.get_barrier_semaphore()
    for k in range(1, n_wide):
        pl.semaphore_signal(
            barrier, inc=1, device_id={"wide": lax.rem(me_wide + k, n_wide)}, device_id_type=MESH
        )
    for k in range(1, n_dp):
        pl.semaphore_signal(
            barrier, inc=1, device_id={"dp": lax.rem(me_dp + k, n_dp)}, device_id_type=MESH
        )
    pl.semaphore_wait(barrier, n_wide + n_dp - 2)

    def exchange(src, slots, me, axis, size, send, recv):
        copies = []
        for k in range(1, size):
            copy = pltpu.make_async_remote_copy(
                src_ref=src,
                dst_ref=slots.at[me],
                send_sem=send.at[k],
                recv_sem=recv.at[k],
                device_id={axis: lax.rem(me + k, size)},
                device_id_type=MESH,
            )
            copy.start()
            copies.append(copy)
        slots[me] = src[...]
        for copy in copies:
            copy.wait()
        total = slots[0]
        for k in range(1, size):
            total = total + slots[k]
        return total

    part[...] = exchange(x_ref, wide_slots, me_wide, "wide", n_wide, s_wide, r_wide)
    o_ref[...] = exchange(part, dp_slots, me_dp, "dp", n_dp, s_dp, r_dp)


def sum_all(parts, ident):
    shapes = [part.shape for part in parts]
    sizes = [part.size for part in parts]
    flat = jnp.concatenate([part.reshape(-1) for part in parts])
    rows = -(-flat.size // 1024) * 8
    flat = jnp.pad(flat, (0, rows * 128 - flat.size)).reshape(rows, 128)
    n_wide = lax.axis_size("wide")
    n_dp = lax.axis_size("dp")
    out = pl.pallas_call(
        functools.partial(sum_kernel, n_wide, n_dp),
        out_shape=jax.ShapeDtypeStruct((rows, 128), jnp.float32),
        in_specs=[pl.BlockSpec(memory_space=pltpu.VMEM)],
        out_specs=pl.BlockSpec(memory_space=pltpu.VMEM),
        scratch_shapes=[
            pltpu.VMEM((n_wide, rows, 128), jnp.float32),
            pltpu.VMEM((n_dp, rows, 128), jnp.float32),
            pltpu.VMEM((rows, 128), jnp.float32),
            pltpu.SemaphoreType.DMA((n_wide,)),
            pltpu.SemaphoreType.DMA((n_wide,)),
            pltpu.SemaphoreType.DMA((n_dp,)),
            pltpu.SemaphoreType.DMA((n_dp,)),
        ],
        compiler_params=pltpu.CompilerParams(collective_id=ident, has_side_effects=True),
    )(flat)
    out = out.reshape(-1)
    found = []
    start = 0
    for shape, size in zip(shapes, sizes):
        found.append(out[start : start + size].reshape(shape))
        start = start + size
    return found


def balance_grad(means, every):
    return balance_weight * 2.0 * (means - jnp.mean(means)) / (EXPERTS * every)


GROUP = 16
PAIRS = EXPERTS // 2
ROWS = PIX * GROUP
LOW = jnp.bfloat16
FULL = jnp.float32
VMEM_CAP = 60 * 1024 * 1024


def sig(value):
    return 0.5 + 0.5 * jnp.tanh(0.5 * value)


def dot_nn(left, right, precision=None):
    return lax.dot_general(
        left, right, (((1,), (0,)), ((), ())), precision=precision, preferred_element_type=FULL
    )


def dot_nt(left, right, precision=None):
    return lax.dot_general(
        left, right, (((1,), (1,)), ((), ())), precision=precision, preferred_element_type=FULL
    )


def dot_tn(left, right, precision=None):
    return lax.dot_general(
        left, right, (((0,), (0,)), ((), ())), precision=precision, preferred_element_type=FULL
    )


def images_block(width):
    return pl.BlockSpec((PIX, GROUP, width), lambda i: (0, i, 0))


def group_block(width):
    return pl.BlockSpec((GROUP, width), lambda i: (i, 0))


def pair_block(width):
    return pl.BlockSpec((PAIRS, GROUP, width), lambda i: (0, i, 0))


def whole(*shape):
    return pl.BlockSpec(shape, lambda i: (0,) * len(shape), pipeline_mode=pl.Buffered(1))


def total_block(*shape):
    return pl.BlockSpec(shape, lambda i: (0,) * len(shape))


def device_kernel(kernel, name, grid, in_specs, outs, out_specs, scratch, flops, moved):
    return pl.pallas_call(
        kernel,
        name=name,
        grid=(grid,),
        in_specs=in_specs,
        out_shape=[jax.ShapeDtypeStruct(shape, dtype) for shape, dtype in outs],
        out_specs=out_specs,
        scratch_shapes=scratch,
        compiler_params=pltpu.CompilerParams(
            vmem_limit_bytes=VMEM_CAP, dimension_semantics=("arbitrary",)
        ),
        cost_estimate=pl.CostEstimate(flops=flops, bytes_accessed=moved, transcendentals=0),
    )


def pair_scale(route, pair, width):
    lane = lax.broadcasted_iota(jnp.int32, (route.shape[0], 2 * width), 1)
    return jnp.where(
        lane < width, route[:, 2 * pair : 2 * pair + 1], route[:, 2 * pair + 1 : 2 * pair + 2]
    )


def pair_columns(sums, width):
    count = sums[0].shape[0]
    lane = lax.broadcasted_iota(jnp.int32, (count, 2 * width), 1)
    place = lax.broadcasted_iota(jnp.int32, (count, EXPERTS), 1)
    found = jnp.zeros((count, EXPERTS), FULL)
    for pair in range(PAIRS):
        first = jnp.sum(jnp.where(lane < width, sums[pair], 0.0), axis=1, keepdims=True)
        second = jnp.sum(jnp.where(lane < width, 0.0, sums[pair]), axis=1, keepdims=True)
        found = found + jnp.where(place == 2 * pair, first, 0.0)
        found = found + jnp.where(place == 2 * pair + 1, second, 0.0)
    return found


def taps_of(pixel):
    row, col = pixel // SIDE, pixel % SIDE
    found = []
    for tap in range(KSIZE * KSIZE):
        at_row, at_col = row + tap // KSIZE - 1, col + tap % KSIZE - 1
        if 0 <= at_row < SIDE and 0 <= at_col < SIDE:
            found.append((tap, at_row * SIDE + at_col))
    return found


def expand_kernel(
    img_ref, hot_ref, router_ref, expand_ref, depth_ref, excite_ref, bias_se_ref, bias_ex_ref,
    hidden_ref, turned_ref, scaled_ref, route_ref, pair_in_ref, pair_out_ref, gate_ref,
    squeeze_ref, pooled_one_ref, pooled_act_ref, route_sum_ref,
    routed, hidden_full, act_full, kern,
):
    pooled = img_ref[0].astype(FULL)
    for pixel in range(1, PIX):
        pooled = pooled + img_ref[pixel].astype(FULL)
    pooled = pooled[:, :C_IN] * (1.0 / PIX)
    pooled_one_ref[...] = pooled
    route = sig(dot_nt(pooled, router_ref[...], HIGH) + hot_ref[...])
    route_ref[...] = route

    @pl.when(pl.program_id(0) == 0)
    def _():
        route_sum_ref[...] = jnp.zeros_like(route_sum_ref)

    route_sum_ref[...] += jnp.sum(route, axis=0, keepdims=True)
    low = route.astype(LOW).astype(FULL)
    for pair in range(PAIRS):
        scale = pair_scale(low, pair, C_IN).astype(LOW)
        pair_in_ref[pair] = scale
        pair_out_ref[pair] = pair_scale(low, pair, C_OUT).astype(LOW)
        place = slice(2 * pair * C_IN, 2 * (pair + 1) * C_IN)
        for pixel in range(PIX):
            routed[pixel, :, place] = img_ref[pixel] * scale
    columns = [low[:, expert : expert + 1] for expert in range(EXPERTS)]
    for tap in range(KSIZE * KSIZE):
        total = columns[0] * depth_ref[tap, 0:1, :]
        for expert in range(1, EXPERTS):
            total = total + columns[expert] * depth_ref[tap, expert : expert + 1, :]
        kern[tap] = total
    product = dot_nt(routed[...].reshape(ROWS, EXPERTS * C_IN), expand_ref[...])
    hidden_full[...] = product.reshape(PIX, GROUP, C_MID)

    def chunk(index, carry):
        lanes = pl.ds(pl.multiple_of(index * 128, 128), 128)
        taps = [kern[tap, :, lanes] for tap in range(KSIZE * KSIZE)]
        start = [None] * PIX

        def fill(row):
            for pixel in range(row * SIDE, row * SIDE + SIDE):
                value = hidden_full[pixel, :, lanes]
                hidden_ref[pixel, :, lanes] = value.astype(LOW)
                start[pixel] = value * sig(value)

        fill(0)
        pooled_act = jnp.zeros((GROUP, 128), FULL)
        for row in range(SIDE):
            if row + 1 < SIDE:
                fill(row + 1)
            for pixel in range(row * SIDE, row * SIDE + SIDE):
                total = None
                for tap, source in taps_of(pixel):
                    term = start[source] * taps[tap]
                    total = term if total is None else total + term
                turned_ref[pixel, :, lanes] = total.astype(LOW)
                act = total * sig(total)
                pooled_act = pooled_act + act
                act_full[pixel, :, lanes] = act
        pooled_act_ref[:, lanes] = pooled_act * (1.0 / PIX)
        return carry

    lax.fori_loop(0, C_MID // 128, chunk, 0)
    squeeze = dot_nt(pooled_act_ref[...], excite_ref[0], HIGH) + bias_se_ref[...]
    squeeze_ref[...] = squeeze
    gate = sig(dot_nn(squeeze * sig(squeeze), excite_ref[1], HIGH) + bias_ex_ref[...])
    gate_ref[...] = gate

    def finish(pixel, carry):
        scaled_ref[pixel] = (act_full[pixel] * gate).astype(LOW)
        return carry

    lax.fori_loop(0, PIX, finish, 0)


def expand_forward(img_two, hot, router, expand_low, depth_full, excite, bias_se, bias_ex):
    images = img_two.shape[1]
    return device_kernel(
        expand_kernel,
        "expand_forward",
        images // GROUP,
        [
            images_block(2 * C_IN), group_block(EXPERTS), whole(EXPERTS, C_IN),
            whole(C_MID, EXPERTS * C_IN), whole(KSIZE * KSIZE, EXPERTS, C_MID),
            whole(2, C_SE, C_MID), whole(1, C_SE), whole(1, C_MID),
        ],
        [
            ((PIX, images, C_MID), LOW), ((PIX, images, C_MID), LOW), ((PIX, images, C_MID), LOW),
            ((images, EXPERTS), FULL), ((PAIRS, images, 2 * C_IN), LOW),
            ((PAIRS, images, 2 * C_OUT), LOW), ((images, C_MID), FULL), ((images, C_SE), FULL),
            ((images, C_IN), FULL), ((images, C_MID), FULL), ((1, EXPERTS), FULL),
        ],
        [
            images_block(C_MID), images_block(C_MID), images_block(C_MID), group_block(EXPERTS),
            pair_block(2 * C_IN), pair_block(2 * C_OUT), group_block(C_MID), group_block(C_SE),
            group_block(C_IN), group_block(C_MID), total_block(1, EXPERTS),
        ],
        [
            pltpu.VMEM((PIX, GROUP, EXPERTS * C_IN), LOW), pltpu.VMEM((PIX, GROUP, C_MID), FULL),
            pltpu.VMEM((PIX, GROUP, C_MID), FULL), pltpu.VMEM((KSIZE * KSIZE, GROUP, C_MID), FULL),
        ],
        2 * PIX * images * EXPERTS * C_IN * C_MID,
        PIX * images * 4 * C_MID * 2,
    )(img_two, hot, router, expand_low, depth_full, excite, bias_se, bias_ex)


def stack_experts(source, stacked, sem):
    copies = [
        pltpu.make_async_copy(
            source.at[:, expert * C_MID : (expert + 1) * C_MID],
            stacked.at[expert * C_OUT : (expert + 1) * C_OUT],
            sem.at[expert],
        )
        for expert in range(EXPERTS)
    ]
    for copy in copies:
        copy.start()
    for copy in copies:
        copy.wait()


def project_kernel(
    scaled_ref, source, pair_ref, each_ref, before_ref, sums_ref, product, weight_ref, sem
):
    half = 2 * 2 * C_OUT
    flat = scaled_ref[...].reshape(ROWS, C_MID)

    @pl.when(pl.program_id(0) == 0)
    def _():
        stack_experts(source, weight_ref, sem)
        sums_ref[...] = jnp.zeros_like(sums_ref)

    for part in range(2):
        product[part] = dot_nt(flat, weight_ref[part * half : (part + 1) * half]).reshape(
            PIX, GROUP, half
        )
    scales = [pair_ref[pair].astype(FULL) for pair in range(PAIRS)]

    def mix(pixel, carry):
        plain, square = carry
        total = jnp.zeros((GROUP, 2 * C_OUT), FULL)
        for pair in range(PAIRS):
            part, place = pair // 2, pair % 2 * 2 * C_OUT
            value = product[part, pixel, :, place : place + 2 * C_OUT]
            each_ref[pixel, :, pair * 2 * C_OUT : (pair + 1) * 2 * C_OUT] = value.astype(LOW)
            total = total + value * scales[pair]
        before = (total + pltpu.roll(total, C_OUT, 1))[:, :C_OUT]
        before_ref[pixel] = before
        return plain + before, square + before * before

    zero = jnp.zeros((GROUP, C_OUT), FULL)
    plain, square = lax.fori_loop(0, PIX, mix, (zero, zero))
    sums_ref[0:1] += jnp.sum(plain, axis=0, keepdims=True)
    sums_ref[1:2] += jnp.sum(square, axis=0, keepdims=True)


def project_forward(scaled, project_low, pair_out):
    images = scaled.shape[1]
    wide = EXPERTS * C_OUT
    return device_kernel(
        project_kernel,
        "project_forward",
        images // GROUP,
        [images_block(C_MID), pl.BlockSpec(memory_space=pl.ANY), pair_block(2 * C_OUT)],
        [((PIX, images, wide), LOW), ((PIX, images, C_OUT), FULL), ((2, C_OUT), FULL)],
        [images_block(wide), images_block(C_OUT), total_block(2, C_OUT)],
        [
            pltpu.VMEM((2, PIX, GROUP, wide // 2), FULL), pltpu.VMEM((wide, C_MID), LOW),
            pltpu.SemaphoreType.DMA((EXPERTS,)),
        ],
        2 * PIX * images * wide * C_MID,
        PIX * images * (wide + C_MID) * 2,
    )(scaled, project_low, pair_out)


def head_kernel(
    before_ref, norm_ref, hot_ref, router_ref, weight_ref,
    widened_ref, twice_ref, route_ref, pair_ref, pooled_ref, sums_ref, route_sum_ref,
    routed, padded,
):
    @pl.when(pl.program_id(0) == 0)
    def _():
        sums_ref[...] = jnp.zeros_like(sums_ref)
        route_sum_ref[...] = jnp.zeros_like(route_sum_ref)
        padded[...] = jnp.zeros_like(padded)

    gain, shift = norm_ref[0:1], norm_ref[1:2]
    pooled = jnp.zeros((GROUP, C_OUT), FULL)
    for pixel in range(PIX):
        normed = (before_ref[pixel] * gain + shift).astype(LOW).astype(FULL)
        pooled = pooled + normed
        padded[:, :C_OUT] = normed
        value = padded[...]
        twice_ref[pixel] = (value + pltpu.roll(value, C_OUT, 1)).astype(LOW)
    pooled = pooled * (1.0 / PIX)
    pooled_ref[...] = pooled
    route = sig(dot_nt(pooled, router_ref[...], HIGH) + hot_ref[...])
    route_ref[...] = route
    route_sum_ref[...] += jnp.sum(route, axis=0, keepdims=True)
    low = route.astype(LOW).astype(FULL)
    for pair in range(PAIRS):
        scale = pair_scale(low, pair, C_OUT).astype(LOW)
        pair_ref[pair] = scale
        place = slice(2 * pair * C_OUT, 2 * (pair + 1) * C_OUT)
        for pixel in range(PIX):
            routed[pixel, :, place] = twice_ref[pixel] * scale
    product = dot_nt(routed[...].reshape(ROWS, EXPERTS * C_OUT), weight_ref[...])
    widened_ref[...] = product.reshape(PIX, GROUP, C_HEAD).astype(LOW)
    sums_ref[0:1] += jnp.sum(product, axis=0, keepdims=True)
    sums_ref[1:2] += jnp.sum(product * product, axis=0, keepdims=True)


def head_forward(before, norm, hot, router, head_low):
    images = before.shape[1]
    wide = EXPERTS * C_OUT
    return device_kernel(
        head_kernel,
        "head_forward",
        images // GROUP,
        [
            images_block(C_OUT), whole(2, C_OUT), group_block(EXPERTS), whole(EXPERTS, C_OUT),
            whole(C_HEAD, wide),
        ],
        [
            ((PIX, images, C_HEAD), LOW), ((PIX, images, 2 * C_OUT), LOW),
            ((images, EXPERTS), FULL), ((PAIRS, images, 2 * C_OUT), LOW), ((images, C_OUT), FULL),
            ((2, C_HEAD), FULL), ((1, EXPERTS), FULL),
        ],
        [
            images_block(C_HEAD), images_block(2 * C_OUT), group_block(EXPERTS),
            pair_block(2 * C_OUT), group_block(C_OUT), total_block(2, C_HEAD),
            total_block(1, EXPERTS),
        ],
        [pltpu.VMEM((PIX, GROUP, wide), LOW), pltpu.VMEM((GROUP, 2 * C_OUT), FULL)],
        2 * PIX * images * wide * C_HEAD,
        PIX * images * (C_HEAD + C_OUT) * 2,
    )(before, norm, hot, router, head_low)


def loss_kernel(
    widened_ref, norm_ref, label_ref, class_ref, bias_ref,
    feats_ref, logits_ref, grad_feats_ref, sums_ref, cross_ref, bias_grad_ref,
    silu_sum, slope_sum, cross_sum,
):
    step = pl.program_id(0)
    rows = pl.ds(pl.multiple_of(step * GROUP, GROUP), GROUP)
    gain, shift, inv, offset = (norm_ref[k : k + 1] for k in range(4))

    def pixel_sums(pixel, carry):
        total, slope, moved = carry
        value = widened_ref[pixel].astype(FULL)
        lifted = value * gain + shift
        part = sig(lifted)
        grown = lifted * part
        bent = part + grown * (1.0 - part)
        return total + grown, slope + bent, moved + bent * (value * inv + offset)

    zero = jnp.zeros((GROUP, C_HEAD), FULL)
    total, slope, moved = lax.fori_loop(0, PIX, pixel_sums, (zero, zero, zero))
    silu_sum[rows] = total
    slope_sum[rows] = slope
    cross_sum[rows] = moved

    @pl.when(step == pl.num_programs(0) - 1)
    def _():
        feats = (silu_sum[...] * (1.0 / PIX)).astype(LOW)
        feats_ref[...] = feats
        logits = dot_nn(feats, class_ref[...]) + bias_ref[...]
        lane = lax.broadcasted_iota(jnp.int32, logits.shape, 1)
        picked = lane == label_ref[...]
        top = jnp.max(logits, axis=1, keepdims=True)
        powers = jnp.exp(logits - top)
        totals = jnp.sum(powers, axis=1, keepdims=True)
        cross = top + jnp.log(totals) - jnp.sum(
            jnp.where(picked, logits, 0.0), axis=1, keepdims=True
        )
        cross_ref[...] = jnp.sum(cross, axis=0, keepdims=True)
        grad = (powers / totals - jnp.where(picked, 1.0, 0.0)) * norm_ref[4:5, 0:1]
        grad = grad.astype(LOW)
        logits_ref[...] = grad
        bias_grad_ref[...] = jnp.sum(grad.astype(FULL), axis=0, keepdims=True)
        grad_feats = dot_nt(grad, class_ref[...]) * (1.0 / PIX)
        grad_feats_ref[...] = grad_feats
        sums_ref[0:1] = jnp.sum(grad_feats * slope_sum[...], axis=0, keepdims=True)
        sums_ref[1:2] = jnp.sum(grad_feats * cross_sum[...], axis=0, keepdims=True)


def loss_part(widened, norm, label, class_low, bias):
    images = widened.shape[1]
    return device_kernel(
        loss_kernel,
        "loss_part",
        images // GROUP,
        [
            images_block(C_HEAD), whole(8, C_HEAD), whole(images, 1), whole(C_HEAD, CLASSES),
            whole(1, CLASSES),
        ],
        [
            ((images, C_HEAD), LOW), ((images, CLASSES), LOW), ((images, C_HEAD), FULL),
            ((2, C_HEAD), FULL), ((1, 1), FULL), ((1, CLASSES), FULL),
        ],
        [
            total_block(images, C_HEAD), total_block(images, CLASSES), total_block(images, C_HEAD),
            total_block(2, C_HEAD), total_block(1, 1), total_block(1, CLASSES),
        ],
        [pltpu.VMEM((images, C_HEAD), FULL)] * 3,
        4 * images * C_HEAD * CLASSES,
        PIX * images * C_HEAD * 2,
    )(widened, norm, label, class_low, bias)


def head_back_kernel(
    widened_ref, grad_feats_ref, coef_ref, weight_ref, pair_ref, twice_ref, before_ref, norm_ref,
    route_ref, balance_ref, router_ref,
    grad_wide_ref, grad_normed_ref, logit_ref, sums_ref,
    product, mixed,
):
    half = 2 * 2 * C_OUT

    @pl.when(pl.program_id(0) == 0)
    def _():
        sums_ref[...] = jnp.zeros_like(sums_ref)

    gain, shift, by_value, constant = (coef_ref[k : k + 1] for k in range(4))
    grad_feats = grad_feats_ref[...]

    def widen(pixel, carry):
        value = widened_ref[pixel].astype(FULL)
        lifted = value * gain + shift
        part = sig(lifted)
        bent = part + lifted * part * (1.0 - part)
        grad = grad_feats * bent * gain + value * by_value + constant
        grad_wide_ref[pixel] = grad.astype(LOW)
        return carry

    lax.fori_loop(0, PIX, widen, 0)
    flat = grad_wide_ref[...].reshape(ROWS, C_HEAD)
    route_sums = []
    for part in range(2):
        product[part] = dot_nn(flat, weight_ref[:, part * half : (part + 1) * half]).reshape(
            PIX, GROUP, half
        )
    scales = [pair_ref[pair].astype(FULL) for pair in range(PAIRS)]

    def mix(pixel, carry):
        twice = twice_ref[pixel].astype(FULL)
        total = jnp.zeros((GROUP, 2 * C_OUT), FULL)
        found = []
        for pair in range(PAIRS):
            part, place = pair // 2, pair % 2 * 2 * C_OUT
            value = product[part, pixel, :, place : place + 2 * C_OUT]
            total = total + value * scales[pair]
            found.append(carry[pair] + value * twice)
        mixed[pixel] = (total + pltpu.roll(total, C_OUT, 1))[:, :C_OUT]
        return tuple(found)

    zero = jnp.zeros((GROUP, 2 * C_OUT), FULL)
    route_sums = lax.fori_loop(0, PIX, mix, (zero,) * PAIRS)
    route = route_ref[...]
    grad_route = pair_columns(route_sums, C_OUT) + balance_ref[...]
    logit = grad_route * route * (1.0 - route)
    logit_ref[...] = logit
    added = dot_nn(logit, router_ref[...], HIGH) * (1.0 / PIX)

    def close(pixel, carry):
        plain, cross = carry
        grad = mixed[pixel] + added
        grad_normed_ref[pixel] = grad
        hat = before_ref[pixel] * norm_ref[0:1] + norm_ref[1:2]
        return plain + grad, cross + grad * hat

    zero = jnp.zeros((GROUP, C_OUT), FULL)
    plain, cross = lax.fori_loop(0, PIX, close, (zero, zero))
    sums_ref[0:1] += jnp.sum(plain, axis=0, keepdims=True)
    sums_ref[1:2] += jnp.sum(cross, axis=0, keepdims=True)


def head_back(
    widened, grad_feats, coef, head_low, pair_two, twice, before, norm, route, balance, router_t
):
    images = widened.shape[1]
    wide = EXPERTS * C_OUT
    return device_kernel(
        head_back_kernel,
        "head_back",
        images // GROUP,
        [
            images_block(C_HEAD), group_block(C_HEAD), whole(4, C_HEAD), whole(C_HEAD, wide),
            pair_block(2 * C_OUT), images_block(2 * C_OUT), images_block(C_OUT), whole(2, C_OUT),
            group_block(EXPERTS), whole(1, EXPERTS), whole(EXPERTS, C_OUT),
        ],
        [
            ((PIX, images, C_HEAD), LOW), ((PIX, images, C_OUT), FULL), ((images, EXPERTS), FULL),
            ((2, C_OUT), FULL),
        ],
        [
            images_block(C_HEAD), images_block(C_OUT), group_block(EXPERTS), total_block(2, C_OUT),
        ],
        [pltpu.VMEM((2, PIX, GROUP, wide // 2), FULL), pltpu.VMEM((PIX, GROUP, C_OUT), FULL)],
        2 * PIX * images * wide * C_HEAD,
        PIX * images * (2 * C_HEAD + C_OUT) * 2,
    )(widened, grad_feats, coef, head_low, pair_two, twice, before, norm, route, balance, router_t)


def kern_grad_kernel(grad_ref, twice_ref, pair_ref, out_ref, turned, routed):
    images = twice_ref.shape[1]

    @pl.when(pl.program_id(0) == 0)
    def _():
        turned[...] = grad_ref[...].reshape(turned.shape[1], turned.shape[0]).T

    scale = pair_ref[0]
    for pixel in range(PIX):
        routed[pixel * images : (pixel + 1) * images] = twice_ref[pixel] * scale
    out_ref[...] = dot_nn(turned[...], routed[...]).astype(LOW)


def kern_grad(grad, twice, pair_scales, name):
    images, out_width, width = grad.shape[1], grad.shape[2], twice.shape[2]
    rows = PIX * images
    return device_kernel(
        kern_grad_kernel,
        name,
        PAIRS,
        [
            whole(PIX, images, out_width), whole(PIX, images, width),
            pl.BlockSpec((1, images, width), lambda i: (i, 0, 0)),
        ],
        [((out_width, PAIRS * width), LOW)],
        [pl.BlockSpec((out_width, width), lambda i: (0, i))],
        [pltpu.VMEM((out_width, rows), LOW), pltpu.VMEM((rows, width), LOW)],
        2 * rows * out_width * PAIRS * width,
        rows * out_width * 2,
    )(grad, twice, pair_scales)[0]


def project_grad_kernel(grad_ref, scaled_ref, scale_ref, out_ref, turned, routed):
    rows = turned.shape[1]

    @pl.when(pl.program_id(0) == 0)
    def _():
        turned[...] = grad_ref[...].reshape(rows, C_OUT).T

    for side in range(2):
        routed[side * C_OUT : (side + 1) * C_OUT] = turned[...] * scale_ref[0, side : side + 1]
    product = dot_nn(routed[...], scaled_ref[...].reshape(rows, C_MID)).astype(LOW)
    for side in range(2):
        out_ref[:, side * C_MID : (side + 1) * C_MID] = product[side * C_OUT : (side + 1) * C_OUT]


def project_grad(grad, scaled, scale):
    images = grad.shape[1]
    rows = PIX * images
    return device_kernel(
        project_grad_kernel,
        "project_grad",
        PAIRS,
        [
            whole(PIX, images, C_OUT), whole(PIX, images, C_MID),
            pl.BlockSpec((1, 2, rows), lambda i: (i, 0, 0)),
        ],
        [((C_OUT, EXPERTS * C_MID), LOW)],
        [pl.BlockSpec((C_OUT, 2 * C_MID), lambda i: (0, i))],
        [pltpu.VMEM((C_OUT, rows), LOW), pltpu.VMEM((2 * C_OUT, rows), LOW)],
        2 * rows * EXPERTS * C_OUT * C_MID,
        rows * (C_OUT + C_MID) * 2,
    )(grad, scaled, scale)[0]


def project_back_kernel(
    grad_ref, before_ref, coef_ref, pair_ref, each_ref, source,
    grad_before_ref, grad_scaled_ref, route_ref,
    routed, padded, weight_ref, sem,
):
    @pl.when(pl.program_id(0) == 0)
    def _():
        stack_experts(source, weight_ref, sem)
        padded[...] = jnp.zeros_like(padded)

    gain, by_value, constant = (coef_ref[k : k + 1] for k in range(3))
    scales = [pair_ref[pair] for pair in range(PAIRS)]

    def turn(pixel, carry):
        grad = grad_ref[pixel] * gain + before_ref[pixel] * by_value + constant
        grad = grad.astype(LOW)
        grad_before_ref[pixel] = grad
        padded[:, :C_OUT] = grad.astype(FULL)
        value = padded[...]
        value = value + pltpu.roll(value, C_OUT, 1)
        low = value.astype(LOW)
        found = []
        for pair in range(PAIRS):
            place = slice(2 * pair * C_OUT, 2 * (pair + 1) * C_OUT)
            routed[pixel, :, place] = low * scales[pair]
            found.append(carry[pair] + each_ref[pixel, :, place].astype(FULL) * value)
        return tuple(found)

    zero = jnp.zeros((GROUP, 2 * C_OUT), FULL)
    route_sums = lax.fori_loop(0, PIX, turn, (zero,) * PAIRS)
    route_ref[...] = pair_columns(route_sums, C_OUT)
    product = dot_nn(routed[...].reshape(ROWS, EXPERTS * C_OUT), weight_ref[...])
    grad_scaled_ref[...] = product.reshape(PIX, GROUP, C_MID).astype(LOW)


def project_back(grad_normed, before, coef, pair_out, each, project_low):
    images = before.shape[1]
    wide = EXPERTS * C_OUT
    return device_kernel(
        project_back_kernel,
        "project_back",
        images // GROUP,
        [
            images_block(C_OUT), images_block(C_OUT), whole(3, C_OUT), pair_block(2 * C_OUT),
            images_block(wide), pl.BlockSpec(memory_space=pl.ANY),
        ],
        [
            ((PIX, images, C_OUT), LOW), ((PIX, images, C_MID), LOW), ((images, EXPERTS), FULL),
        ],
        [images_block(C_OUT), images_block(C_MID), group_block(EXPERTS)],
        [
            pltpu.VMEM((PIX, GROUP, wide), LOW), pltpu.VMEM((GROUP, 2 * C_OUT), FULL),
            pltpu.VMEM((wide, C_MID), LOW), pltpu.SemaphoreType.DMA((EXPERTS,)),
        ],
        2 * PIX * images * wide * C_MID,
        PIX * images * (C_MID + wide) * 2,
    )(grad_normed, before, coef, pair_out, each, project_low)


def expand_back_kernel(
    grad_scaled_ref, turned_ref, hidden_ref, img_ref, gate_ref, squeeze_ref, excite_ref, depth_ref,
    route_ref, route_part_ref, balance_ref, weight_ref,
    grad_hidden_ref, logit_ref, grad_gate_ref, grad_squeeze_ref, grad_depth_ref,
    kern, start, grad_turned, grad_kern, pooled, product,
):
    @pl.when(pl.program_id(0) == 0)
    def _():
        grad_depth_ref[...] = jnp.zeros_like(grad_depth_ref)

    route = route_ref[...]
    low = route.astype(LOW).astype(FULL)
    columns = [low[:, expert : expert + 1] for expert in range(EXPERTS)]
    for tap in range(KSIZE * KSIZE):
        total = columns[0] * depth_ref[tap, 0:1, :]
        for expert in range(1, EXPERTS):
            total = total + columns[expert] * depth_ref[tap, expert : expert + 1, :]
        kern[tap] = total

    def gate_sum(pixel, carry):
        value = turned_ref[pixel].astype(FULL)
        return carry + grad_scaled_ref[pixel].astype(FULL) * (value * sig(value))

    gate = gate_ref[...]
    grad_gate = lax.fori_loop(0, PIX, gate_sum, jnp.zeros((GROUP, C_MID), FULL))
    grad_gate = grad_gate * gate * (1.0 - gate)
    grad_gate_ref[...] = grad_gate
    squeeze = squeeze_ref[...]
    part = sig(squeeze)
    grad_squeeze = dot_nt(grad_gate, excite_ref[1], HIGH) * (part + squeeze * part * (1.0 - part))
    grad_squeeze_ref[...] = grad_squeeze
    pooled[...] = dot_nn(grad_squeeze, excite_ref[0], HIGH) * (1.0 / PIX)

    def chunk(index, carry):
        lanes = pl.ds(pl.multiple_of(index * 128, 128), 128)
        gate_part = gate_ref[:, lanes]
        pooled_part = pooled[:, lanes]
        for pixel in range(PIX):
            value = turned_ref[pixel, :, lanes].astype(FULL)
            part = sig(value)
            grad = grad_scaled_ref[pixel, :, lanes].astype(FULL) * gate_part + pooled_part
            grad_turned[pixel] = grad * (part + value * part * (1.0 - part))
            value = hidden_ref[pixel, :, lanes].astype(FULL)
            start[pixel] = value * sig(value)
        taps = [kern[tap, :, lanes] for tap in range(KSIZE * KSIZE)]
        sums = [None] * (KSIZE * KSIZE)
        for pixel in range(PIX):
            total = None
            here = grad_turned[pixel]
            for tap, source in taps_of(pixel):
                term = start[source] * here
                sums[tap] = term if sums[tap] is None else sums[tap] + term
                term = grad_turned[source] * taps[KSIZE * KSIZE - 1 - tap]
                total = term if total is None else total + term
            value = hidden_ref[pixel, :, lanes].astype(FULL)
            part = sig(value)
            grad = total * (part + value * part * (1.0 - part))
            grad_hidden_ref[pixel, :, lanes] = grad.astype(LOW)
        for tap in range(KSIZE * KSIZE):
            grad_kern[tap, :, lanes] = sums[tap]
        return carry

    lax.fori_loop(0, C_MID // 128, chunk, 0)
    depth_term = jnp.zeros((GROUP, EXPERTS), FULL)
    for tap in range(KSIZE * KSIZE):
        value = grad_kern[tap]
        grad_depth_ref[tap] += dot_tn(low, value, HIGH)
        depth_term = depth_term + dot_nt(value, depth_ref[tap], HIGH)
    product[...] = dot_nn(grad_hidden_ref[...].reshape(ROWS, C_MID), weight_ref[...]).reshape(
        PIX, GROUP, EXPERTS * C_IN
    )

    def route_part(pixel, carry):
        value = img_ref[pixel].astype(FULL)
        return tuple(
            carry[pair] + product[pixel, :, 2 * pair * C_IN : 2 * (pair + 1) * C_IN] * value
            for pair in range(PAIRS)
        )

    zero = jnp.zeros((GROUP, 2 * C_IN), FULL)
    route_sums = lax.fori_loop(0, PIX, route_part, (zero,) * PAIRS)
    grad_route = (
        pair_columns(route_sums, C_IN) + route_part_ref[...] + depth_term + balance_ref[...]
    )
    logit_ref[...] = grad_route * route * (1.0 - route)


def expand_back(
    grad_scaled, turned, hidden, img_two, gate, squeeze, excite, depth_full, route, route_part,
    balance, expand_low,
):
    images = hidden.shape[1]
    taps = KSIZE * KSIZE
    return device_kernel(
        expand_back_kernel,
        "expand_back",
        images // GROUP,
        [
            images_block(C_MID), images_block(C_MID), images_block(C_MID), images_block(2 * C_IN),
            group_block(C_MID), group_block(C_SE), whole(2, C_SE, C_MID),
            whole(taps, EXPERTS, C_MID), group_block(EXPERTS), group_block(EXPERTS),
            whole(1, EXPERTS), whole(C_MID, EXPERTS * C_IN),
        ],
        [
            ((PIX, images, C_MID), LOW), ((images, EXPERTS), FULL), ((images, C_MID), FULL),
            ((images, C_SE), FULL), ((taps, EXPERTS, C_MID), FULL),
        ],
        [
            images_block(C_MID), group_block(EXPERTS), group_block(C_MID), group_block(C_SE),
            total_block(taps, EXPERTS, C_MID),
        ],
        [
            pltpu.VMEM((taps, GROUP, C_MID), FULL), pltpu.VMEM((PIX, GROUP, 128), FULL),
            pltpu.VMEM((PIX, GROUP, 128), FULL), pltpu.VMEM((taps, GROUP, C_MID), FULL),
            pltpu.VMEM((GROUP, C_MID), FULL), pltpu.VMEM((PIX, GROUP, EXPERTS * C_IN), FULL),
        ],
        2 * PIX * images * EXPERTS * C_IN * C_MID,
        PIX * images * 4 * C_MID * 2,
    )(
        grad_scaled, turned, hidden, img_two, gate, squeeze, excite, depth_full, route, route_part,
        balance, expand_low,
    )


def soap_kernel(
    gained, weight_ref, grad_ref, first_ref, second_ref, state_ref,
    first_out, second_out, state_out, weight_out, raised,
):
    step = pl.program_id(0)
    height, width = weight_ref.shape
    half = width // 2
    upper = -(-half // 128) * 128
    lower = half // 128 * 128
    corr_one = 1.0 - beta_one**STEP
    corr_two = 1.0 - beta_two**STEP

    def iota(shape, axis):
        return lax.broadcasted_iota(jnp.int32, shape, axis)

    pick = (iota((height, BLK), 0) % BLK == iota((height, BLK), 1)).astype(FULL)
    pick_t = (iota((BLK, height), 1) % BLK == iota((BLK, height), 0)).astype(FULL)
    same = iota((height, height), 0) // BLK == iota((height, height), 1) // BLK
    ones = same.astype(FULL)

    def spread_out(rows):
        return jnp.where(same, dot_nn(pick, rows, HIGH), 0.0)

    def by_half(product, value):
        first = product(0, value[:, :upper])
        second = product(1, value[:, lower:])
        if upper == lower:
            return jnp.concatenate([first, second], axis=1)
        lane = iota((height, upper - lower), 1)
        middle = jnp.where(lane < half - lower, first[:, lower:], second[:, : upper - lower])
        return jnp.concatenate([first[:, :lower], middle, second[:, upper - lower :]], axis=1)

    old = [state_ref[1, 2 * step + side] for side in range(2)]
    turns = [spread_out(rows) for rows in old]
    grad = grad_ref[...].astype(FULL)
    turned = by_half(lambda side, value: dot_nn(turns[side], value, HIGH), grad)
    first_new = beta_one * first_ref[...] + (1.0 - beta_one) * grad
    second_new = beta_two * second_ref[...] + (1.0 - beta_two) * (turned * turned)
    first_out[...] = first_new
    second_out[...] = second_new
    moment = by_half(lambda side, value: dot_nn(turns[side], value, HIGH), first_new)
    ratio = moment / corr_one / (jnp.sqrt(second_new / corr_two) + eps_adam)
    back = by_half(lambda side, value: dot_tn(turns[side], value, HIGH), ratio)
    weight = weight_ref[...]
    weight_out[...] = weight - rate_matrix * (back + decay * weight)

    for side in range(2):
        if side == 0:
            piece = grad[:, :upper]
            piece = jnp.where(iota(piece.shape, 1) < half, piece, 0.0)
        else:
            piece = grad[:, lower:]
            piece = jnp.where(iota(piece.shape, 1) >= half - lower, piece, 0.0)
        gram = jnp.where(same, dot_nt(piece, piece, HIGH), 0.0)
        summed = beta_two * state_ref[0, 2 * step + side]
        summed = summed + (1.0 - beta_two) * gained * dot_nn(pick_t, gram, HIGH)
        diagonal = jnp.sum(summed * pick_t, axis=0, keepdims=True)
        trace = dot_nn(diagonal, ones, HIGH)
        stats = summed / trace
        state_out[0, 2 * step + side] = stats
        lifted = dot_nn(old[side], spread_out(stats), HIGH)
        for column in range(BLK):
            raised[column, pl.ds(2 * step + side, 1), :] = lifted[column : column + 1]

    @pl.when(step == pl.num_programs(0) - 1)
    def _():
        columns = []
        for index in range(BLK):
            column = raised[index]
            for previous in columns:
                column = column - dot_nn(previous * column, ones, HIGH) * previous
            column = column * lax.rsqrt(dot_nn(column * column, ones, HIGH))
            columns.append(column)
            for expert in range(EXPERTS):
                state_out[1, expert, index : index + 1, :] = column[expert : expert + 1]


def soap(weight, grad, first, second, state, every):
    height, total = weight.shape
    width = total // PAIRS
    turned_state = state.transpose(0, 1, 3, 2)
    gained = stat_gain * every / (total // EXPERTS)
    column = pl.BlockSpec((height, width), lambda i: (0, i))
    sheet = jax.ShapeDtypeStruct(weight.shape, FULL)
    first_new, second_new, state_new, weight_new = device_kernel(
        functools.partial(soap_kernel, gained),
        "soap",
        PAIRS,
        [column, column, column, column, whole(2, EXPERTS, BLK, height)],
        [(weight.shape, FULL), (weight.shape, FULL), (turned_state.shape, FULL),
         (weight.shape, FULL)],
        [column, column, total_block(2, EXPERTS, BLK, height), column],
        [pltpu.VMEM((BLK, EXPERTS, height), FULL)],
        2 * height * height * total,
        weight.size * 26,
    )(weight, grad, first, second, turned_state)
    return (first_new, second_new, state_new.transpose(0, 1, 3, 2), weight_new)


def adam(weight, grad, first, second, rate):
    corr_one = 1.0 - beta_one**STEP
    corr_two = 1.0 - beta_two**STEP
    first_new = beta_one * first + (1.0 - beta_one) * grad
    second_new = beta_two * second + (1.0 - beta_two) * grad * grad
    weight_new = weight - rate * (
        first_new / corr_one / (jnp.sqrt(second_new / corr_two) + eps_adam) + decay * weight
    )
    return (first_new, second_new, weight_new)


def local(
    images,
    dom_label,
    class_label,
    expand_weight,
    expand_first,
    expand_second,
    expand_state,
    project_weight,
    project_first,
    project_second,
    project_state,
    head_weight,
    head_first,
    head_second,
    head_state,
    depth_weight,
    depth_first,
    depth_second,
    classifier_weight,
    classifier_first,
    classifier_second,
    excite_weight,
    excite_first,
    excite_second,
    router_weight,
    router_first,
    router_second,
    gains_weight,
    gains_first,
    gains_second,
):
    low_type = jnp.bfloat16
    images_here = images.shape[0]
    every = images.shape[0] * lax.axis_size("dp") * lax.axis_size("wide")
    count = every * PIX
    bias_se, bias_ex, gain_one, shift_one, gain_two, shift_two, bias_cls = split_gains(gains_weight)
    hot = boost * (dom_label[:, None] == jnp.arange(EXPERTS)[None, :]).astype(jnp.float32)
    img = images.transpose(1, 0, 2)
    img_two = jnp.concatenate([img, img], axis=2)
    expand_low = lax.all_gather(expand_weight.astype(low_type), "wide", axis=0, tiled=True)
    project_low = lax.all_gather(project_weight.astype(low_type), "wide", axis=0, tiled=True)
    head_low = lax.all_gather(head_weight.astype(low_type), "wide", axis=0, tiled=True)
    class_low = lax.all_gather(classifier_weight.astype(low_type), "wide", axis=0, tiled=True)
    depth_own = depth_weight.astype(low_type).transpose(2, 0, 1).reshape(depth_weight.shape[2], -1)
    depth_low = lax.all_gather(depth_own, "wide", axis=0, tiled=True)
    depth_full = depth_low.reshape(C_MID, EXPERTS, KSIZE * KSIZE).transpose(2, 1, 0).astype(FULL)
    excite = excite_weight.transpose(0, 2, 1)
    router = router_weight.T
    router_one, router_two = router[:, :C_IN], router[:, C_IN:]

    (
        hidden, turned, scaled, route_one, pair_in, pair_one, gate, squeeze, pooled_one,
        pooled_act, route_one_sum,
    ) = expand_forward(
        img_two, hot, router_one, expand_low, depth_full, excite, bias_se[None], bias_ex[None]
    )
    each, before, sums_one = project_forward(scaled, project_low, pair_one)
    sums_one, route_one_sum = sum_all((sums_one, route_one_sum), 1)
    center_one = sums_one[0] / count
    inv_one = lax.rsqrt(sums_one[1] / count - center_one * center_one + eps_norm)
    scale_one = inv_one * gain_one
    norm_one = jnp.stack([scale_one, shift_one - center_one * scale_one])
    widened, twice, route_two, pair_two, pooled_two, sums_two, route_two_sum = head_forward(
        before, norm_one, hot, router_two, head_low
    )
    sums_two, route_two_sum = sum_all((sums_two, route_two_sum), 2)
    center_two = sums_two[0] / count
    inv_two = lax.rsqrt(sums_two[1] / count - center_two * center_two + eps_norm)
    scale_two = inv_two * gain_two
    norm_two = jnp.stack(
        [scale_two, shift_two - center_two * scale_two, inv_two, -center_two * inv_two]
        + [jnp.full_like(inv_two, 1.0 / every)] * 4
    )
    feats, grad_logits, grad_feats, back_two, cross_part, grad_bias_cls = loss_part(
        widened, norm_two, class_label[:, None], class_low, bias_cls[None]
    )
    grad_class = dot_tn(feats, grad_logits)
    back_two, cross_total, grad_bias_cls = sum_all((back_two, cross_part, grad_bias_cls), 3)
    means_one = route_one_sum[0] / every
    means_two = route_two_sum[0] / every
    by_value = -scale_two * inv_two * back_two[1] / count
    coef_two = jnp.stack(
        [
            scale_two, shift_two - center_two * scale_two, by_value,
            -scale_two * back_two[0] / count - center_two * by_value,
        ]
    )
    hat_one = jnp.stack([inv_one, -center_one * inv_one])
    grad_widened, grad_normed, grad_logit_two, back_one = head_back(
        widened, grad_feats, coef_two, head_low, pair_two, twice, before, hat_one, route_two,
        balance_grad(means_two, every)[None], router_two,
    )
    grad_head = kern_grad(grad_widened, twice, pair_two, "head_grad")
    grad_head, grad_class, back_one = lax.optimization_barrier((grad_head, grad_class, back_one))
    grad_router_two = dot_tn(pooled_two, grad_logit_two, HIGH)
    (back_one,) = sum_all((back_one,), 4)
    by_value = -scale_one * inv_one * back_one[1] / count
    coef_one = jnp.stack(
        [scale_one, by_value, -scale_one * back_one[0] / count - center_one * by_value]
    )
    grad_before, grad_scaled, route_project = project_back(
        grad_normed, before, coef_one, pair_one, each, project_low
    )
    row_scale = jnp.tile(route_one.astype(low_type).T, (1, PIX)).reshape(PAIRS, 2, -1)
    grad_project = project_grad(grad_before, scaled, row_scale)
    grad_project, grad_scaled = lax.optimization_barrier((grad_project, grad_scaled))
    grad_hidden, grad_logit_one, grad_gate, grad_squeeze, grad_depth = expand_back(
        grad_scaled, turned, hidden, img_two, gate, squeeze, excite, depth_full, route_one,
        route_project, balance_grad(means_one, every)[None], expand_low,
    )
    grad_expand = kern_grad(grad_hidden, img_two, pair_in, "expand_grad")
    grad_excite = jnp.stack(
        [
            dot_tn(pooled_act, grad_squeeze, HIGH),
            dot_tn(grad_gate, squeeze * jax.nn.sigmoid(squeeze), HIGH),
        ]
    )
    grad_router_one = dot_tn(pooled_one, grad_logit_one, HIGH)
    grad_depth = grad_depth.transpose(1, 0, 2)
    grad_bias_se = jnp.sum(grad_squeeze, axis=0)
    grad_bias_ex = jnp.sum(grad_gate, axis=0)
    small = lax.psum(
        (
            grad_excite,
            jnp.concatenate([grad_router_one, grad_router_two], axis=0),
            jnp.concatenate([grad_bias_se, grad_bias_ex]),
        ),
        ("dp", "wide"),
    )
    depth_flat = grad_depth.transpose(2, 0, 1).astype(low_type).reshape(C_MID, -1)
    full = (grad_expand, depth_flat, grad_project, grad_head, grad_class.astype(low_type))
    shares = [
        lax.psum_scatter(grad, "wide", scatter_dimension=0, tiled=True) for grad in full
    ]
    reduced = [lax.psum(share, "dp") for share in shares]
    depth_reduced = reduced[1].reshape(-1, EXPERTS, KSIZE * KSIZE).transpose(1, 2, 0)
    loss = cross_total[0, 0] / every + balance_weight * (
        jnp.mean((means_one - jnp.mean(means_one)) ** 2)
        + jnp.mean((means_two - jnp.mean(means_two)) ** 2)
    )
    grad_gains = jnp.concatenate(
        [small[2], back_one[1], back_one[0], back_two[1], back_two[0], grad_bias_cls[0]]
    )
    expand_out = soap(expand_weight, reduced[0], expand_first, expand_second, expand_state, every)
    project_out = soap(
        project_weight, reduced[2], project_first, project_second, project_state, every
    )
    head_out = soap(head_weight, reduced[3], head_first, head_second, head_state, every)
    depth_out = adam(
        depth_weight, depth_reduced.astype(FULL), depth_first, depth_second, rate_matrix
    )
    class_out = adam(
        classifier_weight, reduced[4].astype(FULL), classifier_first, classifier_second, rate_matrix
    )
    excite_out = adam(excite_weight, small[0], excite_first, excite_second, rate_matrix)
    router_out = adam(router_weight, small[1], router_first, router_second, rate_matrix)
    gains_out = adam(gains_weight, grad_gains, gains_first, gains_second, rate_gains)
    return (
        loss,
        expand_out[0],
        expand_out[1],
        expand_out[2],
        expand_out[3],
        project_out[0],
        project_out[1],
        project_out[2],
        project_out[3],
        head_out[0],
        head_out[1],
        head_out[2],
        head_out[3],
        depth_out[0],
        depth_out[1],
        depth_out[2],
        class_out[0],
        class_out[1],
        class_out[2],
        excite_out[0],
        excite_out[1],
        excite_out[2],
        router_out[0],
        router_out[1],
        router_out[2],
        gains_out[0],
        gains_out[1],
        gains_out[2],
    )


def solution(mesh):
    return jax.shard_map(
        local,
        mesh=mesh,
        in_specs=(
            P(("dp", "wide"), None, None),
            P(("dp", "wide")),
            P(("dp", "wide")),
            P("wide", None),
            P("wide", None),
            P("wide", None),
            P(None, None, "wide", None),
            P("wide", None),
            P("wide", None),
            P("wide", None),
            P(None, None, "wide", None),
            P("wide", None),
            P("wide", None),
            P("wide", None),
            P(None, None, "wide", None),
            P(None, None, "wide"),
            P(None, None, "wide"),
            P(None, None, "wide"),
            P("wide", None),
            P("wide", None),
            P("wide", None),
            P(),
            P(),
            P(),
            P(),
            P(),
            P(),
            P(),
            P(),
            P(),
        ),
        out_specs=(
            P(),
            P("wide", None),
            P("wide", None),
            P(None, None, "wide", None),
            P("wide", None),
            P("wide", None),
            P("wide", None),
            P(None, None, "wide", None),
            P("wide", None),
            P("wide", None),
            P("wide", None),
            P(None, None, "wide", None),
            P("wide", None),
            P(None, None, "wide"),
            P(None, None, "wide"),
            P(None, None, "wide"),
            P("wide", None),
            P("wide", None),
            P("wide", None),
            P(),
            P(),
            P(),
            P(),
            P(),
            P(),
            P(),
            P(),
            P(),
        ),
        check_vma=False,
    )
```

```python
import functools

import jax
import jax.numpy as jnp
from jax import lax
from jax.experimental import pallas as pl
from jax.experimental.pallas import tpu as pltpu
from jax.sharding import PartitionSpec as P

SIDE = 7
PIX = 49
KSIZE = 3
EXPERTS = 8
BLK = 4
STEP = 10
C_IN = 192
C_MID = 1152
C_SE = 48
C_OUT = 320
C_HEAD = 1280
CLASSES = 1000


HIGH = lax.Precision.HIGHEST
beta_one = 0.9
beta_two = 0.95
eps_adam = 1e-08
eps_norm = 1e-05
decay = 0.01
rate_matrix = 0.08
rate_gains = 0.5
boost = 1.0
balance_weight = 4.0
stat_gain = 15000.0


def split_gains(gains):
    widths = [C_SE, C_MID, C_OUT, C_OUT, C_HEAD, C_HEAD, CLASSES]
    pieces = []
    start = 0
    for width in widths:
        pieces.append(gains[start : start + width])
        start = start + width
    return pieces


MESH = pl.DeviceIdType.MESH


def sum_kernel(n_wide, n_dp, x_ref, o_ref, wide_slots, dp_slots, part, s_wide, r_wide, s_dp, r_dp):
    me_wide = lax.axis_index("wide")
    me_dp = lax.axis_index("dp")
    barrier = pltpu.get_barrier_semaphore()
    for k in range(1, n_wide):
        pl.semaphore_signal(
            barrier, inc=1, device_id={"wide": lax.rem(me_wide + k, n_wide)}, device_id_type=MESH
        )
    for k in range(1, n_dp):
        pl.semaphore_signal(
            barrier, inc=1, device_id={"dp": lax.rem(me_dp + k, n_dp)}, device_id_type=MESH
        )
    pl.semaphore_wait(barrier, n_wide + n_dp - 2)

    def exchange(src, slots, me, axis, size, send, recv):
        copies = []
        for k in range(1, size):
            copy = pltpu.make_async_remote_copy(
                src_ref=src,
                dst_ref=slots.at[me],
                send_sem=send.at[k],
                recv_sem=recv.at[k],
                device_id={axis: lax.rem(me + k, size)},
                device_id_type=MESH,
            )
            copy.start()
            copies.append(copy)
        slots[me] = src[...]
        for copy in copies:
            copy.wait()
        total = slots[0]
        for k in range(1, size):
            total = total + slots[k]
        return total

    part[...] = exchange(x_ref, wide_slots, me_wide, "wide", n_wide, s_wide, r_wide)
    o_ref[...] = exchange(part, dp_slots, me_dp, "dp", n_dp, s_dp, r_dp)


def sum_all(parts, ident):
    shapes = [part.shape for part in parts]
    sizes = [part.size for part in parts]
    flat = jnp.concatenate([part.reshape(-1) for part in parts])
    rows = -(-flat.size // 1024) * 8
    flat = jnp.pad(flat, (0, rows * 128 - flat.size)).reshape(rows, 128)
    n_wide = lax.axis_size("wide")
    n_dp = lax.axis_size("dp")
    out = pl.pallas_call(
        functools.partial(sum_kernel, n_wide, n_dp),
        out_shape=jax.ShapeDtypeStruct((rows, 128), jnp.float32),
        in_specs=[pl.BlockSpec(memory_space=pltpu.VMEM)],
        out_specs=pl.BlockSpec(memory_space=pltpu.VMEM),
        scratch_shapes=[
            pltpu.VMEM((n_wide, rows, 128), jnp.float32),
            pltpu.VMEM((n_dp, rows, 128), jnp.float32),
            pltpu.VMEM((rows, 128), jnp.float32),
            pltpu.SemaphoreType.DMA((n_wide,)),
            pltpu.SemaphoreType.DMA((n_wide,)),
            pltpu.SemaphoreType.DMA((n_dp,)),
            pltpu.SemaphoreType.DMA((n_dp,)),
        ],
        compiler_params=pltpu.CompilerParams(collective_id=ident, has_side_effects=True),
    )(flat)
    out = out.reshape(-1)
    found = []
    start = 0
    for shape, size in zip(shapes, sizes):
        found.append(out[start : start + size].reshape(shape))
        start = start + size
    return found


def balance_grad(means, every):
    return balance_weight * 2.0 * (means - jnp.mean(means)) / (EXPERTS * every)


GROUP = 16
PAIRS = EXPERTS // 2
ROWS = PIX * GROUP
CLASS_PAD = 1024
LOW = jnp.bfloat16
FULL = jnp.float32
VMEM_CAP = 60 * 1024 * 1024


def sig(value):
    return 0.5 + 0.5 * jnp.tanh(0.5 * value)


def dot_nn(left, right, precision=None):
    return lax.dot_general(
        left, right, (((1,), (0,)), ((), ())), precision=precision, preferred_element_type=FULL
    )


def dot_nt(left, right, precision=None):
    return lax.dot_general(
        left, right, (((1,), (1,)), ((), ())), precision=precision, preferred_element_type=FULL
    )


def dot_tn(left, right, precision=None):
    return lax.dot_general(
        left, right, (((0,), (0,)), ((), ())), precision=precision, preferred_element_type=FULL
    )


def images_block(width):
    return pl.BlockSpec((PIX, GROUP, width), lambda i: (0, i, 0))


def group_block(width):
    return pl.BlockSpec((GROUP, width), lambda i: (i, 0))


def pair_block(width):
    return pl.BlockSpec((PAIRS, GROUP, width), lambda i: (0, i, 0))


def whole(*shape):
    return pl.BlockSpec(shape, lambda i: (0,) * len(shape), pipeline_mode=pl.Buffered(1))


def total_block(*shape):
    return pl.BlockSpec(shape, lambda i: (0,) * len(shape))


def device_kernel(kernel, name, grid, in_specs, outs, out_specs, scratch, flops, moved):
    return pl.pallas_call(
        kernel,
        name=name,
        grid=(grid,),
        in_specs=in_specs,
        out_shape=[jax.ShapeDtypeStruct(shape, dtype) for shape, dtype in outs],
        out_specs=out_specs,
        scratch_shapes=scratch,
        compiler_params=pltpu.CompilerParams(
            vmem_limit_bytes=VMEM_CAP, dimension_semantics=("arbitrary",)
        ),
        cost_estimate=pl.CostEstimate(flops=flops, bytes_accessed=moved, transcendentals=0),
    )


def pair_scale(route, pair, width):
    lane = lax.broadcasted_iota(jnp.int32, (route.shape[0], 2 * width), 1)
    return jnp.where(
        lane < width, route[:, 2 * pair : 2 * pair + 1], route[:, 2 * pair + 1 : 2 * pair + 2]
    )


def pair_columns(sums, width):
    count = sums[0].shape[0]
    lane = lax.broadcasted_iota(jnp.int32, (count, 2 * width), 1)
    place = lax.broadcasted_iota(jnp.int32, (count, EXPERTS), 1)
    found = jnp.zeros((count, EXPERTS), FULL)
    for pair in range(PAIRS):
        first = jnp.sum(jnp.where(lane < width, sums[pair], 0.0), axis=1, keepdims=True)
        second = jnp.sum(jnp.where(lane < width, 0.0, sums[pair]), axis=1, keepdims=True)
        found = found + jnp.where(place == 2 * pair, first, 0.0)
        found = found + jnp.where(place == 2 * pair + 1, second, 0.0)
    return found


def taps_of(pixel):
    row, col = pixel // SIDE, pixel % SIDE
    found = []
    for tap in range(KSIZE * KSIZE):
        at_row, at_col = row + tap // KSIZE - 1, col + tap % KSIZE - 1
        if 0 <= at_row < SIDE and 0 <= at_col < SIDE:
            found.append((tap, at_row * SIDE + at_col))
    return found


def expand_kernel(
    img_ref, hot_ref, router_ref, expand_ref, depth_ref, excite_ref, bias_se_ref, bias_ex_ref,
    hidden_ref, turned_ref, scaled_ref, route_ref, pair_in_ref, pair_out_ref, gate_ref,
    squeeze_ref, pooled_one_ref, pooled_act_ref, route_sum_ref,
    routed, hidden_full, act_full, kern,
):
    pooled = img_ref[0].astype(FULL)
    for pixel in range(1, PIX):
        pooled = pooled + img_ref[pixel].astype(FULL)
    pooled = pooled[:, :C_IN] * (1.0 / PIX)
    pooled_one_ref[...] = pooled
    route = sig(dot_nt(pooled, router_ref[...], HIGH) + hot_ref[...])
    route_ref[...] = route

    @pl.when(pl.program_id(0) == 0)
    def _():
        route_sum_ref[...] = jnp.zeros_like(route_sum_ref)

    route_sum_ref[...] += jnp.sum(route, axis=0, keepdims=True)
    low = route.astype(LOW).astype(FULL)
    for pair in range(PAIRS):
        scale = pair_scale(low, pair, C_IN).astype(LOW)
        pair_in_ref[pair] = scale
        pair_out_ref[pair] = pair_scale(low, pair, C_OUT).astype(LOW)
        place = slice(2 * pair * C_IN, 2 * (pair + 1) * C_IN)
        for pixel in range(PIX):
            routed[pixel, :, place] = img_ref[pixel] * scale
    columns = [low[:, expert : expert + 1] for expert in range(EXPERTS)]
    for tap in range(KSIZE * KSIZE):
        total = columns[0] * depth_ref[tap, 0:1, :]
        for expert in range(1, EXPERTS):
            total = total + columns[expert] * depth_ref[tap, expert : expert + 1, :]
        kern[tap] = total
    product = dot_nt(routed[...].reshape(ROWS, EXPERTS * C_IN), expand_ref[...])
    hidden_full[...] = product.reshape(PIX, GROUP, C_MID)

    def chunk(index, carry):
        lanes = pl.ds(pl.multiple_of(index * 128, 128), 128)
        taps = [kern[tap, :, lanes] for tap in range(KSIZE * KSIZE)]
        start = [None] * PIX

        def fill(row):
            for pixel in range(row * SIDE, row * SIDE + SIDE):
                value = hidden_full[pixel, :, lanes]
                hidden_ref[pixel, :, lanes] = value.astype(LOW)
                start[pixel] = value * sig(value)

        fill(0)
        pooled_act = jnp.zeros((GROUP, 128), FULL)
        for row in range(SIDE):
            if row + 1 < SIDE:
                fill(row + 1)
            for pixel in range(row * SIDE, row * SIDE + SIDE):
                total = None
                for tap, source in taps_of(pixel):
                    term = start[source] * taps[tap]
                    total = term if total is None else total + term
                turned_ref[pixel, :, lanes] = total.astype(LOW)
                act = total * sig(total)
                pooled_act = pooled_act + act
                act_full[pixel, :, lanes] = act
        pooled_act_ref[:, lanes] = pooled_act * (1.0 / PIX)
        return carry

    lax.fori_loop(0, C_MID // 128, chunk, 0)
    squeeze = dot_nt(pooled_act_ref[...], excite_ref[0], HIGH) + bias_se_ref[...]
    squeeze_ref[...] = squeeze
    gate = sig(dot_nn(squeeze * sig(squeeze), excite_ref[1], HIGH) + bias_ex_ref[...])
    gate_ref[...] = gate

    def finish(pixel, carry):
        scaled_ref[pixel] = (act_full[pixel] * gate).astype(LOW)
        return carry

    lax.fori_loop(0, PIX, finish, 0)


def expand_forward(img_two, hot, router, expand_low, depth_full, excite, bias_se, bias_ex):
    images = img_two.shape[1]
    return device_kernel(
        expand_kernel,
        "expand_forward",
        images // GROUP,
        [
            images_block(2 * C_IN), group_block(EXPERTS), whole(EXPERTS, C_IN),
            whole(C_MID, EXPERTS * C_IN), whole(KSIZE * KSIZE, EXPERTS, C_MID),
            whole(2, C_SE, C_MID), whole(1, C_SE), whole(1, C_MID),
        ],
        [
            ((PIX, images, C_MID), LOW), ((PIX, images, C_MID), LOW), ((PIX, images, C_MID), LOW),
            ((images, EXPERTS), FULL), ((PAIRS, images, 2 * C_IN), LOW),
            ((PAIRS, images, 2 * C_OUT), LOW), ((images, C_MID), FULL), ((images, C_SE), FULL),
            ((images, C_IN), FULL), ((images, C_MID), FULL), ((1, EXPERTS), FULL),
        ],
        [
            images_block(C_MID), images_block(C_MID), images_block(C_MID), group_block(EXPERTS),
            pair_block(2 * C_IN), pair_block(2 * C_OUT), group_block(C_MID), group_block(C_SE),
            group_block(C_IN), group_block(C_MID), total_block(1, EXPERTS),
        ],
        [
            pltpu.VMEM((PIX, GROUP, EXPERTS * C_IN), LOW), pltpu.VMEM((PIX, GROUP, C_MID), FULL),
            pltpu.VMEM((PIX, GROUP, C_MID), FULL), pltpu.VMEM((KSIZE * KSIZE, GROUP, C_MID), FULL),
        ],
        2 * PIX * images * EXPERTS * C_IN * C_MID,
        PIX * images * 4 * C_MID * 2,
    )(img_two, hot, router, expand_low, depth_full, excite, bias_se, bias_ex)


def stack_experts(source, stacked, sem):
    copies = [
        pltpu.make_async_copy(
            source.at[:, expert * C_MID : (expert + 1) * C_MID],
            stacked.at[expert * C_OUT : (expert + 1) * C_OUT],
            sem.at[expert],
        )
        for expert in range(EXPERTS)
    ]
    for copy in copies:
        copy.start()
    for copy in copies:
        copy.wait()


def project_kernel(
    scaled_ref, source, pair_ref, each_ref, before_ref, sums_ref, product, weight_ref, sem
):
    half = 2 * 2 * C_OUT
    flat = scaled_ref[...].reshape(ROWS, C_MID)

    @pl.when(pl.program_id(0) == 0)
    def _():
        stack_experts(source, weight_ref, sem)
        sums_ref[...] = jnp.zeros_like(sums_ref)

    for part in range(2):
        product[part] = dot_nt(flat, weight_ref[part * half : (part + 1) * half]).reshape(
            PIX, GROUP, half
        )
    scales = [pair_ref[pair].astype(FULL) for pair in range(PAIRS)]

    def mix(pixel, carry):
        plain, square = carry
        total = jnp.zeros((GROUP, 2 * C_OUT), FULL)
        for pair in range(PAIRS):
            part, place = pair // 2, pair % 2 * 2 * C_OUT
            value = product[part, pixel, :, place : place + 2 * C_OUT]
            each_ref[pixel, :, pair * 2 * C_OUT : (pair + 1) * 2 * C_OUT] = value.astype(LOW)
            total = total + value * scales[pair]
        before = (total + pltpu.roll(total, C_OUT, 1))[:, :C_OUT]
        before_ref[pixel] = before
        return plain + before, square + before * before

    zero = jnp.zeros((GROUP, C_OUT), FULL)
    plain, square = lax.fori_loop(0, PIX, mix, (zero, zero))
    sums_ref[0:1] += jnp.sum(plain, axis=0, keepdims=True)
    sums_ref[1:2] += jnp.sum(square, axis=0, keepdims=True)


def project_forward(scaled, project_low, pair_out):
    images = scaled.shape[1]
    wide = EXPERTS * C_OUT
    return device_kernel(
        project_kernel,
        "project_forward",
        images // GROUP,
        [images_block(C_MID), pl.BlockSpec(memory_space=pl.ANY), pair_block(2 * C_OUT)],
        [((PIX, images, wide), LOW), ((PIX, images, C_OUT), FULL), ((2, C_OUT), FULL)],
        [images_block(wide), images_block(C_OUT), total_block(2, C_OUT)],
        [
            pltpu.VMEM((2, PIX, GROUP, wide // 2), FULL), pltpu.VMEM((wide, C_MID), LOW),
            pltpu.SemaphoreType.DMA((EXPERTS,)),
        ],
        2 * PIX * images * wide * C_MID,
        PIX * images * (wide + C_MID) * 2,
    )(scaled, project_low, pair_out)


def head_kernel(
    before_ref, norm_ref, hot_ref, router_ref, weight_ref,
    widened_ref, twice_ref, route_ref, pair_ref, pooled_ref, sums_ref, route_sum_ref,
    routed, padded,
):
    @pl.when(pl.program_id(0) == 0)
    def _():
        sums_ref[...] = jnp.zeros_like(sums_ref)
        route_sum_ref[...] = jnp.zeros_like(route_sum_ref)
        padded[...] = jnp.zeros_like(padded)

    gain, shift = norm_ref[0:1], norm_ref[1:2]
    pooled = jnp.zeros((GROUP, C_OUT), FULL)
    for pixel in range(PIX):
        normed = (before_ref[pixel] * gain + shift).astype(LOW).astype(FULL)
        pooled = pooled + normed
        padded[:, :C_OUT] = normed
        value = padded[...]
        twice_ref[pixel] = (value + pltpu.roll(value, C_OUT, 1)).astype(LOW)
    pooled = pooled * (1.0 / PIX)
    pooled_ref[...] = pooled
    route = sig(dot_nt(pooled, router_ref[...], HIGH) + hot_ref[...])
    route_ref[...] = route
    route_sum_ref[...] += jnp.sum(route, axis=0, keepdims=True)
    low = route.astype(LOW).astype(FULL)
    for pair in range(PAIRS):
        scale = pair_scale(low, pair, C_OUT).astype(LOW)
        pair_ref[pair] = scale
        place = slice(2 * pair * C_OUT, 2 * (pair + 1) * C_OUT)
        for pixel in range(PIX):
            routed[pixel, :, place] = twice_ref[pixel] * scale
    product = dot_nt(routed[...].reshape(ROWS, EXPERTS * C_OUT), weight_ref[...])
    widened_ref[...] = product.reshape(PIX, GROUP, C_HEAD).astype(LOW)
    sums_ref[0:1] += jnp.sum(product, axis=0, keepdims=True)
    sums_ref[1:2] += jnp.sum(product * product, axis=0, keepdims=True)


def head_forward(before, norm, hot, router, head_low):
    images = before.shape[1]
    wide = EXPERTS * C_OUT
    return device_kernel(
        head_kernel,
        "head_forward",
        images // GROUP,
        [
            images_block(C_OUT), whole(2, C_OUT), group_block(EXPERTS), whole(EXPERTS, C_OUT),
            whole(C_HEAD, wide),
        ],
        [
            ((PIX, images, C_HEAD), LOW), ((PIX, images, 2 * C_OUT), LOW),
            ((images, EXPERTS), FULL), ((PAIRS, images, 2 * C_OUT), LOW), ((images, C_OUT), FULL),
            ((2, C_HEAD), FULL), ((1, EXPERTS), FULL),
        ],
        [
            images_block(C_HEAD), images_block(2 * C_OUT), group_block(EXPERTS),
            pair_block(2 * C_OUT), group_block(C_OUT), total_block(2, C_HEAD),
            total_block(1, EXPERTS),
        ],
        [pltpu.VMEM((PIX, GROUP, wide), LOW), pltpu.VMEM((GROUP, 2 * C_OUT), FULL)],
        2 * PIX * images * wide * C_HEAD,
        PIX * images * (C_HEAD + C_OUT) * 2,
    )(before, norm, hot, router, head_low)


def loss_kernel(
    widened_ref, norm_ref, label_ref, class_ref, bias_ref,
    feats_ref, logits_ref, grad_feats_ref, sums_ref, cross_ref, bias_grad_ref,
    silu_sum, slope_sum, cross_sum,
):
    step = pl.program_id(0)
    rows = pl.ds(pl.multiple_of(step * GROUP, GROUP), GROUP)
    gain, shift, inv, offset = (norm_ref[k : k + 1] for k in range(4))

    def pixel_sums(pixel, carry):
        total, slope, moved = carry
        value = widened_ref[pixel].astype(FULL)
        lifted = value * gain + shift
        part = sig(lifted)
        grown = lifted * part
        bent = part + grown * (1.0 - part)
        return total + grown, slope + bent, moved + bent * (value * inv + offset)

    zero = jnp.zeros((GROUP, C_HEAD), FULL)
    total, slope, moved = lax.fori_loop(0, PIX, pixel_sums, (zero, zero, zero))
    silu_sum[rows] = total
    slope_sum[rows] = slope
    cross_sum[rows] = moved

    @pl.when(step == pl.num_programs(0) - 1)
    def _():
        feats = (silu_sum[...] * (1.0 / PIX)).astype(LOW)
        feats_ref[...] = feats
        logits = dot_nn(feats, class_ref[...]) + bias_ref[...]
        lane = lax.broadcasted_iota(jnp.int32, logits.shape, 1)
        picked = lane == label_ref[...]
        top = jnp.max(logits, axis=1, keepdims=True)
        powers = jnp.exp(logits - top)
        totals = jnp.sum(powers, axis=1, keepdims=True)
        cross = top + jnp.log(totals) - jnp.sum(
            jnp.where(picked, logits, 0.0), axis=1, keepdims=True
        )
        cross_ref[...] = jnp.sum(cross, axis=0, keepdims=True)
        grad = (powers / totals - jnp.where(picked, 1.0, 0.0)) * norm_ref[4:5, 0:1]
        grad = grad.astype(LOW)
        logits_ref[...] = jnp.zeros_like(logits_ref)
        logits_ref[:, :CLASSES] = grad
        bias_grad_ref[...] = jnp.sum(grad.astype(FULL), axis=0, keepdims=True)
        grad_feats = dot_nt(grad, class_ref[...]) * (1.0 / PIX)
        grad_feats_ref[...] = grad_feats
        sums_ref[0:1] = jnp.sum(grad_feats * slope_sum[...], axis=0, keepdims=True)
        sums_ref[1:2] = jnp.sum(grad_feats * cross_sum[...], axis=0, keepdims=True)


def loss_part(widened, norm, label, class_low, bias):
    images = widened.shape[1]
    return device_kernel(
        loss_kernel,
        "loss_part",
        images // GROUP,
        [
            images_block(C_HEAD), whole(8, C_HEAD), whole(images, 1), whole(C_HEAD, CLASSES),
            whole(1, CLASSES),
        ],
        [
            ((images, C_HEAD), LOW), ((images, CLASS_PAD), LOW), ((images, C_HEAD), FULL),
            ((2, C_HEAD), FULL), ((1, 1), FULL), ((1, CLASSES), FULL),
        ],
        [
            total_block(images, C_HEAD), total_block(images, CLASS_PAD), total_block(images, C_HEAD),
            total_block(2, C_HEAD), total_block(1, 1), total_block(1, CLASSES),
        ],
        [pltpu.VMEM((images, C_HEAD), FULL)] * 3,
        4 * images * C_HEAD * CLASSES,
        PIX * images * C_HEAD * 2,
    )(widened, norm, label, class_low, bias)


def head_back_kernel(
    widened_ref, grad_feats_ref, coef_ref, weight_ref, pair_ref, twice_ref, before_ref, norm_ref,
    route_ref, balance_ref, router_ref,
    grad_wide_ref, grad_normed_ref, logit_ref, sums_ref,
    product, mixed,
):
    half = 2 * 2 * C_OUT

    @pl.when(pl.program_id(0) == 0)
    def _():
        sums_ref[...] = jnp.zeros_like(sums_ref)

    gain, shift, by_value, constant = (coef_ref[k : k + 1] for k in range(4))
    grad_feats = grad_feats_ref[...]

    def widen(pixel, carry):
        value = widened_ref[pixel].astype(FULL)
        lifted = value * gain + shift
        part = sig(lifted)
        bent = part + lifted * part * (1.0 - part)
        grad = grad_feats * bent * gain + value * by_value + constant
        grad_wide_ref[pixel] = grad.astype(LOW)
        return carry

    lax.fori_loop(0, PIX, widen, 0)
    flat = grad_wide_ref[...].reshape(ROWS, C_HEAD)
    route_sums = []
    for part in range(2):
        product[part] = dot_nn(flat, weight_ref[:, part * half : (part + 1) * half]).reshape(
            PIX, GROUP, half
        )
    scales = [pair_ref[pair].astype(FULL) for pair in range(PAIRS)]

    def mix(pixel, carry):
        twice = twice_ref[pixel].astype(FULL)
        total = jnp.zeros((GROUP, 2 * C_OUT), FULL)
        found = []
        for pair in range(PAIRS):
            part, place = pair // 2, pair % 2 * 2 * C_OUT
            value = product[part, pixel, :, place : place + 2 * C_OUT]
            total = total + value * scales[pair]
            found.append(carry[pair] + value * twice)
        mixed[pixel] = (total + pltpu.roll(total, C_OUT, 1))[:, :C_OUT]
        return tuple(found)

    zero = jnp.zeros((GROUP, 2 * C_OUT), FULL)
    route_sums = lax.fori_loop(0, PIX, mix, (zero,) * PAIRS)
    route = route_ref[...]
    grad_route = pair_columns(route_sums, C_OUT) + balance_ref[...]
    logit = grad_route * route * (1.0 - route)
    logit_ref[...] = logit
    added = dot_nn(logit, router_ref[...], HIGH) * (1.0 / PIX)

    def close(pixel, carry):
        plain, cross = carry
        grad = mixed[pixel] + added
        grad_normed_ref[pixel] = grad
        hat = before_ref[pixel] * norm_ref[0:1] + norm_ref[1:2]
        return plain + grad, cross + grad * hat

    zero = jnp.zeros((GROUP, C_OUT), FULL)
    plain, cross = lax.fori_loop(0, PIX, close, (zero, zero))
    sums_ref[0:1] += jnp.sum(plain, axis=0, keepdims=True)
    sums_ref[1:2] += jnp.sum(cross, axis=0, keepdims=True)


def head_back(
    widened, grad_feats, coef, head_low, pair_two, twice, before, norm, route, balance, router_t
):
    images = widened.shape[1]
    wide = EXPERTS * C_OUT
    return device_kernel(
        head_back_kernel,
        "head_back",
        images // GROUP,
        [
            images_block(C_HEAD), group_block(C_HEAD), whole(4, C_HEAD), whole(C_HEAD, wide),
            pair_block(2 * C_OUT), images_block(2 * C_OUT), images_block(C_OUT), whole(2, C_OUT),
            group_block(EXPERTS), whole(1, EXPERTS), whole(EXPERTS, C_OUT),
        ],
        [
            ((PIX, images, C_HEAD), LOW), ((PIX, images, C_OUT), FULL), ((images, EXPERTS), FULL),
            ((2, C_OUT), FULL),
        ],
        [
            images_block(C_HEAD), images_block(C_OUT), group_block(EXPERTS), total_block(2, C_OUT),
        ],
        [pltpu.VMEM((2, PIX, GROUP, wide // 2), FULL), pltpu.VMEM((PIX, GROUP, C_OUT), FULL)],
        2 * PIX * images * wide * C_HEAD,
        PIX * images * (2 * C_HEAD + C_OUT) * 2,
    )(widened, grad_feats, coef, head_low, pair_two, twice, before, norm, route, balance, router_t)


def kern_grad_kernel(grad_ref, twice_ref, pair_ref, out_ref, turned, routed):
    images = twice_ref.shape[1]

    @pl.when(pl.program_id(0) == 0)
    def _():
        turned[...] = grad_ref[...].reshape(turned.shape[1], turned.shape[0]).T

    scale = pair_ref[0]
    for pixel in range(PIX):
        routed[pixel * images : (pixel + 1) * images] = twice_ref[pixel] * scale
    out_ref[0] = dot_nn(turned[...], routed[...]).astype(LOW)


def kern_grad(grad, twice, pair_scales, name):
    images, out_width, width = grad.shape[1], grad.shape[2], twice.shape[2]
    rows = PIX * images
    return device_kernel(
        kern_grad_kernel,
        name,
        PAIRS,
        [
            whole(PIX, images, out_width), whole(PIX, images, width),
            pl.BlockSpec((1, images, width), lambda i: (i, 0, 0)),
        ],
        [((PAIRS, out_width, width), LOW)],
        [pl.BlockSpec((1, out_width, width), lambda i: (i, 0, 0))],
        [pltpu.VMEM((out_width, rows), LOW), pltpu.VMEM((rows, width), LOW)],
        2 * rows * out_width * PAIRS * width,
        rows * out_width * 2,
    )(grad, twice, pair_scales)[0]


def project_grad_kernel(grad_ref, scaled_ref, scale_ref, out_ref, turned, routed):
    rows = turned.shape[1]

    @pl.when(pl.program_id(0) == 0)
    def _():
        turned[...] = grad_ref[...].reshape(rows, C_OUT).T

    for side in range(2):
        routed[side * C_OUT : (side + 1) * C_OUT] = turned[...] * scale_ref[0, side : side + 1]
    product = dot_nn(routed[...], scaled_ref[...].reshape(rows, C_MID)).astype(LOW)
    for side in range(2):
        out_ref[0, :, side * C_MID : (side + 1) * C_MID] = product[
            side * C_OUT : (side + 1) * C_OUT
        ]


def project_grad(grad, scaled, scale):
    images = grad.shape[1]
    rows = PIX * images
    return device_kernel(
        project_grad_kernel,
        "project_grad",
        PAIRS,
        [
            whole(PIX, images, C_OUT), whole(PIX, images, C_MID),
            pl.BlockSpec((1, 2, rows), lambda i: (i, 0, 0)),
        ],
        [((PAIRS, C_OUT, 2 * C_MID), LOW)],
        [pl.BlockSpec((1, C_OUT, 2 * C_MID), lambda i: (i, 0, 0))],
        [pltpu.VMEM((C_OUT, rows), LOW), pltpu.VMEM((2 * C_OUT, rows), LOW)],
        2 * rows * EXPERTS * C_OUT * C_MID,
        rows * (C_OUT + C_MID) * 2,
    )(grad, scaled, scale)[0]


def project_back_kernel(
    grad_ref, before_ref, coef_ref, pair_ref, each_ref, source,
    grad_before_ref, grad_scaled_ref, route_ref,
    routed, padded, weight_ref, sem,
):
    @pl.when(pl.program_id(0) == 0)
    def _():
        stack_experts(source, weight_ref, sem)
        padded[...] = jnp.zeros_like(padded)

    gain, by_value, constant = (coef_ref[k : k + 1] for k in range(3))
    scales = [pair_ref[pair] for pair in range(PAIRS)]

    def turn(pixel, carry):
        grad = grad_ref[pixel] * gain + before_ref[pixel] * by_value + constant
        grad = grad.astype(LOW)
        grad_before_ref[pixel] = grad
        padded[:, :C_OUT] = grad.astype(FULL)
        value = padded[...]
        value = value + pltpu.roll(value, C_OUT, 1)
        low = value.astype(LOW)
        found = []
        for pair in range(PAIRS):
            place = slice(2 * pair * C_OUT, 2 * (pair + 1) * C_OUT)
            routed[pixel, :, place] = low * scales[pair]
            found.append(carry[pair] + each_ref[pixel, :, place].astype(FULL) * value)
        return tuple(found)

    zero = jnp.zeros((GROUP, 2 * C_OUT), FULL)
    route_sums = lax.fori_loop(0, PIX, turn, (zero,) * PAIRS)
    route_ref[...] = pair_columns(route_sums, C_OUT)
    product = dot_nn(routed[...].reshape(ROWS, EXPERTS * C_OUT), weight_ref[...])
    grad_scaled_ref[...] = product.reshape(PIX, GROUP, C_MID).astype(LOW)


def project_back(grad_normed, before, coef, pair_out, each, project_low):
    images = before.shape[1]
    wide = EXPERTS * C_OUT
    return device_kernel(
        project_back_kernel,
        "project_back",
        images // GROUP,
        [
            images_block(C_OUT), images_block(C_OUT), whole(3, C_OUT), pair_block(2 * C_OUT),
            images_block(wide), pl.BlockSpec(memory_space=pl.ANY),
        ],
        [
            ((PIX, images, C_OUT), LOW), ((PIX, images, C_MID), LOW), ((images, EXPERTS), FULL),
        ],
        [images_block(C_OUT), images_block(C_MID), group_block(EXPERTS)],
        [
            pltpu.VMEM((PIX, GROUP, wide), LOW), pltpu.VMEM((GROUP, 2 * C_OUT), FULL),
            pltpu.VMEM((wide, C_MID), LOW), pltpu.SemaphoreType.DMA((EXPERTS,)),
        ],
        2 * PIX * images * wide * C_MID,
        PIX * images * (C_MID + wide) * 2,
    )(grad_normed, before, coef, pair_out, each, project_low)


def expand_back_kernel(
    grad_scaled_ref, turned_ref, hidden_ref, img_ref, gate_ref, squeeze_ref, excite_ref, depth_ref,
    route_ref, route_part_ref, balance_ref, weight_ref,
    grad_hidden_ref, logit_ref, grad_gate_ref, grad_squeeze_ref, grad_depth_ref,
    kern, start, grad_turned, grad_kern, pooled, product,
):
    @pl.when(pl.program_id(0) == 0)
    def _():
        grad_depth_ref[...] = jnp.zeros_like(grad_depth_ref)

    route = route_ref[...]
    low = route.astype(LOW).astype(FULL)
    columns = [low[:, expert : expert + 1] for expert in range(EXPERTS)]
    for tap in range(KSIZE * KSIZE):
        total = columns[0] * depth_ref[tap, 0:1, :]
        for expert in range(1, EXPERTS):
            total = total + columns[expert] * depth_ref[tap, expert : expert + 1, :]
        kern[tap] = total

    def gate_sum(pixel, carry):
        value = turned_ref[pixel].astype(FULL)
        return carry + grad_scaled_ref[pixel].astype(FULL) * (value * sig(value))

    gate = gate_ref[...]
    grad_gate = lax.fori_loop(0, PIX, gate_sum, jnp.zeros((GROUP, C_MID), FULL))
    grad_gate = grad_gate * gate * (1.0 - gate)
    grad_gate_ref[...] = grad_gate
    squeeze = squeeze_ref[...]
    part = sig(squeeze)
    grad_squeeze = dot_nt(grad_gate, excite_ref[1], HIGH) * (part + squeeze * part * (1.0 - part))
    grad_squeeze_ref[...] = grad_squeeze
    pooled[...] = dot_nn(grad_squeeze, excite_ref[0], HIGH) * (1.0 / PIX)

    def chunk(index, carry):
        lanes = pl.ds(pl.multiple_of(index * 128, 128), 128)
        gate_part = gate_ref[:, lanes]
        pooled_part = pooled[:, lanes]
        for pixel in range(PIX):
            value = turned_ref[pixel, :, lanes].astype(FULL)
            part = sig(value)
            grad = grad_scaled_ref[pixel, :, lanes].astype(FULL) * gate_part + pooled_part
            grad_turned[pixel] = grad * (part + value * part * (1.0 - part))
            value = hidden_ref[pixel, :, lanes].astype(FULL)
            start[pixel] = value * sig(value)
        taps = [kern[tap, :, lanes] for tap in range(KSIZE * KSIZE)]
        sums = [None] * (KSIZE * KSIZE)
        for pixel in range(PIX):
            total = None
            here = grad_turned[pixel]
            for tap, source in taps_of(pixel):
                term = start[source] * here
                sums[tap] = term if sums[tap] is None else sums[tap] + term
                term = grad_turned[source] * taps[KSIZE * KSIZE - 1 - tap]
                total = term if total is None else total + term
            value = hidden_ref[pixel, :, lanes].astype(FULL)
            part = sig(value)
            grad = total * (part + value * part * (1.0 - part))
            grad_hidden_ref[pixel, :, lanes] = grad.astype(LOW)
        for tap in range(KSIZE * KSIZE):
            grad_kern[tap, :, lanes] = sums[tap]
        return carry

    lax.fori_loop(0, C_MID // 128, chunk, 0)
    depth_term = jnp.zeros((GROUP, EXPERTS), FULL)
    for tap in range(KSIZE * KSIZE):
        value = grad_kern[tap]
        grad_depth_ref[tap] += dot_tn(low, value, HIGH)
        depth_term = depth_term + dot_nt(value, depth_ref[tap], HIGH)
    product[...] = dot_nn(grad_hidden_ref[...].reshape(ROWS, C_MID), weight_ref[...]).reshape(
        PIX, GROUP, EXPERTS * C_IN
    )

    def route_part(pixel, carry):
        value = img_ref[pixel].astype(FULL)
        return tuple(
            carry[pair] + product[pixel, :, 2 * pair * C_IN : 2 * (pair + 1) * C_IN] * value
            for pair in range(PAIRS)
        )

    zero = jnp.zeros((GROUP, 2 * C_IN), FULL)
    route_sums = lax.fori_loop(0, PIX, route_part, (zero,) * PAIRS)
    grad_route = (
        pair_columns(route_sums, C_IN) + route_part_ref[...] + depth_term + balance_ref[...]
    )
    logit_ref[...] = grad_route * route * (1.0 - route)


def expand_back(
    grad_scaled, turned, hidden, img_two, gate, squeeze, excite, depth_full, route, route_part,
    balance, expand_low,
):
    images = hidden.shape[1]
    taps = KSIZE * KSIZE
    return device_kernel(
        expand_back_kernel,
        "expand_back",
        images // GROUP,
        [
            images_block(C_MID), images_block(C_MID), images_block(C_MID), images_block(2 * C_IN),
            group_block(C_MID), group_block(C_SE), whole(2, C_SE, C_MID),
            whole(taps, EXPERTS, C_MID), group_block(EXPERTS), group_block(EXPERTS),
            whole(1, EXPERTS), whole(C_MID, EXPERTS * C_IN),
        ],
        [
            ((PIX, images, C_MID), LOW), ((images, EXPERTS), FULL), ((images, C_MID), FULL),
            ((images, C_SE), FULL), ((taps, EXPERTS, C_MID), FULL),
        ],
        [
            images_block(C_MID), group_block(EXPERTS), group_block(C_MID), group_block(C_SE),
            total_block(taps, EXPERTS, C_MID),
        ],
        [
            pltpu.VMEM((taps, GROUP, C_MID), FULL), pltpu.VMEM((PIX, GROUP, 128), FULL),
            pltpu.VMEM((PIX, GROUP, 128), FULL), pltpu.VMEM((taps, GROUP, C_MID), FULL),
            pltpu.VMEM((GROUP, C_MID), FULL), pltpu.VMEM((PIX, GROUP, EXPERTS * C_IN), FULL),
        ],
        2 * PIX * images * EXPERTS * C_IN * C_MID,
        PIX * images * 4 * C_MID * 2,
    )(
        grad_scaled, turned, hidden, img_two, gate, squeeze, excite, depth_full, route, route_part,
        balance, expand_low,
    )


def reduce_kernel(n_wide, n_dp, n_full, n_share, *refs):
    n_in = n_full + n_share
    fulls, shares = refs[:n_full], refs[n_full:n_in]
    full_outs, share_outs, spread_out = refs[n_in : n_in + n_full], refs[n_in + n_full : 2 * n_in], refs[2 * n_in]
    scratch = list(refs[2 * n_in + 1 :])
    firsts, seconds, thirds, halves, lineds = (
        [scratch.pop(0) for _ in range(n_full)] for _ in range(5)
    )
    slots = [scratch.pop(0) for _ in range(n_share)]
    send, recv = scratch
    lines = n_wide // 2
    me_wide, me_dp = lax.axis_index("wide"), lax.axis_index("dp")
    core, line = lax.rem(me_wide, 2), lax.div(me_wide, 2)
    sibling = line * 2 + 1 - core
    used = [0]

    barrier = pltpu.get_barrier_semaphore()
    for k in range(1, n_wide):
        pl.semaphore_signal(
            barrier, inc=1, device_id={"wide": lax.rem(me_wide + k, n_wide)}, device_id_type=MESH
        )
    for k in range(1, n_dp):
        pl.semaphore_signal(
            barrier, inc=1, device_id={"dp": lax.rem(me_dp + k, n_dp)}, device_id_type=MESH
        )
    pl.semaphore_wait(barrier, n_wide + n_dp - 2)

    def launch(src, dst, device):
        copy = pltpu.make_async_remote_copy(
            src_ref=src, dst_ref=dst, send_sem=send.at[used[0]], recv_sem=recv.at[used[0]],
            device_id=device, device_id_type=MESH,
        )
        used[0] += 1
        copy.start()
        return copy

    def finish(copies):
        for copy in copies:
            copy.wait()

    def dp_peer(k):
        return lax.rem(me_dp + k, n_dp)

    to_sibling = [
        launch(full.at[:, :, 1 - core], first, {"wide": sibling})
        for full, first in zip(fulls, firsts)
    ]
    scattered = [
        launch(share.at[dp_peer(k)], slot.at[k - 1], {"dp": dp_peer(k)})
        for k in range(1, n_dp)
        for share, slot in zip(shares, slots)
    ]
    finish(to_sibling)
    for full, first, half in zip(fulls, firsts, halves):
        def pair_sum(index, carry, full=full, first=first, half=half):
            at_dp, at_line = lax.div(index, lines), lax.rem(index, lines)
            total = full[at_dp, at_line, core].astype(FULL) + first[at_dp, at_line].astype(FULL)
            half[at_dp, at_line] = total.astype(LOW)
            return carry

        lax.fori_loop(0, n_dp * lines, pair_sum, 0)
    across = [
        launch(half.at[dp_peer(k)], second.at[k - 1], {"dp": dp_peer(k)})
        for k in range(1, n_dp)
        for half, second in zip(halves, seconds)
    ]
    finish(scattered)
    for share, slot, out in zip(shares, slots, share_outs):
        total = share[me_dp].astype(FULL)
        for k in range(1, n_dp):
            total = total + slot[k - 1].astype(FULL)
        out[me_dp] = total.astype(LOW)
    finish(across)
    for half, second, lined in zip(halves, seconds, lineds):
        def dp_sum(at_line, carry, half=half, second=second, lined=lined):
            total = half[me_dp, at_line].astype(FULL)
            for k in range(1, n_dp):
                total = total + second[k - 1, at_line].astype(FULL)
            lined[at_line] = total.astype(LOW)
            return carry

        lax.fori_loop(0, lines, dp_sum, 0)
    along = []
    for k in range(1, lines):
        other = lax.rem(line + k, lines)
        for lined, third in zip(lineds, thirds):
            along.append(launch(lined.at[other], third.at[k - 1], {"wide": other * 2 + core}))
    gathered = [
        launch(out.at[me_dp], out.at[me_dp], {"dp": dp_peer(k)})
        for k in range(1, n_dp)
        for out in share_outs
    ]
    finish(along)
    for lined, third, out in zip(lineds, thirds, full_outs):
        total = lined[line].astype(FULL)
        for k in range(1, lines):
            total = total + third[k - 1].astype(FULL)
        out[me_dp] = total.astype(LOW)
    last = [
        launch(out.at[me_dp], out.at[me_dp], {"dp": dp_peer(k)})
        for out in reversed(full_outs)
        for k in range(1, n_dp)
    ]
    own = full_outs[-1]
    finish(last[: n_dp - 1])
    spread_out[me_wide] = own[...]
    everywhere = [
        launch(own, spread_out.at[me_wide], {"wide": lax.rem(me_wide + k, n_wide)})
        for k in range(1, n_wide)
    ]
    finish(last[n_dp - 1 :] + gathered + everywhere)


def reduce_grads(fulls, shares, ident):
    n_wide, n_dp = lax.axis_size("wide"), lax.axis_size("dp")
    lines = n_wide // 2
    views = [full.reshape((n_dp, lines, 2) + full.shape[2:]) for full in fulls]
    tails = [full.shape[2:] for full in fulls]
    copies = (
        len(fulls) * (1 + (n_dp - 1) * 2 + lines - 1) + len(shares) * 2 * (n_dp - 1) + n_wide - 1
    )
    vmem = pl.BlockSpec(memory_space=pltpu.VMEM)
    outs = [jax.ShapeDtypeStruct((n_dp,) + tail, LOW) for tail in tails]
    outs += [jax.ShapeDtypeStruct(share.shape, LOW) for share in shares]
    outs += [jax.ShapeDtypeStruct((n_wide, n_dp) + tails[-1], LOW)]
    found = pl.pallas_call(
        functools.partial(reduce_kernel, n_wide, n_dp, len(fulls), len(shares)),
        name="reduce_grads",
        out_shape=outs,
        in_specs=[vmem] * (len(fulls) + len(shares)),
        out_specs=[vmem] * len(outs),
        scratch_shapes=[pltpu.VMEM((n_dp, lines) + tail, LOW) for tail in tails]
        + [pltpu.VMEM((n_dp - 1, lines) + tail, LOW) for tail in tails]
        + [pltpu.VMEM((lines - 1,) + tail, LOW) for tail in tails]
        + [pltpu.VMEM((n_dp, lines) + tail, LOW) for tail in tails]
        + [pltpu.VMEM((lines,) + tail, LOW) for tail in tails]
        + [pltpu.VMEM((n_dp - 1,) + share.shape[1:], LOW) for share in shares]
        + [pltpu.SemaphoreType.DMA((copies,)), pltpu.SemaphoreType.DMA((copies,))],
        compiler_params=pltpu.CompilerParams(
            collective_id=ident, has_side_effects=True, vmem_limit_bytes=VMEM_CAP
        ),
    )(*views, *shares)
    return found[: len(fulls)], found[len(fulls) : len(fulls) + len(shares)], found[-1]


def to_pieces(cube, count):
    pairs, rows, width = cube.shape
    if pairs == count:
        return cube
    more = count // pairs
    cube = cube.reshape(pairs, rows, more, width // more).transpose(0, 2, 1, 3)
    return cube.reshape(count, rows, width // more)


def from_pieces(pieces, pairs):
    count, rows, width = pieces.shape
    if pairs == count:
        return pieces
    more = count // pairs
    cube = pieces.reshape(pairs, more, rows, width).transpose(0, 2, 1, 3)
    return cube.reshape(pairs, rows, width * more)


def soap_kernel(
    gained, weight_ref, grad_ref, first_ref, second_ref, state_ref,
    first_out, second_out, state_out, weight_out, raised,
):
    step = pl.program_id(0)
    height, width = weight_ref.shape
    half = width // 2
    upper = -(-half // 128) * 128
    lower = half // 128 * 128
    corr_one = 1.0 - beta_one**STEP
    corr_two = 1.0 - beta_two**STEP

    def iota(shape, axis):
        return lax.broadcasted_iota(jnp.int32, shape, axis)

    pick = (iota((height, BLK), 0) % BLK == iota((height, BLK), 1)).astype(FULL)
    pick_t = (iota((BLK, height), 1) % BLK == iota((BLK, height), 0)).astype(FULL)
    same = iota((height, height), 0) // BLK == iota((height, height), 1) // BLK
    ones = same.astype(FULL)

    def spread_out(rows):
        return jnp.where(same, dot_nn(pick, rows, HIGH), 0.0)

    def by_half(product, value):
        first = product(0, value[:, :upper])
        second = product(1, value[:, lower:])
        if upper == lower:
            return jnp.concatenate([first, second], axis=1)
        lane = iota((height, upper - lower), 1)
        middle = jnp.where(lane < half - lower, first[:, lower:], second[:, : upper - lower])
        return jnp.concatenate([first[:, :lower], middle, second[:, upper - lower :]], axis=1)

    old = [state_ref[1, 2 * step + side] for side in range(2)]
    turns = [spread_out(rows) for rows in old]
    grad = grad_ref[0].astype(FULL)
    turned = by_half(lambda side, value: dot_nn(turns[side], value, HIGH), grad)
    first_new = beta_one * first_ref[...] + (1.0 - beta_one) * grad
    second_new = beta_two * second_ref[...] + (1.0 - beta_two) * (turned * turned)
    first_out[...] = first_new
    second_out[...] = second_new
    moment = by_half(lambda side, value: dot_nn(turns[side], value, HIGH), first_new)
    ratio = moment / corr_one / (jnp.sqrt(second_new / corr_two) + eps_adam)
    back = by_half(lambda side, value: dot_tn(turns[side], value, HIGH), ratio)
    weight = weight_ref[...]
    weight_out[...] = weight - rate_matrix * (back + decay * weight)

    for side in range(2):
        if side == 0:
            piece = grad[:, :upper]
            piece = jnp.where(iota(piece.shape, 1) < half, piece, 0.0)
        else:
            piece = grad[:, lower:]
            piece = jnp.where(iota(piece.shape, 1) >= half - lower, piece, 0.0)
        gram = jnp.where(same, dot_nt(piece, piece, HIGH), 0.0)
        summed = beta_two * state_ref[0, 2 * step + side]
        summed = summed + (1.0 - beta_two) * gained * dot_nn(pick_t, gram, HIGH)
        diagonal = jnp.sum(summed * pick_t, axis=0, keepdims=True)
        trace = dot_nn(diagonal, ones, HIGH)
        stats = summed / trace
        state_out[0, 2 * step + side] = stats
        lifted = dot_nn(old[side], spread_out(stats), HIGH)
        for column in range(BLK):
            raised[column, pl.ds(2 * step + side, 1), :] = lifted[column : column + 1]

    @pl.when(step == pl.num_programs(0) - 1)
    def _():
        columns = []
        for index in range(BLK):
            column = raised[index]
            for previous in columns:
                column = column - dot_nn(previous * column, ones, HIGH) * previous
            column = column * lax.rsqrt(dot_nn(column * column, ones, HIGH))
            columns.append(column)
            for expert in range(EXPERTS):
                state_out[1, expert, index : index + 1, :] = column[expert : expert + 1]


def soap(weight, grad, first, second, state, every):
    height, total = weight.shape
    width = total // PAIRS
    turned_state = state.transpose(0, 1, 3, 2)
    gained = stat_gain * every / (total // EXPERTS)
    column = pl.BlockSpec((height, width), lambda i: (0, i))
    first_new, second_new, state_new, weight_new = device_kernel(
        functools.partial(soap_kernel, gained),
        "soap",
        PAIRS,
        [
            column, pl.BlockSpec((1, height, width), lambda i: (i, 0, 0)), column, column,
            whole(2, EXPERTS, BLK, height),
        ],
        [(weight.shape, FULL), (weight.shape, FULL), (turned_state.shape, FULL),
         (weight.shape, FULL)],
        [column, column, total_block(2, EXPERTS, BLK, height), column],
        [pltpu.VMEM((BLK, EXPERTS, height), FULL)],
        2 * height * height * total,
        weight.size * 26,
    )(weight, grad, first, second, turned_state)
    return (first_new, second_new, state_new.transpose(0, 1, 3, 2), weight_new)


def adam(weight, grad, first, second, rate):
    corr_one = 1.0 - beta_one**STEP
    corr_two = 1.0 - beta_two**STEP
    first_new = beta_one * first + (1.0 - beta_one) * grad
    second_new = beta_two * second + (1.0 - beta_two) * grad * grad
    weight_new = weight - rate * (
        first_new / corr_one / (jnp.sqrt(second_new / corr_two) + eps_adam) + decay * weight
    )
    return (first_new, second_new, weight_new)


def local(
    images,
    dom_label,
    class_label,
    expand_weight,
    expand_first,
    expand_second,
    expand_state,
    project_weight,
    project_first,
    project_second,
    project_state,
    head_weight,
    head_first,
    head_second,
    head_state,
    depth_weight,
    depth_first,
    depth_second,
    classifier_weight,
    classifier_first,
    classifier_second,
    excite_weight,
    excite_first,
    excite_second,
    router_weight,
    router_first,
    router_second,
    gains_weight,
    gains_first,
    gains_second,
):
    low_type = jnp.bfloat16
    images_here = images.shape[0]
    every = images.shape[0] * lax.axis_size("dp") * lax.axis_size("wide")
    count = every * PIX
    bias_se, bias_ex, gain_one, shift_one, gain_two, shift_two, bias_cls = split_gains(gains_weight)
    hot = boost * (dom_label[:, None] == jnp.arange(EXPERTS)[None, :]).astype(jnp.float32)
    img = images.transpose(1, 0, 2)
    img_two = jnp.concatenate([img, img], axis=2)
    expand_low = lax.all_gather(expand_weight.astype(low_type), "wide", axis=0, tiled=True)
    project_low = lax.all_gather(project_weight.astype(low_type), "wide", axis=0, tiled=True)
    head_low = lax.all_gather(head_weight.astype(low_type), "wide", axis=0, tiled=True)
    class_low = lax.all_gather(classifier_weight.astype(low_type), "wide", axis=0, tiled=True)
    depth_own = depth_weight.astype(low_type).transpose(2, 0, 1).reshape(depth_weight.shape[2], -1)
    depth_low = lax.all_gather(depth_own, "wide", axis=0, tiled=True)
    depth_full = depth_low.reshape(C_MID, EXPERTS, KSIZE * KSIZE).transpose(2, 1, 0).astype(FULL)
    excite = excite_weight.transpose(0, 2, 1)
    router = router_weight.T
    router_one, router_two = router[:, :C_IN], router[:, C_IN:]

    (
        hidden, turned, scaled, route_one, pair_in, pair_one, gate, squeeze, pooled_one,
        pooled_act, route_one_sum,
    ) = expand_forward(
        img_two, hot, router_one, expand_low, depth_full, excite, bias_se[None], bias_ex[None]
    )
    each, before, sums_one = project_forward(scaled, project_low, pair_one)
    sums_one, route_one_sum = sum_all((sums_one, route_one_sum), 1)
    center_one = sums_one[0] / count
    inv_one = lax.rsqrt(sums_one[1] / count - center_one * center_one + eps_norm)
    scale_one = inv_one * gain_one
    norm_one = jnp.stack([scale_one, shift_one - center_one * scale_one])
    widened, twice, route_two, pair_two, pooled_two, sums_two, route_two_sum = head_forward(
        before, norm_one, hot, router_two, head_low
    )
    sums_two, route_two_sum = sum_all((sums_two, route_two_sum), 2)
    center_two = sums_two[0] / count
    inv_two = lax.rsqrt(sums_two[1] / count - center_two * center_two + eps_norm)
    scale_two = inv_two * gain_two
    norm_two = jnp.stack(
        [scale_two, shift_two - center_two * scale_two, inv_two, -center_two * inv_two]
        + [jnp.full_like(inv_two, 1.0 / every)] * 4
    )
    feats, grad_logits, grad_feats, back_two, cross_part, grad_bias_cls = loss_part(
        widened, norm_two, class_label[:, None], class_low, bias_cls[None]
    )
    grad_class = jnp.stack(
        [dot_tn(feats, part).astype(low_type) for part in jnp.split(grad_logits, PAIRS, axis=1)]
    )
    grad_class, grad_feats = lax.optimization_barrier((grad_class, grad_feats))
    share_class = lax.psum_scatter(grad_class, "wide", scatter_dimension=1, tiled=True)
    back_two, cross_total, grad_bias_cls = sum_all((back_two, cross_part, grad_bias_cls), 3)
    means_one = route_one_sum[0] / every
    means_two = route_two_sum[0] / every
    by_value = -scale_two * inv_two * back_two[1] / count
    coef_two = jnp.stack(
        [
            scale_two, shift_two - center_two * scale_two, by_value,
            -scale_two * back_two[0] / count - center_two * by_value,
        ]
    )
    hat_one = jnp.stack([inv_one, -center_one * inv_one])
    grad_widened, grad_normed, grad_logit_two, back_one = head_back(
        widened, grad_feats, coef_two, head_low, pair_two, twice, before, hat_one, route_two,
        balance_grad(means_two, every)[None], router_two,
    )
    share_class, twice = lax.optimization_barrier((share_class, twice))
    grad_head = kern_grad(grad_widened, twice, pair_two, "head_grad")
    grad_head, back_one = lax.optimization_barrier((grad_head, back_one))
    share_head = lax.psum_scatter(grad_head, "wide", scatter_dimension=1, tiled=True)
    grad_router_two = dot_tn(pooled_two, grad_logit_two, HIGH)
    (back_one,) = sum_all((back_one,), 4)
    by_value = -scale_one * inv_one * back_one[1] / count
    coef_one = jnp.stack(
        [scale_one, by_value, -scale_one * back_one[0] / count - center_one * by_value]
    )
    grad_before, grad_scaled, route_project = project_back(
        grad_normed, before, coef_one, pair_one, each, project_low
    )
    row_scale = jnp.tile(route_one.astype(low_type).T, (1, PIX)).reshape(PAIRS, 2, -1)
    grad_project = project_grad(grad_before, scaled, row_scale)
    grad_project, grad_scaled, share_head = lax.optimization_barrier(
        (grad_project, grad_scaled, share_head)
    )
    share_project = lax.psum_scatter(grad_project, "wide", scatter_dimension=1, tiled=True)
    grad_hidden, grad_logit_one, grad_gate, grad_squeeze, grad_depth = expand_back(
        grad_scaled, turned, hidden, img_two, gate, squeeze, excite, depth_full, route_one,
        route_project, balance_grad(means_one, every)[None], expand_low,
    )
    share_project, grad_hidden = lax.optimization_barrier((share_project, grad_hidden))
    grad_expand = kern_grad(grad_hidden, img_two, pair_in, "expand_grad")
    grad_excite = jnp.stack(
        [
            dot_tn(grad_squeeze, pooled_act, HIGH),
            dot_tn(squeeze * jax.nn.sigmoid(squeeze), grad_gate, HIGH),
        ]
    )
    grad_router_one = dot_tn(pooled_one, grad_logit_one, HIGH)
    grad_depth = grad_depth.transpose(1, 0, 2)
    grad_bias_se = jnp.sum(grad_squeeze, axis=0)
    grad_bias_ex = jnp.sum(grad_gate, axis=0)
    n_wide, n_dp = lax.axis_size("wide"), lax.axis_size("dp")
    parts = n_wide * n_dp
    depth_piece = grad_depth.size // parts
    extras = [
        grad_depth.reshape(-1, n_wide, depth_weight.shape[2]).transpose(1, 0, 2),
        jnp.concatenate(
            [
                grad_excite.reshape(-1), grad_router_one.reshape(-1), grad_router_two.reshape(-1),
                grad_bias_se, grad_bias_ex,
            ]
        ),
    ]
    depth_part = extras[0].reshape(n_wide, n_dp, depth_piece).transpose(1, 0, 2)
    rest_size = extras[1].size
    rest_piece = -(-rest_size // parts)
    rest_part = jnp.pad(extras[1], (0, rest_piece * parts - rest_size))
    rest_part = rest_part.reshape(n_dp, n_wide, rest_piece)
    extra_rows = -(-(depth_piece + rest_piece) // (16 * 384)) * 16
    extra = jnp.concatenate([depth_part, rest_part], axis=2).astype(low_type)
    extra = jnp.pad(extra, ((0, 0), (0, 0), (0, extra_rows * 384 - extra.shape[2])))
    extra = extra.reshape(n_dp, n_wide, extra_rows, 384)
    pieces = to_pieces(grad_expand, n_dp)
    pieces = pieces.reshape(n_dp, n_wide, -1, pieces.shape[2])
    (own_expand, own_extra), own_shares, every_extra = reduce_grads(
        [pieces, extra],
        [to_pieces(share, n_dp) for share in (share_project, share_head, share_class)],
        5,
    )
    sum_project, sum_head, sum_class = (from_pieces(share, PAIRS) for share in own_shares)
    sum_expand = from_pieces(own_expand, PAIRS)
    sum_class = sum_class.transpose(1, 0, 2).reshape(-1, CLASS_PAD)[:, :CLASSES].astype(FULL)
    own_extra = own_extra.reshape(n_dp, -1)[:, :depth_piece].reshape(EXPERTS, KSIZE * KSIZE, -1)
    rest = every_extra.reshape(n_wide, n_dp, -1)[:, :, depth_piece : depth_piece + rest_piece]
    rest = rest.transpose(1, 0, 2).reshape(-1)[:rest_size].astype(FULL)
    split = grad_excite.size
    sum_excite = rest[:split].reshape(2, C_SE, C_MID).transpose(0, 2, 1)
    sum_router = rest[split : split + router_weight.size].reshape(router_weight.shape)
    sum_bias = rest[split + router_weight.size :]
    loss = cross_total[0, 0] / every + balance_weight * (
        jnp.mean((means_one - jnp.mean(means_one)) ** 2)
        + jnp.mean((means_two - jnp.mean(means_two)) ** 2)
    )
    grad_gains = jnp.concatenate(
        [sum_bias, back_one[1], back_one[0], back_two[1], back_two[0], grad_bias_cls[0]]
    )
    expand_out = soap(expand_weight, sum_expand, expand_first, expand_second, expand_state, every)
    project_out = soap(
        project_weight, sum_project, project_first, project_second, project_state, every
    )
    head_out = soap(head_weight, sum_head, head_first, head_second, head_state, every)
    depth_out = adam(
        depth_weight, own_extra.astype(FULL), depth_first, depth_second, rate_matrix
    )
    class_out = adam(
        classifier_weight, sum_class, classifier_first, classifier_second, rate_matrix
    )
    excite_out = adam(excite_weight, sum_excite, excite_first, excite_second, rate_matrix)
    router_out = adam(router_weight, sum_router, router_first, router_second, rate_matrix)
    gains_out = adam(gains_weight, grad_gains, gains_first, gains_second, rate_gains)
    return (
        loss,
        expand_out[0],
        expand_out[1],
        expand_out[2],
        expand_out[3],
        project_out[0],
        project_out[1],
        project_out[2],
        project_out[3],
        head_out[0],
        head_out[1],
        head_out[2],
        head_out[3],
        depth_out[0],
        depth_out[1],
        depth_out[2],
        class_out[0],
        class_out[1],
        class_out[2],
        excite_out[0],
        excite_out[1],
        excite_out[2],
        router_out[0],
        router_out[1],
        router_out[2],
        gains_out[0],
        gains_out[1],
        gains_out[2],
    )


def solution(mesh):
    return jax.shard_map(
        local,
        mesh=mesh,
        in_specs=(
            P(("dp", "wide"), None, None),
            P(("dp", "wide")),
            P(("dp", "wide")),
            P("wide", None),
            P("wide", None),
            P("wide", None),
            P(None, None, "wide", None),
            P("wide", None),
            P("wide", None),
            P("wide", None),
            P(None, None, "wide", None),
            P("wide", None),
            P("wide", None),
            P("wide", None),
            P(None, None, "wide", None),
            P(None, None, "wide"),
            P(None, None, "wide"),
            P(None, None, "wide"),
            P("wide", None),
            P("wide", None),
            P("wide", None),
            P(),
            P(),
            P(),
            P(),
            P(),
            P(),
            P(),
            P(),
            P(),
        ),
        out_specs=(
            P(),
            P("wide", None),
            P("wide", None),
            P(None, None, "wide", None),
            P("wide", None),
            P("wide", None),
            P("wide", None),
            P(None, None, "wide", None),
            P("wide", None),
            P("wide", None),
            P("wide", None),
            P(None, None, "wide", None),
            P("wide", None),
            P(None, None, "wide"),
            P(None, None, "wide"),
            P(None, None, "wide"),
            P("wide", None),
            P("wide", None),
            P("wide", None),
            P(),
            P(),
            P(),
            P(),
            P(),
            P(),
            P(),
            P(),
            P(),
        ),
        check_vma=False,
    )
```

```python
import functools

import jax
import jax.numpy as jnp
from jax import lax
from jax.experimental import pallas as pl
from jax.experimental.pallas import tpu as pltpu
from jax.sharding import PartitionSpec as P

SIDE = 7
PIX = 49
KSIZE = 3
EXPERTS = 8
BLK = 4
STEP = 10
C_IN = 192
C_MID = 1152
C_SE = 48
C_OUT = 320
C_HEAD = 1280
CLASSES = 1000


HIGH = lax.Precision.HIGHEST
beta_one = 0.9
beta_two = 0.95
eps_adam = 1e-08
eps_norm = 1e-05
decay = 0.01
rate_matrix = 0.08
rate_gains = 0.5
boost = 1.0
balance_weight = 4.0
stat_gain = 15000.0


def split_gains(gains):
    widths = [C_SE, C_MID, C_OUT, C_OUT, C_HEAD, C_HEAD, CLASSES]
    pieces = []
    start = 0
    for width in widths:
        pieces.append(gains[start : start + width])
        start = start + width
    return pieces


MESH = pl.DeviceIdType.MESH


def sum_kernel(n_wide, n_dp, x_ref, o_ref, wide_slots, dp_slots, part, s_wide, r_wide, s_dp, r_dp):
    me_wide = lax.axis_index("wide")
    me_dp = lax.axis_index("dp")
    barrier = pltpu.get_barrier_semaphore()
    for k in range(1, n_wide):
        pl.semaphore_signal(
            barrier, inc=1, device_id={"wide": lax.rem(me_wide + k, n_wide)}, device_id_type=MESH
        )
    for k in range(1, n_dp):
        pl.semaphore_signal(
            barrier, inc=1, device_id={"dp": lax.rem(me_dp + k, n_dp)}, device_id_type=MESH
        )
    pl.semaphore_wait(barrier, n_wide + n_dp - 2)

    def exchange(src, slots, me, axis, size, send, recv):
        copies = []
        for k in range(1, size):
            copy = pltpu.make_async_remote_copy(
                src_ref=src,
                dst_ref=slots.at[me],
                send_sem=send.at[k],
                recv_sem=recv.at[k],
                device_id={axis: lax.rem(me + k, size)},
                device_id_type=MESH,
            )
            copy.start()
            copies.append(copy)
        slots[me] = src[...]
        for copy in copies:
            copy.wait()
        total = slots[0]
        for k in range(1, size):
            total = total + slots[k]
        return total

    part[...] = exchange(x_ref, wide_slots, me_wide, "wide", n_wide, s_wide, r_wide)
    o_ref[...] = exchange(part, dp_slots, me_dp, "dp", n_dp, s_dp, r_dp)


def sum_all(parts, ident):
    shapes = [part.shape for part in parts]
    sizes = [part.size for part in parts]
    flat = jnp.concatenate([part.reshape(-1) for part in parts])
    rows = -(-flat.size // 1024) * 8
    flat = jnp.pad(flat, (0, rows * 128 - flat.size)).reshape(rows, 128)
    n_wide = lax.axis_size("wide")
    n_dp = lax.axis_size("dp")
    out = pl.pallas_call(
        functools.partial(sum_kernel, n_wide, n_dp),
        out_shape=jax.ShapeDtypeStruct((rows, 128), jnp.float32),
        in_specs=[pl.BlockSpec(memory_space=pltpu.VMEM)],
        out_specs=pl.BlockSpec(memory_space=pltpu.VMEM),
        scratch_shapes=[
            pltpu.VMEM((n_wide, rows, 128), jnp.float32),
            pltpu.VMEM((n_dp, rows, 128), jnp.float32),
            pltpu.VMEM((rows, 128), jnp.float32),
            pltpu.SemaphoreType.DMA((n_wide,)),
            pltpu.SemaphoreType.DMA((n_wide,)),
            pltpu.SemaphoreType.DMA((n_dp,)),
            pltpu.SemaphoreType.DMA((n_dp,)),
        ],
        compiler_params=pltpu.CompilerParams(collective_id=ident, has_side_effects=True),
    )(flat)
    out = out.reshape(-1)
    found = []
    start = 0
    for shape, size in zip(shapes, sizes):
        found.append(out[start : start + size].reshape(shape))
        start = start + size
    return found


def balance_grad(means, every):
    return balance_weight * 2.0 * (means - jnp.mean(means)) / (EXPERTS * every)


GROUP = 16
PAIRS = EXPERTS // 2
ROWS = PIX * GROUP
CLASS_PAD = 1024
LOW = jnp.bfloat16
FULL = jnp.float32
VMEM_CAP = 60 * 1024 * 1024


def sig(value):
    return 0.5 + 0.5 * jnp.tanh(0.5 * value)


def dot_nn(left, right, precision=None):
    return lax.dot_general(
        left, right, (((1,), (0,)), ((), ())), precision=precision, preferred_element_type=FULL
    )


def dot_nt(left, right, precision=None):
    return lax.dot_general(
        left, right, (((1,), (1,)), ((), ())), precision=precision, preferred_element_type=FULL
    )


def dot_tn(left, right, precision=None):
    return lax.dot_general(
        left, right, (((0,), (0,)), ((), ())), precision=precision, preferred_element_type=FULL
    )


def images_block(width):
    return pl.BlockSpec((PIX, GROUP, width), lambda i: (0, i, 0))


def group_block(width):
    return pl.BlockSpec((GROUP, width), lambda i: (i, 0))


def pair_block(width):
    return pl.BlockSpec((PAIRS, GROUP, width), lambda i: (0, i, 0))


def whole(*shape):
    return pl.BlockSpec(shape, lambda i: (0,) * len(shape), pipeline_mode=pl.Buffered(1))


def total_block(*shape):
    return pl.BlockSpec(shape, lambda i: (0,) * len(shape))


def device_kernel(kernel, name, grid, in_specs, outs, out_specs, scratch, flops, moved):
    return pl.pallas_call(
        kernel,
        name=name,
        grid=(grid,),
        in_specs=in_specs,
        out_shape=[jax.ShapeDtypeStruct(shape, dtype) for shape, dtype in outs],
        out_specs=out_specs,
        scratch_shapes=scratch,
        compiler_params=pltpu.CompilerParams(
            vmem_limit_bytes=VMEM_CAP, dimension_semantics=("arbitrary",)
        ),
        cost_estimate=pl.CostEstimate(flops=flops, bytes_accessed=moved, transcendentals=0),
    )


def pair_scale(route, pair, width):
    lane = lax.broadcasted_iota(jnp.int32, (route.shape[0], 2 * width), 1)
    return jnp.where(
        lane < width, route[:, 2 * pair : 2 * pair + 1], route[:, 2 * pair + 1 : 2 * pair + 2]
    )


def pair_columns(sums, width):
    count = sums[0].shape[0]
    lane = lax.broadcasted_iota(jnp.int32, (count, 2 * width), 1)
    place = lax.broadcasted_iota(jnp.int32, (count, EXPERTS), 1)
    found = jnp.zeros((count, EXPERTS), FULL)
    for pair in range(PAIRS):
        first = jnp.sum(jnp.where(lane < width, sums[pair], 0.0), axis=1, keepdims=True)
        second = jnp.sum(jnp.where(lane < width, 0.0, sums[pair]), axis=1, keepdims=True)
        found = found + jnp.where(place == 2 * pair, first, 0.0)
        found = found + jnp.where(place == 2 * pair + 1, second, 0.0)
    return found


def taps_of(pixel):
    row, col = pixel // SIDE, pixel % SIDE
    found = []
    for tap in range(KSIZE * KSIZE):
        at_row, at_col = row + tap // KSIZE - 1, col + tap % KSIZE - 1
        if 0 <= at_row < SIDE and 0 <= at_col < SIDE:
            found.append((tap, at_row * SIDE + at_col))
    return found


def expand_kernel(
    img_ref, hot_ref, router_ref, source, depth_ref, excite_ref, bias_se_ref, bias_ex_ref,
    hidden_ref, turned_ref, scaled_ref, route_ref, pair_in_ref, pair_out_ref, gate_ref,
    squeeze_ref, pooled_one_ref, pooled_act_ref, route_sum_ref,
    routed, hidden_full, act_full, kern, expand_ref, sem,
):
    @pl.when(pl.program_id(0) == 0)
    def _():
        for copy in pair_copies(source, expand_ref, sem):
            copy.start()

    pooled = img_ref[0].astype(FULL)
    for pixel in range(1, PIX):
        pooled = pooled + img_ref[pixel].astype(FULL)
    pooled = pooled[:, :C_IN] * (1.0 / PIX)
    pooled_one_ref[...] = pooled
    route = sig(dot_nt(pooled, router_ref[...], HIGH) + hot_ref[...])
    route_ref[...] = route

    @pl.when(pl.program_id(0) == 0)
    def _():
        route_sum_ref[...] = jnp.zeros_like(route_sum_ref)

    route_sum_ref[...] += jnp.sum(route, axis=0, keepdims=True)
    low = route.astype(LOW).astype(FULL)
    for pair in range(PAIRS):
        scale = pair_scale(low, pair, C_IN).astype(LOW)
        pair_in_ref[pair] = scale
        pair_out_ref[pair] = pair_scale(low, pair, C_OUT).astype(LOW)
        place = slice(2 * pair * C_IN, 2 * (pair + 1) * C_IN)
        for pixel in range(PIX):
            routed[pixel, :, place] = img_ref[pixel] * scale
    columns = [low[:, expert : expert + 1] for expert in range(EXPERTS)]
    for tap in range(KSIZE * KSIZE):
        total = columns[0] * depth_ref[tap, 0:1, :]
        for expert in range(1, EXPERTS):
            total = total + columns[expert] * depth_ref[tap, expert : expert + 1, :]
        kern[tap] = total
    flat = routed[...].reshape(ROWS, EXPERTS * C_IN)
    third = C_MID // 3

    @pl.when(pl.program_id(0) == 0)
    def _():
        for copy in pair_copies(source, expand_ref, sem):
            copy.wait()

    def multiply(part):
        place = slice(part * third, (part + 1) * third)
        hidden_full[:, :, place] = dot_nt(flat, expand_ref[place]).reshape(PIX, GROUP, third)

    def chunk(index):
        lanes = slice(index * 128, index * 128 + 128)
        taps = [kern[tap, :, lanes] for tap in range(KSIZE * KSIZE)]
        start = [None] * PIX

        def fill(row):
            for pixel in range(row * SIDE, row * SIDE + SIDE):
                value = hidden_full[pixel, :, lanes]
                hidden_ref[pixel, :, lanes] = value.astype(LOW)
                start[pixel] = value * sig(value)

        fill(0)
        pooled_act = jnp.zeros((GROUP, 128), FULL)
        for row in range(SIDE):
            if row + 1 < SIDE:
                fill(row + 1)
            for pixel in range(row * SIDE, row * SIDE + SIDE):
                total = None
                for tap, source in taps_of(pixel):
                    term = start[source] * taps[tap]
                    total = term if total is None else total + term
                turned_ref[pixel, :, lanes] = total.astype(LOW)
                act = total * sig(total)
                pooled_act = pooled_act + act
                act_full[pixel, :, lanes] = act
        pooled_act_ref[:, lanes] = pooled_act * (1.0 / PIX)

    multiply(0)
    for part in range(3):
        if part < 2:
            multiply(part + 1)
        for index in range(3 * part, 3 * part + 3):
            chunk(index)
    squeeze = dot_nt(pooled_act_ref[...], excite_ref[0], HIGH) + bias_se_ref[...]
    squeeze_ref[...] = squeeze
    gate = sig(dot_nn(squeeze * sig(squeeze), excite_ref[1], HIGH) + bias_ex_ref[...])
    gate_ref[...] = gate

    def finish(pixel, carry):
        scaled_ref[pixel] = (act_full[pixel] * gate).astype(LOW)
        return carry

    lax.fori_loop(0, PIX, finish, 0, unroll=7)


def expand_forward(img_two, hot, router, expand_low, depth_full, excite, bias_se, bias_ex):
    images = img_two.shape[1]
    return device_kernel(
        expand_kernel,
        "expand_forward",
        images // GROUP,
        [
            images_block(2 * C_IN), group_block(EXPERTS), whole(EXPERTS, C_IN),
            pl.BlockSpec(memory_space=pl.ANY), whole(KSIZE * KSIZE, EXPERTS, C_MID),
            whole(2, C_SE, C_MID), whole(1, C_SE), whole(1, C_MID),
        ],
        [
            ((PIX, images, C_MID), LOW), ((PIX, images, C_MID), LOW), ((PIX, images, C_MID), LOW),
            ((images, EXPERTS), FULL), ((PAIRS, images, 2 * C_IN), LOW),
            ((PAIRS, images, 2 * C_OUT), LOW), ((images, C_MID), FULL), ((images, C_SE), FULL),
            ((images, C_IN), FULL), ((images, C_MID), FULL), ((1, EXPERTS), FULL),
        ],
        [
            images_block(C_MID), images_block(C_MID), images_block(C_MID), group_block(EXPERTS),
            pair_block(2 * C_IN), pair_block(2 * C_OUT), group_block(C_MID), group_block(C_SE),
            group_block(C_IN), group_block(C_MID), total_block(1, EXPERTS),
        ],
        [
            pltpu.VMEM((PIX, GROUP, EXPERTS * C_IN), LOW), pltpu.VMEM((PIX, GROUP, C_MID), FULL),
            pltpu.VMEM((PIX, GROUP, C_MID), FULL), pltpu.VMEM((KSIZE * KSIZE, GROUP, C_MID), FULL),
            pltpu.VMEM((C_MID, EXPERTS * C_IN), LOW), pltpu.SemaphoreType.DMA((PAIRS,)),
        ],
        2 * PIX * images * EXPERTS * C_IN * C_MID,
        PIX * images * 4 * C_MID * 2,
    )(img_two, hot, router, expand_low, depth_full, excite, bias_se, bias_ex)


def stack_experts(source, stacked, sem):
    copies = [
        pltpu.make_async_copy(
            source.at[:, expert * C_MID : (expert + 1) * C_MID],
            stacked.at[expert * C_OUT : (expert + 1) * C_OUT],
            sem.at[expert],
        )
        for expert in range(EXPERTS)
    ]
    for copy in copies:
        copy.start()
    for copy in copies:
        copy.wait()


def pair_copies(source, stacked, sem):
    width = source.shape[2]
    return [
        pltpu.make_async_copy(
            source.at[pair], stacked.at[:, pair * width : (pair + 1) * width], sem.at[pair]
        )
        for pair in range(PAIRS)
    ]


def project_kernel(
    scaled_ref, source, pair_ref, each_ref, before_ref, sums_ref, product, weight_ref, sem
):
    half = 2 * 2 * C_OUT
    flat = scaled_ref[...].reshape(ROWS, C_MID)

    @pl.when(pl.program_id(0) == 0)
    def _():
        stack_experts(source, weight_ref, sem)
        sums_ref[...] = jnp.zeros_like(sums_ref)

    total = None
    for part in range(2):
        value = dot_nt(flat, weight_ref[part * half : (part + 1) * half])
        value = value.reshape(PIX, GROUP, half)
        each_ref[:, :, part * half : (part + 1) * half] = value.astype(LOW)
        for side in range(2):
            term = value[:, :, side * 2 * C_OUT : (side + 1) * 2 * C_OUT]
            term = term * pair_ref[2 * part + side].astype(FULL)[None]
            total = term if total is None else total + term
    total = total.reshape(ROWS, 2 * C_OUT)
    before = (total + pltpu.roll(total, C_OUT, 1))[:, :C_OUT]
    before_ref[...] = before.reshape(PIX, GROUP, C_OUT)
    sums_ref[0:1] += jnp.sum(before, axis=0, keepdims=True)
    sums_ref[1:2] += jnp.sum(before * before, axis=0, keepdims=True)


def project_forward(scaled, project_low, pair_out):
    images = scaled.shape[1]
    wide = EXPERTS * C_OUT
    return device_kernel(
        project_kernel,
        "project_forward",
        images // GROUP,
        [images_block(C_MID), pl.BlockSpec(memory_space=pl.ANY), pair_block(2 * C_OUT)],
        [((PIX, images, wide), LOW), ((PIX, images, C_OUT), FULL), ((2, C_OUT), FULL)],
        [images_block(wide), images_block(C_OUT), total_block(2, C_OUT)],
        [
            pltpu.VMEM((2, PIX, GROUP, wide // 2), FULL), pltpu.VMEM((wide, C_MID), LOW),
            pltpu.SemaphoreType.DMA((EXPERTS,)),
        ],
        2 * PIX * images * wide * C_MID,
        PIX * images * (wide + C_MID) * 2,
    )(scaled, project_low, pair_out)


def head_kernel(
    before_ref, norm_ref, hot_ref, router_ref, weight_ref,
    widened_ref, twice_ref, route_ref, pair_ref, pooled_ref, sums_ref, route_sum_ref,
    routed, padded,
):
    @pl.when(pl.program_id(0) == 0)
    def _():
        sums_ref[...] = jnp.zeros_like(sums_ref)
        route_sum_ref[...] = jnp.zeros_like(route_sum_ref)
        padded[...] = jnp.zeros_like(padded)

    gain, shift = norm_ref[0:1], norm_ref[1:2]
    pooled = jnp.zeros((GROUP, C_OUT), FULL)
    for pixel in range(PIX):
        normed = (before_ref[pixel] * gain + shift).astype(LOW).astype(FULL)
        pooled = pooled + normed
        padded[:, :C_OUT] = normed
        value = padded[...]
        twice_ref[pixel] = (value + pltpu.roll(value, C_OUT, 1)).astype(LOW)
    pooled = pooled * (1.0 / PIX)
    pooled_ref[...] = pooled
    route = sig(dot_nt(pooled, router_ref[...], HIGH) + hot_ref[...])
    route_ref[...] = route
    route_sum_ref[...] += jnp.sum(route, axis=0, keepdims=True)
    low = route.astype(LOW).astype(FULL)
    for pair in range(PAIRS):
        scale = pair_scale(low, pair, C_OUT).astype(LOW)
        pair_ref[pair] = scale
        place = slice(2 * pair * C_OUT, 2 * (pair + 1) * C_OUT)
        for pixel in range(PIX):
            routed[pixel, :, place] = twice_ref[pixel] * scale
    product = dot_nt(routed[...].reshape(ROWS, EXPERTS * C_OUT), weight_ref[...])
    widened_ref[...] = product.reshape(PIX, GROUP, C_HEAD).astype(LOW)
    sums_ref[0:1] += jnp.sum(product, axis=0, keepdims=True)
    sums_ref[1:2] += jnp.sum(product * product, axis=0, keepdims=True)


def head_forward(before, norm, hot, router, head_low):
    images = before.shape[1]
    wide = EXPERTS * C_OUT
    return device_kernel(
        head_kernel,
        "head_forward",
        images // GROUP,
        [
            images_block(C_OUT), whole(2, C_OUT), group_block(EXPERTS), whole(EXPERTS, C_OUT),
            whole(C_HEAD, wide),
        ],
        [
            ((PIX, images, C_HEAD), LOW), ((PIX, images, 2 * C_OUT), LOW),
            ((images, EXPERTS), FULL), ((PAIRS, images, 2 * C_OUT), LOW), ((images, C_OUT), FULL),
            ((2, C_HEAD), FULL), ((1, EXPERTS), FULL),
        ],
        [
            images_block(C_HEAD), images_block(2 * C_OUT), group_block(EXPERTS),
            pair_block(2 * C_OUT), group_block(C_OUT), total_block(2, C_HEAD),
            total_block(1, EXPERTS),
        ],
        [pltpu.VMEM((PIX, GROUP, wide), LOW), pltpu.VMEM((GROUP, 2 * C_OUT), FULL)],
        2 * PIX * images * wide * C_HEAD,
        PIX * images * (C_HEAD + C_OUT) * 2,
    )(before, norm, hot, router, head_low)


def loss_kernel(
    widened_ref, norm_ref, label_ref, class_ref, bias_ref,
    feats_ref, logits_ref, grad_feats_ref, sums_ref, cross_ref, bias_grad_ref,
    silu_sum, slope_sum, cross_sum,
):
    step = pl.program_id(0)
    rows = pl.ds(pl.multiple_of(step * GROUP, GROUP), GROUP)

    def chunk(index, carry):
        lanes = pl.ds(pl.multiple_of(index * 128, 128), 128)
        gain, shift, inv, offset = (norm_ref[k : k + 1, lanes] for k in range(4))
        total = slope = moved = jnp.zeros((GROUP, 128), FULL)
        for pixel in range(PIX):
            value = widened_ref[pixel, :, lanes].astype(FULL)
            lifted = value * gain + shift
            part = sig(lifted)
            grown = lifted * part
            bent = part + grown * (1.0 - part)
            total = total + grown
            slope = slope + bent
            moved = moved + bent * (value * inv + offset)
        silu_sum[rows, lanes] = total
        slope_sum[rows, lanes] = slope
        cross_sum[rows, lanes] = moved
        return carry

    lax.fori_loop(0, C_HEAD // 128, chunk, 0)

    @pl.when(step == pl.num_programs(0) - 1)
    def _():
        feats = (silu_sum[...] * (1.0 / PIX)).astype(LOW)
        feats_ref[...] = feats
        logits = dot_nn(feats, class_ref[...]) + bias_ref[...]
        lane = lax.broadcasted_iota(jnp.int32, logits.shape, 1)
        picked = lane == label_ref[...]
        top = jnp.max(logits, axis=1, keepdims=True)
        powers = jnp.exp(logits - top)
        totals = jnp.sum(powers, axis=1, keepdims=True)
        cross = top + jnp.log(totals) - jnp.sum(
            jnp.where(picked, logits, 0.0), axis=1, keepdims=True
        )
        cross_ref[...] = jnp.sum(cross, axis=0, keepdims=True)
        grad = (powers / totals - jnp.where(picked, 1.0, 0.0)) * norm_ref[4:5, 0:1]
        grad = grad.astype(LOW)
        logits_ref[...] = jnp.zeros_like(logits_ref)
        logits_ref[:, :CLASSES] = grad
        bias_grad_ref[...] = jnp.sum(grad.astype(FULL), axis=0, keepdims=True)
        grad_feats = dot_nt(grad, class_ref[...]) * (1.0 / PIX)
        grad_feats_ref[...] = grad_feats
        sums_ref[0:1] = jnp.sum(grad_feats * slope_sum[...], axis=0, keepdims=True)
        sums_ref[1:2] = jnp.sum(grad_feats * cross_sum[...], axis=0, keepdims=True)


def loss_part(widened, norm, label, class_low, bias):
    images = widened.shape[1]
    return device_kernel(
        loss_kernel,
        "loss_part",
        images // GROUP,
        [
            images_block(C_HEAD), whole(8, C_HEAD), whole(images, 1), whole(C_HEAD, CLASSES),
            whole(1, CLASSES),
        ],
        [
            ((images, C_HEAD), LOW), ((images, CLASS_PAD), LOW), ((images, C_HEAD), FULL),
            ((2, C_HEAD), FULL), ((1, 1), FULL), ((1, CLASSES), FULL),
        ],
        [
            total_block(images, C_HEAD), total_block(images, CLASS_PAD), total_block(images, C_HEAD),
            total_block(2, C_HEAD), total_block(1, 1), total_block(1, CLASSES),
        ],
        [pltpu.VMEM((images, C_HEAD), FULL)] * 3,
        4 * images * C_HEAD * CLASSES,
        PIX * images * C_HEAD * 2,
    )(widened, norm, label, class_low, bias)


def head_back_kernel(
    widened_ref, grad_feats_ref, coef_ref, weight_ref, pair_ref, twice_ref, before_ref, norm_ref,
    route_ref, balance_ref, router_ref,
    grad_wide_ref, grad_normed_ref, logit_ref, sums_ref,
    product, mixed,
):
    half = 2 * 2 * C_OUT

    @pl.when(pl.program_id(0) == 0)
    def _():
        sums_ref[...] = jnp.zeros_like(sums_ref)

    gain, shift, by_value, constant = (coef_ref[k : k + 1] for k in range(4))
    grad_feats = grad_feats_ref[...]

    def widen(pixel, carry):
        value = widened_ref[pixel].astype(FULL)
        lifted = value * gain + shift
        part = sig(lifted)
        bent = part + lifted * part * (1.0 - part)
        grad = grad_feats * bent * gain + value * by_value + constant
        grad_wide_ref[pixel] = grad.astype(LOW)
        return carry

    lax.fori_loop(0, PIX, widen, 0, unroll=7)
    flat = grad_wide_ref[...].reshape(ROWS, C_HEAD)
    twice = twice_ref[...].astype(FULL)
    route_sums = []
    total = None
    for part in range(2):
        value = dot_nn(flat, weight_ref[:, part * half : (part + 1) * half])
        value = value.reshape(PIX, GROUP, half)
        for side in range(2):
            piece = value[:, :, side * 2 * C_OUT : (side + 1) * 2 * C_OUT]
            route_sums.append(jnp.sum(piece * twice, axis=0))
            term = piece * pair_ref[2 * part + side].astype(FULL)[None]
            total = term if total is None else total + term
    total = total.reshape(ROWS, 2 * C_OUT)
    mixed[...] = (total + pltpu.roll(total, C_OUT, 1))[:, :C_OUT].reshape(PIX, GROUP, C_OUT)
    route = route_ref[...]
    grad_route = pair_columns(route_sums, C_OUT) + balance_ref[...]
    logit = grad_route * route * (1.0 - route)
    logit_ref[...] = logit
    added = dot_nn(logit, router_ref[...], HIGH) * (1.0 / PIX)

    def close(pixel, carry):
        plain, cross = carry
        grad = mixed[pixel] + added
        grad_normed_ref[pixel] = grad
        hat = before_ref[pixel] * norm_ref[0:1] + norm_ref[1:2]
        return plain + grad, cross + grad * hat

    zero = jnp.zeros((GROUP, C_OUT), FULL)
    plain, cross = lax.fori_loop(0, PIX, close, (zero, zero), unroll=7)
    sums_ref[0:1] += jnp.sum(plain, axis=0, keepdims=True)
    sums_ref[1:2] += jnp.sum(cross, axis=0, keepdims=True)


def head_back(
    widened, grad_feats, coef, head_low, pair_two, twice, before, norm, route, balance, router_t
):
    images = widened.shape[1]
    wide = EXPERTS * C_OUT
    return device_kernel(
        head_back_kernel,
        "head_back",
        images // GROUP,
        [
            images_block(C_HEAD), group_block(C_HEAD), whole(4, C_HEAD), whole(C_HEAD, wide),
            pair_block(2 * C_OUT), images_block(2 * C_OUT), images_block(C_OUT), whole(2, C_OUT),
            group_block(EXPERTS), whole(1, EXPERTS), whole(EXPERTS, C_OUT),
        ],
        [
            ((PIX, images, C_HEAD), LOW), ((PIX, images, C_OUT), FULL), ((images, EXPERTS), FULL),
            ((2, C_OUT), FULL),
        ],
        [
            images_block(C_HEAD), images_block(C_OUT), group_block(EXPERTS), total_block(2, C_OUT),
        ],
        [pltpu.VMEM((2, PIX, GROUP, wide // 2), FULL), pltpu.VMEM((PIX, GROUP, C_OUT), FULL)],
        2 * PIX * images * wide * C_HEAD,
        PIX * images * (2 * C_HEAD + C_OUT) * 2,
    )(widened, grad_feats, coef, head_low, pair_two, twice, before, norm, route, balance, router_t)


def kern_grad_kernel(grad_ref, twice_ref, pair_ref, out_ref, turned, routed):
    images, width = twice_ref.shape[1:]

    @pl.when(pl.program_id(0) == 0)
    def _():
        turned[...] = grad_ref[...].reshape(turned.shape[1], turned.shape[0]).T

    for side in range(2):
        scale = pair_ref[side]
        for pixel in range(PIX):
            routed[pixel * images : (pixel + 1) * images, side * width : (side + 1) * width] = (
                twice_ref[pixel] * scale
            )
    product = dot_nn(turned[...], routed[...])
    for side in range(2):
        out_ref[side] = product[:, side * width : (side + 1) * width].astype(LOW)


def kern_grad(grad, twice, pair_scales, name):
    images, out_width, width = grad.shape[1], grad.shape[2], twice.shape[2]
    rows = PIX * images
    return device_kernel(
        kern_grad_kernel,
        name,
        PAIRS // 2,
        [
            whole(PIX, images, out_width), whole(PIX, images, width),
            pl.BlockSpec((2, images, width), lambda i: (i, 0, 0)),
        ],
        [((PAIRS, out_width, width), LOW)],
        [pl.BlockSpec((2, out_width, width), lambda i: (i, 0, 0))],
        [pltpu.VMEM((out_width, rows), LOW), pltpu.VMEM((rows, 2 * width), LOW)],
        2 * rows * out_width * PAIRS * width,
        rows * out_width * 2,
    )(grad, twice, pair_scales)[0]


def project_grad_kernel(grad_ref, scaled_ref, scale_ref, out_ref, turned, routed):
    rows = turned.shape[1]

    @pl.when(pl.program_id(0) == 0)
    def _():
        turned[...] = grad_ref[...].reshape(rows, C_OUT).T

    for side in range(2):
        routed[side * C_OUT : (side + 1) * C_OUT] = turned[...] * scale_ref[0, side : side + 1]
    product = dot_nn(routed[...], scaled_ref[...].reshape(rows, C_MID))
    owners, _, height, _ = out_ref.shape
    for side in range(2):
        for owner in range(owners):
            place = side * C_OUT + owner * height
            out_ref[owner, 0, :, side * C_MID : (side + 1) * C_MID] = product[
                place : place + height
            ].astype(LOW)


def project_grad(grad, scaled, scale, owners):
    images = grad.shape[1]
    rows = PIX * images
    return device_kernel(
        project_grad_kernel,
        "project_grad",
        PAIRS,
        [
            whole(PIX, images, C_OUT), whole(PIX, images, C_MID),
            pl.BlockSpec((1, 2, rows), lambda i: (i, 0, 0)),
        ],
        [((owners, PAIRS, C_OUT // owners, 2 * C_MID), LOW)],
        [pl.BlockSpec((owners, 1, C_OUT // owners, 2 * C_MID), lambda i: (0, i, 0, 0))],
        [pltpu.VMEM((C_OUT, rows), LOW), pltpu.VMEM((2 * C_OUT, rows), LOW)],
        2 * rows * EXPERTS * C_OUT * C_MID,
        rows * (C_OUT + C_MID) * 2,
    )(grad, scaled, scale)[0]


def project_back_kernel(
    grad_ref, before_ref, coef_ref, pair_ref, each_ref, source,
    grad_before_ref, grad_scaled_ref, route_ref,
    routed, padded, weight_ref, sem,
):
    @pl.when(pl.program_id(0) == 0)
    def _():
        stack_experts(source, weight_ref, sem)
        padded[...] = jnp.zeros_like(padded)

    gain, by_value, constant = (coef_ref[k : k + 1] for k in range(3))
    scales = [pair_ref[pair] for pair in range(PAIRS)]

    def turn(pixel, carry):
        grad = grad_ref[pixel] * gain + before_ref[pixel] * by_value + constant
        grad = grad.astype(LOW)
        grad_before_ref[pixel] = grad
        padded[:, :C_OUT] = grad.astype(FULL)
        value = padded[...]
        value = value + pltpu.roll(value, C_OUT, 1)
        low = value.astype(LOW)
        found = []
        for pair in range(PAIRS):
            place = slice(2 * pair * C_OUT, 2 * (pair + 1) * C_OUT)
            routed[pixel, :, place] = low * scales[pair]
            found.append(carry[pair] + each_ref[pixel, :, place].astype(FULL) * value)
        return tuple(found)

    zero = jnp.zeros((GROUP, 2 * C_OUT), FULL)
    route_sums = lax.fori_loop(0, PIX, turn, (zero,) * PAIRS, unroll=7)
    route_ref[...] = pair_columns(route_sums, C_OUT)
    product = dot_nn(routed[...].reshape(ROWS, EXPERTS * C_OUT), weight_ref[...])
    grad_scaled_ref[...] = product.reshape(PIX, GROUP, C_MID).astype(LOW)


def project_back(grad_normed, before, coef, pair_out, each, project_low):
    images = before.shape[1]
    wide = EXPERTS * C_OUT
    return device_kernel(
        project_back_kernel,
        "project_back",
        images // GROUP,
        [
            images_block(C_OUT), images_block(C_OUT), whole(3, C_OUT), pair_block(2 * C_OUT),
            images_block(wide), pl.BlockSpec(memory_space=pl.ANY),
        ],
        [
            ((PIX, images, C_OUT), LOW), ((PIX, images, C_MID), LOW), ((images, EXPERTS), FULL),
        ],
        [images_block(C_OUT), images_block(C_MID), group_block(EXPERTS)],
        [
            pltpu.VMEM((PIX, GROUP, wide), LOW), pltpu.VMEM((GROUP, 2 * C_OUT), FULL),
            pltpu.VMEM((wide, C_MID), LOW), pltpu.SemaphoreType.DMA((EXPERTS,)),
        ],
        2 * PIX * images * wide * C_MID,
        PIX * images * (C_MID + wide) * 2,
    )(grad_normed, before, coef, pair_out, each, project_low)


def expand_back_kernel(
    grad_scaled_ref, turned_ref, hidden_ref, img_ref, gate_ref, squeeze_ref, excite_ref, depth_ref,
    route_ref, route_part_ref, balance_ref, source,
    grad_hidden_ref, logit_ref, grad_gate_ref, grad_squeeze_ref, grad_depth_ref,
    kern, start, grad_turned, grad_kern, pooled, product, weight_ref, sem,
):
    @pl.when(pl.program_id(0) == 0)
    def _():
        for copy in pair_copies(source, weight_ref, sem):
            copy.start()
        grad_depth_ref[...] = jnp.zeros_like(grad_depth_ref)

    route = route_ref[...]
    low = route.astype(LOW).astype(FULL)
    columns = [low[:, expert : expert + 1] for expert in range(EXPERTS)]
    for tap in range(KSIZE * KSIZE):
        total = columns[0] * depth_ref[tap, 0:1, :]
        for expert in range(1, EXPERTS):
            total = total + columns[expert] * depth_ref[tap, expert : expert + 1, :]
        kern[tap] = total

    def gate_sum(pixel, carry):
        value = turned_ref[pixel].astype(FULL)
        return carry + grad_scaled_ref[pixel].astype(FULL) * (value * sig(value))

    gate = gate_ref[...]
    grad_gate = lax.fori_loop(0, PIX, gate_sum, jnp.zeros((GROUP, C_MID), FULL), unroll=7)
    grad_gate = grad_gate * gate * (1.0 - gate)
    grad_gate_ref[...] = grad_gate
    squeeze = squeeze_ref[...]
    part = sig(squeeze)
    grad_squeeze = dot_nt(grad_gate, excite_ref[1], HIGH) * (part + squeeze * part * (1.0 - part))
    grad_squeeze_ref[...] = grad_squeeze
    pooled[...] = dot_nn(grad_squeeze, excite_ref[0], HIGH) * (1.0 / PIX)

    third = C_MID // 3

    @pl.when(pl.program_id(0) == 0)
    def _():
        for copy in pair_copies(source, weight_ref, sem):
            copy.wait()

    def chunk(index):
        lanes = slice(index * 128, index * 128 + 128)
        gate_part = gate_ref[:, lanes]
        pooled_part = pooled[:, lanes]
        for pixel in range(PIX):
            value = turned_ref[pixel, :, lanes].astype(FULL)
            part = sig(value)
            grad = grad_scaled_ref[pixel, :, lanes].astype(FULL) * gate_part + pooled_part
            grad_turned[index % 2, pixel] = grad * (part + value * part * (1.0 - part))
            value = hidden_ref[pixel, :, lanes].astype(FULL)
            start[index % 2, pixel] = value * sig(value)
        taps = [kern[tap, :, lanes] for tap in range(KSIZE * KSIZE)]
        sums = [None] * (KSIZE * KSIZE)
        for pixel in range(PIX):
            total = None
            here = grad_turned[index % 2, pixel]
            for tap, source in taps_of(pixel):
                term = start[index % 2, source] * here
                sums[tap] = term if sums[tap] is None else sums[tap] + term
                term = grad_turned[index % 2, source] * taps[KSIZE * KSIZE - 1 - tap]
                total = term if total is None else total + term
            value = hidden_ref[pixel, :, lanes].astype(FULL)
            part = sig(value)
            grad = total * (part + value * part * (1.0 - part))
            grad_hidden_ref[pixel, :, lanes] = grad.astype(LOW)
        for tap in range(KSIZE * KSIZE):
            grad_kern[tap, :, lanes] = sums[tap]

    for part in range(3):
        for index in range(3 * part, 3 * part + 3):
            chunk(index)
        inner = slice(part * third, (part + 1) * third)
        term = dot_nn(grad_hidden_ref[:, :, inner].reshape(ROWS, third), weight_ref[inner])
        term = term.reshape(PIX, GROUP, EXPERTS * C_IN)
        product[...] = term if part == 0 else product[...] + term
    place = lax.broadcasted_iota(jnp.int32, (GROUP, EXPERTS), 1)
    depth_term = jnp.zeros((GROUP, EXPERTS), FULL)
    for expert in range(EXPERTS):
        total = jnp.zeros((GROUP, C_MID), FULL)
        for tap in range(KSIZE * KSIZE):
            value = grad_kern[tap]
            total = total + value * depth_ref[tap, expert : expert + 1, :]
            weighed = value * columns[expert]
            grad_depth_ref[tap, expert : expert + 1, :] += jnp.sum(weighed, axis=0, keepdims=True)
        total = jnp.sum(total, axis=1, keepdims=True)
        depth_term = depth_term + jnp.where(place == expert, total, 0.0)
    def route_part(pixel, carry):
        value = img_ref[pixel].astype(FULL)
        return tuple(
            carry[pair] + product[pixel, :, 2 * pair * C_IN : 2 * (pair + 1) * C_IN] * value
            for pair in range(PAIRS)
        )

    zero = jnp.zeros((GROUP, 2 * C_IN), FULL)
    route_sums = lax.fori_loop(0, PIX, route_part, (zero,) * PAIRS, unroll=7)
    grad_route = (
        pair_columns(route_sums, C_IN) + route_part_ref[...] + depth_term + balance_ref[...]
    )
    logit_ref[...] = grad_route * route * (1.0 - route)


def expand_back(
    grad_scaled, turned, hidden, img_two, gate, squeeze, excite, depth_full, route, route_part,
    balance, expand_low,
):
    images = hidden.shape[1]
    taps = KSIZE * KSIZE
    return device_kernel(
        expand_back_kernel,
        "expand_back",
        images // GROUP,
        [
            images_block(C_MID), images_block(C_MID), images_block(C_MID), images_block(2 * C_IN),
            group_block(C_MID), group_block(C_SE), whole(2, C_SE, C_MID),
            whole(taps, EXPERTS, C_MID), group_block(EXPERTS), group_block(EXPERTS),
            whole(1, EXPERTS), pl.BlockSpec(memory_space=pl.ANY),
        ],
        [
            ((PIX, images, C_MID), LOW), ((images, EXPERTS), FULL), ((images, C_MID), FULL),
            ((images, C_SE), FULL), ((taps, EXPERTS, C_MID), FULL),
        ],
        [
            images_block(C_MID), group_block(EXPERTS), group_block(C_MID), group_block(C_SE),
            total_block(taps, EXPERTS, C_MID),
        ],
        [
            pltpu.VMEM((taps, GROUP, C_MID), FULL), pltpu.VMEM((2, PIX, GROUP, 128), FULL),
            pltpu.VMEM((2, PIX, GROUP, 128), FULL), pltpu.VMEM((taps, GROUP, C_MID), FULL),
            pltpu.VMEM((GROUP, C_MID), FULL), pltpu.VMEM((PIX, GROUP, EXPERTS * C_IN), FULL),
            pltpu.VMEM((C_MID, EXPERTS * C_IN), LOW), pltpu.SemaphoreType.DMA((PAIRS,)),
        ],
        2 * PIX * images * EXPERTS * C_IN * C_MID,
        PIX * images * 4 * C_MID * 2,
    )(
        grad_scaled, turned, hidden, img_two, gate, squeeze, excite, depth_full, route, route_part,
        balance, expand_low,
    )


def reduce_kernel(n_wide, n_dp, n_full, n_share, *refs):
    n_in = n_full + n_share
    fulls, shares = refs[:n_full], refs[n_full:n_in]
    full_outs, share_outs, spread_out = refs[n_in : n_in + n_full], refs[n_in + n_full : 2 * n_in], refs[2 * n_in]
    scratch = list(refs[2 * n_in + 1 :])
    firsts, seconds, thirds, halves, lineds = (
        [scratch.pop(0) for _ in range(n_full)] for _ in range(5)
    )
    slots = [scratch.pop(0) for _ in range(n_share)]
    send, recv = scratch
    lines = n_wide // 2
    me_wide, me_dp = lax.axis_index("wide"), lax.axis_index("dp")
    core, line = lax.rem(me_wide, 2), lax.div(me_wide, 2)
    sibling = line * 2 + 1 - core
    used = [0]

    barrier = pltpu.get_barrier_semaphore()
    for k in range(1, n_wide):
        pl.semaphore_signal(
            barrier, inc=1, device_id={"wide": lax.rem(me_wide + k, n_wide)}, device_id_type=MESH
        )
    for k in range(1, n_dp):
        pl.semaphore_signal(
            barrier, inc=1, device_id={"dp": lax.rem(me_dp + k, n_dp)}, device_id_type=MESH
        )
    pl.semaphore_wait(barrier, n_wide + n_dp - 2)

    def launch(src, dst, device):
        copy = pltpu.make_async_remote_copy(
            src_ref=src, dst_ref=dst, send_sem=send.at[used[0]], recv_sem=recv.at[used[0]],
            device_id=device, device_id_type=MESH,
        )
        used[0] += 1
        copy.start()
        return copy

    def finish(copies):
        for copy in copies:
            copy.wait()

    def dp_peer(k):
        return lax.rem(me_dp + k, n_dp)

    to_sibling = [
        launch(full.at[:, :, 1 - core], first, {"wide": sibling})
        for full, first in zip(fulls, firsts)
    ]
    scattered = [
        launch(share.at[dp_peer(k)], slot.at[k - 1], {"dp": dp_peer(k)})
        for k in range(1, n_dp)
        for share, slot in zip(shares, slots)
    ]
    finish(to_sibling)
    for full, first, half in zip(fulls, firsts, halves):
        def pair_sum(index, carry, full=full, first=first, half=half):
            at_dp, at_line = lax.div(index, lines), lax.rem(index, lines)
            total = full[at_dp, at_line, core].astype(FULL) + first[at_dp, at_line].astype(FULL)
            half[at_dp, at_line] = total.astype(LOW)
            return carry

        lax.fori_loop(0, n_dp * lines, pair_sum, 0)
    across = [
        launch(half.at[dp_peer(k)], second.at[k - 1], {"dp": dp_peer(k)})
        for k in range(1, n_dp)
        for half, second in zip(halves, seconds)
    ]
    finish(scattered)
    for share, slot, out in zip(shares, slots, share_outs):
        total = share[me_dp].astype(FULL)
        for k in range(1, n_dp):
            total = total + slot[k - 1].astype(FULL)
        out[me_dp] = total.astype(LOW)
    finish(across)
    for half, second, lined in zip(halves, seconds, lineds):
        def dp_sum(at_line, carry, half=half, second=second, lined=lined):
            total = half[me_dp, at_line].astype(FULL)
            for k in range(1, n_dp):
                total = total + second[k - 1, at_line].astype(FULL)
            lined[at_line] = total.astype(LOW)
            return carry

        lax.fori_loop(0, lines, dp_sum, 0)
    along = []
    for k in range(1, lines):
        other = lax.rem(line + k, lines)
        for lined, third in zip(lineds, thirds):
            along.append(launch(lined.at[other], third.at[k - 1], {"wide": other * 2 + core}))
    gathered = [
        launch(out.at[me_dp], out.at[me_dp], {"dp": dp_peer(k)})
        for k in range(1, n_dp)
        for out in share_outs
    ]
    finish(along)
    for lined, third, out in zip(lineds, thirds, full_outs):
        total = lined[line].astype(FULL)
        for k in range(1, lines):
            total = total + third[k - 1].astype(FULL)
        out[me_dp] = total.astype(LOW)
    last = [
        launch(out.at[me_dp], out.at[me_dp], {"dp": dp_peer(k)})
        for out in reversed(full_outs)
        for k in range(1, n_dp)
    ]
    own = full_outs[-1]
    finish(last[: n_dp - 1])
    spread_out[me_wide] = own[...]
    everywhere = [
        launch(own, spread_out.at[me_wide], {"wide": lax.rem(me_wide + k, n_wide)})
        for k in range(1, n_wide)
    ]
    finish(last[n_dp - 1 :] + gathered + everywhere)


def reduce_grads(fulls, shares, ident):
    n_wide, n_dp = lax.axis_size("wide"), lax.axis_size("dp")
    lines = n_wide // 2
    views = [full.reshape((n_dp, lines, 2) + full.shape[2:]) for full in fulls]
    tails = [full.shape[2:] for full in fulls]
    copies = (
        len(fulls) * (1 + (n_dp - 1) * 2 + lines - 1) + len(shares) * 2 * (n_dp - 1) + n_wide - 1
    )
    vmem = pl.BlockSpec(memory_space=pltpu.VMEM)
    outs = [jax.ShapeDtypeStruct((n_dp,) + tail, LOW) for tail in tails]
    outs += [jax.ShapeDtypeStruct(share.shape, LOW) for share in shares]
    outs += [jax.ShapeDtypeStruct((n_wide, n_dp) + tails[-1], LOW)]
    found = pl.pallas_call(
        functools.partial(reduce_kernel, n_wide, n_dp, len(fulls), len(shares)),
        name="reduce_grads",
        out_shape=outs,
        in_specs=[vmem] * (len(fulls) + len(shares)),
        out_specs=[vmem] * len(outs),
        scratch_shapes=[pltpu.VMEM((n_dp, lines) + tail, LOW) for tail in tails]
        + [pltpu.VMEM((n_dp - 1, lines) + tail, LOW) for tail in tails]
        + [pltpu.VMEM((lines - 1,) + tail, LOW) for tail in tails]
        + [pltpu.VMEM((n_dp, lines) + tail, LOW) for tail in tails]
        + [pltpu.VMEM((lines,) + tail, LOW) for tail in tails]
        + [pltpu.VMEM((n_dp - 1,) + share.shape[1:], LOW) for share in shares]
        + [pltpu.SemaphoreType.DMA((copies,)), pltpu.SemaphoreType.DMA((copies,))],
        compiler_params=pltpu.CompilerParams(
            collective_id=ident, has_side_effects=True, vmem_limit_bytes=VMEM_CAP
        ),
    )(*views, *shares)
    return found[: len(fulls)], found[len(fulls) : len(fulls) + len(shares)], found[-1]


def to_pieces(cube, count):
    pairs, rows, width = cube.shape
    if pairs == count:
        return cube
    more = count // pairs
    cube = cube.reshape(pairs, rows, more, width // more).transpose(0, 2, 1, 3)
    return cube.reshape(count, rows, width // more)


def from_pieces(pieces, pairs):
    count, rows, width = pieces.shape
    if pairs == count:
        return pieces
    more = count // pairs
    cube = pieces.reshape(pairs, more, rows, width).transpose(0, 2, 1, 3)
    return cube.reshape(pairs, rows, width * more)


def send_around(value, hop):
    count = lax.axis_size("dp")
    return lax.ppermute(value, "dp", [(at, (at + hop) % count) for at in range(count)])


def scatter_sum(pieces):
    count, me = lax.axis_size("dp"), lax.axis_index("dp")
    total = lax.dynamic_index_in_dim(pieces, me, 0, keepdims=False).astype(FULL)
    arrived = [
        send_around(lax.dynamic_index_in_dim(pieces, (me + hop) % count, 0, keepdims=False), hop)
        for hop in range(1, count)
    ]
    return total, arrived


def add_arrived(total, arrived):
    for part in arrived:
        total = total + part.astype(FULL)
    return total.astype(LOW)


def spread_sum(piece):
    count, me = lax.axis_size("dp"), lax.axis_index("dp")
    found = jnp.zeros((count,) + piece.shape, piece.dtype)
    for hop in range(count):
        part = piece if hop == 0 else send_around(piece, hop)
        found = lax.dynamic_update_index_in_dim(found, part, (me - hop) % count, 0)
    return found


def gather_kernel(n_wide, n_dp, weight_ref, depth_ref, out_ref, depth_out, send, recv):
    lines = n_wide // 2
    me_wide, me_dp = lax.axis_index("wide"), lax.axis_index("dp")
    core, line = lax.rem(me_wide, 2), lax.div(me_wide, 2)
    sibling = {"wide": line * 2 + 1 - core}
    width = out_ref.shape[4]
    used = [0]

    barrier = pltpu.get_barrier_semaphore()
    for k in range(1, n_wide):
        pl.semaphore_signal(
            barrier, inc=1, device_id={"wide": lax.rem(me_wide + k, n_wide)}, device_id_type=MESH
        )
    for k in range(1, n_dp):
        pl.semaphore_signal(
            barrier, inc=1, device_id={"dp": lax.rem(me_dp + k, n_dp)}, device_id_type=MESH
        )
    for piece in range(n_dp):
        out_ref[piece, line, core] = weight_ref[:, piece * width : (piece + 1) * width].astype(LOW)
    depth_out[me_wide] = depth_ref[...]
    pl.semaphore_wait(barrier, n_wide + n_dp - 2)

    def launch(part, device, ref=out_ref):
        copy = pltpu.make_async_remote_copy(
            src_ref=ref.at[part], dst_ref=ref.at[part], send_sem=send.at[used[0]],
            recv_sem=recv.at[used[0]], device_id=device, device_id_type=MESH,
        )
        used[0] += 1
        copy.start()
        return copy

    def dp_from(hop):
        return lax.rem(me_dp + n_dp - hop, n_dp)

    along = [
        launch((me_dp, line, core), {"wide": lax.rem(line + k, lines) * 2 + core})
        for k in range(1, lines)
    ]
    started = [launch((piece, line, core), sibling) for piece in range(n_dp)]
    started += [
        launch((me_wide,), {"wide": lax.rem(me_wide + k, n_wide)}, depth_out)
        for k in range(1, n_wide)
    ]
    across = []
    for k in range(1, lines):
        source = lax.rem(line + lines - k, lines)
        along[k - 1].wait_recv()
        for hop in range(1, n_dp):
            copy = launch((me_dp, source, core), {"dp": lax.rem(me_dp + hop, n_dp)})
            across.append((copy, hop, source))
        started.append(launch((me_dp, source, core), sibling))
    for copy, hop, source in across:
        copy.wait_recv()
        started.append(launch((dp_from(hop), source, core), sibling))
    for copy in started:
        copy.wait()
    for copy in along:
        copy.wait_send()
    for copy, _, _ in across:
        copy.wait_send()


def gather_expand(weight, depth, ident):
    n_wide, n_dp = lax.axis_size("wide"), lax.axis_size("dp")
    lines = n_wide // 2
    height, width = weight.shape
    copies = (lines - 1) * (1 + n_dp) + (lines - 1) * (n_dp - 1) + n_dp + n_wide - 1
    vmem = pl.BlockSpec(memory_space=pltpu.VMEM)
    found, depths = pl.pallas_call(
        functools.partial(gather_kernel, n_wide, n_dp),
        name="gather_expand",
        out_shape=[
            jax.ShapeDtypeStruct((n_dp, lines, 2, height, width // n_dp), LOW),
            jax.ShapeDtypeStruct((n_wide,) + depth.shape, LOW),
        ],
        in_specs=[vmem] * 2,
        out_specs=[vmem] * 2,
        scratch_shapes=[pltpu.SemaphoreType.DMA((copies,)), pltpu.SemaphoreType.DMA((copies,))],
        compiler_params=pltpu.CompilerParams(
            collective_id=ident, has_side_effects=True, vmem_limit_bytes=VMEM_CAP
        ),
    )(weight, depth)
    return found.reshape(n_dp, n_wide * height, width // n_dp), depths


def soap_kernel(
    gained, weight_ref, grad_ref, first_ref, second_ref, state_ref,
    first_out, second_out, state_out, weight_out, raised,
):
    step = pl.program_id(0)
    height, width = weight_ref.shape
    half = width // 2
    upper = -(-half // 128) * 128
    lower = half // 128 * 128
    corr_one = 1.0 - beta_one**STEP
    corr_two = 1.0 - beta_two**STEP

    def iota(shape, axis):
        return lax.broadcasted_iota(jnp.int32, shape, axis)

    pick = (iota((height, BLK), 0) % BLK == iota((height, BLK), 1)).astype(FULL)
    pick_t = (iota((BLK, height), 1) % BLK == iota((BLK, height), 0)).astype(FULL)
    same = iota((height, height), 0) // BLK == iota((height, height), 1) // BLK
    ones = same.astype(FULL)

    def spread_out(rows):
        return jnp.where(same, dot_nn(pick, rows, HIGH), 0.0)

    def by_half(product, value):
        first = product(0, value[:, :upper])
        second = product(1, value[:, lower:])
        if upper == lower:
            return jnp.concatenate([first, second], axis=1)
        lane = iota((height, upper - lower), 1)
        middle = jnp.where(lane < half - lower, first[:, lower:], second[:, : upper - lower])
        return jnp.concatenate([first[:, :lower], middle, second[:, upper - lower :]], axis=1)

    old = [state_ref[1, 2 * step + side] for side in range(2)]
    turns = [spread_out(rows) for rows in old]
    grad = grad_ref[0].astype(FULL)
    turned = by_half(lambda side, value: dot_nn(turns[side], value, HIGH), grad)
    first_new = beta_one * first_ref[...] + (1.0 - beta_one) * grad
    second_new = beta_two * second_ref[...] + (1.0 - beta_two) * (turned * turned)
    first_out[...] = first_new
    second_out[...] = second_new
    moment = by_half(lambda side, value: dot_nn(turns[side], value, HIGH), first_new)
    ratio = moment / corr_one / (jnp.sqrt(second_new / corr_two) + eps_adam)
    back = by_half(lambda side, value: dot_tn(turns[side], value, HIGH), ratio)
    weight = weight_ref[...]
    weight_out[...] = weight - rate_matrix * (back + decay * weight)

    for side in range(2):
        if side == 0:
            piece = grad[:, :upper]
            piece = jnp.where(iota(piece.shape, 1) < half, piece, 0.0)
        else:
            piece = grad[:, lower:]
            piece = jnp.where(iota(piece.shape, 1) >= half - lower, piece, 0.0)
        gram = jnp.where(same, dot_nt(piece, piece, HIGH), 0.0)
        summed = beta_two * state_ref[0, 2 * step + side]
        summed = summed + (1.0 - beta_two) * gained * dot_nn(pick_t, gram, HIGH)
        diagonal = jnp.sum(summed * pick_t, axis=0, keepdims=True)
        trace = dot_nn(diagonal, ones, HIGH)
        stats = summed / trace
        state_out[0, 2 * step + side] = stats
        lifted = dot_nn(old[side], spread_out(stats), HIGH)
        for column in range(BLK):
            raised[column, pl.ds(2 * step + side, 1), :] = lifted[column : column + 1]

    @pl.when(step == pl.num_programs(0) - 1)
    def _():
        columns = []
        for index in range(BLK):
            column = raised[index]
            for previous in columns:
                column = column - dot_nn(previous * column, ones, HIGH) * previous
            column = column * lax.rsqrt(dot_nn(column * column, ones, HIGH))
            columns.append(column)
            for expert in range(EXPERTS):
                state_out[1, expert, index : index + 1, :] = column[expert : expert + 1]


def soap(weight, grad, first, second, state, every):
    height, total = weight.shape
    width = total // PAIRS
    turned_state = state.transpose(0, 1, 3, 2)
    gained = stat_gain * every / (total // EXPERTS)
    column = pl.BlockSpec((height, width), lambda i: (0, i))
    first_new, second_new, state_new, weight_new = device_kernel(
        functools.partial(soap_kernel, gained),
        "soap",
        PAIRS,
        [
            column, pl.BlockSpec((1, height, width), lambda i: (i, 0, 0)), column, column,
            whole(2, EXPERTS, BLK, height),
        ],
        [(weight.shape, FULL), (weight.shape, FULL), (turned_state.shape, FULL),
         (weight.shape, FULL)],
        [column, column, total_block(2, EXPERTS, BLK, height), column],
        [pltpu.VMEM((BLK, EXPERTS, height), FULL)],
        2 * height * height * total,
        weight.size * 26,
    )(weight, grad, first, second, turned_state)
    return (first_new, second_new, state_new.transpose(0, 1, 3, 2), weight_new)


def adam(weight, grad, first, second, rate):
    corr_one = 1.0 - beta_one**STEP
    corr_two = 1.0 - beta_two**STEP
    first_new = beta_one * first + (1.0 - beta_one) * grad
    second_new = beta_two * second + (1.0 - beta_two) * grad * grad
    weight_new = weight - rate * (
        first_new / corr_one / (jnp.sqrt(second_new / corr_two) + eps_adam) + decay * weight
    )
    return (first_new, second_new, weight_new)


def local(
    images,
    dom_label,
    class_label,
    expand_weight,
    expand_first,
    expand_second,
    expand_state,
    project_weight,
    project_first,
    project_second,
    project_state,
    head_weight,
    head_first,
    head_second,
    head_state,
    depth_weight,
    depth_first,
    depth_second,
    classifier_weight,
    classifier_first,
    classifier_second,
    excite_weight,
    excite_first,
    excite_second,
    router_weight,
    router_first,
    router_second,
    gains_weight,
    gains_first,
    gains_second,
):
    low_type = jnp.bfloat16
    images_here = images.shape[0]
    every = images.shape[0] * lax.axis_size("dp") * lax.axis_size("wide")
    count = every * PIX
    n_wide, n_dp = lax.axis_size("wide"), lax.axis_size("dp")
    bias_se, bias_ex, gain_one, shift_one, gain_two, shift_two, bias_cls = split_gains(gains_weight)
    hot = boost * (dom_label[:, None] == jnp.arange(EXPERTS)[None, :]).astype(jnp.float32)
    img = images.transpose(1, 0, 2)
    img_two = jnp.concatenate([img, img], axis=2)
    project_low = lax.all_gather(project_weight.astype(low_type), "wide", axis=0, tiled=True)
    head_low = lax.all_gather(head_weight.astype(low_type), "wide", axis=0, tiled=True)
    class_low = lax.all_gather(classifier_weight.astype(low_type), "wide", axis=0, tiled=True)
    taps = KSIZE * KSIZE
    depth_own = depth_weight.transpose(1, 0, 2).reshape(taps * EXPERTS, -1).astype(low_type)
    depth_own = jnp.pad(depth_own, ((0, -taps * EXPERTS % 16), (0, 0)))
    expand_low, depth_low = gather_expand(expand_weight, depth_own, 6)
    expand_low = from_pieces(expand_low, PAIRS)
    depth_full = depth_low[:, : taps * EXPERTS].reshape(n_wide, taps, EXPERTS, -1)
    depth_full = depth_full.transpose(1, 2, 0, 3).reshape(taps, EXPERTS, C_MID).astype(FULL)
    excite = excite_weight.transpose(0, 2, 1)
    router = router_weight.T
    router_one, router_two = router[:, :C_IN], router[:, C_IN:]

    (
        hidden, turned, scaled, route_one, pair_in, pair_one, gate, squeeze, pooled_one,
        pooled_act, route_one_sum,
    ) = expand_forward(
        img_two, hot, router_one, expand_low, depth_full, excite, bias_se[None], bias_ex[None]
    )
    each, before, sums_one = project_forward(scaled, project_low, pair_one)
    sums_one, route_one_sum = sum_all((sums_one, route_one_sum), 1)
    center_one = sums_one[0] / count
    inv_one = lax.rsqrt(sums_one[1] / count - center_one * center_one + eps_norm)
    scale_one = inv_one * gain_one
    norm_one = jnp.stack([scale_one, shift_one - center_one * scale_one])
    widened, twice, route_two, pair_two, pooled_two, sums_two, route_two_sum = head_forward(
        before, norm_one, hot, router_two, head_low
    )
    sums_two, route_two_sum = sum_all((sums_two, route_two_sum), 2)
    center_two = sums_two[0] / count
    inv_two = lax.rsqrt(sums_two[1] / count - center_two * center_two + eps_norm)
    scale_two = inv_two * gain_two
    norm_two = jnp.stack(
        [scale_two, shift_two - center_two * scale_two, inv_two, -center_two * inv_two]
        + [jnp.full_like(inv_two, 1.0 / every)] * 4
    )
    feats, grad_logits, grad_feats, back_two, cross_part, grad_bias_cls = loss_part(
        widened, norm_two, class_label[:, None], class_low, bias_cls[None]
    )
    grad_class = jnp.stack(
        [dot_tn(feats, part).astype(low_type) for part in jnp.split(grad_logits, PAIRS, axis=1)]
    )
    grad_class, grad_feats = lax.optimization_barrier((grad_class, grad_feats))
    share_class = lax.psum_scatter(grad_class, "wide", scatter_dimension=1, tiled=True)
    back_two, cross_total, grad_bias_cls = sum_all((back_two, cross_part, grad_bias_cls), 3)
    means_one = route_one_sum[0] / every
    means_two = route_two_sum[0] / every
    by_value = -scale_two * inv_two * back_two[1] / count
    coef_two = jnp.stack(
        [
            scale_two, shift_two - center_two * scale_two, by_value,
            -scale_two * back_two[0] / count - center_two * by_value,
        ]
    )
    hat_one = jnp.stack([inv_one, -center_one * inv_one])
    grad_widened, grad_normed, grad_logit_two, back_one = head_back(
        widened, grad_feats, coef_two, head_low, pair_two, twice, before, hat_one, route_two,
        balance_grad(means_two, every)[None], router_two,
    )
    grad_head = kern_grad(grad_widened, twice, pair_two, "head_grad")
    grad_head, back_one, share_class = lax.optimization_barrier((grad_head, back_one, share_class))
    share_head = lax.psum_scatter(grad_head, "wide", scatter_dimension=1, tiled=True)
    grad_router_two = dot_tn(pooled_two, grad_logit_two, HIGH)
    (back_one,) = sum_all((back_one,), 4)
    by_value = -scale_one * inv_one * back_one[1] / count
    coef_one = jnp.stack(
        [scale_one, by_value, -scale_one * back_one[0] / count - center_one * by_value]
    )
    grad_before, grad_scaled, route_project = project_back(
        grad_normed, before, coef_one, pair_one, each, project_low
    )
    row_scale = jnp.tile(route_one.astype(low_type).T, (1, PIX)).reshape(PAIRS, 2, -1)
    grad_project = project_grad(grad_before, scaled, row_scale, n_wide)
    grad_project, grad_scaled, share_head = lax.optimization_barrier(
        (grad_project, grad_scaled, share_head)
    )
    wide_head = share_head.shape[2]
    own_late, arrived = scatter_sum(
        to_pieces(jnp.concatenate([share_head, share_class], axis=2), n_dp)
    )
    share_project = lax.psum_scatter(grad_project, "wide", scatter_dimension=0, tiled=True)[0]
    grad_hidden, grad_logit_one, grad_gate, grad_squeeze, grad_depth = expand_back(
        grad_scaled, turned, hidden, img_two, gate, squeeze, excite, depth_full, route_one,
        route_project, balance_grad(means_one, every)[None], expand_low,
    )
    arrived, share_project, grad_hidden = lax.optimization_barrier(
        (arrived, share_project, grad_hidden)
    )
    sum_late = spread_sum(add_arrived(own_late, arrived))
    own_project, arrived = scatter_sum(to_pieces(share_project, n_dp))
    grad_expand = kern_grad(grad_hidden, img_two, pair_in, "expand_grad")
    grad_excite = jnp.stack(
        [
            dot_tn(grad_squeeze, pooled_act, HIGH),
            dot_tn(squeeze * jax.nn.sigmoid(squeeze), grad_gate, HIGH),
        ]
    )
    grad_router_one = dot_tn(pooled_one, grad_logit_one, HIGH)
    grad_depth = grad_depth.transpose(1, 0, 2)
    grad_bias_se = jnp.sum(grad_squeeze, axis=0)
    grad_bias_ex = jnp.sum(grad_gate, axis=0)
    sum_late, arrived, grad_expand = lax.optimization_barrier((sum_late, arrived, grad_expand))
    sum_late = from_pieces(sum_late, PAIRS)
    sum_head, sum_class = sum_late[:, :, :wide_head], sum_late[:, :, wide_head:]
    sum_project = from_pieces(spread_sum(add_arrived(own_project, arrived)), PAIRS)
    share_expand = lax.psum_scatter(grad_expand, "wide", scatter_dimension=1, tiled=True)
    parts = n_wide * n_dp
    depth_piece = grad_depth.size // parts
    extras = [
        grad_depth.reshape(-1, n_wide, depth_weight.shape[2]).transpose(1, 0, 2),
        jnp.concatenate(
            [
                grad_excite.reshape(-1), grad_router_one.reshape(-1), grad_router_two.reshape(-1),
                grad_bias_se, grad_bias_ex,
            ]
        ),
    ]
    depth_part = extras[0].reshape(n_wide, n_dp, depth_piece).transpose(1, 0, 2)
    rest_size = extras[1].size
    rest_piece = -(-rest_size // parts)
    rest_part = jnp.pad(extras[1], (0, rest_piece * parts - rest_size))
    rest_part = rest_part.reshape(n_dp, n_wide, rest_piece)
    extra_rows = -(-(depth_piece + rest_piece) // (16 * 128)) * 16
    extra = jnp.concatenate([depth_part, rest_part], axis=2).astype(low_type)
    extra = jnp.pad(extra, ((0, 0), (0, 0), (0, extra_rows * 128 - extra.shape[2])))
    extra = extra.reshape(n_dp, n_wide, extra_rows, 128)
    head_out = soap(head_weight, sum_head, head_first, head_second, head_state, every)
    project_out = soap(
        project_weight, sum_project, project_first, project_second, project_state, every
    )
    sum_class = sum_class.transpose(1, 0, 2).reshape(-1, CLASS_PAD)[:, :CLASSES].astype(FULL)
    class_out = adam(
        classifier_weight, sum_class, classifier_first, classifier_second, rate_matrix
    )
    share_expand, head_out, project_out, class_out = lax.optimization_barrier(
        (share_expand, head_out, project_out, class_out)
    )
    (own_extra,), (own_expand,), every_extra = reduce_grads(
        [extra], [to_pieces(share_expand, n_dp)], 5
    )
    sum_expand = from_pieces(own_expand, PAIRS)
    own_extra = own_extra.reshape(n_dp, -1)[:, :depth_piece].reshape(EXPERTS, KSIZE * KSIZE, -1)
    rest = every_extra.reshape(n_wide, n_dp, -1)[:, :, depth_piece : depth_piece + rest_piece]
    rest = rest.transpose(1, 0, 2).reshape(-1)[:rest_size].astype(FULL)
    split = grad_excite.size
    sum_excite = rest[:split].reshape(2, C_SE, C_MID).transpose(0, 2, 1)
    sum_router = rest[split : split + router_weight.size].reshape(router_weight.shape)
    sum_bias = rest[split + router_weight.size :]
    loss = cross_total[0, 0] / every + balance_weight * (
        jnp.mean((means_one - jnp.mean(means_one)) ** 2)
        + jnp.mean((means_two - jnp.mean(means_two)) ** 2)
    )
    grad_gains = jnp.concatenate(
        [sum_bias, back_one[1], back_one[0], back_two[1], back_two[0], grad_bias_cls[0]]
    )
    expand_out = soap(expand_weight, sum_expand, expand_first, expand_second, expand_state, every)
    depth_out = adam(
        depth_weight, own_extra.astype(FULL), depth_first, depth_second, rate_matrix
    )
    excite_out = adam(excite_weight, sum_excite, excite_first, excite_second, rate_matrix)
    router_out = adam(router_weight, sum_router, router_first, router_second, rate_matrix)
    gains_out = adam(gains_weight, grad_gains, gains_first, gains_second, rate_gains)
    return (
        loss,
        expand_out[0],
        expand_out[1],
        expand_out[2],
        expand_out[3],
        project_out[0],
        project_out[1],
        project_out[2],
        project_out[3],
        head_out[0],
        head_out[1],
        head_out[2],
        head_out[3],
        depth_out[0],
        depth_out[1],
        depth_out[2],
        class_out[0],
        class_out[1],
        class_out[2],
        excite_out[0],
        excite_out[1],
        excite_out[2],
        router_out[0],
        router_out[1],
        router_out[2],
        gains_out[0],
        gains_out[1],
        gains_out[2],
    )


def solution(mesh):
    return jax.shard_map(
        local,
        mesh=mesh,
        in_specs=(
            P(("dp", "wide"), None, None),
            P(("dp", "wide")),
            P(("dp", "wide")),
            P("wide", None),
            P("wide", None),
            P("wide", None),
            P(None, None, "wide", None),
            P("wide", None),
            P("wide", None),
            P("wide", None),
            P(None, None, "wide", None),
            P("wide", None),
            P("wide", None),
            P("wide", None),
            P(None, None, "wide", None),
            P(None, None, "wide"),
            P(None, None, "wide"),
            P(None, None, "wide"),
            P("wide", None),
            P("wide", None),
            P("wide", None),
            P(),
            P(),
            P(),
            P(),
            P(),
            P(),
            P(),
            P(),
            P(),
        ),
        out_specs=(
            P(),
            P("wide", None),
            P("wide", None),
            P(None, None, "wide", None),
            P("wide", None),
            P("wide", None),
            P("wide", None),
            P(None, None, "wide", None),
            P("wide", None),
            P("wide", None),
            P("wide", None),
            P(None, None, "wide", None),
            P("wide", None),
            P(None, None, "wide"),
            P(None, None, "wide"),
            P(None, None, "wide"),
            P("wide", None),
            P("wide", None),
            P("wide", None),
            P(),
            P(),
            P(),
            P(),
            P(),
            P(),
            P(),
            P(),
            P(),
        ),
        check_vma=False,
    )
```

```python
import functools

import jax
import jax.numpy as jnp
from jax import lax
from jax.experimental import pallas as pl
from jax.experimental.pallas import tpu as pltpu
from jax.sharding import PartitionSpec as P

SIDE = 7
PIX = 49
KSIZE = 3
EXPERTS = 8
BLK = 4
STEP = 10
C_IN = 192
C_MID = 1152
C_SE = 48
C_OUT = 320
C_HEAD = 1280
CLASSES = 1000


HIGH = lax.Precision.HIGHEST
beta_one = 0.9
beta_two = 0.95
eps_adam = 1e-08
eps_norm = 1e-05
decay = 0.01
rate_matrix = 0.08
rate_gains = 0.5
boost = 1.0
balance_weight = 4.0
stat_gain = 15000.0


def split_gains(gains):
    widths = [C_SE, C_MID, C_OUT, C_OUT, C_HEAD, C_HEAD, CLASSES]
    pieces = []
    start = 0
    for width in widths:
        pieces.append(gains[start : start + width])
        start = start + width
    return pieces


MESH = pl.DeviceIdType.MESH


def sum_kernel(n_wide, n_dp, count, extra, finish, *refs):
    parts, extras = refs[:count], refs[count : count + extra]
    scratch = list(refs[-(3 * count + 4) :])
    outs = refs[count + extra : len(refs) - len(scratch)]
    wide_slots, dp_slots, halves = (scratch[k * count : (k + 1) * count] for k in range(3))
    s_wide, r_wide, s_dp, r_dp = scratch[3 * count :]
    me_wide = lax.axis_index("wide")
    me_dp = lax.axis_index("dp")
    barrier = pltpu.get_barrier_semaphore()
    for k in range(1, n_wide):
        pl.semaphore_signal(
            barrier, inc=1, device_id={"wide": lax.rem(me_wide + k, n_wide)}, device_id_type=MESH
        )
    for k in range(1, n_dp):
        pl.semaphore_signal(
            barrier, inc=1, device_id={"dp": lax.rem(me_dp + k, n_dp)}, device_id_type=MESH
        )
    pl.semaphore_wait(barrier, n_wide + n_dp - 2)

    def exchange(sources, slots, me, axis, size, send, recv):
        copies = []
        for k in range(1, size):
            for index in range(count):
                copy = pltpu.make_async_remote_copy(
                    src_ref=sources[index],
                    dst_ref=slots[index].at[me],
                    send_sem=send.at[k * count + index],
                    recv_sem=recv.at[k * count + index],
                    device_id={axis: lax.rem(me + k, size)},
                    device_id_type=MESH,
                )
                copy.start()
                copies.append(copy)
        for source, slot in zip(sources, slots):
            slot[me] = source[...]
        for copy in copies:
            copy.wait()
        found = []
        for slot in slots:
            total = slot[0]
            for k in range(1, size):
                total = total + slot[k]
            found.append(total)
        return found

    for half, total in zip(halves, exchange(parts, wide_slots, me_wide, "wide", n_wide, s_wide, r_wide)):
        half[...] = total
    totals = exchange(halves, dp_slots, me_dp, "dp", n_dp, s_dp, r_dp)
    finish(totals, extras, outs)


def sum_all(parts, extras, finish, outs, ident):
    n_wide = lax.axis_size("wide")
    n_dp = lax.axis_size("dp")
    count = len(parts)
    vmem = pl.BlockSpec(memory_space=pltpu.VMEM)
    scratch = [pltpu.VMEM((n_wide,) + part.shape, jnp.float32) for part in parts]
    scratch += [pltpu.VMEM((n_dp,) + part.shape, jnp.float32) for part in parts]
    scratch += [pltpu.VMEM(part.shape, jnp.float32) for part in parts]
    sems = [pltpu.SemaphoreType.DMA((size * count,)) for size in (n_wide, n_wide, n_dp, n_dp)]
    return pl.pallas_call(
        functools.partial(sum_kernel, n_wide, n_dp, count, len(extras), finish),
        name="sum_all",
        out_shape=[jax.ShapeDtypeStruct(shape, jnp.float32) for shape in outs],
        in_specs=[vmem] * (count + len(extras)),
        out_specs=[vmem] * len(outs),
        scratch_shapes=scratch + sems,
        compiler_params=pltpu.CompilerParams(collective_id=ident, has_side_effects=True),
    )(*parts, *extras)


def norm_finish(count, every, totals, extras, outs):
    sums, route = totals
    center = sums[0:1] / count
    inv = lax.rsqrt(sums[1:2] / count - center * center + eps_norm)
    scale = inv * extras[0][...]
    outs[0][0:1] = scale
    outs[0][1:2] = extras[1][...] - center * scale
    outs[0][2:3] = inv
    outs[0][3:4] = -center * inv
    outs[0][4:8] = jnp.full((4, scale.shape[1]), 1.0 / every, jnp.float32)
    outs[1][...] = route


def back_finish(count, totals, extras, outs):
    sums = totals[0]
    norm = extras[0]
    scale, part = norm[0:1], norm[0:1] * sums[1:2] / count
    outs[0][0:2] = norm[0:2]
    outs[0][2:3] = -part * norm[2:3]
    outs[0][3:4] = -scale * sums[0:1] / count - part * norm[3:4]
    for out, total in zip(outs[1:], totals):
        out[...] = total


def balance_grad(means, every):
    return balance_weight * 2.0 * (means - jnp.mean(means)) / (EXPERTS * every)


GROUP = 16
PAIRS = EXPERTS // 2
ROWS = PIX * GROUP
CLASS_PAD = 1024
LOW = jnp.bfloat16
FULL = jnp.float32
VMEM_CAP = 60 * 1024 * 1024


def sig(value):
    return 0.5 + 0.5 * jnp.tanh(0.5 * value)


def silu_of(value):
    half = 0.5 * value
    return half * (1.0 + jnp.tanh(half))


def silu_pair(value):
    half = 0.5 * value
    bent = jnp.tanh(half)
    upper = 1.0 + bent
    return half * upper, upper * (1.0 + half * (1.0 - bent))


def sum_of(terms):
    while len(terms) > 1:
        terms = [
            terms[k] + terms[k + 1] if k + 1 < len(terms) else terms[k]
            for k in range(0, len(terms), 2)
        ]
    return terms[0]


def dot_nn(left, right, precision=None):
    return lax.dot_general(
        left, right, (((1,), (0,)), ((), ())), precision=precision, preferred_element_type=FULL
    )


def dot_nt(left, right, precision=None):
    return lax.dot_general(
        left, right, (((1,), (1,)), ((), ())), precision=precision, preferred_element_type=FULL
    )


def dot_tn(left, right, precision=None):
    return lax.dot_general(
        left, right, (((0,), (0,)), ((), ())), precision=precision, preferred_element_type=FULL
    )


def images_block(width):
    return pl.BlockSpec((PIX, GROUP, width), lambda i: (0, i, 0))


def group_block(width):
    return pl.BlockSpec((GROUP, width), lambda i: (i, 0))


def pair_block(width):
    return pl.BlockSpec((PAIRS, GROUP, width), lambda i: (0, i, 0))


def whole(*shape):
    return pl.BlockSpec(shape, lambda i: (0,) * len(shape), pipeline_mode=pl.Buffered(1))


def total_block(*shape):
    return pl.BlockSpec(shape, lambda i: (0,) * len(shape))


def device_kernel(kernel, name, grid, in_specs, outs, out_specs, scratch, flops, moved, cap=None):
    return pl.pallas_call(
        kernel,
        name=name,
        grid=(grid,),
        in_specs=in_specs,
        out_shape=[jax.ShapeDtypeStruct(shape, dtype) for shape, dtype in outs],
        out_specs=out_specs,
        scratch_shapes=scratch,
        compiler_params=pltpu.CompilerParams(
            vmem_limit_bytes=cap or VMEM_CAP, dimension_semantics=("arbitrary",)
        ),
        cost_estimate=pl.CostEstimate(flops=flops, bytes_accessed=moved, transcendentals=0),
    )


def pair_scale(route, pair, width):
    lane = lax.broadcasted_iota(jnp.int32, (route.shape[0], 2 * width), 1)
    return jnp.where(
        lane < width, route[:, 2 * pair : 2 * pair + 1], route[:, 2 * pair + 1 : 2 * pair + 2]
    )


def pair_columns(sums, width):
    count = sums[0].shape[0]
    lane = lax.broadcasted_iota(jnp.int32, (count, 2 * width), 1)
    place = lax.broadcasted_iota(jnp.int32, (count, EXPERTS), 1)
    found = jnp.zeros((count, EXPERTS), FULL)
    for pair in range(PAIRS):
        first = jnp.sum(jnp.where(lane < width, sums[pair], 0.0), axis=1, keepdims=True)
        second = jnp.sum(jnp.where(lane < width, 0.0, sums[pair]), axis=1, keepdims=True)
        found = found + jnp.where(place == 2 * pair, first, 0.0)
        found = found + jnp.where(place == 2 * pair + 1, second, 0.0)
    return found


def taps_of(pixel):
    row, col = pixel // SIDE, pixel % SIDE
    found = []
    for tap in range(KSIZE * KSIZE):
        at_row, at_col = row + tap // KSIZE - 1, col + tap % KSIZE - 1
        if 0 <= at_row < SIDE and 0 <= at_col < SIDE:
            found.append((tap, at_row * SIDE + at_col))
    return found


def expand_kernel(
    img_ref, hot_ref, router_ref, source, depth_ref, excite_ref, bias_se_ref, bias_ex_ref,
    hidden_ref, turned_ref, scaled_ref, route_ref, pair_in_ref, pair_out_ref, gate_ref,
    squeeze_ref, pooled_one_ref, pooled_act_ref, route_sum_ref,
    routed, hidden_full, act_full, kern, expand_ref, sem,
):
    @pl.when(pl.program_id(0) == 0)
    def _():
        for copy in pair_copies(source, expand_ref, sem):
            copy.start()

    pooled = img_ref[0].astype(FULL)
    for pixel in range(1, PIX):
        pooled = pooled + img_ref[pixel].astype(FULL)
    pooled = pooled[:, :C_IN] * (1.0 / PIX)
    pooled_one_ref[...] = pooled
    route = sig(dot_nt(pooled, router_ref[...], HIGH) + hot_ref[...])
    route_ref[...] = route

    @pl.when(pl.program_id(0) == 0)
    def _():
        route_sum_ref[...] = jnp.zeros_like(route_sum_ref)

    route_sum_ref[...] += jnp.sum(route, axis=0, keepdims=True)
    low = route.astype(LOW).astype(FULL)
    for pair in range(PAIRS):
        scale = pair_scale(low, pair, C_IN).astype(LOW)
        pair_in_ref[pair] = scale
        pair_out_ref[pair] = pair_scale(low, pair, C_OUT).astype(LOW)
        place = slice(2 * pair * C_IN, 2 * (pair + 1) * C_IN)
        for pixel in range(PIX):
            routed[pixel, :, place] = img_ref[pixel] * scale
    columns = [low[:, expert : expert + 1] for expert in range(EXPERTS)]
    for tap in range(KSIZE * KSIZE):
        total = columns[0] * depth_ref[tap, 0:1, :]
        for expert in range(1, EXPERTS):
            total = total + columns[expert] * depth_ref[tap, expert : expert + 1, :]
        kern[tap] = total
    flat = routed[...].reshape(ROWS, EXPERTS * C_IN)
    third = C_MID // 3

    @pl.when(pl.program_id(0) == 0)
    def _():
        for copy in pair_copies(source, expand_ref, sem):
            copy.wait()

    def multiply(part):
        place = slice(part * third, (part + 1) * third)
        hidden_full[:, :, place] = dot_nt(flat, expand_ref[place]).reshape(PIX, GROUP, third)

    def chunk(index):
        lanes = slice(index * 128, index * 128 + 128)
        taps = [kern[tap, :, lanes] for tap in range(KSIZE * KSIZE)]
        start = [None] * PIX

        def fill(row):
            for pixel in range(row * SIDE, row * SIDE + SIDE):
                value = hidden_full[pixel, :, lanes]
                hidden_ref[pixel, :, lanes] = value.astype(LOW)
                start[pixel] = value * sig(value)

        fill(0)
        pooled_act = jnp.zeros((GROUP, 128), FULL)
        for row in range(SIDE):
            if row + 1 < SIDE:
                fill(row + 1)
            for pixel in range(row * SIDE, row * SIDE + SIDE):
                total = None
                for tap, source in taps_of(pixel):
                    term = start[source] * taps[tap]
                    total = term if total is None else total + term
                turned_ref[pixel, :, lanes] = total.astype(LOW)
                act = total * sig(total)
                pooled_act = pooled_act + act
                act_full[pixel, :, lanes] = act
        pooled_act_ref[:, lanes] = pooled_act * (1.0 / PIX)

    multiply(0)
    for part in range(3):
        if part < 2:
            multiply(part + 1)
        for index in range(3 * part, 3 * part + 3):
            chunk(index)
    squeeze = dot_nt(pooled_act_ref[...], excite_ref[0], HIGH) + bias_se_ref[...]
    squeeze_ref[...] = squeeze
    gate = sig(dot_nn(squeeze * sig(squeeze), excite_ref[1], HIGH) + bias_ex_ref[...])
    gate_ref[...] = gate

    def finish(pixel, carry):
        scaled_ref[pixel] = (act_full[pixel] * gate).astype(LOW)
        return carry

    lax.fori_loop(0, PIX, finish, 0, unroll=7)


def expand_forward(img_two, hot, router, expand_low, depth_full, excite, bias_se, bias_ex):
    images = img_two.shape[1]
    return device_kernel(
        expand_kernel,
        "expand_forward",
        images // GROUP,
        [
            images_block(2 * C_IN), group_block(EXPERTS), whole(EXPERTS, C_IN),
            pl.BlockSpec(memory_space=pl.ANY), whole(KSIZE * KSIZE, EXPERTS, C_MID),
            whole(2, C_SE, C_MID), whole(1, C_SE), whole(1, C_MID),
        ],
        [
            ((PIX, images, C_MID), LOW), ((PIX, images, C_MID), LOW), ((PIX, images, C_MID), LOW),
            ((images, EXPERTS), FULL), ((PAIRS, images, 2 * C_IN), LOW),
            ((PAIRS, images, 2 * C_OUT), LOW), ((images, C_MID), FULL), ((images, C_SE), FULL),
            ((images, C_IN), FULL), ((images, C_MID), FULL), ((1, EXPERTS), FULL),
        ],
        [
            images_block(C_MID), images_block(C_MID), images_block(C_MID), group_block(EXPERTS),
            pair_block(2 * C_IN), pair_block(2 * C_OUT), group_block(C_MID), group_block(C_SE),
            group_block(C_IN), group_block(C_MID), total_block(1, EXPERTS),
        ],
        [
            pltpu.VMEM((PIX, GROUP, EXPERTS * C_IN), LOW), pltpu.VMEM((PIX, GROUP, C_MID), FULL),
            pltpu.VMEM((PIX, GROUP, C_MID), FULL), pltpu.VMEM((KSIZE * KSIZE, GROUP, C_MID), FULL),
            pltpu.VMEM((C_MID, EXPERTS * C_IN), LOW), pltpu.SemaphoreType.DMA((PAIRS,)),
        ],
        2 * PIX * images * EXPERTS * C_IN * C_MID,
        PIX * images * 4 * C_MID * 2,
    )(img_two, hot, router, expand_low, depth_full, excite, bias_se, bias_ex)


def stack_experts(source, stacked, sem):
    copies = [
        pltpu.make_async_copy(
            source.at[:, expert * C_MID : (expert + 1) * C_MID],
            stacked.at[expert * C_OUT : (expert + 1) * C_OUT],
            sem.at[expert],
        )
        for expert in range(EXPERTS)
    ]
    for copy in copies:
        copy.start()
    for copy in copies:
        copy.wait()


def pair_copies(source, stacked, sem):
    width = source.shape[2]
    return [
        pltpu.make_async_copy(
            source.at[pair], stacked.at[:, pair * width : (pair + 1) * width], sem.at[pair]
        )
        for pair in range(PAIRS)
    ]


def project_kernel(
    scaled_ref, source, pair_ref, each_ref, before_ref, sums_ref, product, weight_ref, sem
):
    half = 2 * 2 * C_OUT
    flat = scaled_ref[...].reshape(ROWS, C_MID)

    @pl.when(pl.program_id(0) == 0)
    def _():
        stack_experts(source, weight_ref, sem)
        sums_ref[...] = jnp.zeros_like(sums_ref)

    total = None
    for part in range(2):
        value = dot_nt(flat, weight_ref[part * half : (part + 1) * half])
        value = value.reshape(PIX, GROUP, half)
        each_ref[:, :, part * half : (part + 1) * half] = value.astype(LOW)
        for side in range(2):
            term = value[:, :, side * 2 * C_OUT : (side + 1) * 2 * C_OUT]
            term = term * pair_ref[2 * part + side].astype(FULL)[None]
            total = term if total is None else total + term
    total = total.reshape(ROWS, 2 * C_OUT)
    before = (total + pltpu.roll(total, C_OUT, 1))[:, :C_OUT]
    before_ref[...] = before.reshape(PIX, GROUP, C_OUT)
    sums_ref[0:1] += jnp.sum(before, axis=0, keepdims=True)
    sums_ref[1:2] += jnp.sum(before * before, axis=0, keepdims=True)


def project_forward(scaled, project_low, pair_out):
    images = scaled.shape[1]
    wide = EXPERTS * C_OUT
    return device_kernel(
        project_kernel,
        "project_forward",
        images // GROUP,
        [images_block(C_MID), pl.BlockSpec(memory_space=pl.ANY), pair_block(2 * C_OUT)],
        [((PIX, images, wide), LOW), ((PIX, images, C_OUT), FULL), ((2, C_OUT), FULL)],
        [images_block(wide), images_block(C_OUT), total_block(2, C_OUT)],
        [
            pltpu.VMEM((2, PIX, GROUP, wide // 2), FULL), pltpu.VMEM((wide, C_MID), LOW),
            pltpu.SemaphoreType.DMA((EXPERTS,)),
        ],
        2 * PIX * images * wide * C_MID,
        PIX * images * (wide + C_MID) * 2,
    )(scaled, project_low, pair_out)


def head_kernel(
    before_ref, norm_ref, hot_ref, router_ref, weight_ref,
    widened_ref, twice_ref, route_ref, pair_ref, pooled_ref, sums_ref, route_sum_ref,
    routed, padded,
):
    @pl.when(pl.program_id(0) == 0)
    def _():
        sums_ref[...] = jnp.zeros_like(sums_ref)
        route_sum_ref[...] = jnp.zeros_like(route_sum_ref)
        padded[...] = jnp.zeros_like(padded)

    gain, shift = norm_ref[0:1], norm_ref[1:2]
    pooled = jnp.zeros((GROUP, C_OUT), FULL)
    for pixel in range(PIX):
        normed = (before_ref[pixel] * gain + shift).astype(LOW).astype(FULL)
        pooled = pooled + normed
        padded[:, :C_OUT] = normed
        value = padded[...]
        twice_ref[pixel] = (value + pltpu.roll(value, C_OUT, 1)).astype(LOW)
    pooled = pooled * (1.0 / PIX)
    pooled_ref[...] = pooled
    route = sig(dot_nt(pooled, router_ref[...], HIGH) + hot_ref[...])
    route_ref[...] = route
    route_sum_ref[...] += jnp.sum(route, axis=0, keepdims=True)
    low = route.astype(LOW).astype(FULL)
    for pair in range(PAIRS):
        scale = pair_scale(low, pair, C_OUT).astype(LOW)
        pair_ref[pair] = scale
        place = slice(2 * pair * C_OUT, 2 * (pair + 1) * C_OUT)
        for pixel in range(PIX):
            routed[pixel, :, place] = twice_ref[pixel] * scale
    product = dot_nt(routed[...].reshape(ROWS, EXPERTS * C_OUT), weight_ref[...])
    widened_ref[...] = product.reshape(PIX, GROUP, C_HEAD).astype(LOW)
    sums_ref[0:1] += jnp.sum(product, axis=0, keepdims=True)
    sums_ref[1:2] += jnp.sum(product * product, axis=0, keepdims=True)


def head_forward(before, norm, hot, router, head_low):
    images = before.shape[1]
    wide = EXPERTS * C_OUT
    return device_kernel(
        head_kernel,
        "head_forward",
        images // GROUP,
        [
            images_block(C_OUT), whole(8, C_OUT), group_block(EXPERTS), whole(EXPERTS, C_OUT),
            whole(C_HEAD, wide),
        ],
        [
            ((PIX, images, C_HEAD), LOW), ((PIX, images, 2 * C_OUT), LOW),
            ((images, EXPERTS), FULL), ((PAIRS, images, 2 * C_OUT), LOW), ((images, C_OUT), FULL),
            ((2, C_HEAD), FULL), ((1, EXPERTS), FULL),
        ],
        [
            images_block(C_HEAD), images_block(2 * C_OUT), group_block(EXPERTS),
            pair_block(2 * C_OUT), group_block(C_OUT), total_block(2, C_HEAD),
            total_block(1, EXPERTS),
        ],
        [pltpu.VMEM((PIX, GROUP, wide), LOW), pltpu.VMEM((GROUP, 2 * C_OUT), FULL)],
        2 * PIX * images * wide * C_HEAD,
        PIX * images * (C_HEAD + C_OUT) * 2,
    )(before, norm, hot, router, head_low)


def loss_kernel(
    widened_ref, norm_ref, label_ref, class_ref, bias_ref,
    feats_ref, logits_ref, grad_feats_ref, sums_ref, cross_ref, bias_grad_ref,
    silu_sum, slope_sum, cross_sum,
):
    step = pl.program_id(0)
    rows = pl.ds(pl.multiple_of(step * GROUP, GROUP), GROUP)

    def chunk(index, carry):
        lanes = pl.ds(pl.multiple_of(index * 128, 128), 128)
        gain, shift, inv, offset = (norm_ref[k : k + 1, lanes] for k in range(4))
        total = slope = moved = jnp.zeros((GROUP, 128), FULL)
        for pixel in range(PIX):
            value = widened_ref[pixel, :, lanes].astype(FULL)
            lifted = value * gain + shift
            part = sig(lifted)
            grown = lifted * part
            bent = part + grown * (1.0 - part)
            total = total + grown
            slope = slope + bent
            moved = moved + bent * (value * inv + offset)
        silu_sum[rows, lanes] = total
        slope_sum[rows, lanes] = slope
        cross_sum[rows, lanes] = moved
        return carry

    lax.fori_loop(0, C_HEAD // 128, chunk, 0)

    @pl.when(step == pl.num_programs(0) - 1)
    def _():
        feats = (silu_sum[...] * (1.0 / PIX)).astype(LOW)
        feats_ref[...] = feats
        logits = dot_nn(feats, class_ref[...]) + bias_ref[...]
        lane = lax.broadcasted_iota(jnp.int32, logits.shape, 1)
        picked = lane == label_ref[...]
        top = jnp.max(logits, axis=1, keepdims=True)
        powers = jnp.exp(logits - top)
        totals = jnp.sum(powers, axis=1, keepdims=True)
        cross = top + jnp.log(totals) - jnp.sum(
            jnp.where(picked, logits, 0.0), axis=1, keepdims=True
        )
        cross_ref[...] = jnp.sum(cross, axis=0, keepdims=True)
        grad = (powers / totals - jnp.where(picked, 1.0, 0.0)) * norm_ref[4:5, 0:1]
        grad = grad.astype(LOW)
        logits_ref[...] = jnp.zeros_like(logits_ref)
        logits_ref[:, :CLASSES] = grad
        bias_grad_ref[...] = jnp.sum(grad.astype(FULL), axis=0, keepdims=True)
        grad_feats = dot_nt(grad, class_ref[...]) * (1.0 / PIX)
        grad_feats_ref[...] = grad_feats
        sums_ref[0:1] = jnp.sum(grad_feats * slope_sum[...], axis=0, keepdims=True)
        sums_ref[1:2] = jnp.sum(grad_feats * cross_sum[...], axis=0, keepdims=True)


def loss_part(widened, norm, label, class_low, bias):
    images = widened.shape[1]
    return device_kernel(
        loss_kernel,
        "loss_part",
        images // GROUP,
        [
            images_block(C_HEAD), whole(8, C_HEAD), whole(images, 1), whole(C_HEAD, CLASSES),
            whole(1, CLASSES),
        ],
        [
            ((images, C_HEAD), LOW), ((images, CLASS_PAD), LOW), ((images, C_HEAD), FULL),
            ((2, C_HEAD), FULL), ((1, 1), FULL), ((1, CLASSES), FULL),
        ],
        [
            total_block(images, C_HEAD), total_block(images, CLASS_PAD), total_block(images, C_HEAD),
            total_block(2, C_HEAD), total_block(1, 1), total_block(1, CLASSES),
        ],
        [pltpu.VMEM((images, C_HEAD), FULL)] * 3,
        4 * images * C_HEAD * CLASSES,
        PIX * images * C_HEAD * 2,
    )(widened, norm, label, class_low, bias)


def head_back_kernel(
    widened_ref, grad_feats_ref, coef_ref, weight_ref, pair_ref, twice_ref, before_ref, norm_ref,
    route_ref, balance_ref, router_ref,
    grad_wide_ref, grad_normed_ref, logit_ref, sums_ref,
    product, mixed,
):
    half = 2 * 2 * C_OUT

    @pl.when(pl.program_id(0) == 0)
    def _():
        sums_ref[...] = jnp.zeros_like(sums_ref)

    gain, shift, by_value, constant = (coef_ref[k : k + 1] for k in range(4))
    grad_feats = grad_feats_ref[...] * (0.5 * gain)

    def widen(pixel, carry):
        value = widened_ref[pixel].astype(FULL)
        _, bent = silu_pair(value * gain + shift)
        grad = grad_feats * bent + value * by_value + constant
        grad_wide_ref[pixel] = grad.astype(LOW)
        return carry

    lax.fori_loop(0, PIX, widen, 0, unroll=7)
    flat = grad_wide_ref[...].reshape(ROWS, C_HEAD)
    twice = twice_ref[...].astype(FULL)
    route_sums = []
    total = None
    for part in range(2):
        value = dot_nn(flat, weight_ref[:, part * half : (part + 1) * half])
        value = value.reshape(PIX, GROUP, half)
        for side in range(2):
            piece = value[:, :, side * 2 * C_OUT : (side + 1) * 2 * C_OUT]
            route_sums.append(jnp.sum(piece * twice, axis=0))
            term = piece * pair_ref[2 * part + side].astype(FULL)[None]
            total = term if total is None else total + term
    total = total.reshape(ROWS, 2 * C_OUT)
    mixed[...] = (total + pltpu.roll(total, C_OUT, 1))[:, :C_OUT].reshape(PIX, GROUP, C_OUT)
    route = route_ref[...]
    grad_route = pair_columns(route_sums, C_OUT) + balance_ref[...]
    logit = grad_route * route * (1.0 - route)
    logit_ref[...] = logit
    added = dot_nn(logit, router_ref[...], HIGH) * (1.0 / PIX)

    def close(pixel, carry):
        plain, cross = carry
        grad = mixed[pixel] + added
        grad_normed_ref[pixel] = grad
        hat = before_ref[pixel] * norm_ref[2:3] + norm_ref[3:4]
        return plain + grad, cross + grad * hat

    zero = jnp.zeros((GROUP, C_OUT), FULL)
    plain, cross = lax.fori_loop(0, PIX, close, (zero, zero), unroll=7)
    sums_ref[0:1] += jnp.sum(plain, axis=0, keepdims=True)
    sums_ref[1:2] += jnp.sum(cross, axis=0, keepdims=True)


def head_back(
    widened, grad_feats, coef, head_low, pair_two, twice, before, norm, route, balance, router_t
):
    images = widened.shape[1]
    wide = EXPERTS * C_OUT
    return device_kernel(
        head_back_kernel,
        "head_back",
        images // GROUP,
        [
            images_block(C_HEAD), group_block(C_HEAD), whole(4, C_HEAD), whole(C_HEAD, wide),
            pair_block(2 * C_OUT), images_block(2 * C_OUT), images_block(C_OUT), whole(8, C_OUT),
            group_block(EXPERTS), whole(1, EXPERTS), whole(EXPERTS, C_OUT),
        ],
        [
            ((PIX, images, C_HEAD), LOW), ((PIX, images, C_OUT), FULL), ((images, EXPERTS), FULL),
            ((2, C_OUT), FULL),
        ],
        [
            images_block(C_HEAD), images_block(C_OUT), group_block(EXPERTS), total_block(2, C_OUT),
        ],
        [pltpu.VMEM((2, PIX, GROUP, wide // 2), FULL), pltpu.VMEM((PIX, GROUP, C_OUT), FULL)],
        2 * PIX * images * wide * C_HEAD,
        PIX * images * (2 * C_HEAD + C_OUT) * 2,
    )(widened, grad_feats, coef, head_low, pair_two, twice, before, norm, route, balance, router_t)


def kern_grad_kernel(grad_ref, twice_ref, pair_ref, out_ref, turned, routed):
    images, width = twice_ref.shape[1:]

    @pl.when(pl.program_id(0) == 0)
    def _():
        turned[...] = grad_ref[...].reshape(turned.shape[1], turned.shape[0]).T

    for side in range(2):
        scale = pair_ref[side]
        for pixel in range(PIX):
            routed[pixel * images : (pixel + 1) * images, side * width : (side + 1) * width] = (
                twice_ref[pixel] * scale
            )
    product = dot_nn(turned[...], routed[...])
    for side in range(2):
        out_ref[side] = product[:, side * width : (side + 1) * width].astype(LOW)


def kern_grad(grad, twice, pair_scales, name):
    images, out_width, width = grad.shape[1], grad.shape[2], twice.shape[2]
    rows = PIX * images
    return device_kernel(
        kern_grad_kernel,
        name,
        PAIRS // 2,
        [
            whole(PIX, images, out_width), whole(PIX, images, width),
            pl.BlockSpec((2, images, width), lambda i: (i, 0, 0)),
        ],
        [((PAIRS, out_width, width), LOW)],
        [pl.BlockSpec((2, out_width, width), lambda i: (i, 0, 0))],
        [pltpu.VMEM((out_width, rows), LOW), pltpu.VMEM((rows, 2 * width), LOW)],
        2 * rows * out_width * PAIRS * width,
        rows * out_width * 2,
    )(grad, twice, pair_scales)[0]


def project_grad_kernel(grad_ref, scaled_ref, scale_ref, out_ref, turned, routed):
    rows = turned.shape[1]

    @pl.when(pl.program_id(0) == 0)
    def _():
        turned[...] = grad_ref[...].reshape(rows, C_OUT).T

    for side in range(2):
        routed[side * C_OUT : (side + 1) * C_OUT] = turned[...] * scale_ref[0, side : side + 1]
    product = dot_nn(routed[...], scaled_ref[...].reshape(rows, C_MID))
    owners, _, height, _ = out_ref.shape
    for side in range(2):
        for owner in range(owners):
            place = side * C_OUT + owner * height
            out_ref[owner, 0, :, side * C_MID : (side + 1) * C_MID] = product[
                place : place + height
            ].astype(LOW)


def project_grad(grad, scaled, scale, owners):
    images = grad.shape[1]
    rows = PIX * images
    return device_kernel(
        project_grad_kernel,
        "project_grad",
        PAIRS,
        [
            whole(PIX, images, C_OUT), whole(PIX, images, C_MID),
            pl.BlockSpec((1, 2, rows), lambda i: (i, 0, 0)),
        ],
        [((owners, PAIRS, C_OUT // owners, 2 * C_MID), LOW)],
        [pl.BlockSpec((owners, 1, C_OUT // owners, 2 * C_MID), lambda i: (0, i, 0, 0))],
        [pltpu.VMEM((C_OUT, rows), LOW), pltpu.VMEM((2 * C_OUT, rows), LOW)],
        2 * rows * EXPERTS * C_OUT * C_MID,
        rows * (C_OUT + C_MID) * 2,
    )(grad, scaled, scale)[0]


def project_back_kernel(
    grad_ref, before_ref, coef_ref, pair_ref, each_ref, source,
    grad_before_ref, grad_scaled_ref, route_ref,
    routed, padded, twice, weight_ref, sem,
):
    @pl.when(pl.program_id(0) == 0)
    def _():
        stack_experts(source, weight_ref, sem)
        padded[...] = jnp.zeros_like(padded)

    gain, _, by_value, constant = (coef_ref[k : k + 1] for k in range(4))
    scales = [pair_ref[pair] for pair in range(PAIRS)]

    def turn(pixel, carry):
        grad = grad_ref[pixel] * gain + before_ref[pixel] * by_value + constant
        grad = grad.astype(LOW)
        grad_before_ref[pixel] = grad
        padded[:, :C_OUT] = grad.astype(FULL)
        value = padded[...]
        value = (value + pltpu.roll(value, C_OUT, 1)).astype(LOW)
        twice[pixel] = value
        for pair in range(PAIRS):
            place = slice(2 * pair * C_OUT, 2 * (pair + 1) * C_OUT)
            routed[pixel, :, place] = value * scales[pair]
        return carry

    lax.fori_loop(0, PIX, turn, 0, unroll=7)
    product = dot_nn(routed[...].reshape(ROWS, EXPERTS * C_OUT), weight_ref[...])
    grad_scaled_ref[...] = product.reshape(PIX, GROUP, C_MID).astype(LOW)
    route_sums = []
    for pair in range(PAIRS):
        place = slice(2 * pair * C_OUT, 2 * (pair + 1) * C_OUT)
        term = each_ref[:, :, place].astype(FULL) * twice[...].astype(FULL)
        route_sums.append(jnp.sum(term, axis=0))
    route_ref[...] = pair_columns(route_sums, C_OUT)


def project_back(grad_normed, before, coef, pair_out, each, project_low):
    images = before.shape[1]
    wide = EXPERTS * C_OUT
    return device_kernel(
        project_back_kernel,
        "project_back",
        images // GROUP,
        [
            images_block(C_OUT), images_block(C_OUT), whole(4, C_OUT), pair_block(2 * C_OUT),
            images_block(wide), pl.BlockSpec(memory_space=pl.ANY),
        ],
        [
            ((PIX, images, C_OUT), LOW), ((PIX, images, C_MID), LOW), ((images, EXPERTS), FULL),
        ],
        [images_block(C_OUT), images_block(C_MID), group_block(EXPERTS)],
        [
            pltpu.VMEM((PIX, GROUP, wide), LOW), pltpu.VMEM((GROUP, 2 * C_OUT), FULL),
            pltpu.VMEM((PIX, GROUP, 2 * C_OUT), LOW),
            pltpu.VMEM((wide, C_MID), LOW), pltpu.SemaphoreType.DMA((EXPERTS,)),
        ],
        2 * PIX * images * wide * C_MID,
        PIX * images * (C_MID + wide) * 2,

    )(grad_normed, before, coef, pair_out, each, project_low)


def expand_back_kernel(
    grad_scaled_ref, turned_ref, hidden_ref, img_ref, gate_ref, squeeze_ref, excite_ref, depth_ref,
    route_ref, route_part_ref, balance_ref, source,
    grad_hidden_ref, logit_ref, grad_gate_ref, grad_squeeze_ref, grad_depth_ref,
    kern, start, slope, grad_turned, grad_kern, pooled, product, weight_ref, sem,
):
    @pl.when(pl.program_id(0) == 0)
    def _():
        for copy in pair_copies(source, weight_ref, sem):
            copy.start()
        grad_depth_ref[...] = jnp.zeros_like(grad_depth_ref)

    route = route_ref[...]
    low = route.astype(LOW).astype(FULL)
    columns = [low[:, expert : expert + 1] for expert in range(EXPERTS)]
    for tap in range(KSIZE * KSIZE):
        total = columns[0] * depth_ref[tap, 0:1, :]
        for expert in range(1, EXPERTS):
            total = total + columns[expert] * depth_ref[tap, expert : expert + 1, :]
        kern[tap] = total

    def gate_sum(pixel, carry):
        value = turned_ref[pixel].astype(FULL)
        return carry + grad_scaled_ref[pixel].astype(FULL) * silu_of(value)

    gate = gate_ref[...]
    grad_gate = lax.fori_loop(0, PIX, gate_sum, jnp.zeros((GROUP, C_MID), FULL), unroll=7)
    grad_gate = grad_gate * gate * (1.0 - gate)
    grad_gate_ref[...] = grad_gate
    squeeze = squeeze_ref[...]
    part = sig(squeeze)
    grad_squeeze = dot_nt(grad_gate, excite_ref[1], HIGH) * (part + squeeze * part * (1.0 - part))
    grad_squeeze_ref[...] = grad_squeeze
    pooled[...] = dot_nn(grad_squeeze, excite_ref[0], HIGH) * (1.0 / PIX)

    third = C_MID // 3

    @pl.when(pl.program_id(0) == 0)
    def _():
        for copy in pair_copies(source, weight_ref, sem):
            copy.wait()

    def chunk(index):
        lanes = slice(index * 128, index * 128 + 128)
        side = index % 2
        gate_part = 0.5 * gate_ref[:, lanes]
        pooled_part = 0.5 * pooled[:, lanes]
        for pixel in range(PIX):
            _, bent = silu_pair(turned_ref[pixel, :, lanes].astype(FULL))
            grad = grad_scaled_ref[pixel, :, lanes].astype(FULL) * gate_part + pooled_part
            grad_turned[side, pixel] = grad * bent
            value, bent = silu_pair(hidden_ref[pixel, :, lanes].astype(FULL))
            start[side, pixel] = value
            slope[side, pixel] = bent
        taps = [0.5 * kern[tap, :, lanes] for tap in range(KSIZE * KSIZE)]
        sums = [None] * (KSIZE * KSIZE)
        for pixel in range(PIX):
            here = grad_turned[side, pixel]
            terms = []
            for tap, source in taps_of(pixel):
                term = start[side, source] * here
                sums[tap] = term if sums[tap] is None else sums[tap] + term
                terms.append(grad_turned[side, source] * taps[KSIZE * KSIZE - 1 - tap])
            grad_hidden_ref[pixel, :, lanes] = (sum_of(terms) * slope[side, pixel]).astype(LOW)
        for tap in range(KSIZE * KSIZE):
            grad_kern[tap, :, lanes] = sums[tap]

    for part in range(3):
        for index in range(3 * part, 3 * part + 3):
            chunk(index)
        inner = slice(part * third, (part + 1) * third)
        term = dot_nn(grad_hidden_ref[:, :, inner].reshape(ROWS, third), weight_ref[inner])
        term = term.reshape(PIX, GROUP, EXPERTS * C_IN)
        product[...] = term if part == 0 else product[...] + term
    place = lax.broadcasted_iota(jnp.int32, (GROUP, EXPERTS), 1)
    depth_term = jnp.zeros((GROUP, EXPERTS), FULL)
    for expert in range(EXPERTS):
        total = jnp.zeros((GROUP, C_MID), FULL)
        for tap in range(KSIZE * KSIZE):
            value = grad_kern[tap]
            total = total + value * depth_ref[tap, expert : expert + 1, :]
            weighed = value * columns[expert]
            grad_depth_ref[tap, expert : expert + 1, :] += jnp.sum(weighed, axis=0, keepdims=True)
        total = jnp.sum(total, axis=1, keepdims=True)
        depth_term = depth_term + jnp.where(place == expert, total, 0.0)
    def route_part(pixel, carry):
        value = img_ref[pixel].astype(FULL)
        return tuple(
            carry[pair] + product[pixel, :, 2 * pair * C_IN : 2 * (pair + 1) * C_IN] * value
            for pair in range(PAIRS)
        )

    zero = jnp.zeros((GROUP, 2 * C_IN), FULL)
    route_sums = lax.fori_loop(0, PIX, route_part, (zero,) * PAIRS, unroll=7)
    grad_route = (
        pair_columns(route_sums, C_IN) + route_part_ref[...] + depth_term + balance_ref[...]
    )
    logit_ref[...] = grad_route * route * (1.0 - route)


def expand_back(
    grad_scaled, turned, hidden, img_two, gate, squeeze, excite, depth_full, route, route_part,
    balance, expand_low,
):
    images = hidden.shape[1]
    taps = KSIZE * KSIZE
    return device_kernel(
        expand_back_kernel,
        "expand_back",
        images // GROUP,
        [
            images_block(C_MID), images_block(C_MID), images_block(C_MID), images_block(2 * C_IN),
            group_block(C_MID), group_block(C_SE), whole(2, C_SE, C_MID),
            whole(taps, EXPERTS, C_MID), group_block(EXPERTS), group_block(EXPERTS),
            whole(1, EXPERTS), pl.BlockSpec(memory_space=pl.ANY),
        ],
        [
            ((PIX, images, C_MID), LOW), ((images, EXPERTS), FULL), ((images, C_MID), FULL),
            ((images, C_SE), FULL), ((taps, EXPERTS, C_MID), FULL),
        ],
        [
            images_block(C_MID), group_block(EXPERTS), group_block(C_MID), group_block(C_SE),
            total_block(taps, EXPERTS, C_MID),
        ],
        [
            pltpu.VMEM((taps, GROUP, C_MID), FULL), pltpu.VMEM((2, PIX, GROUP, 128), FULL),
            pltpu.VMEM((2, PIX, GROUP, 128), FULL), pltpu.VMEM((2, PIX, GROUP, 128), FULL), pltpu.VMEM((taps, GROUP, C_MID), FULL),
            pltpu.VMEM((GROUP, C_MID), FULL), pltpu.VMEM((PIX, GROUP, EXPERTS * C_IN), FULL),
            pltpu.VMEM((C_MID, EXPERTS * C_IN), LOW), pltpu.SemaphoreType.DMA((PAIRS,)),
        ],
        2 * PIX * images * EXPERTS * C_IN * C_MID,
        PIX * images * 4 * C_MID * 2,
    )(
        grad_scaled, turned, hidden, img_two, gate, squeeze, excite, depth_full, route, route_part,
        balance, expand_low,
    )


def reduce_kernel(n_wide, n_dp, n_full, n_share, *refs):
    n_in = n_full + n_share
    fulls, shares = refs[:n_full], refs[n_full:n_in]
    full_outs, share_outs, spread_out = refs[n_in : n_in + n_full], refs[n_in + n_full : 2 * n_in], refs[2 * n_in]
    scratch = list(refs[2 * n_in + 1 :])
    firsts, seconds, thirds, halves, lineds = (
        [scratch.pop(0) for _ in range(n_full)] for _ in range(5)
    )
    slots = [scratch.pop(0) for _ in range(n_share)]
    send, recv = scratch
    lines = n_wide // 2
    me_wide, me_dp = lax.axis_index("wide"), lax.axis_index("dp")
    core, line = lax.rem(me_wide, 2), lax.div(me_wide, 2)
    sibling = line * 2 + 1 - core
    used = [0]

    barrier = pltpu.get_barrier_semaphore()
    for k in range(1, n_wide):
        pl.semaphore_signal(
            barrier, inc=1, device_id={"wide": lax.rem(me_wide + k, n_wide)}, device_id_type=MESH
        )
    for k in range(1, n_dp):
        pl.semaphore_signal(
            barrier, inc=1, device_id={"dp": lax.rem(me_dp + k, n_dp)}, device_id_type=MESH
        )
    pl.semaphore_wait(barrier, n_wide + n_dp - 2)

    def launch(src, dst, device):
        copy = pltpu.make_async_remote_copy(
            src_ref=src, dst_ref=dst, send_sem=send.at[used[0]], recv_sem=recv.at[used[0]],
            device_id=device, device_id_type=MESH,
        )
        used[0] += 1
        copy.start()
        return copy

    def finish(copies):
        for copy in copies:
            copy.wait()

    def dp_peer(k):
        return lax.rem(me_dp + k, n_dp)

    to_sibling = [
        launch(full.at[:, :, 1 - core], first, {"wide": sibling})
        for full, first in zip(fulls, firsts)
    ]
    scattered = [
        launch(share.at[dp_peer(k)], slot.at[k - 1], {"dp": dp_peer(k)})
        for k in range(1, n_dp)
        for share, slot in zip(shares, slots)
    ]
    finish(to_sibling)
    for full, first, half in zip(fulls, firsts, halves):
        def pair_sum(index, carry, full=full, first=first, half=half):
            at_dp, at_line = lax.div(index, lines), lax.rem(index, lines)
            total = full[at_dp, at_line, core].astype(FULL) + first[at_dp, at_line].astype(FULL)
            half[at_dp, at_line] = total.astype(LOW)
            return carry

        lax.fori_loop(0, n_dp * lines, pair_sum, 0)
    across = [
        launch(half.at[dp_peer(k)], second.at[k - 1], {"dp": dp_peer(k)})
        for k in range(1, n_dp)
        for half, second in zip(halves, seconds)
    ]
    finish(scattered)
    for share, slot, out in zip(shares, slots, share_outs):
        total = share[me_dp].astype(FULL)
        for k in range(1, n_dp):
            total = total + slot[k - 1].astype(FULL)
        out[me_dp] = total.astype(LOW)
    finish(across)
    for half, second, lined in zip(halves, seconds, lineds):
        def dp_sum(at_line, carry, half=half, second=second, lined=lined):
            total = half[me_dp, at_line].astype(FULL)
            for k in range(1, n_dp):
                total = total + second[k - 1, at_line].astype(FULL)
            lined[at_line] = total.astype(LOW)
            return carry

        lax.fori_loop(0, lines, dp_sum, 0)
    along = []
    for k in range(1, lines):
        other = lax.rem(line + k, lines)
        for lined, third in zip(lineds, thirds):
            along.append(launch(lined.at[other], third.at[k - 1], {"wide": other * 2 + core}))
    gathered = [
        launch(out.at[me_dp], out.at[me_dp], {"dp": dp_peer(k)})
        for k in range(1, n_dp)
        for out in share_outs
    ]
    finish(along)
    for lined, third, out in zip(lineds, thirds, full_outs):
        total = lined[line].astype(FULL)
        for k in range(1, lines):
            total = total + third[k - 1].astype(FULL)
        out[me_dp] = total.astype(LOW)
    last = [
        launch(out.at[me_dp], out.at[me_dp], {"dp": dp_peer(k)})
        for out in reversed(full_outs)
        for k in range(1, n_dp)
    ]
    own = full_outs[-1]
    finish(last[: n_dp - 1])
    spread_out[me_wide] = own[...]
    everywhere = [
        launch(own, spread_out.at[me_wide], {"wide": lax.rem(me_wide + k, n_wide)})
        for k in range(1, n_wide)
    ]
    finish(last[n_dp - 1 :] + gathered + everywhere)


def reduce_grads(fulls, shares, ident):
    n_wide, n_dp = lax.axis_size("wide"), lax.axis_size("dp")
    lines = n_wide // 2
    views = [full.reshape((n_dp, lines, 2) + full.shape[2:]) for full in fulls]
    tails = [full.shape[2:] for full in fulls]
    copies = (
        len(fulls) * (1 + (n_dp - 1) * 2 + lines - 1) + len(shares) * 2 * (n_dp - 1) + n_wide - 1
    )
    vmem = pl.BlockSpec(memory_space=pltpu.VMEM)
    outs = [jax.ShapeDtypeStruct((n_dp,) + tail, LOW) for tail in tails]
    outs += [jax.ShapeDtypeStruct(share.shape, LOW) for share in shares]
    outs += [jax.ShapeDtypeStruct((n_wide, n_dp) + tails[-1], LOW)]
    found = pl.pallas_call(
        functools.partial(reduce_kernel, n_wide, n_dp, len(fulls), len(shares)),
        name="reduce_grads",
        out_shape=outs,
        in_specs=[vmem] * (len(fulls) + len(shares)),
        out_specs=[vmem] * len(outs),
        scratch_shapes=[pltpu.VMEM((n_dp, lines) + tail, LOW) for tail in tails]
        + [pltpu.VMEM((n_dp - 1, lines) + tail, LOW) for tail in tails]
        + [pltpu.VMEM((lines - 1,) + tail, LOW) for tail in tails]
        + [pltpu.VMEM((n_dp, lines) + tail, LOW) for tail in tails]
        + [pltpu.VMEM((lines,) + tail, LOW) for tail in tails]
        + [pltpu.VMEM((n_dp - 1,) + share.shape[1:], LOW) for share in shares]
        + [pltpu.SemaphoreType.DMA((copies,)), pltpu.SemaphoreType.DMA((copies,))],
        compiler_params=pltpu.CompilerParams(
            collective_id=ident, has_side_effects=True, vmem_limit_bytes=VMEM_CAP
        ),
    )(*views, *shares)
    return found[: len(fulls)], found[len(fulls) : len(fulls) + len(shares)], found[-1]


def to_pieces(cube, count):
    pairs, rows, width = cube.shape
    if pairs == count:
        return cube
    more = count // pairs
    cube = cube.reshape(pairs, rows, more, width // more).transpose(0, 2, 1, 3)
    return cube.reshape(count, rows, width // more)


def from_pieces(pieces, pairs):
    count, rows, width = pieces.shape
    if pairs == count:
        return pieces
    more = count // pairs
    cube = pieces.reshape(pairs, more, rows, width).transpose(0, 2, 1, 3)
    return cube.reshape(pairs, rows, width * more)


def send_around(value, hop):
    count = lax.axis_size("dp")
    return lax.ppermute(value, "dp", [(at, (at + hop) % count) for at in range(count)])


def scatter_sum(pieces):
    count, me = lax.axis_size("dp"), lax.axis_index("dp")
    total = lax.dynamic_index_in_dim(pieces, me, 0, keepdims=False).astype(FULL)
    arrived = [
        send_around(lax.dynamic_index_in_dim(pieces, (me + hop) % count, 0, keepdims=False), hop)
        for hop in range(1, count)
    ]
    return total, arrived


def add_arrived(total, arrived):
    for part in arrived:
        total = total + part.astype(FULL)
    return total.astype(LOW)


def spread_sum(piece):
    count, me = lax.axis_size("dp"), lax.axis_index("dp")
    found = jnp.zeros((count,) + piece.shape, piece.dtype)
    for hop in range(count):
        part = piece if hop == 0 else send_around(piece, hop)
        found = lax.dynamic_update_index_in_dim(found, part, (me - hop) % count, 0)
    return found


def gather_kernel(n_wide, n_dp, weight_ref, depth_ref, out_ref, depth_out, send, recv):
    lines = n_wide // 2
    me_wide, me_dp = lax.axis_index("wide"), lax.axis_index("dp")
    core, line = lax.rem(me_wide, 2), lax.div(me_wide, 2)
    sibling = {"wide": line * 2 + 1 - core}
    width = out_ref.shape[4]
    used = [0]

    barrier = pltpu.get_barrier_semaphore()
    for k in range(1, n_wide):
        pl.semaphore_signal(
            barrier, inc=1, device_id={"wide": lax.rem(me_wide + k, n_wide)}, device_id_type=MESH
        )
    for k in range(1, n_dp):
        pl.semaphore_signal(
            barrier, inc=1, device_id={"dp": lax.rem(me_dp + k, n_dp)}, device_id_type=MESH
        )
    for piece in range(n_dp):
        out_ref[piece, line, core] = weight_ref[:, piece * width : (piece + 1) * width].astype(LOW)
    depth_out[me_wide] = depth_ref[...]
    pl.semaphore_wait(barrier, n_wide + n_dp - 2)

    def launch(part, device, ref=out_ref):
        copy = pltpu.make_async_remote_copy(
            src_ref=ref.at[part], dst_ref=ref.at[part], send_sem=send.at[used[0]],
            recv_sem=recv.at[used[0]], device_id=device, device_id_type=MESH,
        )
        used[0] += 1
        copy.start()
        return copy

    def dp_from(hop):
        return lax.rem(me_dp + n_dp - hop, n_dp)

    along = [
        launch((me_dp, line, core), {"wide": lax.rem(line + k, lines) * 2 + core})
        for k in range(1, lines)
    ]
    started = [launch((piece, line, core), sibling) for piece in range(n_dp)]
    started += [
        launch((me_wide,), {"wide": lax.rem(me_wide + k, n_wide)}, depth_out)
        for k in range(1, n_wide)
    ]
    across = []
    for k in range(1, lines):
        source = lax.rem(line + lines - k, lines)
        along[k - 1].wait_recv()
        for hop in range(1, n_dp):
            copy = launch((me_dp, source, core), {"dp": lax.rem(me_dp + hop, n_dp)})
            across.append((copy, hop, source))
        started.append(launch((me_dp, source, core), sibling))
    for copy, hop, source in across:
        copy.wait_recv()
        started.append(launch((dp_from(hop), source, core), sibling))
    for copy in started:
        copy.wait()
    for copy in along:
        copy.wait_send()
    for copy, _, _ in across:
        copy.wait_send()


def gather_expand(weight, depth, ident):
    n_wide, n_dp = lax.axis_size("wide"), lax.axis_size("dp")
    lines = n_wide // 2
    height, width = weight.shape
    copies = (lines - 1) * (1 + n_dp) + (lines - 1) * (n_dp - 1) + n_dp + n_wide - 1
    vmem = pl.BlockSpec(memory_space=pltpu.VMEM)
    found, depths = pl.pallas_call(
        functools.partial(gather_kernel, n_wide, n_dp),
        name="gather_expand",
        out_shape=[
            jax.ShapeDtypeStruct((n_dp, lines, 2, height, width // n_dp), LOW),
            jax.ShapeDtypeStruct((n_wide,) + depth.shape, LOW),
        ],
        in_specs=[vmem] * 2,
        out_specs=[vmem] * 2,
        scratch_shapes=[pltpu.SemaphoreType.DMA((copies,)), pltpu.SemaphoreType.DMA((copies,))],
        compiler_params=pltpu.CompilerParams(
            collective_id=ident, has_side_effects=True, vmem_limit_bytes=VMEM_CAP
        ),
    )(weight, depth)
    return found.reshape(n_dp, n_wide * height, width // n_dp), depths


def soap_kernel(
    gained, weight_ref, grad_ref, first_ref, second_ref, state_ref,
    first_out, second_out, state_out, weight_out, raised,
):
    step = pl.program_id(0)
    height, width = weight_ref.shape
    half = width // 2
    upper = -(-half // 128) * 128
    lower = half // 128 * 128
    corr_one = 1.0 - beta_one**STEP
    corr_two = 1.0 - beta_two**STEP

    def iota(shape, axis):
        return lax.broadcasted_iota(jnp.int32, shape, axis)

    pick = (iota((height, BLK), 0) % BLK == iota((height, BLK), 1)).astype(LOW)
    pick_t = (iota((BLK, height), 1) % BLK == iota((BLK, height), 0)).astype(LOW)
    same = iota((height, height), 0) // BLK == iota((height, height), 1) // BLK
    ones = same.astype(LOW)

    def parts(value):
        high = value.astype(LOW)
        return high, (value - high.astype(FULL)).astype(LOW)

    def by_ones(value):
        high, rest = parts(value)
        return dot_nn(high, ones) + dot_nn(rest, ones)

    def spread_out(rows):
        high, rest = parts(rows)
        return jnp.where(same, dot_nn(pick, high) + dot_nn(pick, rest), 0.0)

    def by_half(product, *values):
        first = product(0, *(value[:, :upper] for value in values))
        second = product(1, *(value[:, lower:] for value in values))
        if upper == lower:
            return jnp.concatenate([first, second], axis=1)
        lane = iota((height, upper - lower), 1)
        middle = jnp.where(lane < half - lower, first[:, lower:], second[:, : upper - lower])
        return jnp.concatenate([first[:, :lower], middle, second[:, upper - lower :]], axis=1)

    old = [state_ref[1, 2 * step + side] for side in range(2)]
    turns = [parts(spread_out(rows)) for rows in old]

    def turn(side, high, rest):
        return dot_nn(turns[side][0], high) + dot_nn(turns[side][0], rest) + dot_nn(turns[side][1], high)

    def turn_back(side, high, rest):
        return dot_tn(turns[side][0], high) + dot_tn(turns[side][0], rest) + dot_tn(turns[side][1], high)

    raw = grad_ref[0]
    grad = raw.astype(FULL)
    turned = by_half(
        lambda side, value: dot_nn(turns[side][0], value) + dot_nn(turns[side][1], value), raw
    )
    first_new = beta_one * first_ref[...] + (1.0 - beta_one) * grad
    second_new = beta_two * second_ref[...] + (1.0 - beta_two) * (turned * turned)
    first_out[...] = first_new
    second_out[...] = second_new
    moment = by_half(turn, *parts(first_new))
    ratio = moment / corr_one / (jnp.sqrt(second_new / corr_two) + eps_adam)
    back = by_half(turn_back, *parts(ratio))
    weight = weight_ref[...]
    weight_out[...] = weight - rate_matrix * (back + decay * weight)

    for side in range(2):
        if side == 0:
            piece = grad[:, :upper]
            piece = jnp.where(iota(piece.shape, 1) < half, piece, 0.0)
        else:
            piece = grad[:, lower:]
            piece = jnp.where(iota(piece.shape, 1) >= half - lower, piece, 0.0)
        piece = piece.astype(LOW)
        gram = parts(jnp.where(same, dot_nt(piece, piece), 0.0))
        summed = beta_two * state_ref[0, 2 * step + side]
        summed = summed + (1.0 - beta_two) * gained * (
            dot_nn(pick_t, gram[0]) + dot_nn(pick_t, gram[1])
        )
        diagonal = jnp.sum(summed * pick_t.astype(FULL), axis=0, keepdims=True)
        stats = summed / by_ones(diagonal)
        state_out[0, 2 * step + side] = stats
        high, rest = parts(old[side])
        wide_high, wide_rest = parts(spread_out(stats))
        lifted = dot_nn(high, wide_high) + dot_nn(high, wide_rest) + dot_nn(rest, wide_high)
        for column in range(BLK):
            raised[column, pl.ds(2 * step + side, 1), :] = lifted[column : column + 1]

    @pl.when(step == pl.num_programs(0) - 1)
    def _():
        columns = []
        for index in range(BLK):
            column = raised[index]
            for previous in columns:
                column = column - by_ones(previous * column) * previous
            column = column * lax.rsqrt(by_ones(column * column))
            columns.append(column)
            for expert in range(EXPERTS):
                state_out[1, expert, index : index + 1, :] = column[expert : expert + 1]


def soap(weight, grad, first, second, state, every):
    height, total = weight.shape
    width = total // PAIRS
    turned_state = state.transpose(0, 1, 3, 2)
    gained = stat_gain * every / (total // EXPERTS)
    column = pl.BlockSpec((height, width), lambda i: (0, i))
    first_new, second_new, state_new, weight_new = device_kernel(
        functools.partial(soap_kernel, gained),
        "soap",
        PAIRS,
        [
            column, pl.BlockSpec((1, height, width), lambda i: (i, 0, 0)), column, column,
            whole(2, EXPERTS, BLK, height),
        ],
        [(weight.shape, FULL), (weight.shape, FULL), (turned_state.shape, FULL),
         (weight.shape, FULL)],
        [column, column, total_block(2, EXPERTS, BLK, height), column],
        [pltpu.VMEM((BLK, EXPERTS, height), FULL)],
        2 * height * height * total,
        weight.size * 26,
    )(weight, grad, first, second, turned_state)
    return (first_new, second_new, state_new.transpose(0, 1, 3, 2), weight_new)


def adam(weight, grad, first, second, rate):
    corr_one = 1.0 - beta_one**STEP
    corr_two = 1.0 - beta_two**STEP
    first_new = beta_one * first + (1.0 - beta_one) * grad
    second_new = beta_two * second + (1.0 - beta_two) * grad * grad
    weight_new = weight - rate * (
        first_new / corr_one / (jnp.sqrt(second_new / corr_two) + eps_adam) + decay * weight
    )
    return (first_new, second_new, weight_new)


def local(
    images,
    dom_label,
    class_label,
    expand_weight,
    expand_first,
    expand_second,
    expand_state,
    project_weight,
    project_first,
    project_second,
    project_state,
    head_weight,
    head_first,
    head_second,
    head_state,
    depth_weight,
    depth_first,
    depth_second,
    classifier_weight,
    classifier_first,
    classifier_second,
    excite_weight,
    excite_first,
    excite_second,
    router_weight,
    router_first,
    router_second,
    gains_weight,
    gains_first,
    gains_second,
):
    low_type = jnp.bfloat16
    images_here = images.shape[0]
    every = images.shape[0] * lax.axis_size("dp") * lax.axis_size("wide")
    count = every * PIX
    n_wide, n_dp = lax.axis_size("wide"), lax.axis_size("dp")
    bias_se, bias_ex, gain_one, shift_one, gain_two, shift_two, bias_cls = split_gains(gains_weight)
    hot = boost * (dom_label[:, None] == jnp.arange(EXPERTS)[None, :]).astype(jnp.float32)
    img = images.transpose(1, 0, 2)
    img_two = jnp.concatenate([img, img], axis=2)
    project_low = lax.all_gather(project_weight.astype(low_type), "wide", axis=0, tiled=True)
    head_low = lax.all_gather(head_weight.astype(low_type), "wide", axis=0, tiled=True)
    class_low = lax.all_gather(classifier_weight.astype(low_type), "wide", axis=0, tiled=True)
    taps = KSIZE * KSIZE
    depth_own = depth_weight.transpose(1, 0, 2).reshape(taps * EXPERTS, -1).astype(low_type)
    depth_own = jnp.pad(depth_own, ((0, -taps * EXPERTS % 16), (0, 0)))
    expand_low, depth_low = gather_expand(expand_weight, depth_own, 6)
    expand_low = from_pieces(expand_low, PAIRS)
    depth_full = depth_low[:, : taps * EXPERTS].reshape(n_wide, taps, EXPERTS, -1)
    depth_full = depth_full.transpose(1, 2, 0, 3).reshape(taps, EXPERTS, C_MID).astype(FULL)
    excite = excite_weight.transpose(0, 2, 1)
    router = router_weight.T
    router_one, router_two = router[:, :C_IN], router[:, C_IN:]

    (
        hidden, turned, scaled, route_one, pair_in, pair_one, gate, squeeze, pooled_one,
        pooled_act, route_one_sum,
    ) = expand_forward(
        img_two, hot, router_one, expand_low, depth_full, excite, bias_se[None], bias_ex[None]
    )
    each, before, sums_one = project_forward(scaled, project_low, pair_one)
    norm_one, route_one_sum = sum_all(
        (sums_one, route_one_sum), (gain_one[None], shift_one[None]),
        functools.partial(norm_finish, count, every), ((8, C_OUT), (1, EXPERTS)), 1,
    )
    widened, twice, route_two, pair_two, pooled_two, sums_two, route_two_sum = head_forward(
        before, norm_one, hot, router_two, head_low
    )
    norm_two, route_two_sum = sum_all(
        (sums_two, route_two_sum), (gain_two[None], shift_two[None]),
        functools.partial(norm_finish, count, every), ((8, C_HEAD), (1, EXPERTS)), 2,
    )
    feats, grad_logits, grad_feats, back_two, cross_part, grad_bias_cls = loss_part(
        widened, norm_two, class_label[:, None], class_low, bias_cls[None]
    )
    grad_class = jnp.stack(
        [dot_tn(feats, part).astype(low_type) for part in jnp.split(grad_logits, PAIRS, axis=1)]
    )
    grad_class, grad_feats = lax.optimization_barrier((grad_class, grad_feats))
    share_class = lax.psum_scatter(grad_class, "wide", scatter_dimension=1, tiled=True)
    coef_two, back_two, cross_total, grad_bias_cls = sum_all(
        (back_two, cross_part, grad_bias_cls), (norm_two,), functools.partial(back_finish, count),
        ((4, C_HEAD), (2, C_HEAD), (1, 1), (1, CLASSES)), 3,
    )
    means_one = route_one_sum[0] / every
    means_two = route_two_sum[0] / every
    grad_widened, grad_normed, grad_logit_two, back_one = head_back(
        widened, grad_feats, coef_two, head_low, pair_two, twice, before, norm_one, route_two,
        balance_grad(means_two, every)[None], router_two,
    )
    grad_head = kern_grad(grad_widened, twice, pair_two, "head_grad")
    grad_head, back_one, share_class = lax.optimization_barrier((grad_head, back_one, share_class))
    share_head = lax.psum_scatter(grad_head, "wide", scatter_dimension=1, tiled=True)
    grad_router_two = dot_tn(pooled_two, grad_logit_two, HIGH)
    coef_one, back_one = sum_all(
        (back_one,), (norm_one,), functools.partial(back_finish, count),
        ((4, C_OUT), (2, C_OUT)), 4,
    )
    grad_before, grad_scaled, route_project = project_back(
        grad_normed, before, coef_one, pair_one, each, project_low
    )
    row_scale = jnp.tile(route_one.astype(low_type).T, (1, PIX)).reshape(PAIRS, 2, -1)
    grad_project = project_grad(grad_before, scaled, row_scale, n_wide)
    grad_project, grad_scaled, share_head = lax.optimization_barrier(
        (grad_project, grad_scaled, share_head)
    )
    wide_head = share_head.shape[2]
    own_late, arrived = scatter_sum(
        to_pieces(jnp.concatenate([share_head, share_class], axis=2), n_dp)
    )
    share_project = lax.psum_scatter(grad_project, "wide", scatter_dimension=0, tiled=True)[0]
    grad_hidden, grad_logit_one, grad_gate, grad_squeeze, grad_depth = expand_back(
        grad_scaled, turned, hidden, img_two, gate, squeeze, excite, depth_full, route_one,
        route_project, balance_grad(means_one, every)[None], expand_low,
    )
    arrived, share_project, grad_hidden = lax.optimization_barrier(
        (arrived, share_project, grad_hidden)
    )
    sum_late = spread_sum(add_arrived(own_late, arrived))
    own_project, arrived = scatter_sum(to_pieces(share_project, n_dp))
    grad_expand = kern_grad(grad_hidden, img_two, pair_in, "expand_grad")
    grad_excite = jnp.stack(
        [
            dot_tn(grad_squeeze, pooled_act, HIGH),
            dot_tn(squeeze * jax.nn.sigmoid(squeeze), grad_gate, HIGH),
        ]
    )
    grad_router_one = dot_tn(pooled_one, grad_logit_one, HIGH)
    grad_depth = grad_depth.transpose(1, 0, 2)
    grad_bias_se = jnp.sum(grad_squeeze, axis=0)
    grad_bias_ex = jnp.sum(grad_gate, axis=0)
    sum_late, arrived, grad_expand = lax.optimization_barrier((sum_late, arrived, grad_expand))
    sum_late = from_pieces(sum_late, PAIRS)
    sum_head, sum_class = sum_late[:, :, :wide_head], sum_late[:, :, wide_head:]
    sum_project = from_pieces(spread_sum(add_arrived(own_project, arrived)), PAIRS)
    share_expand = lax.psum_scatter(grad_expand, "wide", scatter_dimension=1, tiled=True)
    parts = n_wide * n_dp
    depth_part = grad_depth.reshape(taps * EXPERTS, n_wide, -1).transpose(1, 0, 2)
    depth_part = depth_part.reshape(n_wide, n_dp, taps * EXPERTS // n_dp, -1).transpose(1, 0, 2, 3)
    rest = jnp.concatenate(
        [
            grad_excite.reshape(-1), grad_router_one.reshape(-1), grad_router_two.reshape(-1),
            grad_bias_se, grad_bias_ex,
        ]
    )
    rest_size = rest.size
    rest_rows = -(-rest_size // (parts * 16 * 128)) * 16
    rest = jnp.pad(rest.astype(low_type), (0, parts * rest_rows * 128 - rest_size))
    rest = rest.reshape(n_dp, n_wide, rest_rows, 128)
    head_out = soap(head_weight, sum_head, head_first, head_second, head_state, every)
    project_out = soap(
        project_weight, sum_project, project_first, project_second, project_state, every
    )
    sum_class = sum_class.transpose(1, 0, 2).reshape(-1, CLASS_PAD)[:, :CLASSES].astype(FULL)
    class_out = adam(
        classifier_weight, sum_class, classifier_first, classifier_second, rate_matrix
    )
    share_expand, head_out, project_out, class_out = lax.optimization_barrier(
        (share_expand, head_out, project_out, class_out)
    )
    (own_depth, _), (own_expand,), rest = reduce_grads(
        [depth_part.astype(low_type), rest], [to_pieces(share_expand, n_dp)], 5
    )
    sum_expand = from_pieces(own_expand, PAIRS)
    sum_depth = own_depth.reshape(EXPERTS, taps, -1).astype(FULL)
    rest = rest.transpose(1, 0, 2, 3).reshape(-1, 128)
    split = grad_excite.size // 128
    sum_excite = rest[:split].reshape(2, C_SE, C_MID).transpose(0, 2, 1).astype(FULL)
    rest = rest[split:].reshape(-1)[: rest_size - grad_excite.size].astype(FULL)
    sum_router = rest[: router_weight.size].reshape(router_weight.shape)
    sum_bias = rest[router_weight.size :]
    loss = cross_total[0, 0] / every + balance_weight * (
        jnp.mean((means_one - jnp.mean(means_one)) ** 2)
        + jnp.mean((means_two - jnp.mean(means_two)) ** 2)
    )
    grad_gains = jnp.concatenate(
        [sum_bias, back_one[1], back_one[0], back_two[1], back_two[0], grad_bias_cls[0]]
    )
    expand_out = soap(expand_weight, sum_expand, expand_first, expand_second, expand_state, every)
    depth_out = adam(
        depth_weight, sum_depth, depth_first, depth_second, rate_matrix
    )
    excite_out = adam(excite_weight, sum_excite, excite_first, excite_second, rate_matrix)
    router_out = adam(router_weight, sum_router, router_first, router_second, rate_matrix)
    gains_out = adam(gains_weight, grad_gains, gains_first, gains_second, rate_gains)
    return (
        loss,
        expand_out[0],
        expand_out[1],
        expand_out[2],
        expand_out[3],
        project_out[0],
        project_out[1],
        project_out[2],
        project_out[3],
        head_out[0],
        head_out[1],
        head_out[2],
        head_out[3],
        depth_out[0],
        depth_out[1],
        depth_out[2],
        class_out[0],
        class_out[1],
        class_out[2],
        excite_out[0],
        excite_out[1],
        excite_out[2],
        router_out[0],
        router_out[1],
        router_out[2],
        gains_out[0],
        gains_out[1],
        gains_out[2],
    )


def solution(mesh):
    return jax.shard_map(
        local,
        mesh=mesh,
        in_specs=(
            P(("dp", "wide"), None, None),
            P(("dp", "wide")),
            P(("dp", "wide")),
            P("wide", None),
            P("wide", None),
            P("wide", None),
            P(None, None, "wide", None),
            P("wide", None),
            P("wide", None),
            P("wide", None),
            P(None, None, "wide", None),
            P("wide", None),
            P("wide", None),
            P("wide", None),
            P(None, None, "wide", None),
            P(None, None, "wide"),
            P(None, None, "wide"),
            P(None, None, "wide"),
            P("wide", None),
            P("wide", None),
            P("wide", None),
            P(),
            P(),
            P(),
            P(),
            P(),
            P(),
            P(),
            P(),
            P(),
        ),
        out_specs=(
            P(),
            P("wide", None),
            P("wide", None),
            P(None, None, "wide", None),
            P("wide", None),
            P("wide", None),
            P("wide", None),
            P(None, None, "wide", None),
            P("wide", None),
            P("wide", None),
            P("wide", None),
            P(None, None, "wide", None),
            P("wide", None),
            P(None, None, "wide"),
            P(None, None, "wide"),
            P(None, None, "wide"),
            P("wide", None),
            P("wide", None),
            P("wide", None),
            P(),
            P(),
            P(),
            P(),
            P(),
            P(),
            P(),
            P(),
            P(),
        ),
        check_vma=False,
    )
```

```python
import functools

import jax
import jax.numpy as jnp
from jax import lax
from jax.experimental import pallas as pl
from jax.experimental.pallas import tpu as pltpu
from jax.sharding import PartitionSpec as P

SIDE = 7
PIX = 49
KSIZE = 3
EXPERTS = 8
BLK = 4
STEP = 10
C_IN = 192
C_MID = 1152
C_SE = 48
C_OUT = 320
C_HEAD = 1280
CLASSES = 1000


HIGH = lax.Precision.HIGHEST
beta_one = 0.9
beta_two = 0.95
eps_adam = 1e-08
eps_norm = 1e-05
decay = 0.01
rate_matrix = 0.08
rate_gains = 0.5
boost = 1.0
balance_weight = 4.0
stat_gain = 15000.0


def split_gains(gains):
    widths = [C_SE, C_MID, C_OUT, C_OUT, C_HEAD, C_HEAD, CLASSES]
    pieces = []
    start = 0
    for width in widths:
        pieces.append(gains[start : start + width])
        start = start + width
    return pieces


MESH = pl.DeviceIdType.MESH


def greet(n_wide, n_dp):
    me_wide, me_dp = lax.axis_index("wide"), lax.axis_index("dp")
    barrier = pltpu.get_barrier_semaphore()
    for k in range(1, n_wide):
        pl.semaphore_signal(
            barrier, inc=1, device_id={"wide": lax.rem(me_wide + k, n_wide)}, device_id_type=MESH
        )
    for k in range(1, n_dp):
        pl.semaphore_signal(
            barrier, inc=1, device_id={"dp": lax.rem(me_dp + k, n_dp)}, device_id_type=MESH
        )


def await_greetings(n_wide, n_dp):
    pl.semaphore_wait(pltpu.get_barrier_semaphore(), n_wide + n_dp - 2)


def sum_scratch(shapes, n_wide, n_dp):
    count = len(shapes)
    found = [pltpu.VMEM((n_wide,) + shape, jnp.float32) for shape in shapes]
    found += [pltpu.VMEM((n_dp,) + shape, jnp.float32) for shape in shapes]
    found += [pltpu.VMEM(shape, jnp.float32) for shape in shapes] * 2
    return found + [
        pltpu.SemaphoreType.DMA((size * count,)) for size in (n_wide, n_wide, n_dp, n_dp)
    ]


def sum_copies(axis, size, sources, slots, send, recv):
    me, count = lax.axis_index(axis), len(sources)
    return [
        pltpu.make_async_remote_copy(
            src_ref=sources[index],
            dst_ref=slots[index].at[me],
            send_sem=send.at[k * count + index],
            recv_sem=recv.at[k * count + index],
            device_id={axis: lax.rem(me + k, size)},
            device_id_type=MESH,
        )
        for k in range(1, size)
        for index in range(count)
    ]


def sum_slots(axis, size, sources, slots):
    me = lax.axis_index(axis)
    for source, slot in zip(sources, slots):
        slot[me] = source[...]
    found = []
    for slot in slots:
        total = slot[0]
        for k in range(1, size):
            total = total + slot[k]
        found.append(total)
    return found


def sum_open(n_wide, n_dp, values, scratch):
    count = len(values)
    wide_slots, own = scratch[:count], scratch[2 * count : 3 * count]
    for ref, value in zip(own, values):
        ref[...] = value
    for copy in sum_copies("wide", n_wide, own, wide_slots, *scratch[4 * count : 4 * count + 2]):
        copy.start()


def sum_close(n_wide, n_dp, scratch):
    count = (len(scratch) - 4) // 4
    wide_slots, dp_slots, own, halves = (scratch[k * count : (k + 1) * count] for k in range(4))
    s_wide, r_wide, s_dp, r_dp = scratch[4 * count :]
    for copy in sum_copies("wide", n_wide, own, wide_slots, s_wide, r_wide):
        copy.wait()
    for half, total in zip(halves, sum_slots("wide", n_wide, own, wide_slots)):
        half[...] = total
    copies = sum_copies("dp", n_dp, halves, dp_slots, s_dp, r_dp)
    for copy in copies:
        copy.start()
    for copy in copies:
        copy.wait()
    return sum_slots("dp", n_dp, halves, dp_slots)


def norm_finish(count, every, totals, extras, outs):
    sums, route = totals
    center = sums[0:1] / count
    inv = lax.rsqrt(sums[1:2] / count - center * center + eps_norm)
    scale = inv * extras[0][...]
    outs[0][0:1] = scale
    outs[0][1:2] = extras[1][...] - center * scale
    outs[0][2:3] = inv
    outs[0][3:4] = -center * inv
    outs[0][4:8] = jnp.full((4, scale.shape[1]), 1.0 / every, jnp.float32)
    outs[1][...] = route


def back_finish(count, totals, extras, outs):
    sums = totals[0]
    norm = extras[0]
    scale, part = norm[0:1], norm[0:1] * sums[1:2] / count
    outs[0][0:2] = norm[0:2]
    outs[0][2:3] = -part * norm[2:3]
    outs[0][3:4] = -scale * sums[0:1] / count - part * norm[3:4]
    for out, total in zip(outs[1:], totals):
        out[...] = total


def balance_grad(means, every):
    return balance_weight * 2.0 * (means - jnp.mean(means)) / (EXPERTS * every)


GROUP = 16
PAIRS = EXPERTS // 2
ROWS = PIX * GROUP
CLASS_PAD = 1024
LOW = jnp.bfloat16
FULL = jnp.float32
VMEM_CAP = 60 * 1024 * 1024


def sig(value):
    return 0.5 + 0.5 * jnp.tanh(0.5 * value)


def silu_of(value):
    half = 0.5 * value
    return half * (1.0 + jnp.tanh(half))


def silu_pair(value):
    half = 0.5 * value
    bent = jnp.tanh(half)
    upper = 1.0 + bent
    return half * upper, upper * (1.0 + half * (1.0 - bent))


def sum_of(terms):
    while len(terms) > 1:
        terms = [
            terms[k] + terms[k + 1] if k + 1 < len(terms) else terms[k]
            for k in range(0, len(terms), 2)
        ]
    return terms[0]


def dot_nn(left, right, precision=None):
    return lax.dot_general(
        left, right, (((1,), (0,)), ((), ())), precision=precision, preferred_element_type=FULL
    )


def dot_nt(left, right, precision=None):
    return lax.dot_general(
        left, right, (((1,), (1,)), ((), ())), precision=precision, preferred_element_type=FULL
    )


def dot_tn(left, right, precision=None):
    return lax.dot_general(
        left, right, (((0,), (0,)), ((), ())), precision=precision, preferred_element_type=FULL
    )


def images_block(width):
    return pl.BlockSpec((PIX, GROUP, width), lambda i: (0, i, 0))


def group_block(width):
    return pl.BlockSpec((GROUP, width), lambda i: (i, 0))


def pair_block(width):
    return pl.BlockSpec((PAIRS, GROUP, width), lambda i: (0, i, 0))


def whole(*shape):
    return pl.BlockSpec(shape, lambda i: (0,) * len(shape), pipeline_mode=pl.Buffered(1))


def total_block(*shape):
    return pl.BlockSpec(shape, lambda i: (0,) * len(shape))


def device_kernel(
    kernel, name, grid, in_specs, outs, out_specs, scratch, flops, moved, ident=None
):
    return pl.pallas_call(
        kernel,
        name=name,
        grid=(grid,),
        in_specs=in_specs,
        out_shape=[jax.ShapeDtypeStruct(shape, dtype) for shape, dtype in outs],
        out_specs=out_specs,
        scratch_shapes=scratch,
        compiler_params=pltpu.CompilerParams(
            vmem_limit_bytes=VMEM_CAP, dimension_semantics=("arbitrary",), collective_id=ident,
            has_side_effects=ident is not None,
        ),
        cost_estimate=pl.CostEstimate(flops=flops, bytes_accessed=moved, transcendentals=0),
    )


def pair_scale(route, pair, width):
    lane = lax.broadcasted_iota(jnp.int32, (route.shape[0], 2 * width), 1)
    return jnp.where(
        lane < width, route[:, 2 * pair : 2 * pair + 1], route[:, 2 * pair + 1 : 2 * pair + 2]
    )


def pair_columns(sums, width):
    count = sums[0].shape[0]
    lane = lax.broadcasted_iota(jnp.int32, (count, 2 * width), 1)
    place = lax.broadcasted_iota(jnp.int32, (count, EXPERTS), 1)
    found = jnp.zeros((count, EXPERTS), FULL)
    for pair in range(PAIRS):
        first = jnp.sum(jnp.where(lane < width, sums[pair], 0.0), axis=1, keepdims=True)
        second = jnp.sum(jnp.where(lane < width, 0.0, sums[pair]), axis=1, keepdims=True)
        found = found + jnp.where(place == 2 * pair, first, 0.0)
        found = found + jnp.where(place == 2 * pair + 1, second, 0.0)
    return found


def taps_of(pixel):
    row, col = pixel // SIDE, pixel % SIDE
    found = []
    for tap in range(KSIZE * KSIZE):
        at_row, at_col = row + tap // KSIZE - 1, col + tap % KSIZE - 1
        if 0 <= at_row < SIDE and 0 <= at_col < SIDE:
            found.append((tap, at_row * SIDE + at_col))
    return found


def expand_kernel(
    img_ref, hot_ref, router_ref, source, depth_ref, excite_ref, bias_se_ref, bias_ex_ref,
    hidden_ref, turned_ref, scaled_ref, route_ref, pair_in_ref, pair_out_ref, gate_ref,
    squeeze_ref, pooled_one_ref, pooled_act_ref, route_sum_ref,
    routed, hidden_full, act_full, kern, expand_ref, sem,
):
    @pl.when(pl.program_id(0) == 0)
    def _():
        for copy in pair_copies(source, expand_ref, sem):
            copy.start()

    pooled = img_ref[0].astype(FULL)
    for pixel in range(1, PIX):
        pooled = pooled + img_ref[pixel].astype(FULL)
    pooled = pooled[:, :C_IN] * (1.0 / PIX)
    pooled_one_ref[...] = pooled
    route = sig(dot_nt(pooled, router_ref[...], HIGH) + hot_ref[...])
    route_ref[...] = route

    @pl.when(pl.program_id(0) == 0)
    def _():
        route_sum_ref[...] = jnp.zeros_like(route_sum_ref)

    route_sum_ref[...] += jnp.sum(route, axis=0, keepdims=True)
    low = route.astype(LOW).astype(FULL)
    for pair in range(PAIRS):
        scale = pair_scale(low, pair, C_IN).astype(LOW)
        pair_in_ref[pair] = scale
        pair_out_ref[pair] = pair_scale(low, pair, C_OUT).astype(LOW)
        place = slice(2 * pair * C_IN, 2 * (pair + 1) * C_IN)
        for pixel in range(PIX):
            routed[pixel, :, place] = img_ref[pixel] * scale
    columns = [low[:, expert : expert + 1] for expert in range(EXPERTS)]
    for tap in range(KSIZE * KSIZE):
        total = columns[0] * depth_ref[tap, 0:1, :]
        for expert in range(1, EXPERTS):
            total = total + columns[expert] * depth_ref[tap, expert : expert + 1, :]
        kern[tap] = total
    flat = routed[...].reshape(ROWS, EXPERTS * C_IN)
    third = C_MID // 3

    @pl.when(pl.program_id(0) == 0)
    def _():
        for copy in pair_copies(source, expand_ref, sem):
            copy.wait()

    def multiply(part):
        place = slice(part * third, (part + 1) * third)
        hidden_full[:, :, place] = dot_nt(flat, expand_ref[place]).reshape(PIX, GROUP, third)

    def chunk(index):
        lanes = slice(index * 128, index * 128 + 128)
        taps = [kern[tap, :, lanes] for tap in range(KSIZE * KSIZE)]
        start = [None] * PIX

        def fill(row):
            for pixel in range(row * SIDE, row * SIDE + SIDE):
                value = hidden_full[pixel, :, lanes]
                hidden_ref[pixel, :, lanes] = value.astype(LOW)
                start[pixel] = value * sig(value)

        fill(0)
        pooled_act = jnp.zeros((GROUP, 128), FULL)
        for row in range(SIDE):
            if row + 1 < SIDE:
                fill(row + 1)
            for pixel in range(row * SIDE, row * SIDE + SIDE):
                total = None
                for tap, source in taps_of(pixel):
                    term = start[source] * taps[tap]
                    total = term if total is None else total + term
                turned_ref[pixel, :, lanes] = total.astype(LOW)
                act = total * sig(total)
                pooled_act = pooled_act + act
                act_full[pixel, :, lanes] = act
        pooled_act_ref[:, lanes] = pooled_act * (1.0 / PIX)

    multiply(0)
    for part in range(3):
        if part < 2:
            multiply(part + 1)
        for index in range(3 * part, 3 * part + 3):
            chunk(index)
    squeeze = dot_nt(pooled_act_ref[...], excite_ref[0], HIGH) + bias_se_ref[...]
    squeeze_ref[...] = squeeze
    gate = sig(dot_nn(squeeze * sig(squeeze), excite_ref[1], HIGH) + bias_ex_ref[...])
    gate_ref[...] = gate

    def finish(pixel, carry):
        scaled_ref[pixel] = (act_full[pixel] * gate).astype(LOW)
        return carry

    lax.fori_loop(0, PIX, finish, 0, unroll=7)


def expand_forward(img_two, hot, router, expand_low, depth_full, excite, bias_se, bias_ex):
    images = img_two.shape[1]
    return device_kernel(
        expand_kernel,
        "expand_forward",
        images // GROUP,
        [
            images_block(2 * C_IN), group_block(EXPERTS), whole(EXPERTS, C_IN),
            pl.BlockSpec(memory_space=pl.ANY), whole(KSIZE * KSIZE, EXPERTS, C_MID),
            whole(2, C_SE, C_MID), whole(1, C_SE), whole(1, C_MID),
        ],
        [
            ((PIX, images, C_MID), LOW), ((PIX, images, C_MID), LOW), ((PIX, images, C_MID), LOW),
            ((images, EXPERTS), FULL), ((PAIRS, images, 2 * C_IN), LOW),
            ((PAIRS, images, 2 * C_OUT), LOW), ((images, C_MID), FULL), ((images, C_SE), FULL),
            ((images, C_IN), FULL), ((images, C_MID), FULL), ((1, EXPERTS), FULL),
        ],
        [
            images_block(C_MID), images_block(C_MID), images_block(C_MID), group_block(EXPERTS),
            pair_block(2 * C_IN), pair_block(2 * C_OUT), group_block(C_MID), group_block(C_SE),
            group_block(C_IN), group_block(C_MID), total_block(1, EXPERTS),
        ],
        [
            pltpu.VMEM((PIX, GROUP, EXPERTS * C_IN), LOW), pltpu.VMEM((PIX, GROUP, C_MID), FULL),
            pltpu.VMEM((PIX, GROUP, C_MID), FULL), pltpu.VMEM((KSIZE * KSIZE, GROUP, C_MID), FULL),
            pltpu.VMEM((C_MID, EXPERTS * C_IN), LOW), pltpu.SemaphoreType.DMA((PAIRS,)),
        ],
        2 * PIX * images * EXPERTS * C_IN * C_MID,
        PIX * images * 4 * C_MID * 2,
    )(img_two, hot, router, expand_low, depth_full, excite, bias_se, bias_ex)


def stack_experts(source, stacked, sem):
    copies = [
        pltpu.make_async_copy(
            source.at[:, expert * C_MID : (expert + 1) * C_MID],
            stacked.at[expert * C_OUT : (expert + 1) * C_OUT],
            sem.at[expert],
        )
        for expert in range(EXPERTS)
    ]
    for copy in copies:
        copy.start()
    for copy in copies:
        copy.wait()


def pair_copies(source, stacked, sem):
    width = source.shape[2]
    return [
        pltpu.make_async_copy(
            source.at[pair], stacked.at[:, pair * width : (pair + 1) * width], sem.at[pair]
        )
        for pair in range(PAIRS)
    ]


def project_kernel(
    n_wide, n_dp, count, every,
    scaled_ref, source, pair_ref, route_ref, gain_ref, shift_ref,
    each_ref, before_ref, norm_ref, route_total_ref,
    weight_ref, sem, sums_ref, *small
):
    half = 2 * 2 * C_OUT
    flat = scaled_ref[...].reshape(ROWS, C_MID)

    @pl.when(pl.program_id(0) == 0)
    def _():
        greet(n_wide, n_dp)
        stack_experts(source, weight_ref, sem)
        sums_ref[...] = jnp.zeros_like(sums_ref)

    total = None
    for part in range(2):
        value = dot_nt(flat, weight_ref[part * half : (part + 1) * half])
        value = value.reshape(PIX, GROUP, half)
        each_ref[:, :, part * half : (part + 1) * half] = value.astype(LOW)
        for side in range(2):
            term = value[:, :, side * 2 * C_OUT : (side + 1) * 2 * C_OUT]
            term = term * pair_ref[2 * part + side].astype(FULL)[None]
            total = term if total is None else total + term
    total = total.reshape(ROWS, 2 * C_OUT)
    before = (total + pltpu.roll(total, C_OUT, 1))[:, :C_OUT]
    before_ref[...] = before.reshape(PIX, GROUP, C_OUT)
    sums_ref[0:1] += jnp.sum(before, axis=0, keepdims=True)
    sums_ref[1:2] += jnp.sum(before * before, axis=0, keepdims=True)

    @pl.when(pl.program_id(0) == pl.num_programs(0) - 1)
    def _():
        await_greetings(n_wide, n_dp)
        sum_open(n_wide, n_dp, [sums_ref[...], route_ref[...]], small)
        totals = sum_close(n_wide, n_dp, small)
        norm_finish(count, every, totals, (gain_ref, shift_ref), (norm_ref, route_total_ref))


def project_forward(scaled, project_low, pair_out, route_sum, gain, shift, every, ident):
    images = scaled.shape[1]
    wide = EXPERTS * C_OUT
    n_wide, n_dp = lax.axis_size("wide"), lax.axis_size("dp")
    return device_kernel(
        functools.partial(project_kernel, n_wide, n_dp, every * PIX, every),
        "project_forward",
        images // GROUP,
        [
            images_block(C_MID), pl.BlockSpec(memory_space=pl.ANY), pair_block(2 * C_OUT),
            whole(1, EXPERTS), whole(1, C_OUT), whole(1, C_OUT),
        ],
        [
            ((PIX, images, wide), LOW), ((PIX, images, C_OUT), FULL), ((8, C_OUT), FULL),
            ((1, EXPERTS), FULL),
        ],
        [
            images_block(wide), images_block(C_OUT), total_block(8, C_OUT),
            total_block(1, EXPERTS),
        ],
        [
            pltpu.VMEM((wide, C_MID), LOW), pltpu.SemaphoreType.DMA((EXPERTS,)),
            pltpu.VMEM((2, C_OUT), FULL),
        ]
        + sum_scratch([(2, C_OUT), (1, EXPERTS)], n_wide, n_dp),
        2 * PIX * images * wide * C_MID,
        PIX * images * (wide + C_MID) * 2,
        ident,
    )(scaled, project_low, pair_out, route_sum, gain, shift)


def head_kernel(
    n_wide, n_dp, count, every,
    before_ref, norm_ref, hot_ref, router_ref, weight_ref, gain_ref, shift_ref,
    widened_ref, twice_ref, route_ref, pair_ref, pooled_ref, new_norm_ref, route_total_ref,
    routed, padded, sums_ref, route_sum_ref, *small
):
    @pl.when(pl.program_id(0) == 0)
    def _():
        greet(n_wide, n_dp)
        sums_ref[...] = jnp.zeros_like(sums_ref)
        route_sum_ref[...] = jnp.zeros_like(route_sum_ref)
        padded[...] = jnp.zeros_like(padded)

    gain, shift = norm_ref[0:1], norm_ref[1:2]
    pooled = jnp.zeros((GROUP, C_OUT), FULL)
    for pixel in range(PIX):
        normed = (before_ref[pixel] * gain + shift).astype(LOW).astype(FULL)
        pooled = pooled + normed
        padded[:, :C_OUT] = normed
        value = padded[...]
        twice_ref[pixel] = (value + pltpu.roll(value, C_OUT, 1)).astype(LOW)
    pooled = pooled * (1.0 / PIX)
    pooled_ref[...] = pooled
    route = sig(dot_nt(pooled, router_ref[...], HIGH) + hot_ref[...])
    route_ref[...] = route
    route_sum_ref[...] += jnp.sum(route, axis=0, keepdims=True)
    low = route.astype(LOW).astype(FULL)
    for pair in range(PAIRS):
        scale = pair_scale(low, pair, C_OUT).astype(LOW)
        pair_ref[pair] = scale
        place = slice(2 * pair * C_OUT, 2 * (pair + 1) * C_OUT)
        for pixel in range(PIX):
            routed[pixel, :, place] = twice_ref[pixel] * scale
    product = dot_nt(routed[...].reshape(ROWS, EXPERTS * C_OUT), weight_ref[...])
    widened_ref[...] = product.reshape(PIX, GROUP, C_HEAD).astype(LOW)
    sums_ref[0:1] += jnp.sum(product, axis=0, keepdims=True)
    sums_ref[1:2] += jnp.sum(product * product, axis=0, keepdims=True)

    @pl.when(pl.program_id(0) == pl.num_programs(0) - 1)
    def _():
        await_greetings(n_wide, n_dp)
        sum_open(n_wide, n_dp, [sums_ref[...], route_sum_ref[...]], small)
        totals = sum_close(n_wide, n_dp, small)
        norm_finish(count, every, totals, (gain_ref, shift_ref), (new_norm_ref, route_total_ref))


def head_forward(before, norm, hot, router, head_low, gain, shift, every, ident):
    images = before.shape[1]
    wide = EXPERTS * C_OUT
    n_wide, n_dp = lax.axis_size("wide"), lax.axis_size("dp")
    return device_kernel(
        functools.partial(head_kernel, n_wide, n_dp, every * PIX, every),
        "head_forward",
        images // GROUP,
        [
            images_block(C_OUT), whole(8, C_OUT), group_block(EXPERTS), whole(EXPERTS, C_OUT),
            whole(C_HEAD, wide), whole(1, C_HEAD), whole(1, C_HEAD),
        ],
        [
            ((PIX, images, C_HEAD), LOW), ((PIX, images, 2 * C_OUT), LOW),
            ((images, EXPERTS), FULL), ((PAIRS, images, 2 * C_OUT), LOW), ((images, C_OUT), FULL),
            ((8, C_HEAD), FULL), ((1, EXPERTS), FULL),
        ],
        [
            images_block(C_HEAD), images_block(2 * C_OUT), group_block(EXPERTS),
            pair_block(2 * C_OUT), group_block(C_OUT), total_block(8, C_HEAD),
            total_block(1, EXPERTS),
        ],
        [
            pltpu.VMEM((PIX, GROUP, wide), LOW), pltpu.VMEM((GROUP, 2 * C_OUT), FULL),
            pltpu.VMEM((2, C_HEAD), FULL), pltpu.VMEM((1, EXPERTS), FULL),
        ]
        + sum_scratch([(2, C_HEAD), (1, EXPERTS)], n_wide, n_dp),
        2 * PIX * images * wide * C_HEAD,
        PIX * images * (C_HEAD + C_OUT) * 2,
        ident,
    )(before, norm, hot, router, head_low, gain, shift)


def loss_kernel(
    n_wide, n_dp, count,
    widened_ref, norm_ref, label_ref, class_ref, bias_ref,
    feats_ref, logits_ref, grad_feats_ref, coef_ref, sums_ref, cross_ref, bias_grad_ref,
    silu_sum, slope_sum, cross_sum, *small
):
    step = pl.program_id(0)

    @pl.when(step == 0)
    def _():
        greet(n_wide, n_dp)

    rows = pl.ds(pl.multiple_of(step * GROUP, GROUP), GROUP)

    def chunk(index, carry):
        lanes = pl.ds(pl.multiple_of(index * 128, 128), 128)
        gain, shift, inv, offset = (norm_ref[k : k + 1, lanes] for k in range(4))
        total = slope = moved = jnp.zeros((GROUP, 128), FULL)
        for pixel in range(PIX):
            value = widened_ref[pixel, :, lanes].astype(FULL)
            lifted = value * gain + shift
            part = sig(lifted)
            grown = lifted * part
            bent = part + grown * (1.0 - part)
            total = total + grown
            slope = slope + bent
            moved = moved + bent * (value * inv + offset)
        silu_sum[rows, lanes] = total
        slope_sum[rows, lanes] = slope
        cross_sum[rows, lanes] = moved
        return carry

    lax.fori_loop(0, C_HEAD // 128, chunk, 0)

    @pl.when(step == pl.num_programs(0) - 1)
    def _():
        feats = (silu_sum[...] * (1.0 / PIX)).astype(LOW)
        feats_ref[...] = feats
        logits = dot_nn(feats, class_ref[...]) + bias_ref[...]
        lane = lax.broadcasted_iota(jnp.int32, logits.shape, 1)
        picked = lane == label_ref[...]
        top = jnp.max(logits, axis=1, keepdims=True)
        powers = jnp.exp(logits - top)
        totals = jnp.sum(powers, axis=1, keepdims=True)
        cross = top + jnp.log(totals) - jnp.sum(
            jnp.where(picked, logits, 0.0), axis=1, keepdims=True
        )
        cross = jnp.sum(cross, axis=0, keepdims=True)
        grad = (powers / totals - jnp.where(picked, 1.0, 0.0)) * norm_ref[4:5, 0:1]
        grad = grad.astype(LOW)
        logits_ref[...] = jnp.zeros_like(logits_ref)
        logits_ref[:, :CLASSES] = grad
        bias_grad = jnp.sum(grad.astype(FULL), axis=0, keepdims=True)
        grad_feats = dot_nt(grad, class_ref[...]) * (1.0 / PIX)
        grad_feats_ref[...] = grad_feats
        sums_ref[0:1] = jnp.sum(grad_feats * slope_sum[...], axis=0, keepdims=True)
        sums_ref[1:2] = jnp.sum(grad_feats * cross_sum[...], axis=0, keepdims=True)
        await_greetings(n_wide, n_dp)
        sum_open(n_wide, n_dp, [sums_ref[...], cross, bias_grad], small)
        totals = sum_close(n_wide, n_dp, small)
        back_finish(count, totals, (norm_ref,), (coef_ref, sums_ref, cross_ref, bias_grad_ref))


def loss_part(widened, norm, label, class_low, bias, every, ident):
    images = widened.shape[1]
    n_wide, n_dp = lax.axis_size("wide"), lax.axis_size("dp")
    return device_kernel(
        functools.partial(loss_kernel, n_wide, n_dp, every * PIX),
        "loss_part",
        images // GROUP,
        [
            images_block(C_HEAD), whole(8, C_HEAD), whole(images, 1), whole(C_HEAD, CLASSES),
            whole(1, CLASSES),
        ],
        [
            ((images, C_HEAD), LOW), ((images, CLASS_PAD), LOW), ((images, C_HEAD), FULL),
            ((4, C_HEAD), FULL), ((2, C_HEAD), FULL), ((1, 1), FULL), ((1, CLASSES), FULL),
        ],
        [
            total_block(images, C_HEAD), total_block(images, CLASS_PAD), total_block(images, C_HEAD),
            total_block(4, C_HEAD), total_block(2, C_HEAD), total_block(1, 1),
            total_block(1, CLASSES),
        ],
        [pltpu.VMEM((images, C_HEAD), FULL)] * 3
        + sum_scratch([(2, C_HEAD), (1, 1), (1, CLASSES)], n_wide, n_dp),
        4 * images * C_HEAD * CLASSES,
        PIX * images * C_HEAD * 2,
        ident,
    )(widened, norm, label, class_low, bias)


def head_back_kernel(
    widened_ref, grad_feats_ref, coef_ref, weight_ref, pair_ref, twice_ref, before_ref, norm_ref,
    route_ref, balance_ref, router_ref,
    grad_wide_ref, grad_normed_ref, logit_ref, sums_ref,
    product, mixed,
):
    half = 2 * 2 * C_OUT

    @pl.when(pl.program_id(0) == 0)
    def _():
        sums_ref[...] = jnp.zeros_like(sums_ref)

    gain, shift, by_value, constant = (coef_ref[k : k + 1] for k in range(4))
    grad_feats = grad_feats_ref[...] * (0.5 * gain)

    def widen(pixel, carry):
        value = widened_ref[pixel].astype(FULL)
        _, bent = silu_pair(value * gain + shift)
        grad = grad_feats * bent + value * by_value + constant
        grad_wide_ref[pixel] = grad.astype(LOW)
        return carry

    lax.fori_loop(0, PIX, widen, 0, unroll=7)
    flat = grad_wide_ref[...].reshape(ROWS, C_HEAD)
    twice = twice_ref[...].astype(FULL)
    route_sums = []
    total = None
    for part in range(2):
        value = dot_nn(flat, weight_ref[:, part * half : (part + 1) * half])
        value = value.reshape(PIX, GROUP, half)
        for side in range(2):
            piece = value[:, :, side * 2 * C_OUT : (side + 1) * 2 * C_OUT]
            route_sums.append(jnp.sum(piece * twice, axis=0))
            term = piece * pair_ref[2 * part + side].astype(FULL)[None]
            total = term if total is None else total + term
    total = total.reshape(ROWS, 2 * C_OUT)
    mixed[...] = (total + pltpu.roll(total, C_OUT, 1))[:, :C_OUT].reshape(PIX, GROUP, C_OUT)
    route = route_ref[...]
    grad_route = pair_columns(route_sums, C_OUT) + balance_ref[...]
    logit = grad_route * route * (1.0 - route)
    logit_ref[...] = logit
    added = dot_nn(logit, router_ref[...], HIGH) * (1.0 / PIX)

    def close(pixel, carry):
        plain, cross = carry
        grad = mixed[pixel] + added
        grad_normed_ref[pixel] = grad
        hat = before_ref[pixel] * norm_ref[2:3] + norm_ref[3:4]
        return plain + grad, cross + grad * hat

    zero = jnp.zeros((GROUP, C_OUT), FULL)
    plain, cross = lax.fori_loop(0, PIX, close, (zero, zero), unroll=7)
    sums_ref[0:1] += jnp.sum(plain, axis=0, keepdims=True)
    sums_ref[1:2] += jnp.sum(cross, axis=0, keepdims=True)


def head_back(
    widened, grad_feats, coef, head_low, pair_two, twice, before, norm, route, balance, router_t
):
    images = widened.shape[1]
    wide = EXPERTS * C_OUT
    return device_kernel(
        head_back_kernel,
        "head_back",
        images // GROUP,
        [
            images_block(C_HEAD), group_block(C_HEAD), whole(4, C_HEAD), whole(C_HEAD, wide),
            pair_block(2 * C_OUT), images_block(2 * C_OUT), images_block(C_OUT), whole(8, C_OUT),
            group_block(EXPERTS), whole(1, EXPERTS), whole(EXPERTS, C_OUT),
        ],
        [
            ((PIX, images, C_HEAD), LOW), ((PIX, images, C_OUT), FULL), ((images, EXPERTS), FULL),
            ((2, C_OUT), FULL),
        ],
        [
            images_block(C_HEAD), images_block(C_OUT), group_block(EXPERTS), total_block(2, C_OUT),
        ],
        [pltpu.VMEM((2, PIX, GROUP, wide // 2), FULL), pltpu.VMEM((PIX, GROUP, C_OUT), FULL)],
        2 * PIX * images * wide * C_HEAD,
        PIX * images * (2 * C_HEAD + C_OUT) * 2,
    )(widened, grad_feats, coef, head_low, pair_two, twice, before, norm, route, balance, router_t)


def kern_grad_kernel(grad_ref, twice_ref, pair_ref, out_ref, turned, routed):
    images, width = twice_ref.shape[1:]

    @pl.when(pl.program_id(0) == 0)
    def _():
        turned[...] = grad_ref[...].reshape(turned.shape[1], turned.shape[0]).T

    for side in range(2):
        scale = pair_ref[side]
        for pixel in range(PIX):
            routed[pixel * images : (pixel + 1) * images, side * width : (side + 1) * width] = (
                twice_ref[pixel] * scale
            )
    product = dot_nn(turned[...], routed[...])
    for side in range(2):
        out_ref[side] = product[:, side * width : (side + 1) * width].astype(LOW)


def kern_grad(grad, twice, pair_scales, name):
    images, out_width, width = grad.shape[1], grad.shape[2], twice.shape[2]
    rows = PIX * images
    return device_kernel(
        kern_grad_kernel,
        name,
        PAIRS // 2,
        [
            whole(PIX, images, out_width), whole(PIX, images, width),
            pl.BlockSpec((2, images, width), lambda i: (i, 0, 0)),
        ],
        [((PAIRS, out_width, width), LOW)],
        [pl.BlockSpec((2, out_width, width), lambda i: (i, 0, 0))],
        [pltpu.VMEM((out_width, rows), LOW), pltpu.VMEM((rows, 2 * width), LOW)],
        2 * rows * out_width * PAIRS * width,
        rows * out_width * 2,
    )(grad, twice, pair_scales)[0]


def head_grad_kernel(
    n_wide, n_dp, count, sums_ref, norm_ref, grad_ref, twice_ref, pair_ref,
    coef_ref, total_ref, out_ref, turned, routed, *small
):
    step = pl.program_id(0)

    @pl.when(step == 0)
    def _():
        greet(n_wide, n_dp)

    kern_grad_kernel(grad_ref, twice_ref, pair_ref, out_ref, turned, routed)

    @pl.when(step == 0)
    def _():
        await_greetings(n_wide, n_dp)
        sum_open(n_wide, n_dp, [sums_ref[...]], small)

    @pl.when(step == pl.num_programs(0) - 1)
    def _():
        totals = sum_close(n_wide, n_dp, small)
        back_finish(count, totals, (norm_ref,), (coef_ref, total_ref))


def head_grad(sums, norm, grad, twice, pair_scales, every, ident):
    images, out_width, width = grad.shape[1], grad.shape[2], twice.shape[2]
    rows = PIX * images
    n_wide, n_dp = lax.axis_size("wide"), lax.axis_size("dp")
    return device_kernel(
        functools.partial(head_grad_kernel, n_wide, n_dp, every * PIX),
        "head_grad",
        PAIRS // 2,
        [
            whole(2, C_OUT), whole(8, C_OUT), whole(PIX, images, out_width),
            whole(PIX, images, width), pl.BlockSpec((2, images, width), lambda i: (i, 0, 0)),
        ],
        [((4, C_OUT), FULL), ((2, C_OUT), FULL), ((PAIRS, out_width, width), LOW)],
        [
            total_block(4, C_OUT), total_block(2, C_OUT),
            pl.BlockSpec((2, out_width, width), lambda i: (i, 0, 0)),
        ],
        [pltpu.VMEM((out_width, rows), LOW), pltpu.VMEM((rows, 2 * width), LOW)]
        + sum_scratch([(2, C_OUT)], n_wide, n_dp),
        2 * rows * out_width * PAIRS * width,
        rows * out_width * 2,
        ident,
    )(sums, norm, grad, twice, pair_scales)


def project_grad_kernel(grad_ref, scaled_ref, scale_ref, out_ref, turned, routed):
    rows = turned.shape[1]

    @pl.when(pl.program_id(0) == 0)
    def _():
        turned[...] = grad_ref[...].reshape(rows, C_OUT).T

    for side in range(2):
        routed[side * C_OUT : (side + 1) * C_OUT] = turned[...] * scale_ref[0, side : side + 1]
    product = dot_nn(routed[...], scaled_ref[...].reshape(rows, C_MID))
    owners, _, height, _ = out_ref.shape
    for side in range(2):
        for owner in range(owners):
            place = side * C_OUT + owner * height
            out_ref[owner, 0, :, side * C_MID : (side + 1) * C_MID] = product[
                place : place + height
            ].astype(LOW)


def project_grad(grad, scaled, scale, owners):
    images = grad.shape[1]
    rows = PIX * images
    return device_kernel(
        project_grad_kernel,
        "project_grad",
        PAIRS,
        [
            whole(PIX, images, C_OUT), whole(PIX, images, C_MID),
            pl.BlockSpec((1, 2, rows), lambda i: (i, 0, 0)),
        ],
        [((owners, PAIRS, C_OUT // owners, 2 * C_MID), LOW)],
        [pl.BlockSpec((owners, 1, C_OUT // owners, 2 * C_MID), lambda i: (0, i, 0, 0))],
        [pltpu.VMEM((C_OUT, rows), LOW), pltpu.VMEM((2 * C_OUT, rows), LOW)],
        2 * rows * EXPERTS * C_OUT * C_MID,
        rows * (C_OUT + C_MID) * 2,
    )(grad, scaled, scale)[0]


def project_back_kernel(
    grad_ref, before_ref, coef_ref, pair_ref, each_ref, source,
    grad_before_ref, grad_scaled_ref, route_ref,
    routed, padded, twice, weight_ref, sem,
):
    @pl.when(pl.program_id(0) == 0)
    def _():
        stack_experts(source, weight_ref, sem)
        padded[...] = jnp.zeros_like(padded)

    gain, _, by_value, constant = (coef_ref[k : k + 1] for k in range(4))
    scales = [pair_ref[pair] for pair in range(PAIRS)]

    def turn(pixel, carry):
        grad = grad_ref[pixel] * gain + before_ref[pixel] * by_value + constant
        grad = grad.astype(LOW)
        grad_before_ref[pixel] = grad
        padded[:, :C_OUT] = grad.astype(FULL)
        value = padded[...]
        value = (value + pltpu.roll(value, C_OUT, 1)).astype(LOW)
        twice[pixel] = value
        for pair in range(PAIRS):
            place = slice(2 * pair * C_OUT, 2 * (pair + 1) * C_OUT)
            routed[pixel, :, place] = value * scales[pair]
        return carry

    lax.fori_loop(0, PIX, turn, 0, unroll=7)
    product = dot_nn(routed[...].reshape(ROWS, EXPERTS * C_OUT), weight_ref[...])
    grad_scaled_ref[...] = product.reshape(PIX, GROUP, C_MID).astype(LOW)
    route_sums = []
    for pair in range(PAIRS):
        place = slice(2 * pair * C_OUT, 2 * (pair + 1) * C_OUT)
        term = each_ref[:, :, place].astype(FULL) * twice[...].astype(FULL)
        route_sums.append(jnp.sum(term, axis=0))
    route_ref[...] = pair_columns(route_sums, C_OUT)


def project_back(grad_normed, before, coef, pair_out, each, project_low):
    images = before.shape[1]
    wide = EXPERTS * C_OUT
    return device_kernel(
        project_back_kernel,
        "project_back",
        images // GROUP,
        [
            images_block(C_OUT), images_block(C_OUT), whole(4, C_OUT), pair_block(2 * C_OUT),
            images_block(wide), pl.BlockSpec(memory_space=pl.ANY),
        ],
        [
            ((PIX, images, C_OUT), LOW), ((PIX, images, C_MID), LOW), ((images, EXPERTS), FULL),
        ],
        [images_block(C_OUT), images_block(C_MID), group_block(EXPERTS)],
        [
            pltpu.VMEM((PIX, GROUP, wide), LOW), pltpu.VMEM((GROUP, 2 * C_OUT), FULL),
            pltpu.VMEM((PIX, GROUP, 2 * C_OUT), LOW),
            pltpu.VMEM((wide, C_MID), LOW), pltpu.SemaphoreType.DMA((EXPERTS,)),
        ],
        2 * PIX * images * wide * C_MID,
        PIX * images * (C_MID + wide) * 2,

    )(grad_normed, before, coef, pair_out, each, project_low)


def expand_back_kernel(
    grad_scaled_ref, turned_ref, hidden_ref, img_ref, gate_ref, squeeze_ref, excite_ref, depth_ref,
    route_ref, route_part_ref, balance_ref, source,
    grad_hidden_ref, logit_ref, grad_gate_ref, grad_squeeze_ref, grad_depth_ref,
    kern, start, slope, grad_turned, grad_kern, pooled, product, weight_ref, sem,
):
    @pl.when(pl.program_id(0) == 0)
    def _():
        for copy in pair_copies(source, weight_ref, sem):
            copy.start()
        grad_depth_ref[...] = jnp.zeros_like(grad_depth_ref)

    route = route_ref[...]
    low = route.astype(LOW).astype(FULL)
    columns = [low[:, expert : expert + 1] for expert in range(EXPERTS)]
    for tap in range(KSIZE * KSIZE):
        total = columns[0] * depth_ref[tap, 0:1, :]
        for expert in range(1, EXPERTS):
            total = total + columns[expert] * depth_ref[tap, expert : expert + 1, :]
        kern[tap] = total

    def gate_sum(pixel, carry):
        value = turned_ref[pixel].astype(FULL)
        return carry + grad_scaled_ref[pixel].astype(FULL) * silu_of(value)

    gate = gate_ref[...]
    grad_gate = lax.fori_loop(0, PIX, gate_sum, jnp.zeros((GROUP, C_MID), FULL), unroll=7)
    grad_gate = grad_gate * gate * (1.0 - gate)
    grad_gate_ref[...] = grad_gate
    squeeze = squeeze_ref[...]
    part = sig(squeeze)
    grad_squeeze = dot_nt(grad_gate, excite_ref[1], HIGH) * (part + squeeze * part * (1.0 - part))
    grad_squeeze_ref[...] = grad_squeeze
    pooled[...] = dot_nn(grad_squeeze, excite_ref[0], HIGH) * (1.0 / PIX)

    third = C_MID // 3

    @pl.when(pl.program_id(0) == 0)
    def _():
        for copy in pair_copies(source, weight_ref, sem):
            copy.wait()

    def chunk(index):
        lanes = slice(index * 128, index * 128 + 128)
        side = index % 2
        gate_part = 0.5 * gate_ref[:, lanes]
        pooled_part = 0.5 * pooled[:, lanes]
        for pixel in range(PIX):
            _, bent = silu_pair(turned_ref[pixel, :, lanes].astype(FULL))
            grad = grad_scaled_ref[pixel, :, lanes].astype(FULL) * gate_part + pooled_part
            grad_turned[side, pixel] = grad * bent
            value, bent = silu_pair(hidden_ref[pixel, :, lanes].astype(FULL))
            start[side, pixel] = value
            slope[side, pixel] = bent
        taps = [0.5 * kern[tap, :, lanes] for tap in range(KSIZE * KSIZE)]
        sums = [None] * (KSIZE * KSIZE)
        for pixel in range(PIX):
            here = grad_turned[side, pixel]
            terms = []
            for tap, source in taps_of(pixel):
                term = start[side, source] * here
                sums[tap] = term if sums[tap] is None else sums[tap] + term
                terms.append(grad_turned[side, source] * taps[KSIZE * KSIZE - 1 - tap])
            grad_hidden_ref[pixel, :, lanes] = (sum_of(terms) * slope[side, pixel]).astype(LOW)
        for tap in range(KSIZE * KSIZE):
            grad_kern[tap, :, lanes] = sums[tap]

    for part in range(3):
        for index in range(3 * part, 3 * part + 3):
            chunk(index)
        inner = slice(part * third, (part + 1) * third)
        term = dot_nn(grad_hidden_ref[:, :, inner].reshape(ROWS, third), weight_ref[inner])
        term = term.reshape(PIX, GROUP, EXPERTS * C_IN)
        product[...] = term if part == 0 else product[...] + term
    place = lax.broadcasted_iota(jnp.int32, (GROUP, EXPERTS), 1)
    depth_term = jnp.zeros((GROUP, EXPERTS), FULL)
    for expert in range(EXPERTS):
        total = jnp.zeros((GROUP, C_MID), FULL)
        for tap in range(KSIZE * KSIZE):
            value = grad_kern[tap]
            total = total + value * depth_ref[tap, expert : expert + 1, :]
            weighed = value * columns[expert]
            grad_depth_ref[tap, expert : expert + 1, :] += jnp.sum(weighed, axis=0, keepdims=True)
        total = jnp.sum(total, axis=1, keepdims=True)
        depth_term = depth_term + jnp.where(place == expert, total, 0.0)
    def route_part(pixel, carry):
        value = img_ref[pixel].astype(FULL)
        return tuple(
            carry[pair] + product[pixel, :, 2 * pair * C_IN : 2 * (pair + 1) * C_IN] * value
            for pair in range(PAIRS)
        )

    zero = jnp.zeros((GROUP, 2 * C_IN), FULL)
    route_sums = lax.fori_loop(0, PIX, route_part, (zero,) * PAIRS, unroll=7)
    grad_route = (
        pair_columns(route_sums, C_IN) + route_part_ref[...] + depth_term + balance_ref[...]
    )
    logit_ref[...] = grad_route * route * (1.0 - route)


def expand_back(
    grad_scaled, turned, hidden, img_two, gate, squeeze, excite, depth_full, route, route_part,
    balance, expand_low,
):
    images = hidden.shape[1]
    taps = KSIZE * KSIZE
    return device_kernel(
        expand_back_kernel,
        "expand_back",
        images // GROUP,
        [
            images_block(C_MID), images_block(C_MID), images_block(C_MID), images_block(2 * C_IN),
            group_block(C_MID), group_block(C_SE), whole(2, C_SE, C_MID),
            whole(taps, EXPERTS, C_MID), group_block(EXPERTS), group_block(EXPERTS),
            whole(1, EXPERTS), pl.BlockSpec(memory_space=pl.ANY),
        ],
        [
            ((PIX, images, C_MID), LOW), ((images, EXPERTS), FULL), ((images, C_MID), FULL),
            ((images, C_SE), FULL), ((taps, EXPERTS, C_MID), FULL),
        ],
        [
            images_block(C_MID), group_block(EXPERTS), group_block(C_MID), group_block(C_SE),
            total_block(taps, EXPERTS, C_MID),
        ],
        [
            pltpu.VMEM((taps, GROUP, C_MID), FULL), pltpu.VMEM((2, PIX, GROUP, 128), FULL),
            pltpu.VMEM((2, PIX, GROUP, 128), FULL), pltpu.VMEM((2, PIX, GROUP, 128), FULL), pltpu.VMEM((taps, GROUP, C_MID), FULL),
            pltpu.VMEM((GROUP, C_MID), FULL), pltpu.VMEM((PIX, GROUP, EXPERTS * C_IN), FULL),
            pltpu.VMEM((C_MID, EXPERTS * C_IN), LOW), pltpu.SemaphoreType.DMA((PAIRS,)),
        ],
        2 * PIX * images * EXPERTS * C_IN * C_MID,
        PIX * images * 4 * C_MID * 2,
    )(
        grad_scaled, turned, hidden, img_two, gate, squeeze, excite, depth_full, route, route_part,
        balance, expand_low,
    )


def reduce_kernel(n_wide, n_dp, n_full, n_share, *refs):
    n_in = n_full + n_share
    fulls, shares = refs[:n_full], refs[n_full:n_in]
    full_outs, share_outs, spread_out = refs[n_in : n_in + n_full], refs[n_in + n_full : 2 * n_in], refs[2 * n_in]
    scratch = list(refs[2 * n_in + 1 :])
    firsts, seconds, thirds, halves, lineds = (
        [scratch.pop(0) for _ in range(n_full)] for _ in range(5)
    )
    slots = [scratch.pop(0) for _ in range(n_share)]
    send, recv = scratch
    lines = n_wide // 2
    me_wide, me_dp = lax.axis_index("wide"), lax.axis_index("dp")
    core, line = lax.rem(me_wide, 2), lax.div(me_wide, 2)
    sibling = line * 2 + 1 - core
    used = [0]

    barrier = pltpu.get_barrier_semaphore()
    for k in range(1, n_wide):
        pl.semaphore_signal(
            barrier, inc=1, device_id={"wide": lax.rem(me_wide + k, n_wide)}, device_id_type=MESH
        )
    for k in range(1, n_dp):
        pl.semaphore_signal(
            barrier, inc=1, device_id={"dp": lax.rem(me_dp + k, n_dp)}, device_id_type=MESH
        )
    pl.semaphore_wait(barrier, n_wide + n_dp - 2)

    def launch(src, dst, device):
        copy = pltpu.make_async_remote_copy(
            src_ref=src, dst_ref=dst, send_sem=send.at[used[0]], recv_sem=recv.at[used[0]],
            device_id=device, device_id_type=MESH,
        )
        used[0] += 1
        copy.start()
        return copy

    def finish(copies):
        for copy in copies:
            copy.wait()

    def dp_peer(k):
        return lax.rem(me_dp + k, n_dp)

    to_sibling = [
        launch(full.at[:, :, 1 - core], first, {"wide": sibling})
        for full, first in zip(fulls, firsts)
    ]
    scattered = [
        launch(share.at[dp_peer(k)], slot.at[k - 1], {"dp": dp_peer(k)})
        for k in range(1, n_dp)
        for share, slot in zip(shares, slots)
    ]
    finish(to_sibling)
    for full, first, half in zip(fulls, firsts, halves):
        def pair_sum(index, carry, full=full, first=first, half=half):
            at_dp, at_line = lax.div(index, lines), lax.rem(index, lines)
            total = full[at_dp, at_line, core].astype(FULL) + first[at_dp, at_line].astype(FULL)
            half[at_dp, at_line] = total.astype(LOW)
            return carry

        lax.fori_loop(0, n_dp * lines, pair_sum, 0)
    across = [
        launch(half.at[dp_peer(k)], second.at[k - 1], {"dp": dp_peer(k)})
        for k in range(1, n_dp)
        for half, second in zip(halves, seconds)
    ]
    finish(scattered)
    for share, slot, out in zip(shares, slots, share_outs):
        total = share[me_dp].astype(FULL)
        for k in range(1, n_dp):
            total = total + slot[k - 1].astype(FULL)
        out[me_dp] = total.astype(LOW)
    finish(across)
    for half, second, lined in zip(halves, seconds, lineds):
        def dp_sum(at_line, carry, half=half, second=second, lined=lined):
            total = half[me_dp, at_line].astype(FULL)
            for k in range(1, n_dp):
                total = total + second[k - 1, at_line].astype(FULL)
            lined[at_line] = total.astype(LOW)
            return carry

        lax.fori_loop(0, lines, dp_sum, 0)
    along = []
    for k in range(1, lines):
        other = lax.rem(line + k, lines)
        for lined, third in zip(lineds, thirds):
            along.append(launch(lined.at[other], third.at[k - 1], {"wide": other * 2 + core}))
    gathered = [
        launch(out.at[me_dp], out.at[me_dp], {"dp": dp_peer(k)})
        for k in range(1, n_dp)
        for out in share_outs
    ]
    finish(along)
    for lined, third, out in zip(lineds, thirds, full_outs):
        total = lined[line].astype(FULL)
        for k in range(1, lines):
            total = total + third[k - 1].astype(FULL)
        out[me_dp] = total.astype(LOW)
    last = [
        launch(out.at[me_dp], out.at[me_dp], {"dp": dp_peer(k)})
        for out in reversed(full_outs)
        for k in range(1, n_dp)
    ]
    own = full_outs[-1]
    finish(last[: n_dp - 1])
    spread_out[me_wide] = own[...]
    everywhere = [
        launch(own, spread_out.at[me_wide], {"wide": lax.rem(me_wide + k, n_wide)})
        for k in range(1, n_wide)
    ]
    finish(last[n_dp - 1 :] + gathered + everywhere)


def reduce_grads(fulls, shares, ident):
    n_wide, n_dp = lax.axis_size("wide"), lax.axis_size("dp")
    lines = n_wide // 2
    views = [full.reshape((n_dp, lines, 2) + full.shape[2:]) for full in fulls]
    tails = [full.shape[2:] for full in fulls]
    copies = (
        len(fulls) * (1 + (n_dp - 1) * 2 + lines - 1) + len(shares) * 2 * (n_dp - 1) + n_wide - 1
    )
    vmem = pl.BlockSpec(memory_space=pltpu.VMEM)
    outs = [jax.ShapeDtypeStruct((n_dp,) + tail, LOW) for tail in tails]
    outs += [jax.ShapeDtypeStruct(share.shape, LOW) for share in shares]
    outs += [jax.ShapeDtypeStruct((n_wide, n_dp) + tails[-1], LOW)]
    found = pl.pallas_call(
        functools.partial(reduce_kernel, n_wide, n_dp, len(fulls), len(shares)),
        name="reduce_grads",
        out_shape=outs,
        in_specs=[vmem] * (len(fulls) + len(shares)),
        out_specs=[vmem] * len(outs),
        scratch_shapes=[pltpu.VMEM((n_dp, lines) + tail, LOW) for tail in tails]
        + [pltpu.VMEM((n_dp - 1, lines) + tail, LOW) for tail in tails]
        + [pltpu.VMEM((lines - 1,) + tail, LOW) for tail in tails]
        + [pltpu.VMEM((n_dp, lines) + tail, LOW) for tail in tails]
        + [pltpu.VMEM((lines,) + tail, LOW) for tail in tails]
        + [pltpu.VMEM((n_dp - 1,) + share.shape[1:], LOW) for share in shares]
        + [pltpu.SemaphoreType.DMA((copies,)), pltpu.SemaphoreType.DMA((copies,))],
        compiler_params=pltpu.CompilerParams(
            collective_id=ident, has_side_effects=True, vmem_limit_bytes=VMEM_CAP
        ),
    )(*views, *shares)
    return found[: len(fulls)], found[len(fulls) : len(fulls) + len(shares)], found[-1]


def to_pieces(cube, count):
    pairs, rows, width = cube.shape
    if pairs == count:
        return cube
    more = count // pairs
    cube = cube.reshape(pairs, rows, more, width // more).transpose(0, 2, 1, 3)
    return cube.reshape(count, rows, width // more)


def from_pieces(pieces, pairs):
    count, rows, width = pieces.shape
    if pairs == count:
        return pieces
    more = count // pairs
    cube = pieces.reshape(pairs, more, rows, width).transpose(0, 2, 1, 3)
    return cube.reshape(pairs, rows, width * more)


def send_around(value, hop):
    count = lax.axis_size("dp")
    return lax.ppermute(value, "dp", [(at, (at + hop) % count) for at in range(count)])


def scatter_sum(pieces):
    count, me = lax.axis_size("dp"), lax.axis_index("dp")
    total = lax.dynamic_index_in_dim(pieces, me, 0, keepdims=False).astype(FULL)
    arrived = [
        send_around(lax.dynamic_index_in_dim(pieces, (me + hop) % count, 0, keepdims=False), hop)
        for hop in range(1, count)
    ]
    return total, arrived


def add_arrived(total, arrived):
    for part in arrived:
        total = total + part.astype(FULL)
    return total.astype(LOW)


def spread_sum(piece):
    count, me = lax.axis_size("dp"), lax.axis_index("dp")
    found = jnp.zeros((count,) + piece.shape, piece.dtype)
    for hop in range(count):
        part = piece if hop == 0 else send_around(piece, hop)
        found = lax.dynamic_update_index_in_dim(found, part, (me - hop) % count, 0)
    return found


def gather_kernel(n_wide, n_dp, weight_ref, depth_ref, out_ref, depth_out, send, recv):
    lines = n_wide // 2
    me_wide, me_dp = lax.axis_index("wide"), lax.axis_index("dp")
    core, line = lax.rem(me_wide, 2), lax.div(me_wide, 2)
    sibling = {"wide": line * 2 + 1 - core}
    width = out_ref.shape[4]
    used = [0]

    barrier = pltpu.get_barrier_semaphore()
    for k in range(1, n_wide):
        pl.semaphore_signal(
            barrier, inc=1, device_id={"wide": lax.rem(me_wide + k, n_wide)}, device_id_type=MESH
        )
    for k in range(1, n_dp):
        pl.semaphore_signal(
            barrier, inc=1, device_id={"dp": lax.rem(me_dp + k, n_dp)}, device_id_type=MESH
        )
    for piece in range(n_dp):
        out_ref[piece, line, core] = weight_ref[:, piece * width : (piece + 1) * width].astype(LOW)
    depth_out[me_wide] = depth_ref[...]
    pl.semaphore_wait(barrier, n_wide + n_dp - 2)

    def launch(part, device, ref=out_ref):
        copy = pltpu.make_async_remote_copy(
            src_ref=ref.at[part], dst_ref=ref.at[part], send_sem=send.at[used[0]],
            recv_sem=recv.at[used[0]], device_id=device, device_id_type=MESH,
        )
        used[0] += 1
        copy.start()
        return copy

    def dp_from(hop):
        return lax.rem(me_dp + n_dp - hop, n_dp)

    along = [
        launch((me_dp, line, core), {"wide": lax.rem(line + k, lines) * 2 + core})
        for k in range(1, lines)
    ]
    started = [launch((piece, line, core), sibling) for piece in range(n_dp)]
    started += [
        launch((me_wide,), {"wide": lax.rem(me_wide + k, n_wide)}, depth_out)
        for k in range(1, n_wide)
    ]
    across = []
    for k in range(1, lines):
        source = lax.rem(line + lines - k, lines)
        along[k - 1].wait_recv()
        for hop in range(1, n_dp):
            copy = launch((me_dp, source, core), {"dp": lax.rem(me_dp + hop, n_dp)})
            across.append((copy, hop, source))
        started.append(launch((me_dp, source, core), sibling))
    for copy, hop, source in across:
        copy.wait_recv()
        started.append(launch((dp_from(hop), source, core), sibling))
    for copy in started:
        copy.wait()
    for copy in along:
        copy.wait_send()
    for copy, _, _ in across:
        copy.wait_send()


def gather_expand(weight, depth, ident):
    n_wide, n_dp = lax.axis_size("wide"), lax.axis_size("dp")
    lines = n_wide // 2
    height, width = weight.shape
    copies = (lines - 1) * (1 + n_dp) + (lines - 1) * (n_dp - 1) + n_dp + n_wide - 1
    vmem = pl.BlockSpec(memory_space=pltpu.VMEM)
    found, depths = pl.pallas_call(
        functools.partial(gather_kernel, n_wide, n_dp),
        name="gather_expand",
        out_shape=[
            jax.ShapeDtypeStruct((n_dp, lines, 2, height, width // n_dp), LOW),
            jax.ShapeDtypeStruct((n_wide,) + depth.shape, LOW),
        ],
        in_specs=[vmem] * 2,
        out_specs=[vmem] * 2,
        scratch_shapes=[pltpu.SemaphoreType.DMA((copies,)), pltpu.SemaphoreType.DMA((copies,))],
        compiler_params=pltpu.CompilerParams(
            collective_id=ident, has_side_effects=True, vmem_limit_bytes=VMEM_CAP
        ),
    )(weight, depth)
    return found.reshape(n_dp, n_wide * height, width // n_dp), depths


def soap_kernel(
    gained, weight_ref, grad_ref, first_ref, second_ref, state_ref,
    first_out, second_out, state_out, weight_out, raised,
):
    step = pl.program_id(0)
    height, width = weight_ref.shape
    half = width // 2
    upper = -(-half // 128) * 128
    lower = half // 128 * 128
    corr_one = 1.0 - beta_one**STEP
    corr_two = 1.0 - beta_two**STEP

    def iota(shape, axis):
        return lax.broadcasted_iota(jnp.int32, shape, axis)

    pick = (iota((height, BLK), 0) % BLK == iota((height, BLK), 1)).astype(LOW)
    pick_t = (iota((BLK, height), 1) % BLK == iota((BLK, height), 0)).astype(LOW)
    same = iota((height, height), 0) // BLK == iota((height, height), 1) // BLK
    ones = same.astype(LOW)

    def parts(value):
        high = value.astype(LOW)
        return high, (value - high.astype(FULL)).astype(LOW)

    def by_ones(value):
        high, rest = parts(value)
        return dot_nn(high, ones) + dot_nn(rest, ones)

    def spread_out(rows):
        high, rest = parts(rows)
        return jnp.where(same, dot_nn(pick, high) + dot_nn(pick, rest), 0.0)

    def by_half(product, *values):
        first = product(0, *(value[:, :upper] for value in values))
        second = product(1, *(value[:, lower:] for value in values))
        if upper == lower:
            return jnp.concatenate([first, second], axis=1)
        lane = iota((height, upper - lower), 1)
        middle = jnp.where(lane < half - lower, first[:, lower:], second[:, : upper - lower])
        return jnp.concatenate([first[:, :lower], middle, second[:, upper - lower :]], axis=1)

    old = [state_ref[1, 2 * step + side] for side in range(2)]
    turns = [parts(spread_out(rows)) for rows in old]

    def turn(side, high, rest):
        return dot_nn(turns[side][0], high) + dot_nn(turns[side][0], rest) + dot_nn(turns[side][1], high)

    def turn_back(side, high, rest):
        return dot_tn(turns[side][0], high) + dot_tn(turns[side][0], rest) + dot_tn(turns[side][1], high)

    raw = grad_ref[0]
    grad = raw.astype(FULL)
    turned = by_half(
        lambda side, value: dot_nn(turns[side][0], value) + dot_nn(turns[side][1], value), raw
    )
    first_new = beta_one * first_ref[...] + (1.0 - beta_one) * grad
    second_new = beta_two * second_ref[...] + (1.0 - beta_two) * (turned * turned)
    first_out[...] = first_new
    second_out[...] = second_new
    moment = by_half(turn, *parts(first_new))
    ratio = moment / corr_one / (jnp.sqrt(second_new / corr_two) + eps_adam)
    back = by_half(turn_back, *parts(ratio))
    weight = weight_ref[...]
    weight_out[...] = weight - rate_matrix * (back + decay * weight)

    for side in range(2):
        if side == 0:
            piece = grad[:, :upper]
            piece = jnp.where(iota(piece.shape, 1) < half, piece, 0.0)
        else:
            piece = grad[:, lower:]
            piece = jnp.where(iota(piece.shape, 1) >= half - lower, piece, 0.0)
        piece = piece.astype(LOW)
        gram = parts(jnp.where(same, dot_nt(piece, piece), 0.0))
        summed = beta_two * state_ref[0, 2 * step + side]
        summed = summed + (1.0 - beta_two) * gained * (
            dot_nn(pick_t, gram[0]) + dot_nn(pick_t, gram[1])
        )
        diagonal = jnp.sum(summed * pick_t.astype(FULL), axis=0, keepdims=True)
        stats = summed / by_ones(diagonal)
        state_out[0, 2 * step + side] = stats
        high, rest = parts(old[side])
        wide_high, wide_rest = parts(spread_out(stats))
        lifted = dot_nn(high, wide_high) + dot_nn(high, wide_rest) + dot_nn(rest, wide_high)
        for column in range(BLK):
            raised[column, pl.ds(2 * step + side, 1), :] = lifted[column : column + 1]

    @pl.when(step == pl.num_programs(0) - 1)
    def _():
        columns = []
        for index in range(BLK):
            column = raised[index]
            for previous in columns:
                column = column - by_ones(previous * column) * previous
            column = column * lax.rsqrt(by_ones(column * column))
            columns.append(column)
            for expert in range(EXPERTS):
                state_out[1, expert, index : index + 1, :] = column[expert : expert + 1]


def soap(weight, grad, first, second, state, every):
    height, total = weight.shape
    width = total // PAIRS
    turned_state = state.transpose(0, 1, 3, 2)
    gained = stat_gain * every / (total // EXPERTS)
    column = pl.BlockSpec((height, width), lambda i: (0, i))
    first_new, second_new, state_new, weight_new = device_kernel(
        functools.partial(soap_kernel, gained),
        "soap",
        PAIRS,
        [
            column, pl.BlockSpec((1, height, width), lambda i: (i, 0, 0)), column, column,
            whole(2, EXPERTS, BLK, height),
        ],
        [(weight.shape, FULL), (weight.shape, FULL), (turned_state.shape, FULL),
         (weight.shape, FULL)],
        [column, column, total_block(2, EXPERTS, BLK, height), column],
        [pltpu.VMEM((BLK, EXPERTS, height), FULL)],
        2 * height * height * total,
        weight.size * 26,
    )(weight, grad, first, second, turned_state)
    return (first_new, second_new, state_new.transpose(0, 1, 3, 2), weight_new)


def adam(weight, grad, first, second, rate):
    corr_one = 1.0 - beta_one**STEP
    corr_two = 1.0 - beta_two**STEP
    first_new = beta_one * first + (1.0 - beta_one) * grad
    second_new = beta_two * second + (1.0 - beta_two) * grad * grad
    weight_new = weight - rate * (
        first_new / corr_one / (jnp.sqrt(second_new / corr_two) + eps_adam) + decay * weight
    )
    return (first_new, second_new, weight_new)


def local(
    images,
    dom_label,
    class_label,
    expand_weight,
    expand_first,
    expand_second,
    expand_state,
    project_weight,
    project_first,
    project_second,
    project_state,
    head_weight,
    head_first,
    head_second,
    head_state,
    depth_weight,
    depth_first,
    depth_second,
    classifier_weight,
    classifier_first,
    classifier_second,
    excite_weight,
    excite_first,
    excite_second,
    router_weight,
    router_first,
    router_second,
    gains_weight,
    gains_first,
    gains_second,
):
    low_type = jnp.bfloat16
    images_here = images.shape[0]
    every = images.shape[0] * lax.axis_size("dp") * lax.axis_size("wide")
    count = every * PIX
    n_wide, n_dp = lax.axis_size("wide"), lax.axis_size("dp")
    bias_se, bias_ex, gain_one, shift_one, gain_two, shift_two, bias_cls = split_gains(gains_weight)
    hot = boost * (dom_label[:, None] == jnp.arange(EXPERTS)[None, :]).astype(jnp.float32)
    img = images.transpose(1, 0, 2)
    img_two = jnp.concatenate([img, img], axis=2)
    project_low = lax.all_gather(project_weight.astype(low_type), "wide", axis=0, tiled=True)
    head_low = lax.all_gather(head_weight.astype(low_type), "wide", axis=0, tiled=True)
    class_low = lax.all_gather(classifier_weight.astype(low_type), "wide", axis=0, tiled=True)
    taps = KSIZE * KSIZE
    depth_own = depth_weight.transpose(1, 0, 2).reshape(taps * EXPERTS, -1).astype(low_type)
    depth_own = jnp.pad(depth_own, ((0, -taps * EXPERTS % 16), (0, 0)))
    expand_low, depth_low = gather_expand(expand_weight, depth_own, 6)
    expand_low = from_pieces(expand_low, PAIRS)
    depth_full = depth_low[:, : taps * EXPERTS].reshape(n_wide, taps, EXPERTS, -1)
    depth_full = depth_full.transpose(1, 2, 0, 3).reshape(taps, EXPERTS, C_MID).astype(FULL)
    excite = excite_weight.transpose(0, 2, 1)
    router = router_weight.T
    router_one, router_two = router[:, :C_IN], router[:, C_IN:]

    (
        hidden, turned, scaled, route_one, pair_in, pair_one, gate, squeeze, pooled_one,
        pooled_act, route_one_sum,
    ) = expand_forward(
        img_two, hot, router_one, expand_low, depth_full, excite, bias_se[None], bias_ex[None]
    )
    each, before, norm_one, route_one_sum = project_forward(
        scaled, project_low, pair_one, route_one_sum, gain_one[None], shift_one[None], every, 1
    )
    widened, twice, route_two, pair_two, pooled_two, norm_two, route_two_sum = head_forward(
        before, norm_one, hot, router_two, head_low, gain_two[None], shift_two[None], every, 2
    )
    feats, grad_logits, grad_feats, coef_two, back_two, cross_total, grad_bias_cls = loss_part(
        widened, norm_two, class_label[:, None], class_low, bias_cls[None], every, 3
    )
    grad_class = jnp.stack(
        [dot_tn(feats, part).astype(low_type) for part in jnp.split(grad_logits, PAIRS, axis=1)]
    )
    grad_class, grad_feats = lax.optimization_barrier((grad_class, grad_feats))
    share_class = lax.psum_scatter(grad_class, "wide", scatter_dimension=1, tiled=True)
    means_one = route_one_sum[0] / every
    means_two = route_two_sum[0] / every
    grad_widened, grad_normed, grad_logit_two, back_one = head_back(
        widened, grad_feats, coef_two, head_low, pair_two, twice, before, norm_one, route_two,
        balance_grad(means_two, every)[None], router_two,
    )
    coef_one, back_one, grad_head = head_grad(
        back_one, norm_one, grad_widened, twice, pair_two, every, 4
    )
    coef_one, share_class = lax.optimization_barrier((coef_one, share_class))
    share_head = lax.psum_scatter(grad_head, "wide", scatter_dimension=1, tiled=True)
    grad_router_two = dot_tn(pooled_two, grad_logit_two, HIGH)
    grad_before, grad_scaled, route_project = project_back(
        grad_normed, before, coef_one, pair_one, each, project_low
    )
    row_scale = jnp.tile(route_one.astype(low_type).T, (1, PIX)).reshape(PAIRS, 2, -1)
    grad_project = project_grad(grad_before, scaled, row_scale, n_wide)
    grad_project, grad_scaled, share_head = lax.optimization_barrier(
        (grad_project, grad_scaled, share_head)
    )
    wide_head = share_head.shape[2]
    own_late, arrived = scatter_sum(
        to_pieces(jnp.concatenate([share_head, share_class], axis=2), n_dp)
    )
    share_project = lax.psum_scatter(grad_project, "wide", scatter_dimension=0, tiled=True)[0]
    grad_hidden, grad_logit_one, grad_gate, grad_squeeze, grad_depth = expand_back(
        grad_scaled, turned, hidden, img_two, gate, squeeze, excite, depth_full, route_one,
        route_project, balance_grad(means_one, every)[None], expand_low,
    )
    arrived, share_project, grad_hidden = lax.optimization_barrier(
        (arrived, share_project, grad_hidden)
    )
    sum_late = spread_sum(add_arrived(own_late, arrived))
    own_project, arrived = scatter_sum(to_pieces(share_project, n_dp))
    grad_expand = kern_grad(grad_hidden, img_two, pair_in, "expand_grad")
    grad_excite = jnp.stack(
        [
            dot_tn(grad_squeeze, pooled_act, HIGH),
            dot_tn(squeeze * jax.nn.sigmoid(squeeze), grad_gate, HIGH),
        ]
    )
    grad_router_one = dot_tn(pooled_one, grad_logit_one, HIGH)
    grad_depth = grad_depth.transpose(1, 0, 2)
    grad_bias_se = jnp.sum(grad_squeeze, axis=0)
    grad_bias_ex = jnp.sum(grad_gate, axis=0)
    sum_late, arrived, grad_expand = lax.optimization_barrier((sum_late, arrived, grad_expand))
    sum_late = from_pieces(sum_late, PAIRS)
    sum_head, sum_class = sum_late[:, :, :wide_head], sum_late[:, :, wide_head:]
    sum_project = from_pieces(spread_sum(add_arrived(own_project, arrived)), PAIRS)
    share_expand = lax.psum_scatter(grad_expand, "wide", scatter_dimension=1, tiled=True)
    parts = n_wide * n_dp
    depth_part = grad_depth.reshape(taps * EXPERTS, n_wide, -1).transpose(1, 0, 2)
    depth_part = depth_part.reshape(n_wide, n_dp, taps * EXPERTS // n_dp, -1).transpose(1, 0, 2, 3)
    rest = jnp.concatenate(
        [
            grad_excite.reshape(-1), grad_router_one.reshape(-1), grad_router_two.reshape(-1),
            grad_bias_se, grad_bias_ex,
        ]
    )
    rest_size = rest.size
    rest_rows = -(-rest_size // (parts * 16 * 128)) * 16
    rest = jnp.pad(rest.astype(low_type), (0, parts * rest_rows * 128 - rest_size))
    rest = rest.reshape(n_dp, n_wide, rest_rows, 128)
    head_out = soap(head_weight, sum_head, head_first, head_second, head_state, every)
    project_out = soap(
        project_weight, sum_project, project_first, project_second, project_state, every
    )
    sum_class = sum_class.transpose(1, 0, 2).reshape(-1, CLASS_PAD)[:, :CLASSES].astype(FULL)
    class_out = adam(
        classifier_weight, sum_class, classifier_first, classifier_second, rate_matrix
    )
    share_expand, head_out, project_out, class_out = lax.optimization_barrier(
        (share_expand, head_out, project_out, class_out)
    )
    (own_depth, _), (own_expand,), rest = reduce_grads(
        [depth_part.astype(low_type), rest], [to_pieces(share_expand, n_dp)], 5
    )
    sum_expand = from_pieces(own_expand, PAIRS)
    sum_depth = own_depth.reshape(EXPERTS, taps, -1).astype(FULL)
    rest = rest.transpose(1, 0, 2, 3).reshape(-1, 128)
    split = grad_excite.size // 128
    sum_excite = rest[:split].reshape(2, C_SE, C_MID).transpose(0, 2, 1).astype(FULL)
    rest = rest[split:].reshape(-1)[: rest_size - grad_excite.size].astype(FULL)
    sum_router = rest[: router_weight.size].reshape(router_weight.shape)
    sum_bias = rest[router_weight.size :]
    loss = cross_total[0, 0] / every + balance_weight * (
        jnp.mean((means_one - jnp.mean(means_one)) ** 2)
        + jnp.mean((means_two - jnp.mean(means_two)) ** 2)
    )
    grad_gains = jnp.concatenate(
        [sum_bias, back_one[1], back_one[0], back_two[1], back_two[0], grad_bias_cls[0]]
    )
    expand_out = soap(expand_weight, sum_expand, expand_first, expand_second, expand_state, every)
    depth_out = adam(
        depth_weight, sum_depth, depth_first, depth_second, rate_matrix
    )
    excite_out = adam(excite_weight, sum_excite, excite_first, excite_second, rate_matrix)
    router_out = adam(router_weight, sum_router, router_first, router_second, rate_matrix)
    gains_out = adam(gains_weight, grad_gains, gains_first, gains_second, rate_gains)
    return (
        loss,
        expand_out[0],
        expand_out[1],
        expand_out[2],
        expand_out[3],
        project_out[0],
        project_out[1],
        project_out[2],
        project_out[3],
        head_out[0],
        head_out[1],
        head_out[2],
        head_out[3],
        depth_out[0],
        depth_out[1],
        depth_out[2],
        class_out[0],
        class_out[1],
        class_out[2],
        excite_out[0],
        excite_out[1],
        excite_out[2],
        router_out[0],
        router_out[1],
        router_out[2],
        gains_out[0],
        gains_out[1],
        gains_out[2],
    )


def solution(mesh):
    return jax.shard_map(
        local,
        mesh=mesh,
        in_specs=(
            P(("dp", "wide"), None, None),
            P(("dp", "wide")),
            P(("dp", "wide")),
            P("wide", None),
            P("wide", None),
            P("wide", None),
            P(None, None, "wide", None),
            P("wide", None),
            P("wide", None),
            P("wide", None),
            P(None, None, "wide", None),
            P("wide", None),
            P("wide", None),
            P("wide", None),
            P(None, None, "wide", None),
            P(None, None, "wide"),
            P(None, None, "wide"),
            P(None, None, "wide"),
            P("wide", None),
            P("wide", None),
            P("wide", None),
            P(),
            P(),
            P(),
            P(),
            P(),
            P(),
            P(),
            P(),
            P(),
        ),
        out_specs=(
            P(),
            P("wide", None),
            P("wide", None),
            P(None, None, "wide", None),
            P("wide", None),
            P("wide", None),
            P("wide", None),
            P(None, None, "wide", None),
            P("wide", None),
            P("wide", None),
            P("wide", None),
            P(None, None, "wide", None),
            P("wide", None),
            P(None, None, "wide"),
            P(None, None, "wide"),
            P(None, None, "wide"),
            P("wide", None),
            P("wide", None),
            P("wide", None),
            P(),
            P(),
            P(),
            P(),
            P(),
            P(),
            P(),
            P(),
            P(),
        ),
        check_vma=False,
    )
```

```python
import functools

import jax
import jax.numpy as jnp
from jax import lax
from jax.experimental import pallas as pl
from jax.experimental.pallas import tpu as pltpu
from jax.sharding import PartitionSpec as P

SIDE = 7
PIX = 49
KSIZE = 3
EXPERTS = 8
BLK = 4
STEP = 10
C_IN = 192
C_MID = 1152
C_SE = 48
C_OUT = 320
C_HEAD = 1280
CLASSES = 1000


HIGH = lax.Precision.HIGHEST
beta_one = 0.9
beta_two = 0.95
eps_adam = 1e-08
eps_norm = 1e-05
decay = 0.01
rate_matrix = 0.08
rate_gains = 0.5
boost = 1.0
balance_weight = 4.0
stat_gain = 15000.0


def split_gains(gains):
    widths = [C_SE, C_MID, C_OUT, C_OUT, C_HEAD, C_HEAD, CLASSES]
    pieces = []
    start = 0
    for width in widths:
        pieces.append(gains[start : start + width])
        start = start + width
    return pieces


MESH = pl.DeviceIdType.MESH


def greet(n_wide, n_dp):
    me_wide, me_dp = lax.axis_index("wide"), lax.axis_index("dp")
    barrier = pltpu.get_barrier_semaphore()
    for k in range(1, n_wide):
        pl.semaphore_signal(
            barrier, inc=1, device_id={"wide": lax.rem(me_wide + k, n_wide)}, device_id_type=MESH
        )
    for k in range(1, n_dp):
        pl.semaphore_signal(
            barrier, inc=1, device_id={"dp": lax.rem(me_dp + k, n_dp)}, device_id_type=MESH
        )


def await_greetings(n_wide, n_dp):
    pl.semaphore_wait(pltpu.get_barrier_semaphore(), n_wide + n_dp - 2)


def sum_scratch(shapes, n_wide, n_dp):
    count = len(shapes)
    found = [pltpu.VMEM((n_wide,) + shape, jnp.float32) for shape in shapes]
    found += [pltpu.VMEM((n_dp,) + shape, jnp.float32) for shape in shapes]
    found += [pltpu.VMEM(shape, jnp.float32) for shape in shapes] * 2
    return found + [
        pltpu.SemaphoreType.DMA((size * count,)) for size in (n_wide, n_wide, n_dp, n_dp)
    ]


def sum_copies(axis, size, sources, slots, send, recv):
    me, count = lax.axis_index(axis), len(sources)
    return [
        pltpu.make_async_remote_copy(
            src_ref=sources[index],
            dst_ref=slots[index].at[me],
            send_sem=send.at[k * count + index],
            recv_sem=recv.at[k * count + index],
            device_id={axis: lax.rem(me + k, size)},
            device_id_type=MESH,
        )
        for k in range(1, size)
        for index in range(count)
    ]


def sum_slots(axis, size, sources, slots):
    me = lax.axis_index(axis)
    for source, slot in zip(sources, slots):
        slot[me] = source[...]
    found = []
    for slot in slots:
        total = slot[0]
        for k in range(1, size):
            total = total + slot[k]
        found.append(total)
    return found


def sum_open(n_wide, n_dp, values, scratch):
    count = len(values)
    wide_slots, own = scratch[:count], scratch[2 * count : 3 * count]
    for ref, value in zip(own, values):
        ref[...] = value
    for copy in sum_copies("wide", n_wide, own, wide_slots, *scratch[4 * count : 4 * count + 2]):
        copy.start()


def sum_middle(n_wide, n_dp, scratch):
    count = (len(scratch) - 4) // 4
    wide_slots, dp_slots, own, halves = (scratch[k * count : (k + 1) * count] for k in range(4))
    s_wide, r_wide, s_dp, r_dp = scratch[4 * count :]
    for copy in sum_copies("wide", n_wide, own, wide_slots, s_wide, r_wide):
        copy.wait()
    for half, total in zip(halves, sum_slots("wide", n_wide, own, wide_slots)):
        half[...] = total
    for copy in sum_copies("dp", n_dp, halves, dp_slots, s_dp, r_dp):
        copy.start()


def sum_end(n_wide, n_dp, scratch):
    count = (len(scratch) - 4) // 4
    dp_slots, halves = scratch[count : 2 * count], scratch[3 * count : 4 * count]
    for copy in sum_copies("dp", n_dp, halves, dp_slots, *scratch[4 * count + 2 :]):
        copy.wait()
    return sum_slots("dp", n_dp, halves, dp_slots)


def sum_close(n_wide, n_dp, scratch):
    sum_middle(n_wide, n_dp, scratch)
    return sum_end(n_wide, n_dp, scratch)


def norm_finish(count, every, totals, extras, outs):
    sums, route = totals
    center = sums[0:1] / count
    inv = lax.rsqrt(sums[1:2] / count - center * center + eps_norm)
    scale = inv * extras[0][...]
    outs[0][0:1] = scale
    outs[0][1:2] = extras[1][...] - center * scale
    outs[0][2:3] = inv
    outs[0][3:4] = -center * inv
    outs[0][4:8] = jnp.full((4, scale.shape[1]), 1.0 / every, jnp.float32)
    outs[1][...] = route


def back_finish(count, totals, extras, outs):
    sums = totals[0]
    norm = extras[0]
    scale, part = norm[0:1], norm[0:1] * sums[1:2] / count
    outs[0][0:2] = norm[0:2]
    outs[0][2:3] = -part * norm[2:3]
    outs[0][3:4] = -scale * sums[0:1] / count - part * norm[3:4]
    for out, total in zip(outs[1:], totals):
        out[...] = total


def balance_grad(means, every):
    return balance_weight * 2.0 * (means - jnp.mean(means)) / (EXPERTS * every)


GROUP = 16
PAIRS = EXPERTS // 2
ROWS = PIX * GROUP
CLASS_PAD = 1024
LOW = jnp.bfloat16
FULL = jnp.float32
VMEM_CAP = 60 * 1024 * 1024


def sig(value):
    return 0.5 + 0.5 * jnp.tanh(0.5 * value)


def silu_of(value):
    half = 0.5 * value
    return half * (1.0 + jnp.tanh(half))


def silu_pair(value):
    half = 0.5 * value
    bent = jnp.tanh(half)
    upper = 1.0 + bent
    return half * upper, upper * (1.0 + half * (1.0 - bent))


def sum_of(terms):
    while len(terms) > 1:
        terms = [
            terms[k] + terms[k + 1] if k + 1 < len(terms) else terms[k]
            for k in range(0, len(terms), 2)
        ]
    return terms[0]


def dot_nn(left, right, precision=None):
    return lax.dot_general(
        left, right, (((1,), (0,)), ((), ())), precision=precision, preferred_element_type=FULL
    )


def dot_nt(left, right, precision=None):
    return lax.dot_general(
        left, right, (((1,), (1,)), ((), ())), precision=precision, preferred_element_type=FULL
    )


def dot_tn(left, right, precision=None):
    return lax.dot_general(
        left, right, (((0,), (0,)), ((), ())), precision=precision, preferred_element_type=FULL
    )


def images_block(width):
    return pl.BlockSpec((PIX, GROUP, width), lambda i: (0, i, 0))


def group_block(width):
    return pl.BlockSpec((GROUP, width), lambda i: (i, 0))


def pair_block(width):
    return pl.BlockSpec((PAIRS, GROUP, width), lambda i: (0, i, 0))


def whole(*shape):
    return pl.BlockSpec(shape, lambda i: (0,) * len(shape), pipeline_mode=pl.Buffered(1))


def total_block(*shape):
    return pl.BlockSpec(shape, lambda i: (0,) * len(shape))


def device_kernel(
    kernel, name, grid, in_specs, outs, out_specs, scratch, flops, moved, ident=None
):
    return pl.pallas_call(
        kernel,
        name=name,
        grid=(grid,),
        in_specs=in_specs,
        out_shape=[jax.ShapeDtypeStruct(shape, dtype) for shape, dtype in outs],
        out_specs=out_specs,
        scratch_shapes=scratch,
        compiler_params=pltpu.CompilerParams(
            vmem_limit_bytes=VMEM_CAP, dimension_semantics=("arbitrary",), collective_id=ident,
            has_side_effects=ident is not None,
        ),
        cost_estimate=pl.CostEstimate(flops=flops, bytes_accessed=moved, transcendentals=0),
    )


def pair_scale(route, pair, width):
    lane = lax.broadcasted_iota(jnp.int32, (route.shape[0], 2 * width), 1)
    return jnp.where(
        lane < width, route[:, 2 * pair : 2 * pair + 1], route[:, 2 * pair + 1 : 2 * pair + 2]
    )


def pair_columns(sums, width):
    count = sums[0].shape[0]
    lane = lax.broadcasted_iota(jnp.int32, (count, 2 * width), 1)
    place = lax.broadcasted_iota(jnp.int32, (count, EXPERTS), 1)
    found = jnp.zeros((count, EXPERTS), FULL)
    for pair in range(PAIRS):
        first = jnp.sum(jnp.where(lane < width, sums[pair], 0.0), axis=1, keepdims=True)
        second = jnp.sum(jnp.where(lane < width, 0.0, sums[pair]), axis=1, keepdims=True)
        found = found + jnp.where(place == 2 * pair, first, 0.0)
        found = found + jnp.where(place == 2 * pair + 1, second, 0.0)
    return found


def taps_of(pixel):
    row, col = pixel // SIDE, pixel % SIDE
    found = []
    for tap in range(KSIZE * KSIZE):
        at_row, at_col = row + tap // KSIZE - 1, col + tap % KSIZE - 1
        if 0 <= at_row < SIDE and 0 <= at_col < SIDE:
            found.append((tap, at_row * SIDE + at_col))
    return found


def expand_kernel(
    img_ref, hot_ref, router_ref, source, depth_ref, excite_ref, bias_se_ref, bias_ex_ref,
    hidden_ref, turned_ref, scaled_ref, route_ref, pair_in_ref, pair_out_ref, gate_ref,
    squeeze_ref, pooled_one_ref, pooled_act_ref, route_sum_ref,
    routed, hidden_full, act_full, kern, expand_ref, sem,
):
    @pl.when(pl.program_id(0) == 0)
    def _():
        for copy in pair_copies(source, expand_ref, sem):
            copy.start()

    pooled = img_ref[0].astype(FULL)
    for pixel in range(1, PIX):
        pooled = pooled + img_ref[pixel].astype(FULL)
    pooled = pooled[:, :C_IN] * (1.0 / PIX)
    pooled_one_ref[...] = pooled
    route = sig(dot_nt(pooled, router_ref[...], HIGH) + hot_ref[...])
    route_ref[...] = route

    @pl.when(pl.program_id(0) == 0)
    def _():
        route_sum_ref[...] = jnp.zeros_like(route_sum_ref)

    route_sum_ref[...] += jnp.sum(route, axis=0, keepdims=True)
    low = route.astype(LOW).astype(FULL)
    for pair in range(PAIRS):
        scale = pair_scale(low, pair, C_IN).astype(LOW)
        pair_in_ref[pair] = scale
        pair_out_ref[pair] = pair_scale(low, pair, C_OUT).astype(LOW)
        place = slice(2 * pair * C_IN, 2 * (pair + 1) * C_IN)
        for pixel in range(PIX):
            routed[pixel, :, place] = img_ref[pixel] * scale
    columns = [low[:, expert : expert + 1] for expert in range(EXPERTS)]
    for tap in range(KSIZE * KSIZE):
        total = columns[0] * depth_ref[tap, 0:1, :]
        for expert in range(1, EXPERTS):
            total = total + columns[expert] * depth_ref[tap, expert : expert + 1, :]
        kern[tap] = total
    flat = routed[...].reshape(ROWS, EXPERTS * C_IN)
    third = C_MID // 3

    @pl.when(pl.program_id(0) == 0)
    def _():
        for copy in pair_copies(source, expand_ref, sem):
            copy.wait()

    def multiply(part):
        place = slice(part * third, (part + 1) * third)
        hidden_full[:, :, place] = dot_nt(flat, expand_ref[place]).reshape(PIX, GROUP, third)

    def chunk(index):
        lanes = slice(index * 128, index * 128 + 128)
        taps = [kern[tap, :, lanes].astype(LOW) for tap in range(KSIZE * KSIZE)]
        start = [None] * PIX

        def fill(row):
            for pixel in range(row * SIDE, row * SIDE + SIDE):
                value = hidden_full[pixel, :, lanes]
                hidden_ref[pixel, :, lanes] = value.astype(LOW)
                start[pixel] = silu_of(value).astype(LOW)

        fill(0)
        pooled_act = jnp.zeros((GROUP, 128), FULL)
        for row in range(SIDE):
            if row + 1 < SIDE:
                fill(row + 1)
            for pixel in range(row * SIDE, row * SIDE + SIDE):
                total = sum_of([start[source] * taps[tap] for tap, source in taps_of(pixel)])
                turned_ref[pixel, :, lanes] = total
                act = silu_of(total.astype(FULL))
                pooled_act = pooled_act + act
                act_full[pixel, :, lanes] = act
        pooled_act_ref[:, lanes] = pooled_act * (1.0 / PIX)

    multiply(0)
    for part in range(3):
        if part < 2:
            multiply(part + 1)
        for index in range(3 * part, 3 * part + 3):
            chunk(index)
    squeeze = dot_nt(pooled_act_ref[...], excite_ref[0], HIGH) + bias_se_ref[...]
    squeeze_ref[...] = squeeze
    gate = sig(dot_nn(squeeze * sig(squeeze), excite_ref[1], HIGH) + bias_ex_ref[...])
    gate_ref[...] = gate

    def finish(pixel, carry):
        scaled_ref[pixel] = (act_full[pixel] * gate).astype(LOW)
        return carry

    lax.fori_loop(0, PIX, finish, 0, unroll=7)


def expand_forward(img_two, hot, router, expand_low, depth_full, excite, bias_se, bias_ex):
    images = img_two.shape[1]
    return device_kernel(
        expand_kernel,
        "expand_forward",
        images // GROUP,
        [
            images_block(2 * C_IN), group_block(EXPERTS), whole(EXPERTS, C_IN),
            pl.BlockSpec(memory_space=pl.ANY), whole(KSIZE * KSIZE, EXPERTS, C_MID),
            whole(2, C_SE, C_MID), whole(1, C_SE), whole(1, C_MID),
        ],
        [
            ((PIX, images, C_MID), LOW), ((PIX, images, C_MID), LOW), ((PIX, images, C_MID), LOW),
            ((images, EXPERTS), FULL), ((PAIRS, images, 2 * C_IN), LOW),
            ((PAIRS, images, 2 * C_OUT), LOW), ((images, C_MID), FULL), ((images, C_SE), FULL),
            ((images, C_IN), FULL), ((images, C_MID), FULL), ((1, EXPERTS), FULL),
        ],
        [
            images_block(C_MID), images_block(C_MID), images_block(C_MID), group_block(EXPERTS),
            pair_block(2 * C_IN), pair_block(2 * C_OUT), group_block(C_MID), group_block(C_SE),
            group_block(C_IN), group_block(C_MID), total_block(1, EXPERTS),
        ],
        [
            pltpu.VMEM((PIX, GROUP, EXPERTS * C_IN), LOW), pltpu.VMEM((PIX, GROUP, C_MID), FULL),
            pltpu.VMEM((PIX, GROUP, C_MID), FULL), pltpu.VMEM((KSIZE * KSIZE, GROUP, C_MID), FULL),
            pltpu.VMEM((C_MID, EXPERTS * C_IN), LOW), pltpu.SemaphoreType.DMA((PAIRS,)),
        ],
        2 * PIX * images * EXPERTS * C_IN * C_MID,
        PIX * images * 4 * C_MID * 2,
    )(img_two, hot, router, expand_low, depth_full, excite, bias_se, bias_ex)


def stack_experts(source, stacked, sem):
    copies = [
        pltpu.make_async_copy(
            source.at[:, expert * C_MID : (expert + 1) * C_MID],
            stacked.at[expert * C_OUT : (expert + 1) * C_OUT],
            sem.at[expert],
        )
        for expert in range(EXPERTS)
    ]
    for copy in copies:
        copy.start()
    for copy in copies:
        copy.wait()


def pair_copies(source, stacked, sem):
    width = source.shape[2]
    return [
        pltpu.make_async_copy(
            source.at[pair], stacked.at[:, pair * width : (pair + 1) * width], sem.at[pair]
        )
        for pair in range(PAIRS)
    ]


def project_kernel(
    n_wide, n_dp, count, every,
    scaled_ref, source, pair_ref, route_ref, gain_ref, shift_ref,
    each_ref, before_ref, norm_ref, route_total_ref,
    weight_ref, sem, sums_ref, *small
):
    half = 2 * 2 * C_OUT
    flat = scaled_ref[...].reshape(ROWS, C_MID)

    @pl.when(pl.program_id(0) == 0)
    def _():
        greet(n_wide, n_dp)
        stack_experts(source, weight_ref, sem)
        sums_ref[...] = jnp.zeros_like(sums_ref)

    total = None
    for part in range(2):
        value = dot_nt(flat, weight_ref[part * half : (part + 1) * half])
        value = value.reshape(PIX, GROUP, half)
        each_ref[:, :, part * half : (part + 1) * half] = value.astype(LOW)
        for side in range(2):
            term = value[:, :, side * 2 * C_OUT : (side + 1) * 2 * C_OUT]
            term = term * pair_ref[2 * part + side].astype(FULL)[None]
            total = term if total is None else total + term
    total = total.reshape(ROWS, 2 * C_OUT)
    before = (total + pltpu.roll(total, C_OUT, 1))[:, :C_OUT]
    before_ref[...] = before.reshape(PIX, GROUP, C_OUT)
    sums_ref[0:1] += jnp.sum(before, axis=0, keepdims=True)
    sums_ref[1:2] += jnp.sum(before * before, axis=0, keepdims=True)

    @pl.when(pl.program_id(0) == pl.num_programs(0) - 1)
    def _():
        await_greetings(n_wide, n_dp)
        sum_open(n_wide, n_dp, [sums_ref[...], route_ref[...]], small)
        totals = sum_close(n_wide, n_dp, small)
        norm_finish(count, every, totals, (gain_ref, shift_ref), (norm_ref, route_total_ref))


def project_forward(scaled, project_low, pair_out, route_sum, gain, shift, every, ident):
    images = scaled.shape[1]
    wide = EXPERTS * C_OUT
    n_wide, n_dp = lax.axis_size("wide"), lax.axis_size("dp")
    return device_kernel(
        functools.partial(project_kernel, n_wide, n_dp, every * PIX, every),
        "project_forward",
        images // GROUP,
        [
            images_block(C_MID), pl.BlockSpec(memory_space=pl.ANY), pair_block(2 * C_OUT),
            whole(1, EXPERTS), whole(1, C_OUT), whole(1, C_OUT),
        ],
        [
            ((PIX, images, wide), LOW), ((PIX, images, C_OUT), FULL), ((8, C_OUT), FULL),
            ((1, EXPERTS), FULL),
        ],
        [
            images_block(wide), images_block(C_OUT), total_block(8, C_OUT),
            total_block(1, EXPERTS),
        ],
        [
            pltpu.VMEM((wide, C_MID), LOW), pltpu.SemaphoreType.DMA((EXPERTS,)),
            pltpu.VMEM((2, C_OUT), FULL),
        ]
        + sum_scratch([(2, C_OUT), (1, EXPERTS)], n_wide, n_dp),
        2 * PIX * images * wide * C_MID,
        PIX * images * (wide + C_MID) * 2,
        ident,
    )(scaled, project_low, pair_out, route_sum, gain, shift)


def head_kernel(
    n_wide, n_dp, count, every,
    before_ref, norm_ref, hot_ref, router_ref, weight_ref, gain_ref, shift_ref,
    widened_ref, twice_ref, route_ref, pair_ref, pooled_ref, new_norm_ref, route_total_ref,
    routed, padded, sums_ref, route_sum_ref, *small
):
    @pl.when(pl.program_id(0) == 0)
    def _():
        greet(n_wide, n_dp)
        sums_ref[...] = jnp.zeros_like(sums_ref)
        route_sum_ref[...] = jnp.zeros_like(route_sum_ref)
        padded[...] = jnp.zeros_like(padded)

    gain, shift = norm_ref[0:1], norm_ref[1:2]
    pooled = jnp.zeros((GROUP, C_OUT), FULL)
    for pixel in range(PIX):
        normed = (before_ref[pixel] * gain + shift).astype(LOW).astype(FULL)
        pooled = pooled + normed
        padded[:, :C_OUT] = normed
        value = padded[...]
        twice_ref[pixel] = (value + pltpu.roll(value, C_OUT, 1)).astype(LOW)
    pooled = pooled * (1.0 / PIX)
    pooled_ref[...] = pooled
    route = sig(dot_nt(pooled, router_ref[...], HIGH) + hot_ref[...])
    route_ref[...] = route
    route_sum_ref[...] += jnp.sum(route, axis=0, keepdims=True)
    low = route.astype(LOW).astype(FULL)
    for pair in range(PAIRS):
        scale = pair_scale(low, pair, C_OUT).astype(LOW)
        pair_ref[pair] = scale
        place = slice(2 * pair * C_OUT, 2 * (pair + 1) * C_OUT)
        for pixel in range(PIX):
            routed[pixel, :, place] = twice_ref[pixel] * scale
    product = dot_nt(routed[...].reshape(ROWS, EXPERTS * C_OUT), weight_ref[...])
    widened_ref[...] = product.reshape(PIX, GROUP, C_HEAD).astype(LOW)
    sums_ref[0:1] += jnp.sum(product, axis=0, keepdims=True)
    sums_ref[1:2] += jnp.sum(product * product, axis=0, keepdims=True)

    @pl.when(pl.program_id(0) == pl.num_programs(0) - 1)
    def _():
        await_greetings(n_wide, n_dp)
        sum_open(n_wide, n_dp, [sums_ref[...], route_sum_ref[...]], small)
        totals = sum_close(n_wide, n_dp, small)
        norm_finish(count, every, totals, (gain_ref, shift_ref), (new_norm_ref, route_total_ref))


def head_forward(before, norm, hot, router, head_low, gain, shift, every, ident):
    images = before.shape[1]
    wide = EXPERTS * C_OUT
    n_wide, n_dp = lax.axis_size("wide"), lax.axis_size("dp")
    return device_kernel(
        functools.partial(head_kernel, n_wide, n_dp, every * PIX, every),
        "head_forward",
        images // GROUP,
        [
            images_block(C_OUT), whole(8, C_OUT), group_block(EXPERTS), whole(EXPERTS, C_OUT),
            whole(C_HEAD, wide), whole(1, C_HEAD), whole(1, C_HEAD),
        ],
        [
            ((PIX, images, C_HEAD), LOW), ((PIX, images, 2 * C_OUT), LOW),
            ((images, EXPERTS), FULL), ((PAIRS, images, 2 * C_OUT), LOW), ((images, C_OUT), FULL),
            ((8, C_HEAD), FULL), ((1, EXPERTS), FULL),
        ],
        [
            images_block(C_HEAD), images_block(2 * C_OUT), group_block(EXPERTS),
            pair_block(2 * C_OUT), group_block(C_OUT), total_block(8, C_HEAD),
            total_block(1, EXPERTS),
        ],
        [
            pltpu.VMEM((PIX, GROUP, wide), LOW), pltpu.VMEM((GROUP, 2 * C_OUT), FULL),
            pltpu.VMEM((2, C_HEAD), FULL), pltpu.VMEM((1, EXPERTS), FULL),
        ]
        + sum_scratch([(2, C_HEAD), (1, EXPERTS)], n_wide, n_dp),
        2 * PIX * images * wide * C_HEAD,
        PIX * images * (C_HEAD + C_OUT) * 2,
        ident,
    )(before, norm, hot, router, head_low, gain, shift)


def loss_kernel(
    n_wide, n_dp, count,
    widened_ref, norm_ref, label_ref, class_ref, bias_ref,
    feats_ref, logits_ref, grad_feats_ref, coef_ref, sums_ref, cross_ref, bias_grad_ref,
    silu_sum, slope_sum, cross_sum, *small
):
    step = pl.program_id(0)

    @pl.when(step == 0)
    def _():
        greet(n_wide, n_dp)

    rows = pl.ds(pl.multiple_of(step * GROUP, GROUP), GROUP)

    def chunk(index, carry):
        lanes = pl.ds(pl.multiple_of(index * 128, 128), 128)
        gain, shift, inv, offset = (norm_ref[k : k + 1, lanes] for k in range(4))
        total = slope = moved = jnp.zeros((GROUP, 128), FULL)
        for pixel in range(PIX):
            value = widened_ref[pixel, :, lanes].astype(FULL)
            lifted = value * gain + shift
            part = sig(lifted)
            grown = lifted * part
            bent = part + grown * (1.0 - part)
            total = total + grown
            slope = slope + bent
            moved = moved + bent * (value * inv + offset)
        silu_sum[rows, lanes] = total
        slope_sum[rows, lanes] = slope
        cross_sum[rows, lanes] = moved
        return carry

    lax.fori_loop(0, C_HEAD // 128, chunk, 0)

    @pl.when(step == pl.num_programs(0) - 1)
    def _():
        feats = (silu_sum[...] * (1.0 / PIX)).astype(LOW)
        feats_ref[...] = feats
        logits = dot_nn(feats, class_ref[...]) + bias_ref[...]
        lane = lax.broadcasted_iota(jnp.int32, logits.shape, 1)
        picked = lane == label_ref[...]
        top = jnp.max(logits, axis=1, keepdims=True)
        powers = jnp.exp(logits - top)
        totals = jnp.sum(powers, axis=1, keepdims=True)
        cross = top + jnp.log(totals) - jnp.sum(
            jnp.where(picked, logits, 0.0), axis=1, keepdims=True
        )
        cross = jnp.sum(cross, axis=0, keepdims=True)
        grad = (powers / totals - jnp.where(picked, 1.0, 0.0)) * norm_ref[4:5, 0:1]
        grad = grad.astype(LOW)
        logits_ref[...] = jnp.zeros_like(logits_ref)
        logits_ref[:, :CLASSES] = grad
        bias_grad = jnp.sum(grad.astype(FULL), axis=0, keepdims=True)
        grad_feats = dot_nt(grad, class_ref[...]) * (1.0 / PIX)
        grad_feats_ref[...] = grad_feats
        sums_ref[0:1] = jnp.sum(grad_feats * slope_sum[...], axis=0, keepdims=True)
        sums_ref[1:2] = jnp.sum(grad_feats * cross_sum[...], axis=0, keepdims=True)
        await_greetings(n_wide, n_dp)
        sum_open(n_wide, n_dp, [sums_ref[...], cross, bias_grad], small)
        totals = sum_close(n_wide, n_dp, small)
        back_finish(count, totals, (norm_ref,), (coef_ref, sums_ref, cross_ref, bias_grad_ref))


def loss_part(widened, norm, label, class_low, bias, every, ident):
    images = widened.shape[1]
    n_wide, n_dp = lax.axis_size("wide"), lax.axis_size("dp")
    return device_kernel(
        functools.partial(loss_kernel, n_wide, n_dp, every * PIX),
        "loss_part",
        images // GROUP,
        [
            images_block(C_HEAD), whole(8, C_HEAD), whole(images, 1), whole(C_HEAD, CLASSES),
            whole(1, CLASSES),
        ],
        [
            ((images, C_HEAD), LOW), ((images, CLASS_PAD), LOW), ((images, C_HEAD), FULL),
            ((4, C_HEAD), FULL), ((2, C_HEAD), FULL), ((1, 1), FULL), ((1, CLASSES), FULL),
        ],
        [
            total_block(images, C_HEAD), total_block(images, CLASS_PAD), total_block(images, C_HEAD),
            total_block(4, C_HEAD), total_block(2, C_HEAD), total_block(1, 1),
            total_block(1, CLASSES),
        ],
        [pltpu.VMEM((images, C_HEAD), FULL)] * 3
        + sum_scratch([(2, C_HEAD), (1, 1), (1, CLASSES)], n_wide, n_dp),
        4 * images * C_HEAD * CLASSES,
        PIX * images * C_HEAD * 2,
        ident,
    )(widened, norm, label, class_low, bias)


def head_back_kernel(
    widened_ref, grad_feats_ref, coef_ref, weight_ref, pair_ref, twice_ref, before_ref, norm_ref,
    route_ref, balance_ref, router_ref,
    grad_wide_ref, grad_normed_ref, logit_ref, sums_ref,
    product, mixed,
):
    half = 2 * 2 * C_OUT

    @pl.when(pl.program_id(0) == 0)
    def _():
        sums_ref[...] = jnp.zeros_like(sums_ref)

    gain, shift, by_value, constant = (coef_ref[k : k + 1] for k in range(4))
    grad_feats = grad_feats_ref[...] * (0.5 * gain)

    def widen(pixel, carry):
        value = widened_ref[pixel].astype(FULL)
        _, bent = silu_pair(value * gain + shift)
        grad = grad_feats * bent + value * by_value + constant
        grad_wide_ref[pixel] = grad.astype(LOW)
        return carry

    lax.fori_loop(0, PIX, widen, 0, unroll=7)
    flat = grad_wide_ref[...].reshape(ROWS, C_HEAD)
    twice = twice_ref[...].astype(FULL)
    route_sums = []
    total = None
    for part in range(2):
        value = dot_nn(flat, weight_ref[:, part * half : (part + 1) * half])
        value = value.reshape(PIX, GROUP, half)
        for side in range(2):
            piece = value[:, :, side * 2 * C_OUT : (side + 1) * 2 * C_OUT]
            route_sums.append(jnp.sum(piece * twice, axis=0))
            term = piece * pair_ref[2 * part + side].astype(FULL)[None]
            total = term if total is None else total + term
    total = total.reshape(ROWS, 2 * C_OUT)
    mixed[...] = (total + pltpu.roll(total, C_OUT, 1))[:, :C_OUT].reshape(PIX, GROUP, C_OUT)
    route = route_ref[...]
    grad_route = pair_columns(route_sums, C_OUT) + balance_ref[...]
    logit = grad_route * route * (1.0 - route)
    logit_ref[...] = logit
    added = dot_nn(logit, router_ref[...], HIGH) * (1.0 / PIX)

    def close(pixel, carry):
        plain, cross = carry
        grad = mixed[pixel] + added
        grad_normed_ref[pixel] = grad
        hat = before_ref[pixel] * norm_ref[2:3] + norm_ref[3:4]
        return plain + grad, cross + grad * hat

    zero = jnp.zeros((GROUP, C_OUT), FULL)
    plain, cross = lax.fori_loop(0, PIX, close, (zero, zero), unroll=7)
    sums_ref[0:1] += jnp.sum(plain, axis=0, keepdims=True)
    sums_ref[1:2] += jnp.sum(cross, axis=0, keepdims=True)


def head_back(
    widened, grad_feats, coef, head_low, pair_two, twice, before, norm, route, balance, router_t
):
    images = widened.shape[1]
    wide = EXPERTS * C_OUT
    return device_kernel(
        head_back_kernel,
        "head_back",
        images // GROUP,
        [
            images_block(C_HEAD), group_block(C_HEAD), whole(4, C_HEAD), whole(C_HEAD, wide),
            pair_block(2 * C_OUT), images_block(2 * C_OUT), images_block(C_OUT), whole(8, C_OUT),
            group_block(EXPERTS), whole(1, EXPERTS), whole(EXPERTS, C_OUT),
        ],
        [
            ((PIX, images, C_HEAD), LOW), ((PIX, images, C_OUT), FULL), ((images, EXPERTS), FULL),
            ((2, C_OUT), FULL),
        ],
        [
            images_block(C_HEAD), images_block(C_OUT), group_block(EXPERTS), total_block(2, C_OUT),
        ],
        [pltpu.VMEM((2, PIX, GROUP, wide // 2), FULL), pltpu.VMEM((PIX, GROUP, C_OUT), FULL)],
        2 * PIX * images * wide * C_HEAD,
        PIX * images * (2 * C_HEAD + C_OUT) * 2,
    )(widened, grad_feats, coef, head_low, pair_two, twice, before, norm, route, balance, router_t)


def kern_grad_kernel(grad_ref, twice_ref, pair_ref, out_ref, turned, routed, between=None):
    images, width = twice_ref.shape[1:]

    @pl.when(pl.program_id(0) == 0)
    def _():
        turned[...] = grad_ref[...].reshape(turned.shape[1], turned.shape[0]).T

    for side in range(2):
        scale = pair_ref[side]
        for pixel in range(PIX):
            routed[pixel * images : (pixel + 1) * images, side * width : (side + 1) * width] = (
                twice_ref[pixel] * scale
            )
    if between is not None:
        between()
    product = dot_nn(turned[...], routed[...])
    for side in range(2):
        out_ref[side] = product[:, side * width : (side + 1) * width].astype(LOW)


def kern_grad(grad, twice, pair_scales, name):
    images, out_width, width = grad.shape[1], grad.shape[2], twice.shape[2]
    rows = PIX * images
    return device_kernel(
        kern_grad_kernel,
        name,
        PAIRS // 2,
        [
            whole(PIX, images, out_width), whole(PIX, images, width),
            pl.BlockSpec((2, images, width), lambda i: (i, 0, 0)),
        ],
        [((PAIRS, out_width, width), LOW)],
        [pl.BlockSpec((2, out_width, width), lambda i: (i, 0, 0))],
        [pltpu.VMEM((out_width, rows), LOW), pltpu.VMEM((rows, 2 * width), LOW)],
        2 * rows * out_width * PAIRS * width,
        rows * out_width * 2,
    )(grad, twice, pair_scales)[0]


def head_grad_kernel(
    n_wide, n_dp, count, sums_ref, norm_ref, grad_ref, twice_ref, pair_ref,
    coef_ref, total_ref, out_ref, turned, routed, *small
):
    step = pl.program_id(0)

    @pl.when(step == 0)
    def _():
        greet(n_wide, n_dp)

    def between():
        @pl.when(step == 0)
        def _():
            await_greetings(n_wide, n_dp)
            sum_open(n_wide, n_dp, [sums_ref[...]], small)

    kern_grad_kernel(grad_ref, twice_ref, pair_ref, out_ref, turned, routed, between)

    @pl.when(step == 0)
    def _():
        sum_middle(n_wide, n_dp, small)

    @pl.when(step == pl.num_programs(0) - 1)
    def _():
        totals = sum_end(n_wide, n_dp, small)
        back_finish(count, totals, (norm_ref,), (coef_ref, total_ref))


def head_grad(sums, norm, grad, twice, pair_scales, every, ident):
    images, out_width, width = grad.shape[1], grad.shape[2], twice.shape[2]
    rows = PIX * images
    n_wide, n_dp = lax.axis_size("wide"), lax.axis_size("dp")
    return device_kernel(
        functools.partial(head_grad_kernel, n_wide, n_dp, every * PIX),
        "head_grad",
        PAIRS // 2,
        [
            whole(2, C_OUT), whole(8, C_OUT), whole(PIX, images, out_width),
            whole(PIX, images, width), pl.BlockSpec((2, images, width), lambda i: (i, 0, 0)),
        ],
        [((4, C_OUT), FULL), ((2, C_OUT), FULL), ((PAIRS, out_width, width), LOW)],
        [
            total_block(4, C_OUT), total_block(2, C_OUT),
            pl.BlockSpec((2, out_width, width), lambda i: (i, 0, 0)),
        ],
        [pltpu.VMEM((out_width, rows), LOW), pltpu.VMEM((rows, 2 * width), LOW)]
        + sum_scratch([(2, C_OUT)], n_wide, n_dp),
        2 * rows * out_width * PAIRS * width,
        rows * out_width * 2,
        ident,
    )(sums, norm, grad, twice, pair_scales)


def project_grad_kernel(grad_ref, scaled_ref, scale_ref, out_ref, turned, routed):
    rows = turned.shape[1]

    @pl.when(pl.program_id(0) == 0)
    def _():
        turned[...] = grad_ref[...].reshape(rows, C_OUT).T

    for side in range(2):
        routed[side * C_OUT : (side + 1) * C_OUT] = turned[...] * scale_ref[0, side : side + 1]
    product = dot_nn(routed[...], scaled_ref[...].reshape(rows, C_MID))
    owners, _, height, _ = out_ref.shape
    for side in range(2):
        for owner in range(owners):
            place = side * C_OUT + owner * height
            out_ref[owner, 0, :, side * C_MID : (side + 1) * C_MID] = product[
                place : place + height
            ].astype(LOW)


def project_grad(grad, scaled, scale, owners):
    images = grad.shape[1]
    rows = PIX * images
    return device_kernel(
        project_grad_kernel,
        "project_grad",
        PAIRS,
        [
            whole(PIX, images, C_OUT), whole(PIX, images, C_MID),
            pl.BlockSpec((1, 2, rows), lambda i: (i, 0, 0)),
        ],
        [((owners, PAIRS, C_OUT // owners, 2 * C_MID), LOW)],
        [pl.BlockSpec((owners, 1, C_OUT // owners, 2 * C_MID), lambda i: (0, i, 0, 0))],
        [pltpu.VMEM((C_OUT, rows), LOW), pltpu.VMEM((2 * C_OUT, rows), LOW)],
        2 * rows * EXPERTS * C_OUT * C_MID,
        rows * (C_OUT + C_MID) * 2,
    )(grad, scaled, scale)[0]


def project_back_kernel(
    grad_ref, before_ref, coef_ref, pair_ref, each_ref, source,
    grad_before_ref, grad_scaled_ref, route_ref,
    routed, padded, twice, weight_ref, sem,
):
    @pl.when(pl.program_id(0) == 0)
    def _():
        stack_experts(source, weight_ref, sem)
        padded[...] = jnp.zeros_like(padded)

    gain, _, by_value, constant = (coef_ref[k : k + 1] for k in range(4))
    scales = [pair_ref[pair] for pair in range(PAIRS)]

    def turn(pixel, carry):
        grad = grad_ref[pixel] * gain + before_ref[pixel] * by_value + constant
        grad = grad.astype(LOW)
        grad_before_ref[pixel] = grad
        padded[:, :C_OUT] = grad.astype(FULL)
        value = padded[...]
        value = (value + pltpu.roll(value, C_OUT, 1)).astype(LOW)
        twice[pixel] = value
        for pair in range(PAIRS):
            place = slice(2 * pair * C_OUT, 2 * (pair + 1) * C_OUT)
            routed[pixel, :, place] = value * scales[pair]
        return carry

    lax.fori_loop(0, PIX, turn, 0, unroll=7)
    product = dot_nn(routed[...].reshape(ROWS, EXPERTS * C_OUT), weight_ref[...])
    grad_scaled_ref[...] = product.reshape(PIX, GROUP, C_MID).astype(LOW)
    route_sums = []
    for pair in range(PAIRS):
        place = slice(2 * pair * C_OUT, 2 * (pair + 1) * C_OUT)
        term = each_ref[:, :, place].astype(FULL) * twice[...].astype(FULL)
        route_sums.append(jnp.sum(term, axis=0))
    route_ref[...] = pair_columns(route_sums, C_OUT)


def project_back(grad_normed, before, coef, pair_out, each, project_low):
    images = before.shape[1]
    wide = EXPERTS * C_OUT
    return device_kernel(
        project_back_kernel,
        "project_back",
        images // GROUP,
        [
            images_block(C_OUT), images_block(C_OUT), whole(4, C_OUT), pair_block(2 * C_OUT),
            images_block(wide), pl.BlockSpec(memory_space=pl.ANY),
        ],
        [
            ((PIX, images, C_OUT), LOW), ((PIX, images, C_MID), LOW), ((images, EXPERTS), FULL),
        ],
        [images_block(C_OUT), images_block(C_MID), group_block(EXPERTS)],
        [
            pltpu.VMEM((PIX, GROUP, wide), LOW), pltpu.VMEM((GROUP, 2 * C_OUT), FULL),
            pltpu.VMEM((PIX, GROUP, 2 * C_OUT), LOW),
            pltpu.VMEM((wide, C_MID), LOW), pltpu.SemaphoreType.DMA((EXPERTS,)),
        ],
        2 * PIX * images * wide * C_MID,
        PIX * images * (C_MID + wide) * 2,

    )(grad_normed, before, coef, pair_out, each, project_low)


def expand_back_kernel(
    grad_scaled_ref, turned_ref, hidden_ref, img_ref, gate_ref, squeeze_ref, excite_ref, depth_ref,
    route_ref, route_part_ref, balance_ref, source,
    grad_hidden_ref, logit_ref, grad_gate_ref, grad_squeeze_ref, grad_depth_ref,
    kern, start, slope, grad_turned, grad_kern, pooled, product, weight_ref, sem,
):
    @pl.when(pl.program_id(0) == 0)
    def _():
        for copy in pair_copies(source, weight_ref, sem):
            copy.start()
        grad_depth_ref[...] = jnp.zeros_like(grad_depth_ref)

    route = route_ref[...]
    low = route.astype(LOW).astype(FULL)
    columns = [low[:, expert : expert + 1] for expert in range(EXPERTS)]
    for tap in range(KSIZE * KSIZE):
        total = columns[0] * depth_ref[tap, 0:1, :]
        for expert in range(1, EXPERTS):
            total = total + columns[expert] * depth_ref[tap, expert : expert + 1, :]
        kern[tap] = total

    def gate_sum(pixel, carry):
        value = turned_ref[pixel].astype(FULL)
        return carry + grad_scaled_ref[pixel].astype(FULL) * silu_of(value)

    gate = gate_ref[...]
    grad_gate = lax.fori_loop(0, PIX, gate_sum, jnp.zeros((GROUP, C_MID), FULL), unroll=7)
    grad_gate = grad_gate * gate * (1.0 - gate)
    grad_gate_ref[...] = grad_gate
    squeeze = squeeze_ref[...]
    part = sig(squeeze)
    grad_squeeze = dot_nt(grad_gate, excite_ref[1], HIGH) * (part + squeeze * part * (1.0 - part))
    grad_squeeze_ref[...] = grad_squeeze
    pooled[...] = dot_nn(grad_squeeze, excite_ref[0], HIGH) * (1.0 / PIX)

    third = C_MID // 3

    @pl.when(pl.program_id(0) == 0)
    def _():
        for copy in pair_copies(source, weight_ref, sem):
            copy.wait()

    def chunk(index):
        lanes = slice(index * 128, index * 128 + 128)
        side = index % 2
        gate_part = 0.5 * gate_ref[:, lanes]
        pooled_part = 0.5 * pooled[:, lanes]
        for pixel in range(PIX):
            _, bent = silu_pair(turned_ref[pixel, :, lanes].astype(FULL))
            grad = grad_scaled_ref[pixel, :, lanes].astype(FULL) * gate_part + pooled_part
            grad_turned[side, pixel] = grad * bent
            value, bent = silu_pair(hidden_ref[pixel, :, lanes].astype(FULL))
            start[side, pixel] = value
            slope[side, pixel] = bent
        taps = [0.5 * kern[tap, :, lanes] for tap in range(KSIZE * KSIZE)]
        sums = [None] * (KSIZE * KSIZE)
        for pixel in range(PIX):
            here = grad_turned[side, pixel]
            terms = []
            for tap, source in taps_of(pixel):
                term = start[side, source] * here
                sums[tap] = term if sums[tap] is None else sums[tap] + term
                terms.append(grad_turned[side, source] * taps[KSIZE * KSIZE - 1 - tap])
            grad_hidden_ref[pixel, :, lanes] = (sum_of(terms) * slope[side, pixel]).astype(LOW)
        for tap in range(KSIZE * KSIZE):
            grad_kern[tap, :, lanes] = sums[tap]

    for part in range(3):
        for index in range(3 * part, 3 * part + 3):
            chunk(index)
        inner = slice(part * third, (part + 1) * third)
        term = dot_nn(grad_hidden_ref[:, :, inner].reshape(ROWS, third), weight_ref[inner])
        term = term.reshape(PIX, GROUP, EXPERTS * C_IN)
        product[...] = term if part == 0 else product[...] + term
    place = lax.broadcasted_iota(jnp.int32, (GROUP, EXPERTS), 1)
    depth_term = jnp.zeros((GROUP, EXPERTS), FULL)
    for expert in range(EXPERTS):
        total = jnp.zeros((GROUP, C_MID), FULL)
        for tap in range(KSIZE * KSIZE):
            value = grad_kern[tap]
            total = total + value * depth_ref[tap, expert : expert + 1, :]
            weighed = value * columns[expert]
            grad_depth_ref[tap, expert : expert + 1, :] += jnp.sum(weighed, axis=0, keepdims=True)
        total = jnp.sum(total, axis=1, keepdims=True)
        depth_term = depth_term + jnp.where(place == expert, total, 0.0)
    def route_part(pixel, carry):
        value = img_ref[pixel].astype(FULL)
        return tuple(
            carry[pair] + product[pixel, :, 2 * pair * C_IN : 2 * (pair + 1) * C_IN] * value
            for pair in range(PAIRS)
        )

    zero = jnp.zeros((GROUP, 2 * C_IN), FULL)
    route_sums = lax.fori_loop(0, PIX, route_part, (zero,) * PAIRS, unroll=7)
    grad_route = (
        pair_columns(route_sums, C_IN) + route_part_ref[...] + depth_term + balance_ref[...]
    )
    logit_ref[...] = grad_route * route * (1.0 - route)


def expand_back(
    grad_scaled, turned, hidden, img_two, gate, squeeze, excite, depth_full, route, route_part,
    balance, expand_low,
):
    images = hidden.shape[1]
    taps = KSIZE * KSIZE
    return device_kernel(
        expand_back_kernel,
        "expand_back",
        images // GROUP,
        [
            images_block(C_MID), images_block(C_MID), images_block(C_MID), images_block(2 * C_IN),
            group_block(C_MID), group_block(C_SE), whole(2, C_SE, C_MID),
            whole(taps, EXPERTS, C_MID), group_block(EXPERTS), group_block(EXPERTS),
            whole(1, EXPERTS), pl.BlockSpec(memory_space=pl.ANY),
        ],
        [
            ((PIX, images, C_MID), LOW), ((images, EXPERTS), FULL), ((images, C_MID), FULL),
            ((images, C_SE), FULL), ((taps, EXPERTS, C_MID), FULL),
        ],
        [
            images_block(C_MID), group_block(EXPERTS), group_block(C_MID), group_block(C_SE),
            total_block(taps, EXPERTS, C_MID),
        ],
        [
            pltpu.VMEM((taps, GROUP, C_MID), FULL), pltpu.VMEM((2, PIX, GROUP, 128), FULL),
            pltpu.VMEM((2, PIX, GROUP, 128), FULL), pltpu.VMEM((2, PIX, GROUP, 128), FULL), pltpu.VMEM((taps, GROUP, C_MID), FULL),
            pltpu.VMEM((GROUP, C_MID), FULL), pltpu.VMEM((PIX, GROUP, EXPERTS * C_IN), FULL),
            pltpu.VMEM((C_MID, EXPERTS * C_IN), LOW), pltpu.SemaphoreType.DMA((PAIRS,)),
        ],
        2 * PIX * images * EXPERTS * C_IN * C_MID,
        PIX * images * 4 * C_MID * 2,
    )(
        grad_scaled, turned, hidden, img_two, gate, squeeze, excite, depth_full, route, route_part,
        balance, expand_low,
    )


def reduce_kernel(n_wide, n_dp, n_full, n_share, *refs):
    n_in = n_full + n_share
    fulls, shares = refs[:n_full], refs[n_full:n_in]
    full_outs, share_outs, spread_out = refs[n_in : n_in + n_full], refs[n_in + n_full : 2 * n_in], refs[2 * n_in]
    scratch = list(refs[2 * n_in + 1 :])
    firsts, seconds, thirds, halves, lineds = (
        [scratch.pop(0) for _ in range(n_full)] for _ in range(5)
    )
    slots = [scratch.pop(0) for _ in range(n_share)]
    send, recv = scratch
    lines = n_wide // 2
    me_wide, me_dp = lax.axis_index("wide"), lax.axis_index("dp")
    core, line = lax.rem(me_wide, 2), lax.div(me_wide, 2)
    sibling = line * 2 + 1 - core
    used = [0]

    barrier = pltpu.get_barrier_semaphore()
    for k in range(1, n_wide):
        pl.semaphore_signal(
            barrier, inc=1, device_id={"wide": lax.rem(me_wide + k, n_wide)}, device_id_type=MESH
        )
    for k in range(1, n_dp):
        pl.semaphore_signal(
            barrier, inc=1, device_id={"dp": lax.rem(me_dp + k, n_dp)}, device_id_type=MESH
        )
    pl.semaphore_wait(barrier, n_wide + n_dp - 2)

    def launch(src, dst, device):
        copy = pltpu.make_async_remote_copy(
            src_ref=src, dst_ref=dst, send_sem=send.at[used[0]], recv_sem=recv.at[used[0]],
            device_id=device, device_id_type=MESH,
        )
        used[0] += 1
        copy.start()
        return copy

    def finish(copies):
        for copy in copies:
            copy.wait()

    def dp_peer(k):
        return lax.rem(me_dp + k, n_dp)

    to_sibling = [
        launch(full.at[:, :, 1 - core], first, {"wide": sibling})
        for full, first in zip(fulls, firsts)
    ]
    scattered = [
        launch(share.at[dp_peer(k)], slot.at[k - 1], {"dp": dp_peer(k)})
        for k in range(1, n_dp)
        for share, slot in zip(shares, slots)
    ]
    finish(to_sibling)
    for full, first, half in zip(fulls, firsts, halves):
        def pair_sum(index, carry, full=full, first=first, half=half):
            at_dp, at_line = lax.div(index, lines), lax.rem(index, lines)
            total = full[at_dp, at_line, core].astype(FULL) + first[at_dp, at_line].astype(FULL)
            half[at_dp, at_line] = total.astype(LOW)
            return carry

        lax.fori_loop(0, n_dp * lines, pair_sum, 0)
    across = [
        launch(half.at[dp_peer(k)], second.at[k - 1], {"dp": dp_peer(k)})
        for k in range(1, n_dp)
        for half, second in zip(halves, seconds)
    ]
    finish(scattered)
    for share, slot, out in zip(shares, slots, share_outs):
        total = share[me_dp].astype(FULL)
        for k in range(1, n_dp):
            total = total + slot[k - 1].astype(FULL)
        out[me_dp] = total.astype(LOW)
    finish(across)
    for half, second, lined in zip(halves, seconds, lineds):
        def dp_sum(at_line, carry, half=half, second=second, lined=lined):
            total = half[me_dp, at_line].astype(FULL)
            for k in range(1, n_dp):
                total = total + second[k - 1, at_line].astype(FULL)
            lined[at_line] = total.astype(LOW)
            return carry

        lax.fori_loop(0, lines, dp_sum, 0)
    along = []
    for k in range(1, lines):
        other = lax.rem(line + k, lines)
        for lined, third in zip(lineds, thirds):
            along.append(launch(lined.at[other], third.at[k - 1], {"wide": other * 2 + core}))
    gathered = [
        launch(out.at[me_dp], out.at[me_dp], {"dp": dp_peer(k)})
        for k in range(1, n_dp)
        for out in share_outs
    ]
    finish(along)
    for lined, third, out in zip(lineds, thirds, full_outs):
        total = lined[line].astype(FULL)
        for k in range(1, lines):
            total = total + third[k - 1].astype(FULL)
        out[me_dp] = total.astype(LOW)
    last = [
        launch(out.at[me_dp], out.at[me_dp], {"dp": dp_peer(k)})
        for out in reversed(full_outs)
        for k in range(1, n_dp)
    ]
    own = full_outs[-1]
    finish(last[: n_dp - 1])
    spread_out[me_wide] = own[...]
    everywhere = [
        launch(own, spread_out.at[me_wide], {"wide": lax.rem(me_wide + k, n_wide)})
        for k in range(1, n_wide)
    ]
    finish(last[n_dp - 1 :] + gathered + everywhere)


def reduce_grads(fulls, shares, ident):
    n_wide, n_dp = lax.axis_size("wide"), lax.axis_size("dp")
    lines = n_wide // 2
    views = [full.reshape((n_dp, lines, 2) + full.shape[2:]) for full in fulls]
    tails = [full.shape[2:] for full in fulls]
    copies = (
        len(fulls) * (1 + (n_dp - 1) * 2 + lines - 1) + len(shares) * 2 * (n_dp - 1) + n_wide - 1
    )
    vmem = pl.BlockSpec(memory_space=pltpu.VMEM)
    outs = [jax.ShapeDtypeStruct((n_dp,) + tail, LOW) for tail in tails]
    outs += [jax.ShapeDtypeStruct(share.shape, LOW) for share in shares]
    outs += [jax.ShapeDtypeStruct((n_wide, n_dp) + tails[-1], LOW)]
    found = pl.pallas_call(
        functools.partial(reduce_kernel, n_wide, n_dp, len(fulls), len(shares)),
        name="reduce_grads",
        out_shape=outs,
        in_specs=[vmem] * (len(fulls) + len(shares)),
        out_specs=[vmem] * len(outs),
        scratch_shapes=[pltpu.VMEM((n_dp, lines) + tail, LOW) for tail in tails]
        + [pltpu.VMEM((n_dp - 1, lines) + tail, LOW) for tail in tails]
        + [pltpu.VMEM((lines - 1,) + tail, LOW) for tail in tails]
        + [pltpu.VMEM((n_dp, lines) + tail, LOW) for tail in tails]
        + [pltpu.VMEM((lines,) + tail, LOW) for tail in tails]
        + [pltpu.VMEM((n_dp - 1,) + share.shape[1:], LOW) for share in shares]
        + [pltpu.SemaphoreType.DMA((copies,)), pltpu.SemaphoreType.DMA((copies,))],
        compiler_params=pltpu.CompilerParams(
            collective_id=ident, has_side_effects=True, vmem_limit_bytes=VMEM_CAP
        ),
    )(*views, *shares)
    return found[: len(fulls)], found[len(fulls) : len(fulls) + len(shares)], found[-1]


def to_pieces(cube, count):
    pairs, rows, width = cube.shape
    if pairs == count:
        return cube
    more = count // pairs
    cube = cube.reshape(pairs, rows, more, width // more).transpose(0, 2, 1, 3)
    return cube.reshape(count, rows, width // more)


def from_pieces(pieces, pairs):
    count, rows, width = pieces.shape
    if pairs == count:
        return pieces
    more = count // pairs
    cube = pieces.reshape(pairs, more, rows, width).transpose(0, 2, 1, 3)
    return cube.reshape(pairs, rows, width * more)


def send_around(value, hop):
    count = lax.axis_size("dp")
    return lax.ppermute(value, "dp", [(at, (at + hop) % count) for at in range(count)])


def scatter_sum(pieces):
    count, me = lax.axis_size("dp"), lax.axis_index("dp")
    total = lax.dynamic_index_in_dim(pieces, me, 0, keepdims=False).astype(FULL)
    arrived = [
        send_around(lax.dynamic_index_in_dim(pieces, (me + hop) % count, 0, keepdims=False), hop)
        for hop in range(1, count)
    ]
    return total, arrived


def add_arrived(total, arrived):
    for part in arrived:
        total = total + part.astype(FULL)
    return total.astype(LOW)


def spread_sum(piece):
    count, me = lax.axis_size("dp"), lax.axis_index("dp")
    found = jnp.zeros((count,) + piece.shape, piece.dtype)
    for hop in range(count):
        part = piece if hop == 0 else send_around(piece, hop)
        found = lax.dynamic_update_index_in_dim(found, part, (me - hop) % count, 0)
    return found


def gather_kernel(n_wide, n_dp, weight_ref, depth_ref, out_ref, depth_out, send, recv):
    lines = n_wide // 2
    me_wide, me_dp = lax.axis_index("wide"), lax.axis_index("dp")
    core, line = lax.rem(me_wide, 2), lax.div(me_wide, 2)
    sibling = {"wide": line * 2 + 1 - core}
    width = out_ref.shape[4]
    used = [0]

    barrier = pltpu.get_barrier_semaphore()
    for k in range(1, n_wide):
        pl.semaphore_signal(
            barrier, inc=1, device_id={"wide": lax.rem(me_wide + k, n_wide)}, device_id_type=MESH
        )
    for k in range(1, n_dp):
        pl.semaphore_signal(
            barrier, inc=1, device_id={"dp": lax.rem(me_dp + k, n_dp)}, device_id_type=MESH
        )
    for piece in range(n_dp):
        out_ref[piece, line, core] = weight_ref[:, piece * width : (piece + 1) * width].astype(LOW)
    depth_out[me_wide] = depth_ref[...]
    pl.semaphore_wait(barrier, n_wide + n_dp - 2)

    def launch(part, device, ref=out_ref):
        copy = pltpu.make_async_remote_copy(
            src_ref=ref.at[part], dst_ref=ref.at[part], send_sem=send.at[used[0]],
            recv_sem=recv.at[used[0]], device_id=device, device_id_type=MESH,
        )
        used[0] += 1
        copy.start()
        return copy

    def dp_from(hop):
        return lax.rem(me_dp + n_dp - hop, n_dp)

    along = [
        launch((me_dp, line, core), {"wide": lax.rem(line + k, lines) * 2 + core})
        for k in range(1, lines)
    ]
    started = [launch((piece, line, core), sibling) for piece in range(n_dp)]
    started += [
        launch((me_wide,), {"wide": lax.rem(me_wide + k, n_wide)}, depth_out)
        for k in range(1, n_wide)
    ]
    across = []
    for k in range(1, lines):
        source = lax.rem(line + lines - k, lines)
        along[k - 1].wait_recv()
        for hop in range(1, n_dp):
            copy = launch((me_dp, source, core), {"dp": lax.rem(me_dp + hop, n_dp)})
            across.append((copy, hop, source))
        started.append(launch((me_dp, source, core), sibling))
    for copy, hop, source in across:
        copy.wait_recv()
        started.append(launch((dp_from(hop), source, core), sibling))
    for copy in started:
        copy.wait()
    for copy in along:
        copy.wait_send()
    for copy, _, _ in across:
        copy.wait_send()


def gather_expand(weight, depth, ident):
    n_wide, n_dp = lax.axis_size("wide"), lax.axis_size("dp")
    lines = n_wide // 2
    height, width = weight.shape
    copies = (lines - 1) * (1 + n_dp) + (lines - 1) * (n_dp - 1) + n_dp + n_wide - 1
    vmem = pl.BlockSpec(memory_space=pltpu.VMEM)
    found, depths = pl.pallas_call(
        functools.partial(gather_kernel, n_wide, n_dp),
        name="gather_expand",
        out_shape=[
            jax.ShapeDtypeStruct((n_dp, lines, 2, height, width // n_dp), LOW),
            jax.ShapeDtypeStruct((n_wide,) + depth.shape, LOW),
        ],
        in_specs=[vmem] * 2,
        out_specs=[vmem] * 2,
        scratch_shapes=[pltpu.SemaphoreType.DMA((copies,)), pltpu.SemaphoreType.DMA((copies,))],
        compiler_params=pltpu.CompilerParams(
            collective_id=ident, has_side_effects=True, vmem_limit_bytes=VMEM_CAP
        ),
    )(weight, depth)
    return found.reshape(n_dp, n_wide * height, width // n_dp), depths


def soap_kernel(
    gained, weight_ref, grad_ref, first_ref, second_ref, state_ref,
    first_out, second_out, state_out, weight_out, raised,
):
    step = pl.program_id(0)
    height, width = weight_ref.shape
    half = width // 2
    upper = -(-half // 128) * 128
    lower = half // 128 * 128
    corr_one = 1.0 - beta_one**STEP
    corr_two = 1.0 - beta_two**STEP

    def iota(shape, axis):
        return lax.broadcasted_iota(jnp.int32, shape, axis)

    pick = (iota((height, BLK), 0) % BLK == iota((height, BLK), 1)).astype(LOW)
    pick_t = (iota((BLK, height), 1) % BLK == iota((BLK, height), 0)).astype(LOW)
    same = iota((height, height), 0) // BLK == iota((height, height), 1) // BLK
    ones = same.astype(LOW)

    def parts(value):
        high = value.astype(LOW)
        return high, (value - high.astype(FULL)).astype(LOW)

    def by_ones(value):
        high, rest = parts(value)
        return dot_nn(high, ones) + dot_nn(rest, ones)

    def spread_out(rows):
        high, rest = parts(rows)
        return jnp.where(same, dot_nn(pick, high) + dot_nn(pick, rest), 0.0)

    def by_half(product, *values):
        first = product(0, *(value[:, :upper] for value in values))
        second = product(1, *(value[:, lower:] for value in values))
        if upper == lower:
            return jnp.concatenate([first, second], axis=1)
        lane = iota((height, upper - lower), 1)
        middle = jnp.where(lane < half - lower, first[:, lower:], second[:, : upper - lower])
        return jnp.concatenate([first[:, :lower], middle, second[:, upper - lower :]], axis=1)

    old = [state_ref[1, 2 * step + side] for side in range(2)]
    turns = [parts(spread_out(rows)) for rows in old]

    def turn(side, high, rest):
        return dot_nn(turns[side][0], high) + dot_nn(turns[side][0], rest) + dot_nn(turns[side][1], high)

    def turn_back(side, high, rest):
        return dot_tn(turns[side][0], high) + dot_tn(turns[side][0], rest) + dot_tn(turns[side][1], high)

    raw = grad_ref[0]
    grad = raw.astype(FULL)
    turned = by_half(
        lambda side, value: dot_nn(turns[side][0], value) + dot_nn(turns[side][1], value), raw
    )
    first_new = beta_one * first_ref[...] + (1.0 - beta_one) * grad
    second_new = beta_two * second_ref[...] + (1.0 - beta_two) * (turned * turned)
    first_out[...] = first_new
    second_out[...] = second_new
    moment = by_half(turn, *parts(first_new))
    ratio = moment / corr_one / (jnp.sqrt(second_new / corr_two) + eps_adam)
    back = by_half(turn_back, *parts(ratio))
    weight = weight_ref[...]
    weight_out[...] = weight - rate_matrix * (back + decay * weight)

    for side in range(2):
        if side == 0:
            piece = grad[:, :upper]
            piece = jnp.where(iota(piece.shape, 1) < half, piece, 0.0)
        else:
            piece = grad[:, lower:]
            piece = jnp.where(iota(piece.shape, 1) >= half - lower, piece, 0.0)
        piece = piece.astype(LOW)
        gram = parts(jnp.where(same, dot_nt(piece, piece), 0.0))
        summed = beta_two * state_ref[0, 2 * step + side]
        summed = summed + (1.0 - beta_two) * gained * (
            dot_nn(pick_t, gram[0]) + dot_nn(pick_t, gram[1])
        )
        diagonal = jnp.sum(summed * pick_t.astype(FULL), axis=0, keepdims=True)
        stats = summed / by_ones(diagonal)
        state_out[0, 2 * step + side] = stats
        high, rest = parts(old[side])
        wide_high, wide_rest = parts(spread_out(stats))
        lifted = dot_nn(high, wide_high) + dot_nn(high, wide_rest) + dot_nn(rest, wide_high)
        for column in range(BLK):
            raised[column, pl.ds(2 * step + side, 1), :] = lifted[column : column + 1]

    @pl.when(step == pl.num_programs(0) - 1)
    def _():
        columns = []
        for index in range(BLK):
            column = raised[index]
            for previous in columns:
                column = column - by_ones(previous * column) * previous
            column = column * lax.rsqrt(by_ones(column * column))
            columns.append(column)
            for expert in range(EXPERTS):
                state_out[1, expert, index : index + 1, :] = column[expert : expert + 1]


def soap(weight, grad, first, second, state, every):
    height, total = weight.shape
    width = total // PAIRS
    turned_state = state.transpose(0, 1, 3, 2)
    gained = stat_gain * every / (total // EXPERTS)
    column = pl.BlockSpec((height, width), lambda i: (0, i))
    first_new, second_new, state_new, weight_new = device_kernel(
        functools.partial(soap_kernel, gained),
        "soap",
        PAIRS,
        [
            column, pl.BlockSpec((1, height, width), lambda i: (i, 0, 0)), column, column,
            whole(2, EXPERTS, BLK, height),
        ],
        [(weight.shape, FULL), (weight.shape, FULL), (turned_state.shape, FULL),
         (weight.shape, FULL)],
        [column, column, total_block(2, EXPERTS, BLK, height), column],
        [pltpu.VMEM((BLK, EXPERTS, height), FULL)],
        2 * height * height * total,
        weight.size * 26,
    )(weight, grad, first, second, turned_state)
    return (first_new, second_new, state_new.transpose(0, 1, 3, 2), weight_new)


def adam(weight, grad, first, second, rate):
    corr_one = 1.0 - beta_one**STEP
    corr_two = 1.0 - beta_two**STEP
    first_new = beta_one * first + (1.0 - beta_one) * grad
    second_new = beta_two * second + (1.0 - beta_two) * grad * grad
    weight_new = weight - rate * (
        first_new / corr_one / (jnp.sqrt(second_new / corr_two) + eps_adam) + decay * weight
    )
    return (first_new, second_new, weight_new)


def local(
    images,
    dom_label,
    class_label,
    expand_weight,
    expand_first,
    expand_second,
    expand_state,
    project_weight,
    project_first,
    project_second,
    project_state,
    head_weight,
    head_first,
    head_second,
    head_state,
    depth_weight,
    depth_first,
    depth_second,
    classifier_weight,
    classifier_first,
    classifier_second,
    excite_weight,
    excite_first,
    excite_second,
    router_weight,
    router_first,
    router_second,
    gains_weight,
    gains_first,
    gains_second,
):
    low_type = jnp.bfloat16
    images_here = images.shape[0]
    every = images.shape[0] * lax.axis_size("dp") * lax.axis_size("wide")
    count = every * PIX
    n_wide, n_dp = lax.axis_size("wide"), lax.axis_size("dp")
    bias_se, bias_ex, gain_one, shift_one, gain_two, shift_two, bias_cls = split_gains(gains_weight)
    hot = boost * (dom_label[:, None] == jnp.arange(EXPERTS)[None, :]).astype(jnp.float32)
    img = images.transpose(1, 0, 2)
    img_two = jnp.concatenate([img, img], axis=2)
    project_low = lax.all_gather(project_weight.astype(low_type), "wide", axis=0, tiled=True)
    head_low = lax.all_gather(head_weight.astype(low_type), "wide", axis=0, tiled=True)
    class_low = lax.all_gather(classifier_weight.astype(low_type), "wide", axis=0, tiled=True)
    taps = KSIZE * KSIZE
    depth_own = depth_weight.transpose(1, 0, 2).reshape(taps * EXPERTS, -1).astype(low_type)
    depth_own = jnp.pad(depth_own, ((0, -taps * EXPERTS % 16), (0, 0)))
    expand_low, depth_low = gather_expand(expand_weight, depth_own, 6)
    expand_low = from_pieces(expand_low, PAIRS)
    depth_full = depth_low[:, : taps * EXPERTS].reshape(n_wide, taps, EXPERTS, -1)
    depth_full = depth_full.transpose(1, 2, 0, 3).reshape(taps, EXPERTS, C_MID).astype(FULL)
    excite = excite_weight.transpose(0, 2, 1)
    router = router_weight.T
    router_one, router_two = router[:, :C_IN], router[:, C_IN:]

    (
        hidden, turned, scaled, route_one, pair_in, pair_one, gate, squeeze, pooled_one,
        pooled_act, route_one_sum,
    ) = expand_forward(
        img_two, hot, router_one, expand_low, depth_full, excite, bias_se[None], bias_ex[None]
    )
    each, before, norm_one, route_one_sum = project_forward(
        scaled, project_low, pair_one, route_one_sum, gain_one[None], shift_one[None], every, 1
    )
    widened, twice, route_two, pair_two, pooled_two, norm_two, route_two_sum = head_forward(
        before, norm_one, hot, router_two, head_low, gain_two[None], shift_two[None], every, 2
    )
    feats, grad_logits, grad_feats, coef_two, back_two, cross_total, grad_bias_cls = loss_part(
        widened, norm_two, class_label[:, None], class_low, bias_cls[None], every, 3
    )
    grad_class = jnp.stack(
        [dot_tn(feats, part).astype(low_type) for part in jnp.split(grad_logits, PAIRS, axis=1)]
    )
    grad_class, grad_feats = lax.optimization_barrier((grad_class, grad_feats))
    share_class = lax.psum_scatter(grad_class, "wide", scatter_dimension=1, tiled=True)
    means_one = route_one_sum[0] / every
    means_two = route_two_sum[0] / every
    grad_widened, grad_normed, grad_logit_two, back_one = head_back(
        widened, grad_feats, coef_two, head_low, pair_two, twice, before, norm_one, route_two,
        balance_grad(means_two, every)[None], router_two,
    )
    coef_one, back_one, grad_head = head_grad(
        back_one, norm_one, grad_widened, twice, pair_two, every, 4
    )
    coef_one, share_class = lax.optimization_barrier((coef_one, share_class))
    share_head = lax.psum_scatter(grad_head, "wide", scatter_dimension=1, tiled=True)
    grad_router_two = dot_tn(pooled_two, grad_logit_two, HIGH)
    grad_before, grad_scaled, route_project = project_back(
        grad_normed, before, coef_one, pair_one, each, project_low
    )
    row_scale = jnp.tile(route_one.astype(low_type).T, (1, PIX)).reshape(PAIRS, 2, -1)
    grad_project = project_grad(grad_before, scaled, row_scale, n_wide)
    grad_project, grad_scaled, share_head = lax.optimization_barrier(
        (grad_project, grad_scaled, share_head)
    )
    wide_head = share_head.shape[2]
    own_late, arrived = scatter_sum(
        to_pieces(jnp.concatenate([share_head, share_class], axis=2), n_dp)
    )
    share_project = lax.psum_scatter(grad_project, "wide", scatter_dimension=0, tiled=True)[0]
    grad_hidden, grad_logit_one, grad_gate, grad_squeeze, grad_depth = expand_back(
        grad_scaled, turned, hidden, img_two, gate, squeeze, excite, depth_full, route_one,
        route_project, balance_grad(means_one, every)[None], expand_low,
    )
    arrived, share_project, grad_hidden = lax.optimization_barrier(
        (arrived, share_project, grad_hidden)
    )
    sum_late = spread_sum(add_arrived(own_late, arrived))
    own_project, arrived = scatter_sum(to_pieces(share_project, n_dp))
    grad_expand = kern_grad(grad_hidden, img_two, pair_in, "expand_grad")
    grad_excite = jnp.stack(
        [
            dot_tn(grad_squeeze, pooled_act, HIGH),
            dot_tn(squeeze * jax.nn.sigmoid(squeeze), grad_gate, HIGH),
        ]
    )
    grad_router_one = dot_tn(pooled_one, grad_logit_one, HIGH)
    grad_depth = grad_depth.transpose(1, 0, 2)
    grad_bias_se = jnp.sum(grad_squeeze, axis=0)
    grad_bias_ex = jnp.sum(grad_gate, axis=0)
    sum_late, arrived, grad_expand = lax.optimization_barrier((sum_late, arrived, grad_expand))
    sum_late = from_pieces(sum_late, PAIRS)
    sum_head, sum_class = sum_late[:, :, :wide_head], sum_late[:, :, wide_head:]
    sum_project = from_pieces(spread_sum(add_arrived(own_project, arrived)), PAIRS)
    share_expand = lax.psum_scatter(grad_expand, "wide", scatter_dimension=1, tiled=True)
    parts = n_wide * n_dp
    depth_part = grad_depth.reshape(taps * EXPERTS, n_wide, -1).transpose(1, 0, 2)
    depth_part = depth_part.reshape(n_wide, n_dp, taps * EXPERTS // n_dp, -1).transpose(1, 0, 2, 3)
    rest = jnp.concatenate(
        [
            grad_excite.reshape(-1), grad_router_one.reshape(-1), grad_router_two.reshape(-1),
            grad_bias_se, grad_bias_ex,
        ]
    )
    rest_size = rest.size
    rest_rows = -(-rest_size // (parts * 16 * 128)) * 16
    rest = jnp.pad(rest.astype(low_type), (0, parts * rest_rows * 128 - rest_size))
    rest = rest.reshape(n_dp, n_wide, rest_rows, 128)
    head_out = soap(head_weight, sum_head, head_first, head_second, head_state, every)
    project_out = soap(
        project_weight, sum_project, project_first, project_second, project_state, every
    )
    sum_class = sum_class.transpose(1, 0, 2).reshape(-1, CLASS_PAD)[:, :CLASSES].astype(FULL)
    class_out = adam(
        classifier_weight, sum_class, classifier_first, classifier_second, rate_matrix
    )
    share_expand, head_out, project_out, class_out = lax.optimization_barrier(
        (share_expand, head_out, project_out, class_out)
    )
    (own_depth, _), (own_expand,), rest = reduce_grads(
        [depth_part.astype(low_type), rest], [to_pieces(share_expand, n_dp)], 5
    )
    sum_expand = from_pieces(own_expand, PAIRS)
    sum_depth = own_depth.reshape(EXPERTS, taps, -1).astype(FULL)
    rest = rest.transpose(1, 0, 2, 3).reshape(-1, 128)
    split = grad_excite.size // 128
    sum_excite = rest[:split].reshape(2, C_SE, C_MID).transpose(0, 2, 1).astype(FULL)
    rest = rest[split:].reshape(-1)[: rest_size - grad_excite.size].astype(FULL)
    sum_router = rest[: router_weight.size].reshape(router_weight.shape)
    sum_bias = rest[router_weight.size :]
    loss = cross_total[0, 0] / every + balance_weight * (
        jnp.mean((means_one - jnp.mean(means_one)) ** 2)
        + jnp.mean((means_two - jnp.mean(means_two)) ** 2)
    )
    grad_gains = jnp.concatenate(
        [sum_bias, back_one[1], back_one[0], back_two[1], back_two[0], grad_bias_cls[0]]
    )
    expand_out = soap(expand_weight, sum_expand, expand_first, expand_second, expand_state, every)
    depth_out = adam(
        depth_weight, sum_depth, depth_first, depth_second, rate_matrix
    )
    excite_out = adam(excite_weight, sum_excite, excite_first, excite_second, rate_matrix)
    router_out = adam(router_weight, sum_router, router_first, router_second, rate_matrix)
    gains_out = adam(gains_weight, grad_gains, gains_first, gains_second, rate_gains)
    return (
        loss,
        expand_out[0],
        expand_out[1],
        expand_out[2],
        expand_out[3],
        project_out[0],
        project_out[1],
        project_out[2],
        project_out[3],
        head_out[0],
        head_out[1],
        head_out[2],
        head_out[3],
        depth_out[0],
        depth_out[1],
        depth_out[2],
        class_out[0],
        class_out[1],
        class_out[2],
        excite_out[0],
        excite_out[1],
        excite_out[2],
        router_out[0],
        router_out[1],
        router_out[2],
        gains_out[0],
        gains_out[1],
        gains_out[2],
    )


def solution(mesh):
    return jax.shard_map(
        local,
        mesh=mesh,
        in_specs=(
            P(("dp", "wide"), None, None),
            P(("dp", "wide")),
            P(("dp", "wide")),
            P("wide", None),
            P("wide", None),
            P("wide", None),
            P(None, None, "wide", None),
            P("wide", None),
            P("wide", None),
            P("wide", None),
            P(None, None, "wide", None),
            P("wide", None),
            P("wide", None),
            P("wide", None),
            P(None, None, "wide", None),
            P(None, None, "wide"),
            P(None, None, "wide"),
            P(None, None, "wide"),
            P("wide", None),
            P("wide", None),
            P("wide", None),
            P(),
            P(),
            P(),
            P(),
            P(),
            P(),
            P(),
            P(),
            P(),
        ),
        out_specs=(
            P(),
            P("wide", None),
            P("wide", None),
            P(None, None, "wide", None),
            P("wide", None),
            P("wide", None),
            P("wide", None),
            P(None, None, "wide", None),
            P("wide", None),
            P("wide", None),
            P("wide", None),
            P(None, None, "wide", None),
            P("wide", None),
            P(None, None, "wide"),
            P(None, None, "wide"),
            P(None, None, "wide"),
            P("wide", None),
            P("wide", None),
            P("wide", None),
            P(),
            P(),
            P(),
            P(),
            P(),
            P(),
            P(),
            P(),
            P(),
        ),
        check_vma=False,
    )
```
